32 devices in a mesh: ctx: 16 (over z, y, x), wsh: 2 (over core).
Axes of the slice: x: 2, y: 2, z: 4, core: 2. Of those that a mesh axis runs over, the one named last changes fastest.
Arguments:
- tokens_in: bfloat16 [8192, 1088], P(('ctx', 'wsh')), may hold values from -6 to 6
- doc_lengths: int32 [8], replicated, may hold values from 1 to 4096, 8192 in all
- doc_adapter: int32 [8], replicated, may hold values from 0 to 7
- norm1_gain: bfloat16 [1088], P('wsh'), may hold values from 0.5 to 1.5
- norm1_bias: bfloat16 [1088], P('wsh'), may hold values from -1.75 to 1.75
- norm2_gain: bfloat16 [1088], P('wsh'), may hold values from 0.5 to 1.5
- norm2_bias: bfloat16 [1088], P('wsh'), may hold values from -1.75 to 1.75
- w_query: bfloat16 [1088, 1088], P('wsh'), may hold values from -0.1875 to 0.1875
- w_key: bfloat16 [1088, 1088], P('wsh'), may hold values from -0.1875 to 0.1875
- w_value: bfloat16 [1088, 1088], P('wsh'), may hold values from -0.1875 to 0.1875
- w_out: bfloat16 [1088, 1088], P('wsh'), may hold values from -0.75 to 0.75
- w_up: bfloat16 [1088, 4352], P('wsh'), may hold values from -0.1875 to 0.1875
- w_down: bfloat16 [4352, 1088], P(None, 'wsh'), may hold values from -0.09375 to 0.09375
- a_query: bfloat16 [1088, 128], replicated, may hold values from -0.1875 to 0.1875
- b_query: bfloat16 [128, 1088], replicated, may hold values from -1.5 to 1.5
- a_key: bfloat16 [1088, 128], replicated, may hold values from -0.1875 to 0.1875
- b_key: bfloat16 [128, 1088], replicated, may hold values from -1.5 to 1.5
- a_value: bfloat16 [1088, 128], replicated, may hold values from -0.1875 to 0.1875
- b_value: bfloat16 [128, 1088], replicated, may hold values from -1.5 to 1.5
- a_out: bfloat16 [1088, 128], replicated, may hold values from -0.75 to 0.75
- b_out: bfloat16 [128, 1088], replicated, may hold values from -1.5 to 1.5
- a_up: bfloat16 [1088, 128], replicated, may hold values from -0.1875 to 0.1875
- b_up: bfloat16 [128, 4352], replicated, may hold values from -1.5 to 1.5
- a_down: bfloat16 [4352, 128], replicated, may hold values from -0.09375 to 0.09375
- b_down: bfloat16 [128, 1088], replicated, may hold values from -1.5 to 1.5
- cotangent: bfloat16 [8192, 1088], P(('ctx', 'wsh')), may hold values from -6 to 6
Outputs:
- output: bfloat16 [8192, 1088], P(('ctx', 'wsh'))
- grad_in: bfloat16 [8192, 1088], P(('ctx', 'wsh'))
- grad_a_query: float32 [1088, 128], replicated
- grad_b_query: float32 [128, 1088], replicated
- grad_a_key: float32 [1088, 128], replicated
- grad_b_key: float32 [128, 1088], replicated
- grad_a_value: float32 [1088, 128], replicated
- grad_b_value: float32 [128, 1088], replicated
- grad_a_out: float32 [1088, 128], replicated
- grad_b_out: float32 [128, 1088], replicated
- grad_a_up: float32 [1088, 128], replicated
- grad_b_up: float32 [128, 4352], replicated
- grad_a_down: float32 [4352, 128], replicated
- grad_b_down: float32 [128, 1088], replicated
The draws below stay inside these ranges and needn't reach their ends.
Inputs may be any that keep to these rules, and one draw needn't show every extreme that they name: `doc_lengths`: the documents lie end to end in the stream and fill it; the longest has exactly 4096 tokens.
All inputs are finite; a program needn't handle non-finite values.
Results may differ from the reference program's by a relative error of at most 0.019.
Values may be sent and summed in bfloat16 or wider, within the bound.
No kernel may reach another device: no remote copies, remote signals or barrier semaphores. Data moves between devices by JAX's collectives and lax.ppermute only.
A program may use at most 320 MiB of HBM per device.

```python
import math
import jax
import jax.numpy as jnp
import numpy as np
from jax import lax

HEADS = 17
HEAD = 64
D = 1088
FF = 4352
RANK = 16
ADAPTERS = 8
ADW = 128
TOK_DEV = 256
DOC_MAX = 4096
TOK_BLK = 512
HOPS = 8
TOKENS = 8192
NDOCS = 8
N_WSH = 2


def with_ends(entries, own_key, smallest, largest):
    spot = [jax.random.randint(jax.random.fold_in(own_key, axis), (), 0, length) for axis, length in enumerate(entries.shape)]
    main_axis = entries.shape.index(max(entries.shape))
    next_to = spot[:main_axis] + [(spot[main_axis] + 1) % entries.shape[main_axis]] + spot[main_axis + 1:]
    return entries.at[tuple(spot)].set(smallest).at[tuple(next_to)].set(largest)


def level_of(own_key, extent, split, low, largest):
    level = 1.0
    for dim, shards_of in split:
        heights = jax.random.uniform(jax.random.fold_in(jax.random.fold_in(own_key, 6), dim), (shards_of,), jnp.float32, low / len(split), largest / len(split))
        level = level * jnp.repeat(jnp.exp(heights), extent[dim] // shards_of).reshape((-1,) + (1,) * (len(extent) - 1 - dim))
    return level


def split_up(count, total, limit, skew):
    portions = [(1 << 20) // math.isqrt(rank ** skew) + 1 for rank in range(2, count + 1)]
    spare, given = total - limit - (count - 1), [1] * (count - 1)
    while spare > 0:
        candidates = [i for i in range(count - 1) if given[i] < limit]
        whole, budget = sum([portions[i] for i in candidates]), spare
        for i in candidates:
            extra = min(limit - given[i], max(1, budget * portions[i] // whole), spare)
            given[i] = given[i] + extra
            spare = spare - extra
    return np.array([limit] + given)


def ragged(stream_key, number_of, total, bound, slope):
    if number_of == 2:
        one = jax.random.randint(stream_key, (), max(1, total - bound), min(bound, total - 1) + 1)
        return jnp.stack([one, total - one])
    lengths = jnp.asarray(split_up(number_of, total, bound, slope), jnp.int32)
    twos = (number_of - 1) // 2
    giver, taker = lengths[1:1 + 2 * twos:2], lengths[2:2 + 2 * twos:2]
    slack = jnp.minimum(giver - 1, bound - taker)
    moved = jax.random.randint(jax.random.fold_in(stream_key, 1), (twos,), 0, 1 << 20) % (slack + 1)
    lengths = lengths.at[1:1 + 2 * twos:2].set(giver - moved).at[2:2 + 2 * twos:2].set(taker + moved)
    return lengths[jax.random.permutation(jax.random.fold_in(stream_key, 2), number_of)]


def scatter_about(own_key, dims, scale, most, pieces=(), kind=jnp.bfloat16):
    values = jax.random.normal(own_key, dims, jnp.float32) * scale
    if len(pieces) > 0:
        values = level_of(own_key, dims, pieces, -0.22, 0.18) * values
    return jnp.clip(values, min=-most, max=most).astype(kind)


def setup_inputs(seed: int = 0) -> dict:
    splits = jax.random.split(jax.random.key(seed), 27)
    return {
        "tokens_in": scatter_about(splits[0], (TOKENS, D), 1.0, 6.0, ((0, 32),)),
        "doc_lengths": ragged(splits[1], NDOCS, TOKENS, DOC_MAX, 1).astype(jnp.int32),
        "doc_adapter": with_ends(jax.random.randint(splits[2], (NDOCS,), 0, ADAPTERS), jax.random.fold_in(splits[2], 1), 0, ADAPTERS - 1).astype(jnp.int32),
        "norm1_gain": jnp.clip(1.0 + 0.1 * jax.random.normal(splits[3], (D,), jnp.float32), 0.5, 1.5).astype(jnp.bfloat16),
        "norm1_bias": scatter_about(splits[4], (D,), 0.3, 1.75, ((0, 2),)),
        "norm2_gain": jnp.clip(1.0 + 0.1 * jax.random.normal(splits[5], (D,), jnp.float32), 0.5, 1.5).astype(jnp.bfloat16),
        "norm2_bias": scatter_about(splits[6], (D,), 0.3, 1.75, ((0, 2),)),
        "w_query": scatter_about(splits[7], (D, D), D ** -0.5, 0.1875, ((0, 2),)),
        "w_key": scatter_about(splits[8], (D, D), D ** -0.5, 0.1875, ((0, 2),)),
        "w_value": scatter_about(splits[9], (D, D), D ** -0.5, 0.1875, ((0, 2),)),
        "w_out": scatter_about(splits[10], (D, D), (D // 16) ** -0.5, 0.75, ((0, 2),)),
        "w_up": scatter_about(splits[11], (D, FF), D ** -0.5, 0.1875, ((0, 2),)),
        "w_down": scatter_about(splits[12], (FF, D), FF ** -0.5, 0.09375, ((1, 2),)),
        "a_query": scatter_about(splits[13], (D, ADW), D ** -0.5, 0.1875),
        "b_query": scatter_about(splits[14], (ADW, D), RANK ** -0.5, 1.5),
        "a_key": scatter_about(splits[15], (D, ADW), D ** -0.5, 0.1875),
        "b_key": scatter_about(splits[16], (ADW, D), RANK ** -0.5, 1.5),
        "a_value": scatter_about(splits[17], (D, ADW), D ** -0.5, 0.1875),
        "b_value": scatter_about(splits[18], (ADW, D), RANK ** -0.5, 1.5),
        "a_out": scatter_about(splits[19], (D, ADW), (D // 16) ** -0.5, 0.75),
        "b_out": scatter_about(splits[20], (ADW, D), RANK ** -0.5, 1.5),
        "a_up": scatter_about(splits[21], (D, ADW), D ** -0.5, 0.1875),
        "b_up": scatter_about(splits[22], (ADW, FF), RANK ** -0.5, 1.5),
        "a_down": scatter_about(splits[23], (FF, ADW), FF ** -0.5, 0.09375),
        "b_down": scatter_about(splits[24], (ADW, D), RANK ** -0.5, 1.5),
        "cotangent": scatter_about(splits[25], (TOKENS, D), 1.0, 6.0, ((0, 32),)),
    }


@jax.custom_vjp
def low(v):
    return lax.optimization_barrier(v.astype(jnp.bfloat16)).astype(jnp.float32)

@jax.custom_vjp
def low_back(v):
    return v

def low_keep(v):
    return (low(v), None)

def low_pass(kept, grad):
    return (grad,)

def back_keep(v):
    return (v, None)

def back_low(kept, grad):
    return (low(grad),)
low.defvjp(low_keep, low_pass)
low_back.defvjp(back_keep, back_low)
EPSILON = 1e-05
NEG_FILL = -1e+30
HIGH = lax.Precision.HIGHEST

def layer_norm(values, gain, shift):
    row_mean = lax.optimization_barrier(jnp.mean(values, axis=-1, keepdims=True))
    centered = values - row_mean
    variance = lax.optimization_barrier(jnp.mean(centered * centered, axis=-1, keepdims=True))
    return centered * lax.rsqrt(variance + EPSILON) * gain + shift

def plain_dot(left, right):
    return jnp.dot(left, right, precision=HIGH, preferred_element_type=jnp.float32)

def adapted(hidden, weight, down_a, up_b, adapter_mask):
    inner = low(low_back(adapter_mask * plain_dot(hidden, down_a)))
    return plain_dot(hidden, weight) + plain_dot(inner, up_b)

def document_of(positions, doc_ends):
    inside = (doc_ends[None, :] <= positions[:, None]).astype(jnp.int32)
    return lax.optimization_barrier(jnp.sum(inside, axis=1)).astype(jnp.int32)

def attention(query, keys, values, doc_index):
    reach = HOPS * TOK_BLK
    span = reach + TOK_BLK
    keys_pad = jnp.concatenate([jnp.zeros((reach, D), jnp.float32), keys], axis=0)
    values_pad = jnp.concatenate([jnp.zeros((reach, D), jnp.float32), values], axis=0)
    docs_pad = jnp.concatenate([jnp.full((reach,), -1, jnp.int32), doc_index], axis=0)
    scaling = HEAD ** (-0.5)

    @jax.checkpoint
    def one_block(number):
        row_start = (number * TOK_DEV).astype(jnp.int32)
        key_start = (number // N_WSH * TOK_BLK).astype(jnp.int32)
        query_rows = lax.dynamic_slice_in_dim(query, row_start, TOK_DEV, 0).reshape(TOK_DEV, HEADS, HEAD)
        key_rows = lax.dynamic_slice_in_dim(keys_pad, key_start, span, 0).reshape(span, HEADS, HEAD)
        value_rows = lax.dynamic_slice_in_dim(values_pad, key_start, span, 0).reshape(span, HEADS, HEAD)
        query_docs = lax.dynamic_slice_in_dim(doc_index, row_start, TOK_DEV, 0)
        key_docs = lax.dynamic_slice_in_dim(docs_pad, key_start, span, 0)
        query_pos = row_start + reach + jnp.arange(TOK_DEV, dtype=jnp.int32)
        key_pos = key_start + jnp.arange(span, dtype=jnp.int32)
        allowed = (key_docs[None, :] == query_docs[:, None]) & (key_pos[None, :] <= query_pos[:, None])
        scores = low_back(jnp.einsum('qhd,khd->hqk', query_rows, key_rows, precision=HIGH) * scaling)
        scores = jnp.where(allowed[None], scores, NEG_FILL)
        row_max = lax.optimization_barrier(jnp.max(scores, axis=-1, keepdims=True))
        exponent = jnp.exp(scores - row_max)
        probs = low(exponent / lax.optimization_barrier(jnp.sum(exponent, axis=-1, keepdims=True)))
        mixed = jnp.einsum('hqk,khd->qhd', probs, value_rows, precision=HIGH)
        return mixed.reshape(TOK_DEV, D)
    numbers = jnp.arange(TOKENS // TOK_DEV, dtype=jnp.int32)
    return lax.map(one_block, numbers).reshape(TOKENS, D)

def reference(tokens_in, doc_lengths, doc_adapter, norm1_gain, norm1_bias, norm2_gain, norm2_bias, w_query, w_key, w_value, w_out, w_up, w_down, a_query, b_query, a_key, b_key, a_value, b_value, a_out, b_out, a_up, b_up, a_down, b_down, cotangent):
    doc_ends = jnp.cumsum(doc_lengths).astype(jnp.int32)
    positions = jnp.arange(TOKENS, dtype=jnp.int32)
    doc_index = document_of(positions, doc_ends)
    doc_numbers = jnp.arange(NDOCS, dtype=jnp.int32)
    token_adapter = lax.optimization_barrier(jnp.sum(jnp.where(doc_index[:, None] == doc_numbers[None, :], doc_adapter[None, :], 0), axis=1)).astype(jnp.int32)
    columns = jnp.arange(ADW, dtype=jnp.int32) // RANK
    adapter_mask = (token_adapter[:, None] == columns[None, :]).astype(jnp.float32)
    gains = [item.astype(jnp.float32) for item in (norm1_gain, norm1_bias, norm2_gain, norm2_bias)]
    mains = [item.astype(jnp.float32) for item in (w_query, w_key, w_value, w_out, w_up, w_down)]
    adapters = tuple((item.astype(jnp.float32) for item in (a_query, b_query, a_key, b_key, a_value, b_value, a_out, b_out, a_up, b_up, a_down, b_down)))

    def forward(stream, pairs):
        hidden_one = low(layer_norm(stream, gains[0], gains[1]))
        query = low(low_back(adapted(hidden_one, mains[0], pairs[0], pairs[1], adapter_mask)))
        keys = low(low_back(adapted(hidden_one, mains[1], pairs[2], pairs[3], adapter_mask)))
        values = low(low_back(adapted(hidden_one, mains[2], pairs[4], pairs[5], adapter_mask)))
        mixed = low(low_back(attention(query, keys, values, doc_index)))
        middle = stream + low_back(adapted(mixed, mains[3], pairs[6], pairs[7], adapter_mask))
        hidden_two = low(layer_norm(middle, gains[2], gains[3]))
        upward = low_back(adapted(hidden_two, mains[4], pairs[8], pairs[9], adapter_mask))
        active = low(jax.nn.gelu(upward, approximate=True))
        return middle + adapted(active, mains[5], pairs[10], pairs[11], adapter_mask)
    stream = tokens_in.astype(jnp.float32)
    result, pullback = jax.vjp(forward, stream, adapters)
    grad_stream, grad_pairs = pullback(cotangent.astype(jnp.float32))
    norm_factor = TOKENS ** (-0.5)
    return (result.astype(jnp.bfloat16), grad_stream.astype(jnp.bfloat16), grad_pairs[0] * norm_factor, grad_pairs[1] * norm_factor, grad_pairs[2] * norm_factor, grad_pairs[3] * norm_factor, grad_pairs[4] * norm_factor, grad_pairs[5] * norm_factor, grad_pairs[6] * norm_factor, grad_pairs[7] * norm_factor, grad_pairs[8] * norm_factor, grad_pairs[9] * norm_factor, grad_pairs[10] * norm_factor, grad_pairs[11] * norm_factor)
```

```python
import jax
import jax.numpy as jnp
from jax import lax
from jax.experimental import pallas as pl
from jax.experimental.pallas import tpu as pltpu
from jax.sharding import PartitionSpec as P

HEAD = 64
RANK = 16
DOC_MAX = 4096


EPSILON = 1e-05
NEG_FILL = -1e30
SCALING = HEAD ** (-0.5)
SWAP = [(0, 1), (1, 0)]
VMEM_BYTES = 48 * 1024 * 1024


def norm_parts(values, gain, shift):
    row_mean = jnp.mean(values, axis=-1, keepdims=True)
    centered = values - row_mean
    variance = jnp.mean(centered * centered, axis=-1, keepdims=True)
    inverse = lax.rsqrt(variance + EPSILON)
    normed = centered * inverse
    return (normed * gain + shift, normed, inverse)


def norm_back(grad, normed, inverse, gain):
    scaled = grad * gain
    return inverse * (
        scaled
        - jnp.mean(scaled, axis=-1, keepdims=True)
        - normed * jnp.mean(scaled * normed, axis=-1, keepdims=True)
    )


def dot(left, right, lc=1, rc=0):
    return lax.dot_general(
        left, right, (((lc,), (rc,)), ((), ())), preferred_element_type=jnp.float32
    )


def query_columns(meta_ref, starts_ref, i):
    rows = lax.broadcasted_iota(jnp.int32, (starts_ref.shape[1], 1), 0)
    return starts_ref[i], meta_ref[i, 2] + rows


def masked_scores(query, keys, j, first_key, doc_start, query_pos):
    scores = dot(query, keys)
    key_pos = first_key + j * keys.shape[1] + lax.broadcasted_iota(jnp.int32, (1, keys.shape[1]), 1)
    allowed = (key_pos >= doc_start) & (key_pos <= query_pos)
    return jnp.where(allowed, scores, NEG_FILL)


def forward_kernel(meta_ref, starts_ref, query_ref, pair_ref, low_ref, mixed_ref, lse_ref):
    chunks, _, rows = query_ref.shape

    def chunk(i, carry):
        query = (query_ref[i].astype(jnp.float32) * SCALING).T.astype(jnp.bfloat16)
        doc_start, query_pos = query_columns(meta_ref, starts_ref, i)
        offset = pl.multiple_of(meta_ref[i, 3], 2 * HEAD)

        def block(j, state):
            row_max, row_sum, total = state
            keys = pair_ref[j, pl.ds(offset, HEAD), :]
            values = pair_ref[j, pl.ds(offset + HEAD, HEAD), :]
            scores = masked_scores(query, keys, j, meta_ref[i, 4], doc_start, query_pos)
            new_max = jnp.maximum(row_max, jnp.max(scores, axis=1, keepdims=True))
            probs = jnp.exp(scores - new_max)
            shrink = jnp.exp(row_max - new_max)
            row_sum = row_sum * shrink + jnp.sum(probs, axis=1, keepdims=True)
            total = total * shrink + dot(probs.astype(jnp.bfloat16), values, 1, 1)
            return new_max, row_sum, total

        state = (
            jnp.full((rows, 1), NEG_FILL, jnp.float32),
            jnp.zeros((rows, 1), jnp.float32),
            jnp.zeros((rows, HEAD), jnp.float32),
        )
        row_max, row_sum, total = lax.fori_loop(meta_ref[i, 0], meta_ref[i, 1] + 1, block, state)
        mixed = total / row_sum
        mixed_ref[i] = mixed
        low_ref[i] = mixed.T.astype(jnp.bfloat16)
        lse_ref[i] = row_max + jnp.log(row_sum)
        return carry

    lax.fori_loop(0, chunks, chunk, 0)


def backward_kernel(
    meta_ref, starts_ref, query_ref, pair_ref, grad_ref, mixed_ref, lse_ref, dq_ref, dpair_ref, sum_ref
):
    chunks, _, rows = query_ref.shape
    blocks = pair_ref.shape[0]

    def clear(j, carry):
        sum_ref[j] = jnp.zeros(sum_ref.shape[1:], jnp.float32)
        return carry

    lax.fori_loop(0, blocks, clear, 0)

    def chunk(i, carry):
        query_f = query_ref[i].astype(jnp.float32) * SCALING
        query_t = query_f.astype(jnp.bfloat16)
        query = query_f.T.astype(jnp.bfloat16)
        grad_t = grad_ref[i]
        grad_f = grad_t.astype(jnp.float32).T
        grad = grad_f.astype(jnp.bfloat16)
        delta = jnp.sum(grad_f * mixed_ref[i], axis=1, keepdims=True)
        lse = lse_ref[i]
        doc_start, query_pos = query_columns(meta_ref, starts_ref, i)
        offset = pl.multiple_of(meta_ref[i, 3], 2 * HEAD)

        def block(j, total):
            keys = pair_ref[j, pl.ds(offset, HEAD), :]
            values = pair_ref[j, pl.ds(offset + HEAD, HEAD), :]
            scores = masked_scores(query, keys, j, meta_ref[i, 4], doc_start, query_pos)
            probs = jnp.exp(scores - lse)
            prob_grad = dot(grad, values)
            score_grad = (probs * (prob_grad - delta)).astype(jnp.bfloat16)
            sum_ref[j, pl.ds(offset, HEAD), :] += dot(query_t, score_grad)
            sum_ref[j, pl.ds(offset + HEAD, HEAD), :] += dot(grad_t, probs.astype(jnp.bfloat16))
            return total + dot(score_grad, keys, 1, 1)

        total = lax.fori_loop(
            meta_ref[i, 0], meta_ref[i, 1] + 1, block, jnp.zeros((rows, HEAD), jnp.float32)
        )
        dq_ref[i] = (total * SCALING).T.astype(jnp.bfloat16)
        return carry

    lax.fori_loop(0, chunks, chunk, 0)

    def finish(j, carry):
        dpair_ref[j] = sum_ref[j].astype(jnp.bfloat16)
        return carry

    lax.fori_loop(0, blocks, finish, 0)


SMEM_SPEC = pl.BlockSpec(memory_space=pltpu.SMEM)
VMEM_SPEC = pl.BlockSpec(memory_space=pltpu.VMEM)


def attention_forward(meta, starts, query, pair):
    chunks, _, rows = query.shape
    return pl.pallas_call(
        forward_kernel,
        out_shape=(
            jax.ShapeDtypeStruct(query.shape, jnp.bfloat16),
            jax.ShapeDtypeStruct((chunks, rows, HEAD), jnp.float32),
            jax.ShapeDtypeStruct((chunks, rows, 1), jnp.float32),
        ),
        in_specs=[SMEM_SPEC] + [VMEM_SPEC] * 3,
        out_specs=(VMEM_SPEC,) * 3,
        compiler_params=pltpu.CompilerParams(vmem_limit_bytes=VMEM_BYTES),
        name="attention_forward",
    )(meta, starts, query, pair)


def attention_backward(meta, starts, query, pair, grad, mixed, lse):
    return pl.pallas_call(
        backward_kernel,
        out_shape=(
            jax.ShapeDtypeStruct(query.shape, jnp.bfloat16),
            jax.ShapeDtypeStruct(pair.shape, jnp.bfloat16),
        ),
        in_specs=[SMEM_SPEC] + [VMEM_SPEC] * 6,
        out_specs=(VMEM_SPEC,) * 2,
        scratch_shapes=[pltpu.VMEM(pair.shape, jnp.float32)],
        compiler_params=pltpu.CompilerParams(vmem_limit_bytes=VMEM_BYTES),
        name="attention_backward",
    )(meta, starts, query, pair, grad, mixed, lse)


def summed_rows(packed, cycle_size):
    wide = packed.shape[0]
    bits = cycle_size.bit_length() - 1
    unit = 3 * 2 * cycle_size * 8
    rows = -(-wide // unit) * unit
    packed = jnp.pad(packed, ((0, rows - wide), (0, 0)))
    place, core = lax.axis_index("ctx"), lax.axis_index("wsh")

    def halves(array, bit):
        size = array.shape[0] // 2
        kept = lax.dynamic_slice_in_dim(array, bit * size, size, 0)
        sent = lax.dynamic_slice_in_dim(array, (1 - bit) * size, size, 0)
        return kept, sent

    def joined(own, other, bit):
        size = own.shape[0]
        whole = jnp.concatenate([own, own], axis=0)
        return lax.dynamic_update_slice_in_dim(whole, other, (1 - bit) * size, 0)

    def exchange(array, bit):
        return lax.ppermute(array, "ctx", [(i, i ^ (1 << bit)) for i in range(cycle_size)])

    kept, sent = halves(packed, core)
    mine = kept + lax.ppermute(sent, "wsh", SWAP)
    third = mine.shape[0] // 3
    parts = [mine[i * third : (i + 1) * third] for i in range(3)]
    low = min(3, bits)
    orders = [[(s + i) % low for s in range(low)] + list(range(low, bits)) for i in range(3)]
    for step in range(bits):
        following = []
        for part, order in zip(parts, orders):
            kept, sent = halves(part, (place >> order[step]) & 1)
            following.append(kept + exchange(sent, order[step]))
        parts = following
    for step in reversed(range(bits)):
        parts = [
            joined(part, exchange(part, order[step]), (place >> order[step]) & 1)
            for part, order in zip(parts, orders)
        ]
    mine = jnp.concatenate(parts, axis=0)
    return joined(mine, lax.ppermute(mine, "wsh", SWAP), core)[:wide]


def local(
    tokens_in,
    doc_lengths,
    doc_adapter,
    norm1_gain,
    norm1_bias,
    norm2_gain,
    norm2_bias,
    w_query,
    w_key,
    w_value,
    w_out,
    w_up,
    w_down,
    a_query,
    b_query,
    a_key,
    b_key,
    a_value,
    b_value,
    a_out,
    b_out,
    a_up,
    b_up,
    a_down,
    b_down,
    cotangent,
):
    group_size = lax.axis_size("wsh")
    cycle_size = lax.axis_size("ctx")
    tok_dev, width_all = tokens_in.shape
    head_count = width_all // HEAD
    block_len = tok_dev * group_size
    hop_count = (DOC_MAX + block_len - 2) // block_len
    span = head_count - 1
    cycle_pos = lax.axis_index("ctx")
    core = lax.axis_index("wsh")
    half = width_all // group_size

    first_row = cycle_pos * block_len + core * tok_dev
    doc_ends = jnp.cumsum(doc_lengths)
    doc_starts = doc_ends - doc_lengths
    query_pos = first_row + jnp.arange(tok_dev, dtype=jnp.int32)
    query_docs = jnp.sum((doc_ends[None, :] <= query_pos[:, None]).astype(jnp.int32), axis=1)
    doc_numbers = jnp.arange(doc_lengths.shape[0], dtype=jnp.int32)
    token_adapter = jnp.sum(
        jnp.where(query_docs[:, None] == doc_numbers[None, :], doc_adapter[None, :], 0), axis=1
    )
    columns = jnp.arange(a_query.shape[1], dtype=jnp.int32) // RANK
    adapter_mask = (token_adapter[:, None] == columns[None, :]).astype(jnp.float32)
    mask_low = adapter_mask.astype(jnp.bfloat16)

    team = cycle_pos // span
    past = hop_count if cycle_size > span else 0
    first_key = (team * span - past) * block_len
    chunk_pos = jnp.concatenate(
        [
            (team * span + jnp.arange(span, dtype=jnp.int32)) * block_len + core * tok_dev,
            first_row[None],
        ]
    ).astype(jnp.int32)
    row_pos = chunk_pos[:, None] + jnp.arange(tok_dev, dtype=jnp.int32)[None, :]
    row_starts = jnp.max(
        jnp.where(doc_starts[None, None, :] <= row_pos[:, :, None], doc_starts[None, None, :], 0), axis=2
    )
    meta = jnp.stack(
        [
            (row_starts[:, 0] - first_key) // block_len,
            (chunk_pos - first_key) // block_len,
            chunk_pos,
            jnp.where(jnp.arange(span + 1) == span, 2 * HEAD, 0),
            jnp.full((span + 1,), first_key),
        ],
        axis=1,
    ).astype(jnp.int32)
    starts_col = row_starts[:, :, None].astype(jnp.int32)

    def swap(array):
        return lax.ppermute(array, "wsh", SWAP)

    def ordered(own, other, axis):
        return jnp.where(
            core == 0,
            jnp.concatenate([own, other], axis=axis),
            jnp.concatenate([other, own], axis=axis),
        )

    def own_other(array):
        return (
            lax.dynamic_slice_in_dim(array, core * half, half, 1),
            lax.dynamic_slice_in_dim(array, (1 - core) * half, half, 1),
        )

    if cycle_size > span:
        teams = [[t * span + i for i in range(span)] for t in range(cycle_size // span)]
    else:
        teams = None

    def exchange(blocks):
        return lax.all_to_all(blocks, "ctx", 0, 0, tiled=True, axis_index_groups=teams)

    gains = jnp.stack([norm1_gain, norm1_bias, norm2_gain, norm2_bias])
    gains = ordered(gains, swap(gains), 1).astype(jnp.float32)
    weights = [w_query, w_key, w_value, w_out, w_up, w_down]
    others = [swap(item) for item in weights]

    stream = tokens_in.astype(jnp.float32)
    norm_one, normed_one, inverse_one = norm_parts(stream, gains[0], gains[1])
    hidden_one = norm_one.astype(jnp.bfloat16)
    hidden_own, hidden_other = own_other(hidden_one)

    def projected(number, down_a, up_b):
        inner = (adapter_mask * dot(hidden_one, down_a)).astype(jnp.bfloat16)
        total = (
            dot(weights[number], hidden_own, 0, 1)
            + dot(others[number], hidden_other, 0, 1)
            + dot(up_b, inner, 0, 1)
        )
        return total.astype(jnp.bfloat16).reshape(head_count, HEAD, tok_dev), inner

    query_t, inner_query = projected(0, a_query, b_query)
    keys_t, inner_key = projected(1, a_key, b_key)
    values_t, inner_value = projected(2, a_value, b_value)

    last_pair = jnp.concatenate([keys_t[span:], values_t[span:]], axis=1)
    outgoing = jnp.concatenate(
        [
            query_t[:span],
            keys_t[:span],
            values_t[:span],
            jnp.broadcast_to(last_pair, (span, 2 * HEAD, tok_dev)),
        ],
        axis=1,
    )
    incoming = exchange(outgoing)
    query_all = jnp.concatenate([incoming[:, :HEAD], query_t[span:]], axis=0)
    pair_own = incoming[:, HEAD:]
    pair = ordered(pair_own, swap(pair_own), 2)
    ahead = [(i, i + span) for i in range(cycle_size - span)]
    back = [(i + span, i) for i in range(cycle_size - span)]
    if past:
        pair = jnp.concatenate([lax.ppermute(pair[span - past :], "ctx", ahead), pair], axis=0)

    low_all, mixed_all, lse_all = attention_forward(meta, starts_col, query_all, pair)
    mixed_t = jnp.concatenate([exchange(low_all[:span]), low_all[span:]], axis=0)
    mixed_t = mixed_t.reshape(width_all, tok_dev)
    mixed_low = mixed_t.T

    mixed_own, mixed_other = own_other(mixed_low)
    inner_out = (adapter_mask * dot(mixed_low, a_out)).astype(jnp.bfloat16)
    middle = stream + (
        dot(mixed_own, w_out) + dot(mixed_other, others[3]) + dot(inner_out, b_out)
    )
    norm_two, normed_two, inverse_two = norm_parts(middle, gains[2], gains[3])
    hidden_two = norm_two.astype(jnp.bfloat16)
    two_own, two_other = own_other(hidden_two)
    inner_up = (adapter_mask * dot(hidden_two, a_up)).astype(jnp.bfloat16)
    upward = dot(two_own, w_up) + dot(two_other, others[4]) + dot(inner_up, b_up)
    active_full, gelu_pull = jax.vjp(lambda value: jax.nn.gelu(value, approximate=True), upward)
    active = active_full.astype(jnp.bfloat16)
    inner_down = (adapter_mask * dot(active, a_down)).astype(jnp.bfloat16)
    down_out = ordered(dot(active, w_down), dot(active, others[5]), 1) + dot(inner_down, b_down)
    output = (middle + down_out).astype(jnp.bfloat16)

    def adapter_back(grad, up_b):
        return dot(grad, up_b, 1, 1).astype(jnp.bfloat16) * mask_low

    grad_own, grad_other = own_other(cotangent)
    down_grad = adapter_back(cotangent, b_down)
    active_grad = (
        dot(grad_own, w_down, 1, 1) + dot(grad_other, others[5], 1, 1) + dot(down_grad, a_down, 1, 1)
    )
    up_grad = gelu_pull(active_grad)[0].astype(jnp.bfloat16)
    up_inner_grad = adapter_back(up_grad, b_up)
    hidden_two_grad = ordered(dot(up_grad, w_up, 1, 1), dot(up_grad, others[4], 1, 1), 1) + dot(
        up_inner_grad, a_up, 1, 1
    )
    middle_grad = cotangent.astype(jnp.float32) + norm_back(
        hidden_two_grad, normed_two, inverse_two, gains[2]
    )
    branch_grad = middle_grad.astype(jnp.bfloat16)
    out_inner_grad = adapter_back(branch_grad, b_out)
    mixed_grad_t = ordered(
        dot(w_out, branch_grad, 1, 1), dot(others[3], branch_grad, 1, 1), 0
    ) + dot(a_out, out_inner_grad, 1, 1)
    mixed_grad_t = mixed_grad_t.astype(jnp.bfloat16).reshape(head_count, HEAD, tok_dev)

    grad_all = jnp.concatenate([exchange(mixed_grad_t[:span]), mixed_grad_t[span:]], axis=0)
    dq_all, dpair = attention_backward(
        meta, starts_col, query_all, pair, grad_all, mixed_all, lse_all
    )
    dpair_own = lax.dynamic_slice_in_dim(dpair, core * tok_dev, tok_dev, 2)
    dpair_sent = lax.dynamic_slice_in_dim(dpair, (1 - core) * tok_dev, tok_dev, 2)
    dpair_sum = dpair_own.astype(jnp.float32) + swap(dpair_sent).astype(jnp.float32)
    if past:
        returned = lax.ppermute(dpair_sum[:past].astype(jnp.bfloat16), "ctx", back)
        dpair_sum = dpair_sum[past:]
        dpair_sum = dpair_sum.at[span - past :].add(returned.astype(jnp.float32))
    outgoing_back = jnp.concatenate([dq_all[:span], dpair_sum.astype(jnp.bfloat16)], axis=1)
    incoming_back = exchange(outgoing_back)
    last_sum = jnp.sum(incoming_back[:, 3 * HEAD :].astype(jnp.float32), axis=0).astype(jnp.bfloat16)

    def gathered(first, last):
        main = incoming_back[:, first : first + HEAD].reshape(span * HEAD, tok_dev)
        return jnp.concatenate([main, last], axis=0)

    grads_t = [
        gathered(0, dq_all[span]),
        gathered(HEAD, last_sum[:HEAD]),
        gathered(2 * HEAD, last_sum[HEAD:]),
    ]

    own_sum, other_sum, adapter_sum = 0.0, 0.0, 0.0
    late = []
    for number, (grad_t, down_a, up_b, inner) in enumerate(
        zip(
            grads_t,
            (a_query, a_key, a_value),
            (b_query, b_key, b_value),
            (inner_query, inner_key, inner_value),
        )
    ):
        inner_grad = dot(grad_t, up_b, 0, 1).astype(jnp.bfloat16) * mask_low
        own_sum = own_sum + dot(grad_t, weights[number], 0, 1)
        other_sum = other_sum + dot(grad_t, others[number], 0, 1)
        adapter_sum = adapter_sum + dot(inner_grad, down_a, 1, 1)
        late.append(dot(hidden_one, inner_grad, 0, 0))
        late.append(dot(grad_t, inner, 1, 0))
    hidden_one_grad = ordered(own_sum, other_sum, 1) + adapter_sum
    stream_grad = middle_grad + norm_back(hidden_one_grad, normed_one, inverse_one, gains[0])
    grad_in = stream_grad.astype(jnp.bfloat16)

    norm_factor = (tok_dev * group_size * cycle_size) ** (-0.5)
    early = lax.psum(
        tuple(
            item.astype(jnp.bfloat16)
            for item in (
                dot(mixed_low, out_inner_grad, 0, 0),
                dot(inner_out, branch_grad, 0, 0),
                dot(hidden_two, up_inner_grad, 0, 0),
                dot(inner_up, up_grad, 0, 0),
                dot(active, down_grad, 0, 0),
                dot(inner_down, cotangent, 0, 0),
            )
        ),
        ("ctx", "wsh"),
    )
    early = [item.astype(jnp.float32) * norm_factor for item in early]
    packed = jnp.concatenate([item.astype(jnp.bfloat16) for item in late], axis=0)
    late_sum = summed_rows(packed, cycle_size).astype(jnp.float32) * norm_factor
    late_sum = [late_sum[i * width_all : (i + 1) * width_all] for i in range(6)]
    return (
        output,
        grad_in,
        late_sum[0],
        late_sum[1].T,
        late_sum[2],
        late_sum[3].T,
        late_sum[4],
        late_sum[5].T,
        *early,
    )


def solution(mesh):
    return jax.shard_map(
        local,
        mesh=mesh,
        in_specs=(
            P(("ctx", "wsh"), None),
            P(),
            P(),
            P("wsh"),
            P("wsh"),
            P("wsh"),
            P("wsh"),
            P("wsh", None),
            P("wsh", None),
            P("wsh", None),
            P("wsh", None),
            P("wsh", None),
            P(None, "wsh"),
            P(),
            P(),
            P(),
            P(),
            P(),
            P(),
            P(),
            P(),
            P(),
            P(),
            P(),
            P(),
            P(("ctx", "wsh"), None),
        ),
        out_specs=(
            P(("ctx", "wsh"), None),
            P(("ctx", "wsh"), None),
            P(),
            P(),
            P(),
            P(),
            P(),
            P(),
            P(),
            P(),
            P(),
            P(),
            P(),
            P(),
        ),
        check_vma=False,
    )
```

```python
import functools
import math

import jax
import jax.numpy as jnp
from jax import lax
from jax.experimental import pallas as pl
from jax.experimental.pallas import tpu as pltpu
from jax.sharding import PartitionSpec as P

HEAD = 64
RANK = 16
DOC_MAX = 4096


EPSILON = 1e-05
NEG_FILL = -1e30
SCALING = HEAD ** (-0.5)
SWAP = [(0, 1), (1, 0)]
VMEM_BYTES = 48 * 1024 * 1024


def norm_parts(values, gain, shift):
    row_mean = jnp.mean(values, axis=-1, keepdims=True)
    centered = values - row_mean
    variance = jnp.mean(centered * centered, axis=-1, keepdims=True)
    inverse = lax.rsqrt(variance + EPSILON)
    normed = centered * inverse
    return (normed * gain + shift, normed, inverse)


def norm_back(grad, normed, inverse, gain):
    scaled = grad * gain
    return inverse * (
        scaled
        - jnp.mean(scaled, axis=-1, keepdims=True)
        - normed * jnp.mean(scaled * normed, axis=-1, keepdims=True)
    )


def dot(left, right, lc=1, rc=0):
    return lax.dot_general(
        left, right, (((lc,), (rc,)), ((), ())), preferred_element_type=jnp.float32
    )


def group_lanes(meta_ref, starts_ref, g, rows, skip):
    lanes = lax.broadcasted_iota(jnp.int32, (1, starts_ref.shape[2]), 1)
    return starts_ref[g], meta_ref[g, 2] + lanes + jnp.where(lanes >= rows, skip, 0)


def side_by_side(ref, first, count):
    return jnp.concatenate([ref[first + k, 0:HEAD, :] for k in range(count)], axis=1)


def masked(scores, j, first_key, doc_start, query_pos):
    size = scores.shape[0]
    key_pos = first_key + j * size + lax.broadcasted_iota(jnp.int32, (size, 1), 0)
    allowed = (key_pos >= doc_start) & (key_pos <= query_pos)
    return jnp.where(allowed, scores, NEG_FILL)


def forward_kernel(
    pair_at, first_chunk, per_group, meta_ref, starts_ref, query_ref, own_ref, other_ref,
    low_ref, mixed_ref, lse_ref, rows_ref, values_ref,
):
    groups, _, lanes = starts_ref.shape
    rows = own_ref.shape[2]
    size = 2 * rows
    core, first_key = meta_ref[0, 3], meta_ref[0, 4]

    def spread(j, carry):
        for ref, side in ((own_ref, core), (other_ref, 1 - core)):
            spot = pl.multiple_of(side * rows, rows)
            pair = ref[j, pair_at : pair_at + 2 * HEAD, :]
            rows_ref[pl.ds(pl.multiple_of(j * size + spot, rows), rows), :] = pair.T
            values_ref[j, :, pl.ds(spot, rows)] = pair[HEAD:]
        return carry

    lax.fori_loop(meta_ref[0, 5], meta_ref[0, 6] + 1, spread, 0)

    def group(g, carry):
        query = side_by_side(query_ref, first_chunk + g * per_group, per_group)
        query = (query.astype(jnp.float32) * SCALING).astype(jnp.bfloat16)
        query = jnp.concatenate([query, jnp.zeros_like(query)], axis=0)
        doc_start, query_pos = group_lanes(meta_ref, starts_ref, g, rows, size - rows)

        def block(j, state):
            row_max, row_sum, total = state
            keys = rows_ref[pl.ds(pl.multiple_of(j * size, size), size), :]
            scores = masked(dot(keys, query), j, first_key, doc_start, query_pos)
            new_max = jnp.maximum(row_max, jnp.max(scores, axis=0, keepdims=True))
            probs = jnp.exp(scores - new_max)
            shrink = jnp.exp(row_max - new_max)
            row_sum = row_sum * shrink + jnp.sum(probs, axis=0, keepdims=True)
            total = total * shrink + dot(values_ref[j], probs.astype(jnp.bfloat16))
            return new_max, row_sum, total

        state = (
            jnp.full((1, lanes), NEG_FILL, jnp.float32),
            jnp.zeros((1, lanes), jnp.float32),
            jnp.zeros((HEAD, lanes), jnp.float32),
        )
        row_max, row_sum, total = lax.fori_loop(meta_ref[g, 0], meta_ref[g, 1] + 1, block, state)
        mixed = total / row_sum
        mixed_ref[g] = mixed
        for k in range(per_group):
            low_ref[g * per_group + k] = mixed[:, k * rows : (k + 1) * rows].astype(jnp.bfloat16)
        lse_ref[g] = row_max + jnp.log(row_sum)
        return carry

    lax.fori_loop(0, groups, group, 0)


def backward_kernel(
    pair_at, first_chunk, per_group, meta_ref, starts_ref, query_ref, own_ref, other_ref,
    rows_ref, grad_ref, mixed_ref, lse_ref, dq_ref, kept_ref, sent_ref, keys_ref, sum_ref,
):
    groups, _, lanes = starts_ref.shape
    rows = own_ref.shape[2]
    size = 2 * rows
    core, first_key = meta_ref[0, 3], meta_ref[0, 4]

    def prepare(j, carry):
        for ref, side in ((own_ref, core), (other_ref, 1 - core)):
            spot = pl.multiple_of(side * rows, rows)
            keys_ref[j, :, pl.ds(spot, rows)] = ref[j, pair_at : pair_at + HEAD, :]
        return carry

    lax.fori_loop(meta_ref[0, 5], meta_ref[0, 6] + 1, prepare, 0)
    sum_ref[...] = jnp.zeros(sum_ref.shape, jnp.float32)

    def group(g, carry):
        query = side_by_side(query_ref, first_chunk + g * per_group, per_group)
        query = (query.astype(jnp.float32) * SCALING).astype(jnp.bfloat16)
        grad = side_by_side(grad_ref, g * per_group, per_group)
        nothing = jnp.zeros_like(query)
        query_low = jnp.concatenate([query, nothing], axis=0)
        grad_high = jnp.concatenate([nothing, grad], axis=0)
        both = jnp.concatenate([query_low, grad_high], axis=1).T
        delta = jnp.sum(grad.astype(jnp.float32) * mixed_ref[g], axis=0, keepdims=True)
        lse = lse_ref[g]
        doc_start, query_pos = group_lanes(meta_ref, starts_ref, g, rows, size - rows)

        def block(j, total):
            spot = pl.ds(pl.multiple_of(j * size, size), size)
            pair = rows_ref[spot, :]
            scores = masked(dot(pair, query_low), j, first_key, doc_start, query_pos)
            probs = jnp.exp(scores - lse)
            prob_grad = dot(pair, grad_high)
            score_grad = (probs * (prob_grad - delta)).astype(jnp.bfloat16)
            sum_ref[spot, :] += dot(
                jnp.concatenate([score_grad, probs.astype(jnp.bfloat16)], axis=1), both
            )
            return total + dot(keys_ref[j], score_grad)

        total = lax.fori_loop(
            meta_ref[g, 0], meta_ref[g, 1] + 1, block, jnp.zeros((HEAD, lanes), jnp.float32)
        )
        total = (total * SCALING).astype(jnp.bfloat16)
        for k in range(per_group):
            dq_ref[g * per_group + k] = total[:, k * rows : (k + 1) * rows]
        return carry

    lax.fori_loop(0, groups, group, 0)

    def finish(j, carry):
        for ref, side in ((kept_ref, core), (sent_ref, 1 - core)):
            spot = pl.ds(pl.multiple_of(j * size + side * rows, rows), rows)
            ref[j] = sum_ref[spot, :].T.astype(ref.dtype)
        return carry

    lax.fori_loop(0, kept_ref.shape[0], finish, 0)


def cost(microseconds):
    return pl.CostEstimate(
        flops=microseconds * 1_000_000_000, bytes_accessed=microseconds * 1_000_000, transcendentals=0
    )


SMEM_SPEC = pl.BlockSpec(memory_space=pltpu.SMEM)
VMEM_SPEC = pl.BlockSpec(memory_space=pltpu.VMEM)


def attention_forward(plan, query, own, other, name, microseconds):
    meta, starts, pair_at, first_chunk, per_group = plan
    groups, _, lanes = starts.shape
    blocks, _, rows = own.shape
    return pl.pallas_call(
        functools.partial(forward_kernel, pair_at, first_chunk, per_group),
        out_shape=(
            jax.ShapeDtypeStruct((groups * per_group, HEAD, rows), jnp.bfloat16),
            jax.ShapeDtypeStruct((groups, HEAD, lanes), jnp.float32),
            jax.ShapeDtypeStruct((groups, 1, lanes), jnp.float32),
            jax.ShapeDtypeStruct((blocks * 2 * rows, 2 * HEAD), jnp.bfloat16),
        ),
        in_specs=[SMEM_SPEC] + [VMEM_SPEC] * 4,
        out_specs=(VMEM_SPEC,) * 4,
        scratch_shapes=[pltpu.VMEM((blocks, HEAD, 2 * rows), jnp.bfloat16)],
        compiler_params=pltpu.CompilerParams(vmem_limit_bytes=VMEM_BYTES),
        cost_estimate=cost(microseconds),
        name=name,
    )(meta, starts, query, own, other)


def attention_backward(plan, query, own, other, pair_rows, grad, mixed, lse, name, microseconds):
    meta, starts, pair_at, first_chunk, per_group = plan
    groups, _, lanes = starts.shape
    blocks, _, rows = own.shape
    return pl.pallas_call(
        functools.partial(backward_kernel, pair_at, first_chunk, per_group),
        out_shape=(
            jax.ShapeDtypeStruct((groups * per_group, HEAD, rows), jnp.bfloat16),
            jax.ShapeDtypeStruct((blocks, 2 * HEAD, rows), jnp.float32),
            jax.ShapeDtypeStruct((blocks, 2 * HEAD, rows), jnp.bfloat16),
        ),
        in_specs=[SMEM_SPEC] + [VMEM_SPEC] * 8,
        out_specs=(VMEM_SPEC,) * 3,
        scratch_shapes=[
            pltpu.VMEM((blocks, HEAD, 2 * rows), jnp.bfloat16),
            pltpu.VMEM((blocks * 2 * rows, 2 * HEAD), jnp.float32),
        ],
        compiler_params=pltpu.CompilerParams(vmem_limit_bytes=VMEM_BYTES),
        cost_estimate=cost(microseconds),
        name=name,
    )(meta, starts, query, own, other, pair_rows, grad, mixed, lse)


def gelu_parts(value):
    scale = (2.0 / math.pi) ** 0.5
    square = value * value
    bent = jnp.tanh(scale * value * (1.0 + 0.044715 * square))
    upper = 0.5 * (1.0 + bent)
    slope = 0.5 * value * (1.0 - bent * bent) * scale * (1.0 + 3 * 0.044715 * square)
    return value * upper, upper + slope


def column_norm(values, gain, shift):
    row_mean = jnp.mean(values, axis=0, keepdims=True)
    centered = values - row_mean
    variance = jnp.mean(centered * centered, axis=0, keepdims=True)
    inverse = lax.rsqrt(variance + EPSILON)
    normed = centered * inverse
    return (normed * gain + shift, normed, inverse)


def column_norm_back(grad, normed, inverse, gain):
    scaled = grad * gain
    return inverse * (
        scaled
        - jnp.mean(scaled, axis=0, keepdims=True)
        - normed * jnp.mean(scaled * normed, axis=0, keepdims=True)
    )


def middle_kernel(
    core_ref, mixed_ref, stream_ref, cotangent_ref, mask_ref, gains_ref,
    out_own_ref, out_other_ref, a_out_ref, b_out_ref, a_up_ref, b_down_ref,
    up_own_ref, up_other_ref, b_up_ref, down_own_ref, down_other_ref, a_down_ref,
    output_ref, middle_grad_ref, mixed_grad_ref,
    packed_ref,
    middle_ref, hidden_ref, hidden_own_ref, hidden_other_ref, cot_own_ref, cot_other_ref,
    inner_out_ref, inner_up_ref, down_grad_ref, inner_down_ref, up_grad_ref,
    down_ref, back_ref,
):
    tile, width, wide = up_own_ref.shape[1], mixed_ref.shape[0], packed_ref.shape[0]
    wide = (wide - 4 * width) // 2
    step = pl.program_id(0)
    core = core_ref[0]
    half = out_own_ref.shape[0]
    low = jnp.bfloat16
    own_rows = pl.ds(pl.multiple_of(core * half, 32), half)
    other_rows = pl.ds(pl.multiple_of((1 - core) * half, 32), half)

    @pl.when(step == 0)
    def _():
        mask = mask_ref[...]
        mixed_own = mixed_ref[own_rows, :].T
        mixed_other = mixed_ref[other_rows, :].T
        inner_out = (mask * (dot(mixed_ref[...].T, a_out_ref[...]))).astype(low)
        inner_out_ref[...] = inner_out
        branch = dot(mixed_own, out_own_ref[...]) + dot(mixed_other, out_other_ref[...])
        branch = branch.T + dot(b_out_ref[...], inner_out.T)
        middle = stream_ref[...].astype(jnp.float32) + branch
        middle_ref[...] = middle
        hidden = column_norm(middle, gains_ref[:, 2:3], gains_ref[:, 3:4])[0].astype(low)
        hidden_ref[...] = hidden
        hidden_own_ref[...] = hidden_ref[own_rows, :].T
        hidden_other_ref[...] = hidden_ref[other_rows, :].T
        inner_up_ref[...] = (mask * dot(hidden.T, a_up_ref[...])).astype(low)
        cot_own_ref[...] = cotangent_ref[own_rows, :].T
        cot_other_ref[...] = cotangent_ref[other_rows, :].T
        inner_grad = dot(cotangent_ref[...].T, b_down_ref[...])
        down_grad_ref[...] = inner_grad.astype(low) * mask.astype(low)
        for ref in (inner_down_ref, up_grad_ref, down_ref, back_ref):
            ref[...] = jnp.zeros(ref.shape, ref.dtype)

    up_own, up_other, down_own, down_other = (
        ref[...] for ref in (up_own_ref, up_other_ref, down_own_ref, down_other_ref)
    )
    inner_up, down_grad, a_down = inner_up_ref[...], down_grad_ref[...], a_down_ref[...]
    upward = (
        dot(hidden_own_ref[...], up_own)
        + dot(hidden_other_ref[...], up_other)
        + dot(inner_up, b_up_ref[...])
    )
    active_grad = (
        dot(cot_own_ref[...], down_own)
        + dot(cot_other_ref[...], down_other)
        + dot(down_grad, a_down.T)
    )
    active, slope = gelu_parts(upward)
    active = active.astype(low)
    up_grad = (active_grad * slope).astype(low)
    active_t, up_grad_t = active.T, up_grad.T
    down_ref[own_rows, :] += dot(down_own, active_t)
    down_ref[other_rows, :] += dot(down_other, active_t)
    back_ref[own_rows, :] += dot(up_own, up_grad_t)
    back_ref[other_rows, :] += dot(up_other, up_grad_t)
    inner_down_ref[...] += dot(active, a_down)
    up_grad_ref[...] += dot(b_up_ref[...], up_grad_t)
    here = pl.multiple_of(step * tile, tile)
    packed_ref[pl.ds(here, tile), :] = dot(up_grad_t, inner_up).astype(low)
    packed_ref[pl.ds(wide + here, tile), :] = dot(active_t, down_grad).astype(low)

    @pl.when(step == pl.num_programs(0) - 1)
    def _():
        mask = mask_ref[...]
        mask_low = mask.astype(low)
        cotangent = cotangent_ref[...]
        inner_down = (mask * inner_down_ref[...]).astype(low)
        middle = middle_ref[...]
        down = down_ref[...] + dot(b_down_ref[...], inner_down.T)
        output_ref[...] = (middle + down).astype(low)
        narrow = [packed_ref.at[pl.ds(2 * wide + k * width, width), :] for k in range(4)]
        narrow[0][...] = dot(cotangent, inner_down).astype(low)
        inner_grad = up_grad_ref[...].astype(low).T * mask_low
        hidden_grad = back_ref[...] + dot(a_up_ref[...], inner_grad.T)
        narrow[1][...] = dot(hidden_ref[...], inner_grad).astype(low)
        gain = gains_ref[:, 2:3]
        _, normed, inverse = column_norm(middle, gain, gain)
        middle_grad = cotangent.astype(jnp.float32) + column_norm_back(
            hidden_grad, normed, inverse, gain
        )
        middle_grad_ref[...] = middle_grad
        branch = middle_grad.astype(low)
        out_grad = dot(branch.T, b_out_ref[...]).astype(low) * mask_low
        turned = out_grad.T
        for rows, weight in ((own_rows, out_own_ref[...]), (other_rows, out_other_ref[...])):
            back = dot(weight, branch) + dot(a_out_ref[rows, :], turned)
            mixed_grad_ref[rows, :] = back.astype(low)
        narrow[2][...] = dot(mixed_ref[...], out_grad).astype(low)
        narrow[3][...] = dot(branch, inner_out_ref[...]).astype(low)


def middle_part(
    core, mixed_t, tokens_t, cotangent_t, mask, gains_t, out_pair, a_out, b_out_t, a_up, b_down_t,
    up_pair, b_up, down_pair_t, a_down,
):
    width, rows = mixed_t.shape
    half = width // 2
    inner, wide = b_up.shape
    tile = 2 * inner
    low = jnp.bfloat16

    def fixed(shape):
        return pl.BlockSpec(shape, lambda f: (0,) * len(shape), pipeline_mode=pl.Buffered(1))

    def out(shape):
        return pl.BlockSpec(shape, lambda f: (0,) * len(shape))

    def columns(height):
        return pl.BlockSpec((height, tile), lambda f: (0, f))

    def lines(length):
        return pl.BlockSpec((tile, length), lambda f: (f, 0))

    operands = (
        mixed_t, tokens_t, cotangent_t, mask, gains_t, *out_pair, a_out, b_out_t, a_up, b_down_t
    )
    shapes = (
        ((width, rows), low), ((width, rows), jnp.float32), ((width, rows), low),
        ((2 * wide + 4 * width, inner), low),
    )
    return pl.pallas_call(
        middle_kernel,
        grid=(wide // tile,),
        out_shape=tuple(jax.ShapeDtypeStruct(*item) for item in shapes),
        in_specs=[SMEM_SPEC]
        + [fixed(item.shape) for item in operands]
        + [columns(half), columns(half), columns(inner), columns(half), columns(half), lines(inner)],
        out_specs=tuple(out(item[0]) for item in shapes),
        scratch_shapes=[
            pltpu.VMEM((width, rows), jnp.float32),
            pltpu.VMEM((width, rows), low),
            *[pltpu.VMEM((rows, half), low)] * 4,
            *[pltpu.VMEM((rows, inner), low)] * 3,
            pltpu.VMEM((rows, inner), jnp.float32),
            pltpu.VMEM((inner, rows), jnp.float32),
            *[pltpu.VMEM((width, rows), jnp.float32)] * 2,
        ],
        compiler_params=pltpu.CompilerParams(
            vmem_limit_bytes=VMEM_BYTES, dimension_semantics=("arbitrary",)
        ),
        cost_estimate=cost(1),
        name="middle_part",
    )(core, *operands, *up_pair, b_up, *down_pair_t, a_down)


def summed_rows(packed, cycle_size):
    wide = packed.shape[0]
    bits = cycle_size.bit_length() - 1
    unit = 3 * 2 * cycle_size * 8
    rows = -(-wide // unit) * unit
    packed = jnp.pad(packed, ((0, rows - wide), (0, 0)))
    place, core = lax.axis_index("ctx"), lax.axis_index("wsh")

    def halves(array, bit):
        size = array.shape[0] // 2
        kept = lax.dynamic_slice_in_dim(array, bit * size, size, 0)
        sent = lax.dynamic_slice_in_dim(array, (1 - bit) * size, size, 0)
        return kept, sent

    def joined(own, other, bit):
        size = own.shape[0]
        whole = jnp.concatenate([own, own], axis=0)
        return lax.dynamic_update_slice_in_dim(whole, other, (1 - bit) * size, 0)

    def exchange(array, bit):
        return lax.ppermute(array, "ctx", [(i, i ^ (1 << bit)) for i in range(cycle_size)])

    kept, sent = halves(packed, core)
    mine = kept + lax.ppermute(sent, "wsh", SWAP)
    third = mine.shape[0] // 3
    parts = [mine[i * third : (i + 1) * third] for i in range(3)]
    low = min(3, bits)
    orders = [[(s + i) % low for s in range(low)] + list(range(low, bits)) for i in range(3)]
    for step in range(bits):
        following = []
        for part, order in zip(parts, orders):
            kept, sent = halves(part, (place >> order[step]) & 1)
            following.append(kept + exchange(sent, order[step]))
        parts = following
    for step in reversed(range(bits)):
        parts = [
            joined(part, exchange(part, order[step]), (place >> order[step]) & 1)
            for part, order in zip(parts, orders)
        ]
    mine = jnp.concatenate(parts, axis=0)
    return joined(mine, lax.ppermute(mine, "wsh", SWAP), core)[:wide]


def halved(array, bit, cycle_size):
    size = array.shape[0] // 2
    side = (lax.axis_index("ctx") >> bit) & 1
    kept = lax.dynamic_slice_in_dim(array, side * size, size, 0)
    sent = lax.dynamic_slice_in_dim(array, (1 - side) * size, size, 0)
    return kept + lax.ppermute(sent, "ctx", [(i, i ^ (1 << bit)) for i in range(cycle_size)])


def local(
    tokens_in,
    doc_lengths,
    doc_adapter,
    norm1_gain,
    norm1_bias,
    norm2_gain,
    norm2_bias,
    w_query,
    w_key,
    w_value,
    w_out,
    w_up,
    w_down,
    a_query,
    b_query,
    a_key,
    b_key,
    a_value,
    b_value,
    a_out,
    b_out,
    a_up,
    b_up,
    a_down,
    b_down,
    cotangent,
):
    group_size = lax.axis_size("wsh")
    cycle_size = lax.axis_size("ctx")
    tok_dev, width_all = tokens_in.shape
    head_count = width_all // HEAD
    block_len = tok_dev * group_size
    hop_count = (DOC_MAX + block_len - 2) // block_len
    span = head_count - 1
    cycle_pos = lax.axis_index("ctx")
    core = lax.axis_index("wsh")
    half = width_all // group_size

    first_row = cycle_pos * block_len + core * tok_dev
    doc_ends = jnp.cumsum(doc_lengths)
    doc_starts = doc_ends - doc_lengths
    query_pos = first_row + jnp.arange(tok_dev, dtype=jnp.int32)
    query_docs = jnp.sum((doc_ends[None, :] <= query_pos[:, None]).astype(jnp.int32), axis=1)
    doc_numbers = jnp.arange(doc_lengths.shape[0], dtype=jnp.int32)
    token_adapter = jnp.sum(
        jnp.where(query_docs[:, None] == doc_numbers[None, :], doc_adapter[None, :], 0), axis=1
    )
    columns = jnp.arange(a_query.shape[1], dtype=jnp.int32) // RANK
    adapter_mask = (token_adapter[:, None] == columns[None, :]).astype(jnp.float32)
    mask_low = adapter_mask.astype(jnp.bfloat16)

    team = cycle_pos // span
    past = hop_count if cycle_size > span else 0
    first_key = (team * span - past) * block_len
    key_blocks = past + span

    def plan(chunk_pos, pair_at, first_chunk, per_group):
        groups = chunk_pos.shape[0] // per_group
        row_pos = chunk_pos[:, None] + jnp.arange(tok_dev, dtype=jnp.int32)[None, :]
        began = doc_starts[None, None, :] <= row_pos[:, :, None]
        row_starts = jnp.max(jnp.where(began, doc_starts[None, None, :], 0), axis=2)
        row_starts = row_starts.reshape(groups, 1, per_group * tok_dev)
        chunk_pos = chunk_pos.reshape(groups, per_group)
        first = (row_starts[:, 0, 0] - first_key) // block_len
        last = (chunk_pos[:, -1] - first_key) // block_len
        same = jnp.ones((groups,), jnp.int32)
        whole = per_group > 1
        meta = [
            first,
            last,
            chunk_pos[:, 0],
            same * core,
            same * first_key,
            same * 0 if whole else first,
            same * (key_blocks - 1) if whole else last,
        ]
        meta = jnp.stack(meta, axis=1).astype(jnp.int32)
        return meta, row_starts.astype(jnp.int32), pair_at, first_chunk, per_group

    team_pos = (team * span + jnp.arange(span, dtype=jnp.int32)) * block_len + core * tok_dev
    main_plan = plan(team_pos.astype(jnp.int32), HEAD, past, 2)
    last_plan = plan(first_row[None].astype(jnp.int32), 0, 0, 1)

    def swap(array):
        return lax.ppermute(array, "wsh", SWAP)

    def ordered(own, other, axis):
        return jnp.where(
            core == 0,
            jnp.concatenate([own, other], axis=axis),
            jnp.concatenate([other, own], axis=axis),
        )

    def own_other(array):
        return (
            lax.dynamic_slice_in_dim(array, core * half, half, 1),
            lax.dynamic_slice_in_dim(array, (1 - core) * half, half, 1),
        )

    if cycle_size > span:
        teams = [[t * span + i for i in range(span)] for t in range(cycle_size // span)]
    else:
        teams = None

    def exchange(blocks):
        return lax.all_to_all(blocks, "ctx", 0, 0, tiled=True, axis_index_groups=teams)

    gains = jnp.stack([norm1_gain, norm1_bias, norm2_gain, norm2_bias])
    gains = ordered(gains, swap(gains), 1).astype(jnp.float32)
    weights = [w_query, w_key, w_value, w_out, w_up, w_down.T]
    others = [swap(item) for item in weights]

    stream = tokens_in.astype(jnp.float32)
    norm_one, normed_one, inverse_one = norm_parts(stream, gains[0], gains[1])
    hidden_one = norm_one.astype(jnp.bfloat16)
    hidden_own, hidden_other = own_other(hidden_one)

    def projected(number, down_a, up_b):
        inner = (adapter_mask * dot(hidden_one, down_a)).astype(jnp.bfloat16)
        total = (
            dot(weights[number], hidden_own, 0, 1)
            + dot(others[number], hidden_other, 0, 1)
            + dot(up_b, inner, 0, 1)
        )
        return total.astype(jnp.bfloat16).reshape(head_count, HEAD, tok_dev), inner

    query_t, inner_query = projected(0, a_query, b_query)
    keys_t, inner_key = projected(1, a_key, b_key)
    values_t, inner_value = projected(2, a_value, b_value)

    ahead = [(i, i + span) for i in range(cycle_size - span)]
    back = [(i + span, i) for i in range(cycle_size - span)]

    def with_past(blocks):
        if not past:
            return blocks
        return jnp.concatenate([lax.ppermute(blocks[span - past :], "ctx", ahead), blocks], axis=0)

    incoming = exchange(jnp.concatenate([query_t[:span], keys_t[:span], values_t[:span]], axis=1))
    last_pair = jnp.concatenate([keys_t[span:], values_t[span:]], axis=1)
    incoming, last_pair = lax.optimization_barrier((incoming, last_pair))
    own = with_past(incoming)
    other = swap(own)
    last_own = exchange(jnp.broadcast_to(last_pair, (span, 2 * HEAD, tok_dev)))
    low_main, mixed_main, lse_main, rows_main = attention_forward(
        main_plan, own, own, other, "attention_forward", 30
    )
    low_main, last_own = lax.optimization_barrier((low_main, last_own))
    last_own = with_past(last_own)
    last_other = swap(last_own)
    low_last, mixed_last, lse_last, rows_last = attention_forward(
        last_plan, query_t[span:], last_own, last_other, "last_forward", 3
    )
    mixed_t = jnp.concatenate([exchange(low_main), low_last], axis=0)
    mixed_t = mixed_t.reshape(width_all, tok_dev)

    output_t, middle_grad_t, mixed_grad_t, early = middle_part(
        core[None], mixed_t, tokens_in.T, cotangent.T, adapter_mask, gains.T, (w_out, others[3]),
        a_out, b_out.T, a_up, b_down.T, (w_up, others[4]), b_up, (w_down.T, others[5]), a_down,
    )
    mixed_grad_t = mixed_grad_t.reshape(head_count, HEAD, tok_dev)

    bits = cycle_size.bit_length() - 1
    lanes = early.shape[1]
    share = early.shape[0] // 2
    early_sent = lax.dynamic_slice_in_dim(early, (1 - core) * share, share, 0)
    early_kept = lax.dynamic_slice_in_dim(early, core * share, share, 0)
    early = halved(early_kept + swap(early_sent), 0, cycle_size)

    def pair_back(kept, sent):
        total = kept + swap(sent).astype(jnp.float32)
        if past:
            returned = lax.ppermute(total[:past].astype(jnp.bfloat16), "ctx", back)
            total = total[past:].at[span - past :].add(returned.astype(jnp.float32))
        return total.astype(jnp.bfloat16)

    dq_last, kept_last, sent_last = attention_backward(
        last_plan, query_t[span:], last_own, last_other, rows_last,
        mixed_grad_t[span:], mixed_last, lse_last, "last_backward", 6,
    )
    grad_main = exchange(mixed_grad_t[:span])
    dpair_last = pair_back(kept_last, sent_last)
    grad_main, dpair_last, early = lax.optimization_barrier((grad_main, dpair_last, early))
    dpair_last = exchange(dpair_last)
    dq_main, kept_main, sent_main = attention_backward(
        main_plan, own, own, other, rows_main, grad_main, mixed_main, lse_main,
        "attention_backward", 40
    )
    dq_main, dpair_last, early = lax.optimization_barrier((dq_main, dpair_last, early))
    for bit in range(1, bits):
        early = halved(early, bit, cycle_size)
    early = lax.all_gather(early, ("ctx", "wsh"), axis=0, tiled=False)
    last_sum = jnp.sum(dpair_last.astype(jnp.float32), axis=0).astype(jnp.bfloat16)
    incoming_back = exchange(jnp.concatenate([dq_main, pair_back(kept_main, sent_main)], axis=1))

    def gathered(first, last):
        main = incoming_back[:, first : first + HEAD].reshape(span * HEAD, tok_dev)
        return jnp.concatenate([main, last], axis=0)

    grads_t = [
        gathered(0, dq_last[0]),
        gathered(HEAD, last_sum[:HEAD]),
        gathered(2 * HEAD, last_sum[HEAD:]),
    ]

    own_sum, other_sum, adapter_sum = 0.0, 0.0, 0.0
    late = []
    for number, (grad_t, down_a, up_b, inner) in enumerate(
        zip(
            grads_t,
            (a_query, a_key, a_value),
            (b_query, b_key, b_value),
            (inner_query, inner_key, inner_value),
        )
    ):
        inner_grad = dot(grad_t, up_b, 0, 1).astype(jnp.bfloat16) * mask_low
        own_sum = own_sum + dot(grad_t, weights[number], 0, 1)
        other_sum = other_sum + dot(grad_t, others[number], 0, 1)
        adapter_sum = adapter_sum + dot(inner_grad, down_a, 1, 1)
        late.append(dot(hidden_one, inner_grad, 0, 0))
        late.append(dot(grad_t, inner, 1, 0))
    hidden_one_grad = ordered(own_sum, other_sum, 1) + adapter_sum
    stream_grad = middle_grad_t.T + norm_back(hidden_one_grad, normed_one, inverse_one, gains[0])
    grad_in = stream_grad.astype(jnp.bfloat16)

    norm_factor = (tok_dev * group_size * cycle_size) ** (-0.5)
    packed = jnp.concatenate([item.astype(jnp.bfloat16) for item in late], axis=0)
    late_sum, early = lax.optimization_barrier((summed_rows(packed, cycle_size), early))
    early = early.reshape((2,) * (bits + 1) + (share // cycle_size, lanes))
    early = jnp.transpose(early, tuple(reversed(range(bits + 1))) + (bits + 1, bits + 2))
    early = early.reshape(group_size * share, lanes)
    early = early.astype(jnp.float32) * norm_factor
    wide = b_up.shape[1]
    narrow = [early[2 * wide + k * width_all : 2 * wide + (k + 1) * width_all] for k in range(4)]
    late_sum = late_sum.astype(jnp.float32) * norm_factor
    late_sum = [late_sum[i * width_all : (i + 1) * width_all] for i in range(6)]
    return (
        output_t.T,
        grad_in,
        late_sum[0],
        late_sum[1].T,
        late_sum[2],
        late_sum[3].T,
        late_sum[4],
        late_sum[5].T,
        narrow[2],
        narrow[3].T,
        narrow[1],
        early[:wide].T,
        early[wide : 2 * wide],
        narrow[0].T,
    )


def solution(mesh):
    return jax.shard_map(
        local,
        mesh=mesh,
        in_specs=(
            P(("ctx", "wsh"), None),
            P(),
            P(),
            P("wsh"),
            P("wsh"),
            P("wsh"),
            P("wsh"),
            P("wsh", None),
            P("wsh", None),
            P("wsh", None),
            P("wsh", None),
            P("wsh", None),
            P(None, "wsh"),
            P(),
            P(),
            P(),
            P(),
            P(),
            P(),
            P(),
            P(),
            P(),
            P(),
            P(),
            P(),
            P(("ctx", "wsh"), None),
        ),
        out_specs=(
            P(("ctx", "wsh"), None),
            P(("ctx", "wsh"), None),
            P(),
            P(),
            P(),
            P(),
            P(),
            P(),
            P(),
            P(),
            P(),
            P(),
            P(),
            P(),
        ),
        check_vma=False,
    )
```

```python
import functools
import math

import jax
import jax.numpy as jnp
from jax import lax
from jax.experimental import pallas as pl
from jax.experimental.pallas import tpu as pltpu
from jax.sharding import PartitionSpec as P

HEAD = 64
RANK = 16
DOC_MAX = 4096


EPSILON = 1e-05
NEG_FILL = -1e30
SCALING = HEAD ** (-0.5)
SWAP = [(0, 1), (1, 0)]
VMEM_BYTES = 60 * 1024 * 1024


def norm_parts(values, gain, shift):
    row_mean = jnp.mean(values, axis=-1, keepdims=True)
    centered = values - row_mean
    variance = jnp.mean(centered * centered, axis=-1, keepdims=True)
    inverse = lax.rsqrt(variance + EPSILON)
    normed = centered * inverse
    return (normed * gain + shift, normed, inverse)


def norm_back(grad, normed, inverse, gain):
    scaled = grad * gain
    return inverse * (
        scaled
        - jnp.mean(scaled, axis=-1, keepdims=True)
        - normed * jnp.mean(scaled * normed, axis=-1, keepdims=True)
    )


def dot(left, right, lc=1, rc=0):
    return lax.dot_general(
        left, right, (((lc,), (rc,)), ((), ())), preferred_element_type=jnp.float32
    )


DOC_SLOTS = 64


def side_by_side(ref, first, count):
    return jnp.concatenate([ref[first + k, 0:HEAD, :] for k in range(count)], axis=1)


def marked_queries(query_ref, first, count, docs):
    query = side_by_side(query_ref, first, count)
    query = (query.astype(jnp.float32) * SCALING).astype(jnp.bfloat16)
    number = lax.broadcasted_iota(jnp.int32, (DOC_SLOTS, docs.shape[1]), 0)
    marks = jnp.where(number == docs, 0.0, NEG_FILL).astype(jnp.bfloat16)
    return query, jnp.concatenate([query, marks], axis=0)


def marked_keys(pair, bounds_ref, first_pos):
    rows = pair.shape[0]
    place = first_pos + lax.broadcasted_iota(jnp.int32, (rows, DOC_SLOTS), 0)
    marks = (place >= bounds_ref[0:1, :]) & (place < bounds_ref[1:2, :])
    marks = jnp.where(marks, 1.0, 0.0).astype(jnp.bfloat16)
    return jnp.concatenate([pair[:, :HEAD], marks], axis=1)


def causal(scores, first_pos, query_pos):
    row = lax.broadcasted_iota(jnp.int32, scores.shape, 0)
    return jnp.where(row <= query_pos - first_pos, scores, NEG_FILL)


def group_lanes(meta_ref, g, lanes, rows):
    lane = lax.broadcasted_iota(jnp.int32, (1, lanes), 1)
    return meta_ref[g, 2] + lane + jnp.where(lane >= rows, rows, 0)


def span_walk(meta_ref, g, size, block, state):
    def spot(t):
        first = pl.multiple_of(t * size, size)
        return pl.ds(first, size), meta_ref[0, 4] + first

    state = lax.fori_loop(
        meta_ref[g, 0], meta_ref[g, 1], lambda t, state: block(*spot(t), False, state), state
    )
    return block(*spot(meta_ref[g, 1]), True, state)


def forward_kernel(
    pair_at, first_chunk, per_group, meta_ref, docs_ref, bounds_ref, query_ref, own_ref, other_ref,
    low_ref, mixed_ref, lse_ref, keys_ref, values_ref,
):
    groups, _, lanes = docs_ref.shape
    blocks, _, rows = own_ref.shape
    size = 2 * rows
    core, first_key = meta_ref[0, 3], meta_ref[0, 4]

    def spread(j, carry):
        for ref, side in ((own_ref, core), (other_ref, 1 - core)):
            first = pl.multiple_of(j * size + side * rows, rows)
            pair = ref[j, pair_at : pair_at + 2 * HEAD, :]
            keys_ref[pl.ds(first, rows), :] = marked_keys(pair.T, bounds_ref, first_key + first)
            values_ref[:, pl.ds(first, rows)] = pair[HEAD:]
        return carry

    lax.fori_loop(2 * meta_ref[0, 5], 2 * meta_ref[0, 6] + 2, spread, 0)

    def group(g, carry):
        _, query = marked_queries(query_ref, first_chunk + g * per_group, per_group, docs_ref[g])
        query_pos = group_lanes(meta_ref, g, lanes, rows)

        def block(spot, first_pos, last, state):
            row_max, row_sum, total = state
            scores = dot(keys_ref[spot, :], query)
            if last:
                scores = causal(scores, first_pos, query_pos)
            new_max = jnp.maximum(row_max, jnp.max(scores, axis=0, keepdims=True))
            probs = jnp.exp(scores - new_max)
            shrink = jnp.exp(row_max - new_max)
            row_sum = row_sum * shrink + jnp.sum(probs, axis=0, keepdims=True)
            total = total * shrink + dot(values_ref[:, spot], probs.astype(jnp.bfloat16))
            return new_max, row_sum, total

        state = (
            jnp.full((1, lanes), NEG_FILL, jnp.float32),
            jnp.zeros((1, lanes), jnp.float32),
            jnp.zeros((HEAD, lanes), jnp.float32),
        )
        row_max, row_sum, total = span_walk(meta_ref, g, 2 * size, block, state)
        mixed = total / row_sum
        mixed_ref[g] = mixed
        for k in range(per_group):
            low_ref[g * per_group + k] = mixed[:, k * rows : (k + 1) * rows].astype(jnp.bfloat16)
        lse_ref[g] = row_max + jnp.log(row_sum)
        return carry

    lax.fori_loop(0, groups, group, 0)


def backward_kernel(
    pair_at, first_chunk, per_group, turned, meta_ref, docs_ref, bounds_ref, query_ref, own_ref,
    other_ref, grad_ref, mixed_ref, lse_ref, dq_ref, kept_ref, sent_ref,
    keys_ref, rows_ref, keys_t_ref, sum_ref,
):
    groups, _, lanes = docs_ref.shape
    blocks, _, rows = own_ref.shape
    size = 2 * rows
    core, first_key = meta_ref[0, 3], meta_ref[0, 4]

    def spread(j, carry):
        for ref, side in ((own_ref, core), (other_ref, 1 - core)):
            first = pl.multiple_of(j * size + side * rows, rows)
            pair = ref[j, pair_at : pair_at + 2 * HEAD, :]
            turned_pair = pair.T
            rows_ref[pl.ds(first, rows), :] = turned_pair
            keys_ref[pl.ds(first, rows), :] = marked_keys(turned_pair, bounds_ref, first_key + first)
            keys_t_ref[:, pl.ds(first, rows)] = pair[:HEAD]
        return carry

    lax.fori_loop(2 * meta_ref[0, 5], 2 * meta_ref[0, 6] + 2, spread, 0)
    sum_ref[...] = jnp.zeros(sum_ref.shape, jnp.float32)

    def group(g, carry):
        first = first_chunk + g * per_group
        query, query_marked = marked_queries(query_ref, first, per_group, docs_ref[g])
        grad = side_by_side(grad_ref, g * per_group, per_group)
        nothing = jnp.zeros_like(query)
        query_low = jnp.concatenate([query, nothing], axis=0)
        grad_high = jnp.concatenate([nothing, grad], axis=0)
        both = jnp.concatenate([query_low, grad_high], axis=1).T
        delta = jnp.sum(grad.astype(jnp.float32) * mixed_ref[g], axis=0, keepdims=True)
        lse = lse_ref[g]
        query_pos = group_lanes(meta_ref, g, lanes, rows)

        def block(spot, first_pos, last, total):
            scores = dot(keys_ref[spot, :], query_marked)
            if last:
                scores = causal(scores, first_pos, query_pos)
            probs = jnp.exp(scores - lse)
            prob_grad = dot(rows_ref[spot, :], grad_high)
            score_grad = (probs * (prob_grad - delta)).astype(jnp.bfloat16)
            sum_ref[spot, :] += dot(
                jnp.concatenate([score_grad, probs.astype(jnp.bfloat16)], axis=1), both
            )
            return total + dot(keys_t_ref[:, spot], score_grad)

        total = span_walk(meta_ref, g, 2 * size, block, jnp.zeros((HEAD, lanes), jnp.float32))
        total = (total * SCALING).astype(jnp.bfloat16)
        for k in range(per_group):
            dq_ref[g * per_group + k] = total[:, k * rows : (k + 1) * rows]
        return carry

    lax.fori_loop(0, groups, group, 0)

    def finish(j, carry):
        for ref, side in ((kept_ref, core), (sent_ref, 1 - core)):
            spot = pl.ds(pl.multiple_of(j * size + side * rows, rows), rows)
            total = sum_ref[spot, :]
            ref[j] = (total.T if turned else total).astype(ref.dtype)
        return carry

    lax.fori_loop(0, blocks, finish, 0)


def cost(microseconds):
    return pl.CostEstimate(
        flops=microseconds * 1_000_000_000, bytes_accessed=microseconds * 1_000_000, transcendentals=0
    )


SMEM_SPEC = pl.BlockSpec(memory_space=pltpu.SMEM)
VMEM_SPEC = pl.BlockSpec(memory_space=pltpu.VMEM)


def attention_forward(plan, query, own, other, name, microseconds):
    meta, docs, bounds, pair_at, first_chunk, per_group = plan
    groups, _, lanes = docs.shape
    blocks, _, rows = own.shape
    keys = blocks * 2 * rows
    return pl.pallas_call(
        functools.partial(forward_kernel, pair_at, first_chunk, per_group),
        out_shape=(
            jax.ShapeDtypeStruct((groups * per_group, HEAD, rows), jnp.bfloat16),
            jax.ShapeDtypeStruct((groups, HEAD, lanes), jnp.float32),
            jax.ShapeDtypeStruct((groups, 1, lanes), jnp.float32),
        ),
        in_specs=[SMEM_SPEC] + [VMEM_SPEC] * 5,
        out_specs=(VMEM_SPEC,) * 3,
        scratch_shapes=[
            pltpu.VMEM((keys, HEAD + DOC_SLOTS), jnp.bfloat16),
            pltpu.VMEM((HEAD, keys), jnp.bfloat16),
        ],
        compiler_params=pltpu.CompilerParams(vmem_limit_bytes=VMEM_BYTES),
        cost_estimate=cost(microseconds),
        name=name,
    )(meta, docs, bounds, query, own, other)


def attention_backward(
    plan, query, own, other, grad, mixed, lse, turned, name, microseconds
):
    meta, docs, bounds, pair_at, first_chunk, per_group = plan
    groups, _, lanes = docs.shape
    blocks, _, rows = own.shape
    keys = blocks * 2 * rows
    part = (blocks, 2 * HEAD, rows) if turned else (blocks, rows, 2 * HEAD)
    return pl.pallas_call(
        functools.partial(backward_kernel, pair_at, first_chunk, per_group, turned),
        out_shape=(
            jax.ShapeDtypeStruct((groups * per_group, HEAD, rows), jnp.bfloat16),
            jax.ShapeDtypeStruct(part, jnp.float32),
            jax.ShapeDtypeStruct(part, jnp.bfloat16),
        ),
        in_specs=[SMEM_SPEC] + [VMEM_SPEC] * 8,
        out_specs=(VMEM_SPEC,) * 3,
        scratch_shapes=[
            pltpu.VMEM((keys, HEAD + DOC_SLOTS), jnp.bfloat16),
            pltpu.VMEM((keys, 2 * HEAD), jnp.bfloat16),
            pltpu.VMEM((HEAD, keys), jnp.bfloat16),
            pltpu.VMEM((keys, 2 * HEAD), jnp.float32),
        ],
        compiler_params=pltpu.CompilerParams(vmem_limit_bytes=VMEM_BYTES),
        cost_estimate=cost(microseconds),
        name=name,
    )(meta, docs, bounds, query, own, other, grad, mixed, lse)


def gelu_parts(value):
    scale = (2.0 / math.pi) ** 0.5
    square = value * value
    bent = jnp.tanh(scale * value * (1.0 + 0.044715 * square))
    upper = 0.5 * (1.0 + bent)
    slope = 0.5 * value * (1.0 - bent * bent) * scale * (1.0 + 3 * 0.044715 * square)
    return value * upper, upper + slope


def column_norm(values, gain, shift):
    row_mean = jnp.mean(values, axis=0, keepdims=True)
    centered = values - row_mean
    variance = jnp.mean(centered * centered, axis=0, keepdims=True)
    inverse = lax.rsqrt(variance + EPSILON)
    normed = centered * inverse
    return (normed * gain + shift, normed, inverse)


def column_norm_back(grad, normed, inverse, gain):
    scaled = grad * gain
    return inverse * (
        scaled
        - jnp.mean(scaled, axis=0, keepdims=True)
        - normed * jnp.mean(scaled * normed, axis=0, keepdims=True)
    )


def half_rows(core, half):
    return (
        pl.ds(pl.multiple_of(core * half, 32), half),
        pl.ds(pl.multiple_of((1 - core) * half, 32), half),
    )


def middle_kernel(
    tile, core_ref, mixed_main_ref, mixed_last_ref, stream_ref, cotangent_ref, mask_ref, gains_ref,
    a_out_ref, b_out_ref, a_up_ref, b_down_ref, *refs,
):
    remote, refs = refs[:8], refs[8:]
    output_ref, middle_grad_ref, main_grad_ref, last_grad_ref, kept_ref, sent_ref = refs[:6]
    places, refs = refs[6:14], refs[14:]
    (
        mixed_ref, middle_ref, hidden_ref, hidden_own_ref, hidden_other_ref, cot_own_ref,
        cot_other_ref, inner_out_ref, inner_up_ref, down_grad_ref, inner_down_ref, up_grad_ref,
        down_ref, back_ref, semaphores,
    ) = refs
    out_own_ref, out_other_ref, up_own_ref, up_other_ref, b_up_ref = places[:5]
    down_own_ref, down_other_ref, a_down_ref = places[5:]
    core = core_ref[0]
    half, wide = up_own_ref.shape
    width = 2 * half
    full = wide // tile
    low = jnp.bfloat16
    own_rows, other_rows = half_rows(core, half)

    def copies(first, size, number):
        spot = pl.ds(first, size)
        cut = [(slice(None), spot)] * 5 + [(spot, slice(None))]
        return [
            pltpu.make_async_copy(source.at[where], place.at[where], semaphores.at[number, i])
            for i, (source, place, where) in enumerate(zip(remote[2:], places[2:], cut))
        ]

    firsts = [pltpu.make_async_copy(remote[i], places[i], semaphores.at[full + 1, i]) for i in range(2)]
    for copy in firsts:
        copy.start()
    for k in range(full + 1):
        for copy in copies(k * tile, min(tile, wide - k * tile), k):
            copy.start()

    def put(first, rows, other):
        spot = pl.ds(first, rows.shape[0])

        @pl.when(core == 0)
        def _():
            kept_ref[spot, :] = rows
            sent_ref[spot, :] = other

        @pl.when(core == 1)
        def _():
            kept_ref[spot, :] = other
            sent_ref[spot, :] = rows

    mask = mask_ref[...]
    mask_low = mask.astype(low)
    main = mixed_main_ref.shape[0] * HEAD
    mixed_ref[:main, :] = mixed_main_ref[...].reshape(main, mixed_main_ref.shape[2])
    mixed_ref[main:, :] = mixed_last_ref[0]
    inner_out = (mask * (dot(mixed_ref[...].T, a_out_ref[...]))).astype(low)
    inner_out_ref[...] = inner_out
    cotangent = cotangent_ref[...]
    cot_own_ref[...] = cotangent_ref[own_rows, :].T
    cot_other_ref[...] = cotangent_ref[other_rows, :].T
    down_grad_ref[...] = dot(cotangent.T, b_down_ref[...]).astype(low) * mask_low
    for copy in firsts:
        copy.wait()
    branch = dot(mixed_ref[own_rows, :].T, out_own_ref[...])
    branch = branch + dot(mixed_ref[other_rows, :].T, out_other_ref[...])
    branch = branch.T + dot(b_out_ref[...], inner_out.T)
    middle = stream_ref[...].astype(jnp.float32) + branch
    middle_ref[...] = middle
    hidden = column_norm(middle, gains_ref[:, 2:3], gains_ref[:, 3:4])[0].astype(low)
    hidden_ref[...] = hidden
    hidden_own_ref[...] = hidden_ref[own_rows, :].T
    hidden_other_ref[...] = hidden_ref[other_rows, :].T
    inner_up_ref[...] = (mask * dot(hidden.T, a_up_ref[...])).astype(low)
    for ref in (inner_down_ref, up_grad_ref, down_ref, back_ref):
        ref[...] = jnp.zeros(ref.shape, ref.dtype)

    def step(k, size):
        first = k * tile if isinstance(k, int) else pl.multiple_of(k * tile, tile)
        for copy in copies(first, size, k):
            copy.wait()
        columns = (slice(None), pl.ds(first, size))
        up_own, up_other, b_up = up_own_ref[columns], up_other_ref[columns], b_up_ref[columns]
        down_own, down_other = down_own_ref[columns], down_other_ref[columns]
        a_down = a_down_ref[pl.ds(first, size), :]
        inner_up, down_grad = inner_up_ref[...], down_grad_ref[...]
        upward = dot(hidden_own_ref[...], up_own) + dot(hidden_other_ref[...], up_other)
        upward = upward + dot(inner_up, b_up)
        active_grad = dot(cot_own_ref[...], down_own) + dot(cot_other_ref[...], down_other)
        active_grad = active_grad + dot(down_grad, a_down.T)
        active, slope = gelu_parts(upward)
        active = active.astype(low)
        up_grad = (active_grad * slope).astype(low)
        active_t, up_grad_t = active.T, up_grad.T
        down_ref[own_rows, :] += dot(down_own, active_t)
        down_ref[other_rows, :] += dot(down_other, active_t)
        back_ref[own_rows, :] += dot(up_own, up_grad_t)
        back_ref[other_rows, :] += dot(up_other, up_grad_t)
        inner_down_ref[...] += dot(active, a_down)
        up_grad_ref[...] += dot(b_up, up_grad_t)
        put(first, dot(up_grad_t, inner_up).astype(low), dot(active_t, down_grad).astype(low))

    def loop(k, carry):
        step(k, tile)
        return carry

    lax.fori_loop(0, full, loop, 0)
    if wide % tile:
        step(full, wide % tile)

    inner_down = (mask * inner_down_ref[...]).astype(low)
    middle = middle_ref[...]
    down = down_ref[...] + dot(b_down_ref[...], inner_down.T)
    output_ref[...] = (middle + down).astype(low)
    inner_grad = up_grad_ref[...].astype(low).T * mask_low
    hidden_grad = back_ref[...] + dot(a_up_ref[...], inner_grad.T)
    gain = gains_ref[:, 2:3]
    _, normed, inverse = column_norm(middle, gain, gain)
    middle_grad = cotangent_ref[...].astype(jnp.float32)
    middle_grad = middle_grad + column_norm_back(hidden_grad, normed, inverse, gain)
    middle_grad_ref[...] = middle_grad
    branch = middle_grad.astype(low)
    out_grad = dot(branch.T, b_out_ref[...]).astype(low) * mask_low
    put(wide, dot(cotangent_ref[...], inner_down).astype(low), dot(mixed_ref[...], out_grad).astype(low))
    put(
        wide + width,
        dot(hidden_ref[...], inner_grad).astype(low),
        dot(branch, inner_out_ref[...]).astype(low),
    )
    spare = slice(wide + 2 * width, kept_ref.shape[0])
    if spare.start < spare.stop:
        kept_ref[spare, :] = jnp.zeros((spare.stop - spare.start, kept_ref.shape[1]), low)
        sent_ref[spare, :] = jnp.zeros((spare.stop - spare.start, kept_ref.shape[1]), low)
    turned = out_grad.T
    for rows, weight in ((own_rows, out_own_ref[...]), (other_rows, out_other_ref[...])):
        back = dot(weight, branch) + dot(a_out_ref[rows, :], turned)
        hidden_ref[rows, :] = back.astype(low)
    main_grad_ref[...] = hidden_ref[:main, :].reshape(main_grad_ref.shape)
    last_grad_ref[0] = hidden_ref[main:, :]


def padded(size, unit):
    return -(-size // unit) * unit


def middle_part(
    core, mixed_main, mixed_last, tokens_t, cotangent_t, mask, gains_t, out_pair, a_out, b_out_t,
    a_up, b_down_t, up_pair, b_up, down_pair_t, a_down, unit,
):
    width, rows = tokens_t.shape
    half = width // 2
    inner, wide = b_up.shape
    tile = 512
    low = jnp.bfloat16
    operands = (
        mixed_main, mixed_last, tokens_t, cotangent_t, mask, gains_t, a_out, b_out_t, a_up, b_down_t
    )
    remote = (*out_pair, *up_pair, b_up, *down_pair_t, a_down)
    share = (padded(wide + 2 * width, unit), inner)
    shapes = (
        ((width, rows), low), ((width, rows), jnp.float32), (mixed_main.shape, low),
        (mixed_last.shape, low), (share, low), (share, low),
    )
    return pl.pallas_call(
        functools.partial(middle_kernel, tile),
        out_shape=tuple(jax.ShapeDtypeStruct(*item) for item in shapes),
        in_specs=[SMEM_SPEC]
        + [VMEM_SPEC] * len(operands)
        + [pl.BlockSpec(memory_space=pl.ANY)] * len(remote),
        out_specs=(VMEM_SPEC,) * len(shapes),
        scratch_shapes=[
            *[pltpu.VMEM(item.shape, item.dtype) for item in remote],
            pltpu.VMEM((width, rows), low),
            pltpu.VMEM((width, rows), jnp.float32),
            pltpu.VMEM((width, rows), low),
            *[pltpu.VMEM((rows, half), low)] * 4,
            *[pltpu.VMEM((rows, inner), low)] * 3,
            pltpu.VMEM((rows, inner), jnp.float32),
            pltpu.VMEM((inner, rows), jnp.float32),
            *[pltpu.VMEM((width, rows), jnp.float32)] * 2,
            pltpu.SemaphoreType.DMA((wide // tile + 2, 6)),
        ],
        compiler_params=pltpu.CompilerParams(vmem_limit_bytes=VMEM_BYTES),
        cost_estimate=cost(20),
        name="middle_part",
    )(core, *operands, *remote)


def fetched(refs, places, semaphores):
    copies = [
        pltpu.make_async_copy(ref, place, semaphores.at[i])
        for i, (ref, place) in enumerate(zip(refs, places))
    ]
    for copy in copies:
        copy.start()
    return copies


def whole_call(kernel, shapes, scratch, operands, remote, microseconds, name):
    space = [pltpu.VMEM(item.shape, item.dtype) for item in remote]
    return pl.pallas_call(
        kernel,
        out_shape=tuple(jax.ShapeDtypeStruct(*item) for item in shapes),
        in_specs=[SMEM_SPEC]
        + [VMEM_SPEC] * (len(operands) - 1)
        + [pl.BlockSpec(memory_space=pl.ANY)] * len(remote),
        out_specs=(VMEM_SPEC,) * len(shapes),
        scratch_shapes=[pltpu.VMEM(*item) for item in scratch]
        + space
        + ([pltpu.SemaphoreType.DMA((len(remote),))] if remote else []),
        compiler_params=pltpu.CompilerParams(vmem_limit_bytes=VMEM_BYTES),
        cost_estimate=cost(microseconds),
        name=name,
    )(*operands, *remote)


def entry_kernel(
    place_ref, lengths_ref, adapters_ref, tokens_ref, gains_own_ref, gains_other_ref, *refs
):
    remote, (hidden_ref, inner_ref, mask_ref, gains_ref), downs, semaphores = (
        refs[:3], refs[3:7], refs[7:10], refs[10],
    )
    copies = fetched(remote, downs, semaphores)
    rows, inner = mask_ref.shape
    half = gains_own_ref.shape[1]
    own_rows, other_rows = half_rows(place_ref[0], half)
    for spot, ref in ((own_rows, gains_own_ref), (other_rows, gains_other_ref)):
        gains_ref[spot, :] = ref[...].astype(jnp.float32).T
    values = tokens_ref[...].astype(jnp.float32)
    hidden = column_norm(values, gains_ref[:, 0:1], gains_ref[:, 1:2])[0].astype(jnp.bfloat16)
    hidden_ref[...] = hidden
    hidden_rows = hidden.T
    place = place_ref[1] + lax.broadcasted_iota(jnp.int32, (rows, inner), 0)
    column = lax.broadcasted_iota(jnp.int32, (rows, inner), 1) // RANK

    def document(d, state):
        start, mask = state
        end = start + lengths_ref[d]
        chosen = (place >= start) & (place < end) & (column == adapters_ref[d])
        return end, jnp.where(chosen, 1.0, mask)

    state = (jnp.int32(0), jnp.zeros((rows, inner), jnp.float32))
    _, mask = lax.fori_loop(0, lengths_ref.shape[0], document, state)
    mask_ref[...] = mask
    for n in range(3):
        copies[n].wait()
        inner_ref[n] = (mask * dot(hidden_rows, downs[n][...])).astype(jnp.bfloat16)


def projection_kernel(core_ref, hidden_ref, inner_ref, *refs):
    remote, (heads_ref, query_ref, pair_ref), local_refs, semaphores = (
        refs[:9], refs[9:12], refs[12:21], refs[21],
    )
    copies = fetched(remote, local_refs, semaphores)
    own_rows, other_rows = half_rows(core_ref[0], local_refs[0].shape[0])
    hidden_own = hidden_ref[own_rows, :].T
    hidden_other = hidden_ref[other_rows, :].T
    count = heads_ref.shape[0]
    for n in range(3):
        for copy in copies[3 * n : 3 * n + 3]:
            copy.wait()
        own, up, other = local_refs[3 * n : 3 * n + 3]
        total = (dot(hidden_own, own[...]) + dot(hidden_other, other[...])).T
        total = (total + dot(up[...], inner_ref[n].T)).astype(jnp.bfloat16)
        for c in range(count):
            heads_ref[c, n * HEAD : (n + 1) * HEAD, :] = total[c * HEAD : (c + 1) * HEAD]
        if n == 0:
            query_ref[0] = total[count * HEAD :]
        else:
            pair_ref[(n - 1) * HEAD : n * HEAD, :] = total[count * HEAD :]


def projections(place, lengths, adapters, tokens_t, gains, gains_other, weights, others, downs, ups_t):
    width, rows = tokens_t.shape
    inner = downs[0].shape[1]
    low = jnp.bfloat16
    any_spec = pl.BlockSpec(memory_space=pl.ANY)
    hidden_t, inners, mask, gains_t = pl.pallas_call(
        entry_kernel,
        out_shape=(
            jax.ShapeDtypeStruct((width, rows), low),
            jax.ShapeDtypeStruct((3, rows, inner), low),
            jax.ShapeDtypeStruct((rows, inner), jnp.float32),
            jax.ShapeDtypeStruct((width, gains.shape[0]), jnp.float32),
        ),
        in_specs=[SMEM_SPEC] * 3 + [VMEM_SPEC] * 3 + [any_spec] * 3,
        out_specs=(VMEM_SPEC,) * 4,
        scratch_shapes=[pltpu.VMEM(item.shape, item.dtype) for item in downs]
        + [pltpu.SemaphoreType.DMA((3,))],
        compiler_params=pltpu.CompilerParams(vmem_limit_bytes=VMEM_BYTES),
        cost_estimate=cost(1),
        name="entry",
    )(place, lengths, adapters, tokens_t, gains, gains_other, *downs)
    count = width // HEAD - 1
    remote = [item for group in zip(weights, ups_t, others) for item in group]
    heads, last_query, last_pair = whole_call(
        projection_kernel,
        (((count, 3 * HEAD, rows), low), ((1, HEAD, rows), low), ((2 * HEAD, rows), low)),
        (), (place, hidden_t, inners), remote, 4, "projection",
    )
    return heads, last_query, last_pair, hidden_t, inners, mask, gains_t


def gathered_grad(n, heads_ref, last_query_ref, last_pair_ref, grad_ref):
    count = heads_ref.shape[0]
    for c in range(count):
        grad_ref[c * HEAD : (c + 1) * HEAD, :] = heads_ref[c, n * HEAD : (n + 1) * HEAD, :]
    if n == 0:
        grad_ref[count * HEAD :, :] = last_query_ref[0]
    else:
        grad_ref[count * HEAD :, :] = last_pair_ref[...].T[(n - 1) * HEAD : n * HEAD]
    return grad_ref[...]


def projections_late_kernel(
    core_ref, heads_ref, last_query_ref, last_pair_ref, hidden_ref, inner_ref, mask_ref, *refs
):
    remote, (kept_ref, sent_ref, inner_grad_ref, grad_ref), ups, semaphores = (
        refs[:3], refs[3:7], refs[7:10], refs[10],
    )
    copies = fetched(remote, ups, semaphores)
    core = core_ref[0]
    low = jnp.bfloat16
    width, share = hidden_ref.shape[0], kept_ref.shape[0]
    mask_low = mask_ref[...].astype(low)
    hidden = hidden_ref[...]

    def keep(first, rows):
        done = 0
        while done < rows.shape[0]:
            side, spot = divmod(first + done, share)
            size = min(rows.shape[0] - done, share - spot)
            store(side, slice(spot, spot + size), rows[done : done + size])
            done += size

    def store(side, spot, rows):
        @pl.when(core == side)
        def _():
            kept_ref[spot, :] = rows

        @pl.when(core != side)
        def _():
            sent_ref[spot, :] = rows

    keep(6 * width, jnp.zeros((2 * share - 6 * width, kept_ref.shape[1]), low))
    for n in range(3):
        grad = gathered_grad(n, heads_ref, last_query_ref, last_pair_ref, grad_ref)
        copies[n].wait()
        inner_grad = dot(grad.T, ups[n][...]).astype(low) * mask_low
        inner_grad_ref[n] = inner_grad
        keep(2 * n * width, dot(hidden, inner_grad).astype(low))
        keep((2 * n + 1) * width, dot(grad, inner_ref[n]).astype(low))


def projections_late(core, heads, last_query, last_pair, hidden_t, inners, mask, ups_t, unit):
    width, rows = hidden_t.shape
    low = jnp.bfloat16
    share = padded(6 * width, 2 * unit) // 2
    return whole_call(
        projections_late_kernel,
        (((share, mask.shape[1]), low), ((share, mask.shape[1]), low), (inners.shape, low)),
        (((width, rows), low),),
        (core, heads, last_query, last_pair, hidden_t, inners, mask), ups_t, 5, "projections_late",
    )


def projections_back_kernel(
    core_ref, heads_ref, last_query_ref, last_pair_ref, inner_grad_ref, gains_ref, tokens_ref, *refs
):
    remote, (grad_in_ref, grad_ref, sum_ref), local_refs, semaphores = (
        refs[:10], refs[10:13], refs[13:23], refs[23],
    )
    copies = fetched(remote, local_refs, semaphores)
    downs, weights, others, middle_grad_ref = (
        local_refs[:3], local_refs[3:6], local_refs[6:9], local_refs[9],
    )
    own_rows, other_rows = half_rows(core_ref[0], weights[0].shape[0])
    for n in range(3):
        grad = gathered_grad(n, heads_ref, last_query_ref, last_pair_ref, grad_ref)
        turned = inner_grad_ref[n].T
        copies[n].wait()
        for rows, weight, copy in (
            (own_rows, weights[n], copies[3 + n]), (other_rows, others[n], copies[6 + n])
        ):
            copy.wait()
            part = dot(weight[...], grad) + dot(downs[n][rows, :], turned)
            sum_ref[rows, :] = part if n == 0 else sum_ref[rows, :] + part
    gain = gains_ref[:, 0:1]
    _, normed, inverse = column_norm(tokens_ref[...].astype(jnp.float32), gain, gain)
    back = column_norm_back(sum_ref[...], normed, inverse, gain)
    copies[9].wait()
    grad_in_ref[...] = (middle_grad_ref[...] + back).astype(jnp.bfloat16)


def projections_back(
    core, heads, last_query, last_pair, inner_grads, gains_t, tokens_t, middle_grad_t,
    weights, others, downs,
):
    width, rows = tokens_t.shape
    low = jnp.bfloat16
    return whole_call(
        projections_back_kernel,
        (((width, rows), low),),
        (((width, rows), low), ((width, rows), jnp.float32)),
        (core, heads, last_query, last_pair, inner_grads, gains_t, tokens_t),
        (*downs, *weights, *others, middle_grad_t),
        8, "projections_back",
    )[0]


def steps_of(cycle_size):
    bits = cycle_size.bit_length() - 1
    return [(bit, min(2, bits - bit)) for bit in range(0, bits, 2)]


def partners(cycle_size, step, k):
    return [(i, i ^ (k << step[0])) for i in range(cycle_size)]


def scattered(array, step, cycle_size):
    count = 1 << step[1]
    mine = (lax.axis_index("ctx") >> step[0]) & (count - 1)
    blocks = array.reshape(count, array.shape[0] // count, array.shape[1])

    def block(number):
        return lax.dynamic_index_in_dim(blocks, number, 0, keepdims=False)

    total = block(mine).astype(jnp.float32)
    for k in range(1, count):
        got = lax.ppermute(block(mine ^ k), "ctx", partners(cycle_size, step, k))
        total = total + got.astype(jnp.float32)
    return total.astype(array.dtype)


def collected(share, step, cycle_size):
    count = 1 << step[1]
    mine = (lax.axis_index("ctx") >> step[0]) & (count - 1)
    whole = jnp.zeros((count, *share.shape), share.dtype)
    whole = lax.dynamic_update_index_in_dim(whole, share, mine, 0)
    for k in range(1, count):
        got = lax.ppermute(share, "ctx", partners(cycle_size, step, k))
        whole = lax.dynamic_update_index_in_dim(whole, got, mine ^ k, 0)
    return whole.reshape(count * share.shape[0], share.shape[1])


def pair_sum(kept, sent):
    return kept + lax.ppermute(sent, "wsh", SWAP)


def early_finish_kernel(
    factor, core_ref, own_ref, other_ref,
    b_up_ref, a_down_ref, b_down_ref, a_up_ref, a_out_ref, b_out_ref,
):
    wide, width = a_down_ref.shape[0], a_up_ref.shape[0]

    def finish(first_ref, second_ref):
        def part(ref, first, count):
            return ref[first : first + count, :].astype(jnp.float32) * factor

        for k in range(wide // 256):
            b_up_ref[:, k * 256 : (k + 1) * 256] = part(first_ref, k * 256, 256).T
        a_down_ref[...] = part(second_ref, 0, wide)
        b_down_ref[...] = part(first_ref, wide, width)
        a_up_ref[...] = part(first_ref, wide + width, width)
        a_out_ref[...] = part(second_ref, wide, width)
        b_out_ref[...] = part(second_ref, wide + width, width)

    @pl.when(core_ref[0] == 0)
    def _():
        finish(own_ref, other_ref)

    @pl.when(core_ref[0] == 1)
    def _():
        finish(other_ref, own_ref)


def late_finish_kernel(factor, core_ref, own_ref, other_ref, *refs):
    core = core_ref[0]
    targets, late_ref = refs[:6], refs[6]
    for side, ref in ((core, own_ref), (1 - core, other_ref)):
        late_ref[side] = ref[...].astype(jnp.float32) * factor
    width, share = targets[0].shape[0], late_ref.shape[1]
    for n, ref in enumerate(targets):
        done = 0
        while done < width:
            side, spot = divmod(n * width + done, share)
            rows = min(width - done, share - spot)
            ref[done : done + rows, :] = late_ref[side, spot : spot + rows, :]
            done += rows


def finished(kernel, factor, core, own, other, shapes, scratch, name):
    return whole_call(
        functools.partial(kernel, factor), [(shape, jnp.float32) for shape in shapes], scratch,
        (core, own, other), (), 1, name,
    )


def local(
    tokens_in,
    doc_lengths,
    doc_adapter,
    norm1_gain,
    norm1_bias,
    norm2_gain,
    norm2_bias,
    w_query,
    w_key,
    w_value,
    w_out,
    w_up,
    w_down,
    a_query,
    b_query,
    a_key,
    b_key,
    a_value,
    b_value,
    a_out,
    b_out,
    a_up,
    b_up,
    a_down,
    b_down,
    cotangent,
):
    group_size = lax.axis_size("wsh")
    cycle_size = lax.axis_size("ctx")
    tok_dev, width_all = tokens_in.shape
    head_count = width_all // HEAD
    block_len = tok_dev * group_size
    hop_count = (DOC_MAX + block_len - 2) // block_len
    span = head_count - 1
    cycle_pos = lax.axis_index("ctx")
    core = lax.axis_index("wsh")
    half = width_all // group_size

    first_row = cycle_pos * block_len + core * tok_dev
    doc_ends = jnp.cumsum(doc_lengths)
    doc_starts = doc_ends - doc_lengths

    team = cycle_pos // span
    past = hop_count if cycle_size > span else 0
    first_key = (team * span - past) * block_len
    key_blocks = past + span

    slots = DOC_SLOTS - doc_lengths.shape[0]
    bounds = jnp.stack([jnp.pad(doc_starts, (0, slots)), jnp.pad(doc_ends, (0, slots))])

    def plan(chunk_pos, pair_at, first_chunk, per_group):
        groups = chunk_pos.shape[0] // per_group
        row_pos = chunk_pos[:, None] + jnp.arange(tok_dev, dtype=jnp.int32)[None, :]
        row_docs = jnp.sum((doc_ends[None, None, :] <= row_pos[:, :, None]).astype(jnp.int32), axis=2)
        row_docs = row_docs.reshape(groups, 1, per_group * tok_dev)
        chunk_pos = chunk_pos.reshape(groups, per_group)
        began = jnp.where(doc_starts[None, :] <= chunk_pos[:, :1], doc_starts[None, :], 0)
        first = (jnp.max(began, axis=1) - first_key) // (2 * block_len)
        last = (chunk_pos[:, -1] - first_key) // (2 * block_len)
        same = jnp.ones((groups,), jnp.int32)
        whole = per_group > 1
        meta = [
            first,
            last,
            chunk_pos[:, 0],
            same * core,
            same * first_key,
            same * 0 if whole else first,
            same * (key_blocks // 2 - 1) if whole else last,
        ]
        meta = jnp.stack(meta, axis=1).astype(jnp.int32)
        docs = row_docs.astype(jnp.int32)
        return meta, docs, bounds.astype(jnp.int32), pair_at, first_chunk, per_group

    team_pos = (team * span + jnp.arange(span, dtype=jnp.int32)) * block_len + core * tok_dev
    main_plan = plan(team_pos.astype(jnp.int32), HEAD, past, 2)
    last_plan = plan(first_row[None].astype(jnp.int32), 0, 0, 1)

    def swap(array):
        return lax.ppermute(array, "wsh", SWAP)

    if cycle_size > span:
        teams = [[t * span + i for i in range(span)] for t in range(cycle_size // span)]
    else:
        teams = None

    def exchange(blocks):
        return lax.all_to_all(blocks, "ctx", 0, 0, tiled=True, axis_index_groups=teams)

    gains = jnp.stack([norm1_gain, norm1_bias, norm2_gain, norm2_bias])
    weights = [w_query, w_key, w_value, w_out, w_up, w_down.T]
    others = [swap(item) for item in weights]

    downs = (a_query, a_key, a_value)
    ups_t = (b_query.T, b_key.T, b_value.T)
    tokens_t = tokens_in.T
    core_1 = jnp.stack([core, first_row]).astype(jnp.int32)
    heads, last_query, last_pair, hidden_t, inners, adapter_mask, gains_t = projections(
        core_1, doc_lengths, doc_adapter, tokens_t, gains, swap(gains), weights[:3], others[:3],
        downs, ups_t,
    )

    ahead = [(i, i + span) for i in range(cycle_size - span)]
    back = [(i + span, i) for i in range(cycle_size - span)]

    def with_past(blocks):
        if not past:
            return blocks
        return jnp.concatenate([lax.ppermute(blocks[span - past :], "ctx", ahead), blocks], axis=0)

    steps = steps_of(cycle_size)
    unit = 16 * cycle_size
    incoming = exchange(heads)
    incoming, last_pair = lax.optimization_barrier((incoming, last_pair))
    own = with_past(incoming)
    other = swap(own)
    last_own = exchange(jnp.broadcast_to(last_pair, (span, 2 * HEAD, tok_dev)))
    low_main, total_main, lse_main = attention_forward(
        main_plan, own, own, other, "attention_forward", 30
    )
    low_main, last_own = lax.optimization_barrier((low_main, last_own))
    last_own = with_past(last_own)
    last_other = swap(last_own)
    low_last, mixed_last, lse_last = attention_forward(
        last_plan, last_query, last_own, last_other, "last_forward", 0
    )
    mixed_main = exchange(low_main)

    output_t, middle_grad_t, main_grad, last_out_grad, early_kept, early_sent = middle_part(
        core_1, mixed_main, low_last, tokens_t, cotangent.T, adapter_mask, gains_t,
        (w_out, others[3]), a_out, b_out.T, a_up, b_down.T, (w_up, others[4]), b_up,
        (w_down.T, others[5]), a_down, unit,
    )

    def pair_back(kept, sent):
        total = kept + swap(sent).astype(jnp.float32)
        if past:
            returned = lax.ppermute(total[:past].astype(jnp.bfloat16), "ctx", back)
            total = total[past:].at[span - past :].add(returned.astype(jnp.float32))
        return total.astype(jnp.bfloat16)

    dq_last, kept_last, sent_last = attention_backward(
        last_plan, last_query, last_own, last_other,
        last_out_grad, mixed_last, lse_last, False, "last_backward", 0,
    )
    grad_main = exchange(main_grad)
    dpair_last = pair_back(kept_last, sent_last)
    plane = 1 << steps[0][1]
    lines = cycle_size // plane
    planes = [[l * plane + p for p in range(plane)] for l in range(lines)]
    digits = (2,) * (cycle_size.bit_length() - 3) + (plane,)
    if cycle_size > span:
        zero = jnp.zeros((cycle_size // span, *dpair_last.shape), dpair_last.dtype)
        dpair_last = lax.dynamic_update_index_in_dim(zero, dpair_last, team, 0)
    order = tuple(reversed(range(len(digits)))) + (len(digits), len(digits) + 1)
    dpair_last = jnp.transpose(dpair_last.reshape(digits + dpair_last.shape[-2:]), order)
    early = pair_sum(early_kept, early_sent)
    lanes = early.shape[1]
    early_rows, last_rows = early.shape[0] // cycle_size, tok_dev
    shared = jnp.concatenate(
        [
            early.reshape(plane, lines, early_rows, lanes),
            dpair_last.reshape(plane, lines, last_rows, lanes),
        ],
        axis=2,
    )
    grad_main, shared = lax.optimization_barrier((grad_main, shared))
    shared = lax.all_to_all(shared, "ctx", 0, 0, tiled=True, axis_index_groups=planes)
    dq_main, kept_main, sent_main = attention_backward(
        main_plan, own, own, other, grad_main, total_main, lse_main,
        True, "attention_backward", 40
    )
    dq_main, kept_main, sent_main, shared = lax.optimization_barrier(
        (dq_main, kept_main, sent_main, shared)
    )
    incoming_back = exchange(jnp.concatenate([dq_main, pair_back(kept_main, sent_main)], axis=1))
    shared = jnp.sum(shared.astype(jnp.float32), axis=0).astype(jnp.bfloat16)
    shared = shared.reshape(lines * (early_rows + last_rows), lanes)
    singles = [(bit, 1) for bit in range(2, cycle_size.bit_length() - 1)]
    for step in singles:
        shared = scattered(shared, step, cycle_size)
    early, last_sum = shared[:early_rows], shared[early_rows:]

    late_kept, late_sent, inner_grads = projections_late(
        core_1, incoming_back, dq_last, last_sum, hidden_t, inners, adapter_mask, ups_t, unit
    )
    late, early, inner_grads = lax.optimization_barrier(
        (pair_sum(late_kept, late_sent), early, inner_grads)
    )
    grad_in_t = projections_back(
        core_1, incoming_back, dq_last, last_sum, inner_grads, gains_t, tokens_t, middle_grad_t,
        weights[:3], others[:3], downs,
    )

    norm_factor = (tok_dev * group_size * cycle_size) ** (-0.5)
    singles = singles[::-1]
    late = scattered(late, steps[0], cycle_size)
    for step in singles[:1]:
        early = collected(early, step, cycle_size)
    late, early, grad_in_t = lax.optimization_barrier((late, early, grad_in_t))
    for step in steps[1:]:
        late = scattered(late, step, cycle_size)
    for step in singles[1:]:
        early = collected(early, step, cycle_size)
    late, early = lax.optimization_barrier((late, early))
    early = collected(early, steps[0], cycle_size)
    for step in reversed(steps):
        late = collected(late, step, cycle_size)
    late, early = lax.optimization_barrier((late, early))
    early_other = swap(early)
    wide = b_up.shape[1]
    early = finished(
        early_finish_kernel, norm_factor, core_1, early, early_other,
        [(lanes, wide), (wide, lanes)] + [(width_all, lanes)] * 4, (), "early_finish",
    )
    late, early = lax.optimization_barrier((late, early))
    g_b_up, g_a_down, g_b_down, g_a_up, g_a_out, g_b_out = early
    late = finished(
        late_finish_kernel, norm_factor, core_1, late, swap(late), [(width_all, lanes)] * 6,
        (((2, *late.shape), jnp.float32),), "late_finish",
    )
    return (
        output_t.T,
        grad_in_t.T,
        late[0],
        late[1].T,
        late[2],
        late[3].T,
        late[4],
        late[5].T,
        g_a_out,
        g_b_out.T,
        g_a_up,
        g_b_up,
        g_a_down,
        g_b_down.T,
    )


def solution(mesh):
    return jax.shard_map(
        local,
        mesh=mesh,
        in_specs=(
            P(("ctx", "wsh"), None),
            P(),
            P(),
            P("wsh"),
            P("wsh"),
            P("wsh"),
            P("wsh"),
            P("wsh", None),
            P("wsh", None),
            P("wsh", None),
            P("wsh", None),
            P("wsh", None),
            P(None, "wsh"),
            P(),
            P(),
            P(),
            P(),
            P(),
            P(),
            P(),
            P(),
            P(),
            P(),
            P(),
            P(),
            P(("ctx", "wsh"), None),
        ),
        out_specs=(
            P(("ctx", "wsh"), None),
            P(("ctx", "wsh"), None),
            P(),
            P(),
            P(),
            P(),
            P(),
            P(),
            P(),
            P(),
            P(),
            P(),
            P(),
            P(),
        ),
        check_vma=False,
    )
```

```python
import functools
import math

import jax
import jax.numpy as jnp
from jax import lax
from jax.experimental import pallas as pl
from jax.experimental.pallas import tpu as pltpu
from jax.sharding import PartitionSpec as P

HEAD = 64
RANK = 16
DOC_MAX = 4096


EPSILON = 1e-05
NEG_FILL = -1e30
SCALING = HEAD ** (-0.5)
SWAP = [(0, 1), (1, 0)]
VMEM_BYTES = 60 * 1024 * 1024


def norm_parts(values, gain, shift):
    row_mean = jnp.mean(values, axis=-1, keepdims=True)
    centered = values - row_mean
    variance = jnp.mean(centered * centered, axis=-1, keepdims=True)
    inverse = lax.rsqrt(variance + EPSILON)
    normed = centered * inverse
    return (normed * gain + shift, normed, inverse)


def norm_back(grad, normed, inverse, gain):
    scaled = grad * gain
    return inverse * (
        scaled
        - jnp.mean(scaled, axis=-1, keepdims=True)
        - normed * jnp.mean(scaled * normed, axis=-1, keepdims=True)
    )


def dot(left, right, lc=1, rc=0):
    return lax.dot_general(
        left, right, (((lc,), (rc,)), ((), ())), preferred_element_type=jnp.float32
    )


DOC_SLOTS = 64


def side_by_side(ref, first, count):
    return jnp.concatenate([ref[first + k, 0:HEAD, :] for k in range(count)], axis=1)


def marked_queries(query_ref, first, count, docs):
    query = side_by_side(query_ref, first, count)
    query = (query.astype(jnp.float32) * SCALING).astype(jnp.bfloat16)
    number = lax.broadcasted_iota(jnp.int32, (DOC_SLOTS, docs.shape[1]), 0)
    marks = jnp.where(number == docs, 0.0, NEG_FILL).astype(jnp.bfloat16)
    return query, jnp.concatenate([query, marks], axis=0)


def marked_keys(pair, bounds_ref, first_pos):
    rows = pair.shape[0]
    place = first_pos + lax.broadcasted_iota(jnp.int32, (rows, DOC_SLOTS), 0)
    marks = (place >= bounds_ref[0:1, :]) & (place < bounds_ref[1:2, :])
    marks = jnp.where(marks, 1.0, 0.0).astype(jnp.bfloat16)
    return jnp.concatenate([pair[:, :HEAD], marks], axis=1)


def causal(scores, first_pos, query_pos):
    row = lax.broadcasted_iota(jnp.int32, scores.shape, 0)
    return jnp.where(row <= query_pos - first_pos, scores, NEG_FILL)


def group_lanes(meta_ref, g, lanes, rows):
    lane = lax.broadcasted_iota(jnp.int32, (1, lanes), 1)
    return meta_ref[g, 2] + lane + jnp.where(lane >= rows, rows, 0)


def span_walk(meta_ref, g, size, block, state):
    def spot(t):
        first = pl.multiple_of(t * size, size)
        return pl.ds(first, size), meta_ref[0, 4] + first

    state = lax.fori_loop(
        meta_ref[g, 0], meta_ref[g, 1], lambda t, state: block(*spot(t), False, state), state
    )
    return block(*spot(meta_ref[g, 1]), True, state)


def span_copies(remote, places, semaphores, t):
    spot = pl.ds(2 * t, 2)
    return [
        pltpu.make_async_copy(source.at[spot], place.at[spot], semaphores.at[t, i])
        for i, (source, place) in enumerate(zip(remote, places))
    ]


def start_spans(meta_ref, groups, remote, places, semaphores):
    def start(t, carry):
        for copy in span_copies(remote, places, semaphores, t):
            copy.start()
        return carry

    lax.fori_loop(meta_ref[0, 5], meta_ref[groups - 1, 1] + 1, start, 0)


def new_blocks(meta_ref, g, remote, places, semaphores, rows, use):
    core = meta_ref[0, 3]

    def span(t, carry):
        for copy in span_copies(remote, places, semaphores, t):
            copy.wait()
        for k in range(2):
            for place, side in zip(places, (core, 1 - core)):
                use(pl.multiple_of(((2 * t + k) * 2 + side) * rows, rows), place.at[2 * t + k])
        return carry

    lax.fori_loop(meta_ref[g, 5], meta_ref[g, 1] + 1, span, 0)


def forward_kernel(
    pair_at, first_chunk, per_group, meta_ref, docs_ref, bounds_ref, own_ref, other_ref, *refs
):
    apart = len(refs) - 8
    query_ref, (low_ref, mixed_ref, lse_ref, own_place, other_place) = refs[0], refs[apart : apart + 5]
    keys_ref, values_ref, semaphores = refs[apart + 5 :]
    query_ref = query_ref if apart else own_place
    groups, _, lanes = docs_ref.shape
    rows = own_place.shape[2]
    remote, places = (own_ref, other_ref), (own_place, other_place)
    first_key = meta_ref[0, 4]
    start_spans(meta_ref, groups, remote, places, semaphores)

    def spread(first, pair_ref):
        pair = pair_ref[pair_at : pair_at + 2 * HEAD, :]
        keys_ref[pl.ds(first, rows), :] = marked_keys(pair.T, bounds_ref, first_key + first)
        values_ref[:, pl.ds(first, rows)] = pair[HEAD:]

    def group(g, carry):
        new_blocks(meta_ref, g, remote, places, semaphores, rows, spread)
        _, query = marked_queries(query_ref, first_chunk + g * per_group, per_group, docs_ref[g])
        query_pos = group_lanes(meta_ref, g, lanes, rows)

        def block(spot, first_pos, last, state):
            row_max, row_sum, total = state
            scores = dot(keys_ref[spot, :], query)
            if last:
                scores = causal(scores, first_pos, query_pos)
            new_max = jnp.maximum(row_max, jnp.max(scores, axis=0, keepdims=True))
            probs = jnp.exp(scores - new_max)
            shrink = jnp.exp(row_max - new_max)
            row_sum = row_sum * shrink + jnp.sum(probs, axis=0, keepdims=True)
            total = total * shrink + dot(values_ref[:, spot], probs.astype(jnp.bfloat16))
            return new_max, row_sum, total

        state = (
            jnp.full((1, lanes), NEG_FILL, jnp.float32),
            jnp.zeros((1, lanes), jnp.float32),
            jnp.zeros((HEAD, lanes), jnp.float32),
        )
        row_max, row_sum, total = span_walk(meta_ref, g, 4 * rows, block, state)
        mixed = total / row_sum
        mixed_ref[g] = mixed
        for k in range(per_group):
            low_ref[g * per_group + k] = mixed[:, k * rows : (k + 1) * rows].astype(jnp.bfloat16)
        lse_ref[g] = row_max + jnp.log(row_sum)
        return carry

    lax.fori_loop(0, groups, group, 0)


def backward_kernel(
    pair_at, first_chunk, per_group, turned, meta_ref, docs_ref, bounds_ref, own_ref, other_ref, *refs
):
    apart = len(refs) - 16
    grad_ref, mixed_ref, lse_ref = refs[apart : apart + 3]
    dq_ref, kept_ref, sent_ref, own_place, other_place, kept_place, sent_place = refs[apart + 3 : apart + 10]
    keys_ref, rows_ref, keys_t_ref, sum_ref, semaphores, out_semaphores = refs[apart + 10 :]
    query_ref = refs[0] if apart else own_place
    groups, _, lanes = docs_ref.shape
    blocks, _, rows = own_place.shape
    remote, places = (own_ref, other_ref), (own_place, other_place)
    core, first_key = meta_ref[0, 3], meta_ref[0, 4]
    start_spans(meta_ref, groups, remote, places, semaphores)
    if apart:
        sum_ref[...] = jnp.zeros(sum_ref.shape, jnp.float32)

    def spread(first, pair_ref):
        pair = pair_ref[pair_at : pair_at + 2 * HEAD, :]
        turned_pair = pair.T
        rows_ref[pl.ds(first, rows), :] = turned_pair
        keys_ref[pl.ds(first, rows), :] = marked_keys(turned_pair, bounds_ref, first_key + first)
        keys_t_ref[:, pl.ds(first, rows)] = pair[:HEAD]
        if not apart:
            sum_ref[pl.ds(first, rows), :] = jnp.zeros((rows, 2 * HEAD), jnp.float32)

    def group(g, carry):
        new_blocks(meta_ref, g, remote, places, semaphores, rows, spread)
        first = first_chunk + g * per_group
        query, query_marked = marked_queries(query_ref, first, per_group, docs_ref[g])
        grad = side_by_side(grad_ref, g * per_group, per_group)
        nothing = jnp.zeros_like(query)
        query_low = jnp.concatenate([query, nothing], axis=0)
        grad_high = jnp.concatenate([nothing, grad], axis=0)
        both = jnp.concatenate([query_low, grad_high], axis=1).T
        delta = jnp.sum(grad.astype(jnp.float32) * mixed_ref[g], axis=0, keepdims=True)
        lse = lse_ref[g]
        query_pos = group_lanes(meta_ref, g, lanes, rows)

        def block(spot, first_pos, last, total):
            scores = dot(keys_ref[spot, :], query_marked)
            if last:
                scores = causal(scores, first_pos, query_pos)
            probs = jnp.exp(scores - lse)
            prob_grad = dot(rows_ref[spot, :], grad_high)
            score_grad = (probs * (prob_grad - delta)).astype(jnp.bfloat16)
            sum_ref[spot, :] += dot(
                jnp.concatenate([score_grad, probs.astype(jnp.bfloat16)], axis=1), both
            )
            return total + dot(keys_t_ref[:, spot], score_grad)

        total = span_walk(meta_ref, g, 4 * rows, block, jnp.zeros((HEAD, lanes), jnp.float32))
        total = (total * SCALING).astype(jnp.bfloat16)
        for k in range(per_group):
            dq_ref[g * per_group + k] = total[:, k * rows : (k + 1) * rows]
        return carry

    lax.fori_loop(0, groups, group, 0)

    def out_copies(j):
        return [
            pltpu.make_async_copy(place.at[j], ref.at[j], out_semaphores.at[j, i])
            for i, (place, ref) in enumerate(((kept_place, kept_ref), (sent_place, sent_ref)))
        ]

    def finish(j, carry):
        for ref, side in ((kept_place, core), (sent_place, 1 - core)):
            spot = pl.ds(pl.multiple_of((2 * j + side) * rows, rows), rows)
            total = sum_ref[spot, :]
            ref[j] = (total.T if turned else total).astype(ref.dtype)
        for copy in out_copies(j):
            copy.start()
        return carry

    def finished(j, carry):
        for copy in out_copies(j):
            copy.wait()
        return carry

    lax.fori_loop(0, blocks, finish, 0)
    lax.fori_loop(0, blocks, finished, 0)


def cost(microseconds):
    return pl.CostEstimate(
        flops=microseconds * 1_000_000_000, bytes_accessed=microseconds * 1_000_000, transcendentals=0
    )


SMEM_SPEC = pl.BlockSpec(memory_space=pltpu.SMEM)
VMEM_SPEC = pl.BlockSpec(memory_space=pltpu.VMEM)


ANY_SPEC = pl.BlockSpec(memory_space=pl.ANY)


def attention_forward(plan, own, other, query, name, microseconds):
    meta, docs, bounds, pair_at, first_chunk, per_group = plan
    groups, _, lanes = docs.shape
    blocks, _, rows = own.shape
    keys = blocks * 2 * rows
    return pl.pallas_call(
        functools.partial(forward_kernel, pair_at, first_chunk, per_group),
        out_shape=(
            jax.ShapeDtypeStruct((groups * per_group, HEAD, rows), jnp.bfloat16),
            jax.ShapeDtypeStruct((groups, HEAD, lanes), jnp.float32),
            jax.ShapeDtypeStruct((groups, 1, lanes), jnp.float32),
        ),
        in_specs=[SMEM_SPEC] + [VMEM_SPEC] * 2 + [ANY_SPEC] * 2 + [VMEM_SPEC] * len(query),
        out_specs=(VMEM_SPEC,) * 3,
        scratch_shapes=[
            *[pltpu.VMEM(own.shape, jnp.bfloat16)] * 2,
            pltpu.VMEM((keys, HEAD + DOC_SLOTS), jnp.bfloat16),
            pltpu.VMEM((HEAD, keys), jnp.bfloat16),
            pltpu.SemaphoreType.DMA((blocks // 2, 2)),
        ],
        compiler_params=pltpu.CompilerParams(vmem_limit_bytes=VMEM_BYTES),
        cost_estimate=cost(microseconds),
        name=name,
    )(meta, docs, bounds, own, other, *query)


def attention_backward(plan, own, other, query, grad, mixed, lse, turned, name, microseconds):
    meta, docs, bounds, pair_at, first_chunk, per_group = plan
    groups, _, lanes = docs.shape
    blocks, _, rows = own.shape
    keys = blocks * 2 * rows
    part = (blocks, 2 * HEAD, rows) if turned else (blocks, rows, 2 * HEAD)
    return pl.pallas_call(
        functools.partial(backward_kernel, pair_at, first_chunk, per_group, turned),
        out_shape=(
            jax.ShapeDtypeStruct((groups * per_group, HEAD, rows), jnp.bfloat16),
            jax.ShapeDtypeStruct(part, jnp.float32),
            jax.ShapeDtypeStruct(part, jnp.bfloat16),
        ),
        in_specs=[SMEM_SPEC] + [VMEM_SPEC] * 2 + [ANY_SPEC] * 2 + [VMEM_SPEC] * (len(query) + 3),
        out_specs=(VMEM_SPEC, ANY_SPEC, ANY_SPEC),
        scratch_shapes=[
            *[pltpu.VMEM(own.shape, jnp.bfloat16)] * 2,
            pltpu.VMEM(part, jnp.float32),
            pltpu.VMEM(part, jnp.bfloat16),
            pltpu.VMEM((keys, HEAD + DOC_SLOTS), jnp.bfloat16),
            pltpu.VMEM((keys, 2 * HEAD), jnp.bfloat16),
            pltpu.VMEM((HEAD, keys), jnp.bfloat16),
            pltpu.VMEM((keys, 2 * HEAD), jnp.float32),
            pltpu.SemaphoreType.DMA((blocks // 2, 2)),
            pltpu.SemaphoreType.DMA((blocks, 2)),
        ],
        compiler_params=pltpu.CompilerParams(vmem_limit_bytes=VMEM_BYTES),
        cost_estimate=cost(microseconds),
        name=name,
    )(meta, docs, bounds, own, other, *query, grad, mixed, lse)


def gelu_parts(value):
    scale = (2.0 / math.pi) ** 0.5
    square = value * value
    bent = jnp.tanh(scale * value * (1.0 + 0.044715 * square))
    upper = 0.5 * (1.0 + bent)
    slope = 0.5 * value * (1.0 - bent * bent) * scale * (1.0 + 3 * 0.044715 * square)
    return value * upper, upper + slope


def column_norm(values, gain, shift):
    row_mean = jnp.mean(values, axis=0, keepdims=True)
    centered = values - row_mean
    variance = jnp.mean(centered * centered, axis=0, keepdims=True)
    inverse = lax.rsqrt(variance + EPSILON)
    normed = centered * inverse
    return (normed * gain + shift, normed, inverse)


def column_norm_back(grad, normed, inverse, gain):
    scaled = grad * gain
    return inverse * (
        scaled
        - jnp.mean(scaled, axis=0, keepdims=True)
        - normed * jnp.mean(scaled * normed, axis=0, keepdims=True)
    )


def fetched(refs, places, semaphores):
    copies = [
        pltpu.make_async_copy(ref, place, semaphores.at[i])
        for i, (ref, place) in enumerate(zip(refs, places))
    ]
    for copy in copies:
        copy.start()
    return copies


def half_rows(core, half):
    return (
        pl.ds(pl.multiple_of(core * half, 32), half),
        pl.ds(pl.multiple_of((1 - core) * half, 32), half),
    )


def middle_kernel(
    tile, core_ref, *refs
):
    sources, remote, results, (kept_ref, sent_ref), places, result_places, refs = (
        refs[:10], refs[10:18], refs[18:22], refs[22:24], refs[24:34], refs[34:38], refs[38:],
    )
    (
        mixed_main_ref, mixed_last_ref, mask_ref, a_out_ref, cotangent_ref, b_down_ref, b_out_ref,
        stream_ref, gains_ref, a_up_ref,
    ) = places
    output_ref, middle_grad_ref, main_grad_ref, last_grad_ref = result_places
    (
        out_ref, up_ref, b_up_ref, down_w_ref, a_down_ref, kept_place, sent_place,
        mixed_ref, middle_ref, hidden_ref, hidden_rows_ref, cot_rows_ref, inner_out_ref,
        inner_up_ref, down_grad_ref, inner_down_ref, up_grad_ref, down_ref, back_ref,
        semaphores, out_semaphores, place_semaphores, result_semaphores,
    ) = refs
    core = core_ref[0]
    half, wide = remote[2].shape
    width = 2 * half
    full = wide // tile
    low = jnp.bfloat16
    sides = half_rows(core, half)

    def copies(first, size, number):
        spot = pl.ds(first, size)
        pairs = [(remote[2 + i].at[:, spot], up_ref.at[sides[i], spot]) for i in range(2)]
        pairs += [(remote[5 + i].at[:, spot], down_w_ref.at[sides[i], spot]) for i in range(2)]
        pairs += [(remote[4].at[:, spot], b_up_ref.at[:, spot])]
        pairs += [(remote[7].at[spot, :], a_down_ref.at[spot, :])]
        return [
            pltpu.make_async_copy(source, place, semaphores.at[number, i])
            for i, (source, place) in enumerate(pairs)
        ]

    firsts = [
        pltpu.make_async_copy(remote[i], out_ref.at[sides[i], :], semaphores.at[full + 1, i])
        for i in range(2)
    ]
    given = fetched(sources[:6], places[:6], place_semaphores)
    for copy in firsts:
        copy.start()
    later = [
        pltpu.make_async_copy(sources[i], places[i], place_semaphores.at[i]) for i in range(6, 10)
    ]
    for copy in later:
        copy.start()

    def give(i):
        copy = pltpu.make_async_copy(result_places[i], results[i], result_semaphores.at[i])
        copy.start()
        return copy

    def start_chunk(k):
        @pl.when(k < full)
        def _():
            for copy in copies(pl.multiple_of(k * tile, tile), tile, k):
                copy.start()

        if wide % tile:

            @pl.when(k == full)
            def _():
                for copy in copies(full * tile, wide % tile, full):
                    copy.start()

    def out_copies(first, size, number):
        spot = pl.ds(first, size)
        pairs = ((kept_place, kept_ref), (sent_place, sent_ref))
        return [
            pltpu.make_async_copy(place.at[spot, :], ref.at[spot, :], out_semaphores.at[number, i])
            for i, (place, ref) in enumerate(pairs)
        ]

    def put(first, rows, other):
        spot = pl.ds(first, rows.shape[0])

        @pl.when(core == 0)
        def _():
            kept_place[spot, :] = rows
            sent_place[spot, :] = other

        @pl.when(core == 1)
        def _():
            kept_place[spot, :] = other
            sent_place[spot, :] = rows

    for copy in given[:4]:
        copy.wait()
    mask = mask_ref[...]
    mask_low = mask.astype(low)
    main = mixed_main_ref.shape[0] * HEAD
    mixed_ref[:main, :] = mixed_main_ref[...].reshape(main, mixed_main_ref.shape[2])
    mixed_ref[main:, :] = mixed_last_ref[0]
    mixed_rows = mixed_ref[...].T
    inner_out = (mask * (dot(mixed_rows, a_out_ref[...]))).astype(low)
    inner_out_ref[...] = inner_out
    for copy in given[4:]:
        copy.wait()
    cot_rows = cotangent_ref[...].T
    cot_rows_ref[...] = cot_rows
    down_grad_ref[...] = dot(cot_rows, b_down_ref[...]).astype(low) * mask_low
    for copy in (*firsts, *later):
        copy.wait()
    start_chunk(0)
    start_chunk(1)
    branch = dot(mixed_rows, out_ref[...]).T + dot(b_out_ref[...], inner_out.T)
    middle = stream_ref[...].astype(jnp.float32) + branch
    middle_ref[...] = middle
    hidden = column_norm(middle, gains_ref[:, 2:3], gains_ref[:, 3:4])[0].astype(low)
    hidden_ref[...] = hidden
    hidden_rows = hidden.T
    hidden_rows_ref[...] = hidden_rows
    inner_up_ref[...] = (mask * dot(hidden_rows, a_up_ref[...])).astype(low)
    for ref in (inner_down_ref, up_grad_ref, down_ref, back_ref):
        ref[...] = jnp.zeros(ref.shape, ref.dtype)

    def step(k, size):
        first = k * tile if isinstance(k, int) else pl.multiple_of(k * tile, tile)
        for copy in copies(first, size, k):
            copy.wait()
        start_chunk(k + 2)
        spot = pl.ds(first, size)
        up, b_up, down_w, a_down = up_ref[:, spot], b_up_ref[:, spot], down_w_ref[:, spot], a_down_ref[spot, :]
        inner_up, down_grad = inner_up_ref[...], down_grad_ref[...]
        upward = dot(hidden_rows_ref[...], up) + dot(inner_up, b_up)
        active_grad = dot(cot_rows_ref[...], down_w) + dot(down_grad, a_down.T)
        active, slope = gelu_parts(upward)
        active = active.astype(low)
        up_grad = (active_grad * slope).astype(low)
        active_t, up_grad_t = active.T, up_grad.T
        down_ref[...] += dot(down_w, active_t)
        back_ref[...] += dot(up, up_grad_t)
        inner_down_ref[...] += dot(active, a_down)
        up_grad_ref[...] += dot(b_up, up_grad_t)
        put(first, dot(up_grad_t, inner_up).astype(low), dot(active_t, down_grad).astype(low))
        for copy in out_copies(first, size, k):
            copy.start()

    def loop(k, carry):
        step(k, tile)
        return carry

    lax.fori_loop(0, full, loop, 0)
    if wide % tile:
        step(full, wide % tile)

    inner_down = (mask * inner_down_ref[...]).astype(low)
    middle = middle_ref[...]
    inner_grad = up_grad_ref[...].astype(low).T * mask_low
    hidden_grad = back_ref[...] + dot(a_up_ref[...], inner_grad.T)
    gain = gains_ref[:, 2:3]
    _, normed, inverse = column_norm(middle, gain, gain)
    middle_grad = cotangent_ref[...].astype(jnp.float32)
    middle_grad = middle_grad + column_norm_back(hidden_grad, normed, inverse, gain)
    middle_grad_ref[...] = middle_grad
    given = [give(1)]
    branch = middle_grad.astype(low)
    out_grad = dot(branch.T, b_out_ref[...]).astype(low) * mask_low
    put(wide, dot(cotangent_ref[...], inner_down).astype(low), dot(mixed_ref[...], out_grad).astype(low))
    put(
        wide + width,
        dot(hidden_ref[...], inner_grad).astype(low),
        dot(branch, inner_out_ref[...]).astype(low),
    )
    narrow = kept_place.shape[0] - wide
    spare = narrow - 2 * width
    if spare:
        nothing = jnp.zeros((spare, kept_place.shape[1]), low)
        put(wide + 2 * width, nothing, nothing)
    for copy in out_copies(wide, narrow, full + 1):
        copy.start()
    back = (dot(out_ref[...], branch) + dot(a_out_ref[...], out_grad.T)).astype(low)
    main_grad_ref[...] = back[:main].reshape(main_grad_ref.shape)
    last_grad_ref[0] = back[main:]
    given += [give(2), give(3)]
    down = down_ref[...] + dot(b_down_ref[...], inner_down.T)
    output_ref[...] = (middle + down).astype(low)
    given += [give(0)]

    def finished(k, carry):
        for copy in out_copies(pl.multiple_of(k * tile, tile), tile, k):
            copy.wait()
        return carry

    lax.fori_loop(0, full, finished, 0)
    if wide % tile:
        for copy in out_copies(full * tile, wide % tile, full):
            copy.wait()
    for copy in (*out_copies(wide, narrow, full + 1), *given):
        copy.wait()


def padded(size, unit):
    return -(-size // unit) * unit


def middle_part(
    core, mixed_main, mixed_last, tokens_t, cotangent_t, mask, gains_t, out_pair, a_out, b_out_t,
    a_up, b_down_t, up_pair, b_up, down_pair_t, a_down, unit,
):
    width, rows = tokens_t.shape
    half = width // 2
    inner, wide = b_up.shape
    tile = 512
    low = jnp.bfloat16
    operands = (
        mixed_main, mixed_last, mask, a_out, cotangent_t, b_down_t, b_out_t, tokens_t, gains_t, a_up
    )
    remote = (*out_pair, *up_pair, b_up, *down_pair_t, a_down)
    share = (padded(wide + 2 * width, unit), inner)
    shapes = (
        ((width, rows), low), ((width, rows), jnp.float32), (mixed_main.shape, low),
        (mixed_last.shape, low), (share, low), (share, low),
    )
    return pl.pallas_call(
        functools.partial(middle_kernel, tile),
        out_shape=tuple(jax.ShapeDtypeStruct(*item) for item in shapes),
        in_specs=[SMEM_SPEC] + [ANY_SPEC] * (len(operands) + len(remote)),
        out_specs=(ANY_SPEC,) * 6,
        scratch_shapes=[
            *[pltpu.VMEM(item.shape, item.dtype) for item in operands],
            *[pltpu.VMEM(*item) for item in shapes[:4]],
            pltpu.VMEM((width, width), low),
            pltpu.VMEM((width, wide), low),
            pltpu.VMEM((inner, wide), low),
            pltpu.VMEM((width, wide), low),
            pltpu.VMEM((wide, inner), low),
            *[pltpu.VMEM(share, low)] * 2,
            pltpu.VMEM((width, rows), low),
            pltpu.VMEM((width, rows), jnp.float32),
            pltpu.VMEM((width, rows), low),
            *[pltpu.VMEM((rows, width), low)] * 2,
            *[pltpu.VMEM((rows, inner), low)] * 3,
            pltpu.VMEM((rows, inner), jnp.float32),
            pltpu.VMEM((inner, rows), jnp.float32),
            *[pltpu.VMEM((width, rows), jnp.float32)] * 2,
            pltpu.SemaphoreType.DMA((wide // tile + 2, 6)),
            pltpu.SemaphoreType.DMA((wide // tile + 2, 2)),
            pltpu.SemaphoreType.DMA((len(operands),)),
            pltpu.SemaphoreType.DMA((4,)),
        ],
        compiler_params=pltpu.CompilerParams(vmem_limit_bytes=VMEM_BYTES),
        cost_estimate=cost(20),
        name="middle_part",
    )(core, *operands, *remote)


def whole_call(kernel, shapes, scratch, operands, remote, microseconds, name):
    space = [pltpu.VMEM(item.shape, item.dtype) for item in remote]
    return pl.pallas_call(
        kernel,
        out_shape=tuple(jax.ShapeDtypeStruct(*item) for item in shapes),
        in_specs=[SMEM_SPEC]
        + [VMEM_SPEC] * (len(operands) - 1)
        + [pl.BlockSpec(memory_space=pl.ANY)] * len(remote),
        out_specs=(VMEM_SPEC,) * len(shapes),
        scratch_shapes=[pltpu.VMEM(*item) for item in scratch]
        + space
        + ([pltpu.SemaphoreType.DMA((len(remote),))] if remote else []),
        compiler_params=pltpu.CompilerParams(vmem_limit_bytes=VMEM_BYTES),
        cost_estimate=cost(microseconds),
        name=name,
    )(*operands, *remote)


def entry_kernel(
    place_ref, lengths_ref, adapters_ref, tokens_ref, gains_own_ref, gains_other_ref, *refs
):
    remote, results, refs = refs[:12], refs[12:19], refs[19:]
    places, (weight_ref, up_ref, down_ref, semaphores, result_semaphores) = refs[:7], refs[7:]
    hidden_ref, inner_ref, mask_ref, gains_ref, heads_ref, query_ref, pairs_ref = places
    rows, inner = mask_ref.shape
    half = gains_own_ref.shape[1]
    sides = half_rows(place_ref[0], half)
    copies = []
    for n in range(3):
        down, own, up, other = remote[4 * n : 4 * n + 4]
        pairs = (
            (down, down_ref.at[n]), (up, up_ref.at[n]),
            (own, weight_ref.at[n, sides[0], :]), (other, weight_ref.at[n, sides[1], :]),
        )
        for i, (source, place) in enumerate(pairs):
            copies.append(pltpu.make_async_copy(source, place, semaphores.at[4 * n + i]))
    for copy in copies:
        copy.start()

    def give(i):
        copy = pltpu.make_async_copy(places[i], results[i], result_semaphores.at[i])
        copy.start()
        return copy

    for spot, ref in zip(sides, (gains_own_ref, gains_other_ref)):
        gains_ref[spot, :] = ref[...].astype(jnp.float32).T
    values = tokens_ref[...].astype(jnp.float32)
    hidden = column_norm(values, gains_ref[:, 0:1], gains_ref[:, 1:2])[0].astype(jnp.bfloat16)
    hidden_ref[...] = hidden
    hidden_rows = hidden.T
    place = place_ref[1] + lax.broadcasted_iota(jnp.int32, (rows, inner), 0)
    column = lax.broadcasted_iota(jnp.int32, (rows, inner), 1) // RANK

    def document(d, state):
        start, mask = state
        end = start + lengths_ref[d]
        chosen = (place >= start) & (place < end) & (column == adapters_ref[d])
        return end, jnp.where(chosen, 1.0, mask)

    state = (jnp.int32(0), jnp.zeros((rows, inner), jnp.float32))
    _, mask = lax.fori_loop(0, lengths_ref.shape[0], document, state)
    mask_ref[...] = mask
    given = [give(0), give(2), give(3)]
    count = heads_ref.shape[0]
    for n in range(3):
        for copy in copies[4 * n : 4 * n + 4]:
            copy.wait()
        products = (mask * dot(hidden_rows, down_ref[n])).astype(jnp.bfloat16)
        inner_ref[n] = products
        total = dot(hidden_rows, weight_ref[n]).T + dot(up_ref[n], products.T)
        total = total.astype(jnp.bfloat16)
        for c in range(count):
            heads_ref[c, n * HEAD : (n + 1) * HEAD, :] = total[c * HEAD : (c + 1) * HEAD]
        if n == 0:
            query_ref[0] = total[count * HEAD :]
        else:
            for c in range(count):
                pairs_ref[c, (n - 1) * HEAD : n * HEAD, :] = total[count * HEAD :]
    for copy in (*given, *[give(i) for i in (1, 4, 5, 6)]):
        copy.wait()


def projections(place, lengths, adapters, tokens_t, gains, gains_other, weights, others, downs, ups_t):
    width, rows = tokens_t.shape
    inner = downs[0].shape[1]
    low = jnp.bfloat16
    count = width // HEAD - 1
    remote = [item for group in zip(downs, weights, ups_t, others) for item in group]
    shapes = (
        ((width, rows), low), ((3, rows, inner), low), ((rows, inner), jnp.float32),
        ((width, gains.shape[0]), jnp.float32), ((count, 3 * HEAD, rows), low),
        ((1, HEAD, rows), low), ((count, 2 * HEAD, rows), low),
    )
    return pl.pallas_call(
        entry_kernel,
        out_shape=tuple(jax.ShapeDtypeStruct(*item) for item in shapes),
        in_specs=[SMEM_SPEC] * 3 + [VMEM_SPEC] * 3 + [ANY_SPEC] * len(remote),
        out_specs=(ANY_SPEC,) * len(shapes),
        scratch_shapes=[pltpu.VMEM(*item) for item in shapes]
        + [
            pltpu.VMEM((3, width, width), low),
            pltpu.VMEM((3, width, inner), low),
            pltpu.VMEM((3, width, inner), low),
            pltpu.SemaphoreType.DMA((12,)),
            pltpu.SemaphoreType.DMA((len(shapes),)),
        ],
        compiler_params=pltpu.CompilerParams(vmem_limit_bytes=VMEM_BYTES),
        cost_estimate=cost(6),
        name="entry",
    )(place, lengths, adapters, tokens_t, gains, gains_other, *remote)


def gathered_grad(n, heads_ref, last_query_ref, last_pair_ref, grad_ref):
    count = heads_ref.shape[0]
    for c in range(count):
        grad_ref[c * HEAD : (c + 1) * HEAD, :] = heads_ref[c, n * HEAD : (n + 1) * HEAD, :]
    if n == 0:
        grad_ref[count * HEAD :, :] = last_query_ref[0]
    else:
        grad_ref[count * HEAD :, :] = last_pair_ref[...].T[(n - 1) * HEAD : n * HEAD]
    return grad_ref[...]


def projections_late_kernel(core_ref, *refs):
    sources, (kept_ref, sent_ref, inner_grad_ref), refs = refs[:9], refs[9:12], refs[12:]
    places, (kept_place, sent_place, grad_ref, semaphores, out_semaphores) = refs[:9], refs[9:]
    heads_ref, last_query_ref, last_pair_ref, mask_ref, hidden_ref, inner_ref, *ups = places
    copies = fetched(sources, places, semaphores)
    core = core_ref[0]
    low = jnp.bfloat16
    width, share = hidden_ref.shape[0], kept_place.shape[0]

    def store(side, spot, rows):
        @pl.when(core == side)
        def _():
            kept_place[spot, :] = rows

        @pl.when(core != side)
        def _():
            sent_place[spot, :] = rows

    def keep(first, rows):
        done = 0
        while done < rows.shape[0]:
            side, spot = divmod(first + done, share)
            size = min(rows.shape[0] - done, share - spot)
            store(side, slice(spot, spot + size), rows[done : done + size])
            done += size

    keep(6 * width, jnp.zeros((2 * share - 6 * width, kept_place.shape[1]), low))
    for copy in copies[:6]:
        copy.wait()
    mask_low = mask_ref[...].astype(low)
    hidden = hidden_ref[...]
    for n in range(3):
        grad = gathered_grad(n, heads_ref, last_query_ref, last_pair_ref, grad_ref)
        copies[6 + n].wait()
        inner_grad = dot(grad.T, ups[n][...]).astype(low) * mask_low
        inner_grad_ref[n] = inner_grad
        keep(2 * n * width, dot(hidden, inner_grad).astype(low))
        keep((2 * n + 1) * width, dot(grad, inner_ref[n]).astype(low))
    given = fetched((kept_place, sent_place), (kept_ref, sent_ref), out_semaphores)
    for copy in given:
        copy.wait()


def projections_late(core, heads, last_query, last_pair, hidden_t, inners, mask, ups_t, unit):
    width, rows = hidden_t.shape
    low = jnp.bfloat16
    share = (padded(6 * width, 2 * unit) // 2, mask.shape[1])
    operands = (heads, last_query, last_pair, mask, hidden_t, inners, *ups_t)
    return pl.pallas_call(
        projections_late_kernel,
        out_shape=(
            jax.ShapeDtypeStruct(share, low),
            jax.ShapeDtypeStruct(share, low),
            jax.ShapeDtypeStruct(inners.shape, low),
        ),
        in_specs=[SMEM_SPEC] + [ANY_SPEC] * len(operands),
        out_specs=(ANY_SPEC, ANY_SPEC, VMEM_SPEC),
        scratch_shapes=[pltpu.VMEM(item.shape, item.dtype) for item in operands]
        + [
            pltpu.VMEM(share, low),
            pltpu.VMEM(share, low),
            pltpu.VMEM((width, rows), low),
            pltpu.SemaphoreType.DMA((len(operands),)),
            pltpu.SemaphoreType.DMA((2,)),
        ],
        compiler_params=pltpu.CompilerParams(vmem_limit_bytes=VMEM_BYTES),
        cost_estimate=cost(5),
        name="projections_late",
    )(core, *operands)


def projections_back_kernel(
    core_ref, heads_ref, last_query_ref, last_pair_ref, inner_grad_ref, gains_ref, tokens_ref, *refs
):
    remote, (grad_in_ref, grad_ref, sum_ref), local_refs, semaphores = (
        refs[:10], refs[10:13], refs[13:23], refs[23],
    )
    copies = fetched(remote, local_refs, semaphores)
    downs, weights, others, middle_grad_ref = (
        local_refs[:3], local_refs[3:6], local_refs[6:9], local_refs[9],
    )
    own_rows, other_rows = half_rows(core_ref[0], weights[0].shape[0])
    for n in range(3):
        grad = gathered_grad(n, heads_ref, last_query_ref, last_pair_ref, grad_ref)
        turned = inner_grad_ref[n].T
        copies[n].wait()
        for rows, weight, copy in (
            (own_rows, weights[n], copies[3 + n]), (other_rows, others[n], copies[6 + n])
        ):
            copy.wait()
            part = dot(weight[...], grad) + dot(downs[n][rows, :], turned)
            sum_ref[rows, :] = part if n == 0 else sum_ref[rows, :] + part
    gain = gains_ref[:, 0:1]
    _, normed, inverse = column_norm(tokens_ref[...].astype(jnp.float32), gain, gain)
    back = column_norm_back(sum_ref[...], normed, inverse, gain)
    copies[9].wait()
    grad_in_ref[...] = (middle_grad_ref[...] + back).astype(jnp.bfloat16)


def projections_back(
    core, heads, last_query, last_pair, inner_grads, gains_t, tokens_t, middle_grad_t,
    weights, others, downs,
):
    width, rows = tokens_t.shape
    low = jnp.bfloat16
    return whole_call(
        projections_back_kernel,
        (((width, rows), low),),
        (((width, rows), low), ((width, rows), jnp.float32)),
        (core, heads, last_query, last_pair, inner_grads, gains_t, tokens_t),
        (*downs, *weights, *others, middle_grad_t),
        8, "projections_back",
    )[0]


def steps_of(cycle_size):
    bits = cycle_size.bit_length() - 1
    return [(bit, min(2, bits - bit)) for bit in range(0, bits, 2)]


def partners(cycle_size, step, k):
    return [(i, i ^ (k << step[0])) for i in range(cycle_size)]


def scattered(array, step, cycle_size):
    count = 1 << step[1]
    mine = (lax.axis_index("ctx") >> step[0]) & (count - 1)
    blocks = array.reshape(count, array.shape[0] // count, array.shape[1])

    def block(number):
        return lax.dynamic_index_in_dim(blocks, number, 0, keepdims=False)

    total = block(mine).astype(jnp.float32)
    for k in range(1, count):
        got = lax.ppermute(block(mine ^ k), "ctx", partners(cycle_size, step, k))
        total = total + got.astype(jnp.float32)
    return total.astype(array.dtype)


def collected(share, step, cycle_size):
    count = 1 << step[1]
    mine = (lax.axis_index("ctx") >> step[0]) & (count - 1)
    blocks = [share]
    for k in range(1, count):
        blocks.append(lax.ppermute(share, "ctx", partners(cycle_size, step, k)))
    for bit in range(step[1]):
        turned = ((mine >> bit) & 1) == 1
        blocks = [jnp.where(turned, blocks[k ^ (1 << bit)], blocks[k]) for k in range(count)]
    return jnp.concatenate(blocks, axis=0)


def pair_sum(kept, sent):
    return kept + lax.ppermute(sent, "wsh", SWAP)


def early_finish_kernel(
    factor, core_ref, own_ref, other_ref,
    b_up_ref, a_down_ref, b_down_ref, a_up_ref, a_out_ref, b_out_ref,
):
    wide, width = a_down_ref.shape[0], a_up_ref.shape[0]

    def finish(first_ref, second_ref):
        def part(ref, first, count):
            return ref[first : first + count, :].astype(jnp.float32) * factor

        for k in range(wide // 256):
            b_up_ref[:, k * 256 : (k + 1) * 256] = part(first_ref, k * 256, 256).T
        a_down_ref[...] = part(second_ref, 0, wide)
        b_down_ref[...] = part(first_ref, wide, width)
        a_up_ref[...] = part(first_ref, wide + width, width)
        a_out_ref[...] = part(second_ref, wide, width)
        b_out_ref[...] = part(second_ref, wide + width, width)

    @pl.when(core_ref[0] == 0)
    def _():
        finish(own_ref, other_ref)

    @pl.when(core_ref[0] == 1)
    def _():
        finish(other_ref, own_ref)


def late_finish_kernel(factor, core_ref, own_ref, other_ref, *refs):
    core = core_ref[0]
    targets, late_ref = refs[:6], refs[6]
    for side, ref in ((core, own_ref), (1 - core, other_ref)):
        late_ref[side] = ref[...].astype(jnp.float32) * factor
    width, share = targets[0].shape[0], late_ref.shape[1]
    for n, ref in enumerate(targets):
        done = 0
        while done < width:
            side, spot = divmod(n * width + done, share)
            rows = min(width - done, share - spot)
            ref[done : done + rows, :] = late_ref[side, spot : spot + rows, :]
            done += rows


def finished(kernel, factor, core, own, other, shapes, scratch, name):
    return whole_call(
        functools.partial(kernel, factor), [(shape, jnp.float32) for shape in shapes], scratch,
        (core, own, other), (), 1, name,
    )


def local(
    tokens_in,
    doc_lengths,
    doc_adapter,
    norm1_gain,
    norm1_bias,
    norm2_gain,
    norm2_bias,
    w_query,
    w_key,
    w_value,
    w_out,
    w_up,
    w_down,
    a_query,
    b_query,
    a_key,
    b_key,
    a_value,
    b_value,
    a_out,
    b_out,
    a_up,
    b_up,
    a_down,
    b_down,
    cotangent,
):
    group_size = lax.axis_size("wsh")
    cycle_size = lax.axis_size("ctx")
    tok_dev, width_all = tokens_in.shape
    head_count = width_all // HEAD
    block_len = tok_dev * group_size
    hop_count = (DOC_MAX + block_len - 2) // block_len
    span = head_count - 1
    cycle_pos = lax.axis_index("ctx")
    core = lax.axis_index("wsh")
    half = width_all // group_size

    first_row = cycle_pos * block_len + core * tok_dev
    doc_ends = jnp.cumsum(doc_lengths)
    doc_starts = doc_ends - doc_lengths

    team = cycle_pos // span
    past = hop_count if cycle_size > span else 0
    first_key = (team * span - past) * block_len
    key_blocks = past + span

    slots = DOC_SLOTS - doc_lengths.shape[0]
    bounds = jnp.stack([jnp.pad(doc_starts, (0, slots)), jnp.pad(doc_ends, (0, slots))])

    def plan(chunk_pos, pair_at, first_chunk, per_group):
        groups = chunk_pos.shape[0] // per_group
        row_pos = chunk_pos[:, None] + jnp.arange(tok_dev, dtype=jnp.int32)[None, :]
        row_docs = jnp.sum((doc_ends[None, None, :] <= row_pos[:, :, None]).astype(jnp.int32), axis=2)
        row_docs = row_docs.reshape(groups, 1, per_group * tok_dev)
        chunk_pos = chunk_pos.reshape(groups, per_group)
        began = jnp.where(doc_starts[None, :] <= chunk_pos[:, :1], doc_starts[None, :], 0)
        first = (jnp.max(began, axis=1) - first_key) // (2 * block_len)
        last = (chunk_pos[:, -1] - first_key) // (2 * block_len)
        same = jnp.ones((groups,), jnp.int32)
        whole = per_group > 1
        meta = [
            first,
            last,
            chunk_pos[:, 0],
            same * core,
            same * first_key,
            jnp.concatenate([first[:1] * 0, last[:-1] + 1]) if whole else first,
        ]
        meta = jnp.stack(meta, axis=1).astype(jnp.int32)
        docs = row_docs.astype(jnp.int32)
        return meta, docs, bounds.astype(jnp.int32), pair_at, first_chunk, per_group

    team_pos = (team * span + jnp.arange(span, dtype=jnp.int32)) * block_len + core * tok_dev
    main_plan = plan(team_pos.astype(jnp.int32), HEAD, past, 2)
    last_plan = plan(first_row[None].astype(jnp.int32), 0, 0, 1)

    def swap(array):
        return lax.ppermute(array, "wsh", SWAP)

    if cycle_size > span:
        teams = [[t * span + i for i in range(span)] for t in range(cycle_size // span)]
    else:
        teams = None

    def exchange(blocks):
        return lax.all_to_all(blocks, "ctx", 0, 0, tiled=True, axis_index_groups=teams)

    gains = jnp.stack([norm1_gain, norm1_bias, norm2_gain, norm2_bias])
    weights = [w_query, w_key, w_value, w_out, w_up, w_down.T]
    others = [swap(item) for item in weights]

    downs = (a_query, a_key, a_value)
    ups_t = (b_query.T, b_key.T, b_value.T)
    tokens_t = tokens_in.T
    core_1 = jnp.stack([core, first_row]).astype(jnp.int32)
    hidden_t, inners, adapter_mask, gains_t, heads, last_query, last_pairs = projections(
        core_1, doc_lengths, doc_adapter, tokens_t, gains, swap(gains), weights[:3], others[:3],
        downs, ups_t,
    )

    ahead = [(i, i + span) for i in range(cycle_size - span)]
    back = [(i + span, i) for i in range(cycle_size - span)]

    def with_past(blocks):
        if not past:
            return blocks
        return jnp.concatenate([lax.ppermute(blocks[span - past :], "ctx", ahead), blocks], axis=0)

    steps = steps_of(cycle_size)
    unit = 16 * cycle_size
    incoming = exchange(heads)
    incoming, last_pairs = lax.optimization_barrier((incoming, last_pairs))
    own = with_past(incoming)
    other = swap(own)
    last_own = exchange(last_pairs)
    low_main, total_main, lse_main = attention_forward(
        main_plan, own, other, (), "attention_forward", 30
    )
    low_main, last_own = lax.optimization_barrier((low_main, last_own))
    last_own = with_past(last_own)
    last_other = swap(last_own)
    low_last, mixed_last, lse_last = attention_forward(
        last_plan, last_own, last_other, (last_query,), "last_forward", 0
    )
    mixed_main = exchange(low_main)

    output_t, middle_grad_t, main_grad, last_out_grad, early_kept, early_sent = middle_part(
        core_1, mixed_main, low_last, tokens_t, cotangent.T, adapter_mask, gains_t,
        (w_out, others[3]), a_out, b_out.T, a_up, b_down.T, (w_up, others[4]), b_up,
        (w_down.T, others[5]), a_down, unit,
    )

    def pair_total(kept, sent):
        total = kept + swap(sent).astype(jnp.float32)
        if past:
            returned = lax.ppermute(total[:past].astype(jnp.bfloat16), "ctx", back)
            total = total[past:].at[span - past :].add(returned.astype(jnp.float32))
        return total

    def pair_back(dq, kept, sent):
        total = jnp.concatenate([dq.astype(jnp.float32), pair_total(kept, sent)], axis=1)
        return total.astype(jnp.bfloat16)

    dq_last, kept_last, sent_last = attention_backward(
        last_plan, last_own, last_other, (last_query,),
        last_out_grad, mixed_last, lse_last, False, "last_backward", 0,
    )
    grad_main = exchange(main_grad)
    dpair_last = pair_total(kept_last, sent_last).astype(jnp.bfloat16)
    plane = 1 << steps[0][1]
    lines = cycle_size // plane
    planes = [[l * plane + p for p in range(plane)] for l in range(lines)]
    digits = (2,) * (cycle_size.bit_length() - 3) + (plane,)
    if cycle_size > span:
        zero = jnp.zeros((cycle_size // span, *dpair_last.shape), dpair_last.dtype)
        dpair_last = lax.dynamic_update_index_in_dim(zero, dpair_last, team, 0)
    order = tuple(reversed(range(len(digits)))) + (len(digits), len(digits) + 1)
    dpair_last = jnp.transpose(dpair_last.reshape(digits + dpair_last.shape[-2:]), order)
    early = pair_sum(early_kept, early_sent)
    lanes = early.shape[1]
    early_rows, last_rows = early.shape[0] // cycle_size, tok_dev
    shared = jnp.concatenate(
        [
            early.reshape(plane, lines, early_rows, lanes),
            dpair_last.reshape(plane, lines, last_rows, lanes),
        ],
        axis=2,
    )
    grad_main, shared = lax.optimization_barrier((grad_main, shared))
    shared = lax.all_to_all(shared, "ctx", 0, 0, tiled=True, axis_index_groups=planes)
    dq_main, kept_main, sent_main = attention_backward(
        main_plan, own, other, (), grad_main, total_main, lse_main,
        True, "attention_backward", 40
    )
    dq_main, kept_main, sent_main, shared = lax.optimization_barrier(
        (dq_main, kept_main, sent_main, shared)
    )
    shared = jnp.sum(shared.astype(jnp.float32), axis=0).astype(jnp.bfloat16)
    shared = shared.reshape(lines * (early_rows + last_rows), lanes)
    incoming_back = exchange(pair_back(dq_main, kept_main, sent_main))
    singles = [(bit, 1) for bit in range(2, cycle_size.bit_length() - 1)]
    for step in singles:
        shared = scattered(shared, step, cycle_size)
    early, last_sum = shared[:early_rows], shared[early_rows:]

    late_kept, late_sent, inner_grads = projections_late(
        core_1, incoming_back, dq_last, last_sum, hidden_t, inners, adapter_mask, ups_t, unit
    )
    singles = singles[::-1]
    for step in singles[:1]:
        early = collected(early, step, cycle_size)
    late, early, inner_grads = lax.optimization_barrier(
        (pair_sum(late_kept, late_sent), early, inner_grads)
    )
    grad_in_t = projections_back(
        core_1, incoming_back, dq_last, last_sum, inner_grads, gains_t, tokens_t, middle_grad_t,
        weights[:3], others[:3], downs,
    )

    norm_factor = (tok_dev * group_size * cycle_size) ** (-0.5)
    late = scattered(late, steps[0], cycle_size)
    for step in singles[1:]:
        early = collected(early, step, cycle_size)
    late, early, grad_in_t = lax.optimization_barrier((late, early, grad_in_t))
    for step in steps[1:]:
        late = scattered(late, step, cycle_size)
    early = collected(early, steps[0], cycle_size)
    late, early = lax.optimization_barrier((late, early))
    early_other = swap(early)
    for step in reversed(steps[1:]):
        late = collected(late, step, cycle_size)
    late, early_other = lax.optimization_barrier((late, early_other))
    late = collected(late, steps[0], cycle_size)
    wide = b_up.shape[1]
    early = finished(
        early_finish_kernel, norm_factor, core_1, early, early_other,
        [(lanes, wide), (wide, lanes)] + [(width_all, lanes)] * 4, (), "early_finish",
    )
    late, early = lax.optimization_barrier((late, early))
    g_b_up, g_a_down, g_b_down, g_a_up, g_a_out, g_b_out = early
    late = finished(
        late_finish_kernel, norm_factor, core_1, late, swap(late), [(width_all, lanes)] * 6,
        (((2, *late.shape), jnp.float32),), "late_finish",
    )
    return (
        output_t.T,
        grad_in_t.T,
        late[0],
        late[1].T,
        late[2],
        late[3].T,
        late[4],
        late[5].T,
        g_a_out,
        g_b_out.T,
        g_a_up,
        g_b_up,
        g_a_down,
        g_b_down.T,
    )


def solution(mesh):
    return jax.shard_map(
        local,
        mesh=mesh,
        in_specs=(
            P(("ctx", "wsh"), None),
            P(),
            P(),
            P("wsh"),
            P("wsh"),
            P("wsh"),
            P("wsh"),
            P("wsh", None),
            P("wsh", None),
            P("wsh", None),
            P("wsh", None),
            P("wsh", None),
            P(None, "wsh"),
            P(),
            P(),
            P(),
            P(),
            P(),
            P(),
            P(),
            P(),
            P(),
            P(),
            P(),
            P(),
            P(("ctx", "wsh"), None),
        ),
        out_specs=(
            P(("ctx", "wsh"), None),
            P(("ctx", "wsh"), None),
            P(),
            P(),
            P(),
            P(),
            P(),
            P(),
            P(),
            P(),
            P(),
            P(),
            P(),
            P(),
        ),
        check_vma=False,
    )
```

```python
import functools
import math

import jax
import jax.numpy as jnp
from jax import lax
from jax.experimental import pallas as pl
from jax.experimental.pallas import tpu as pltpu
from jax.sharding import PartitionSpec as P

HEAD = 64
RANK = 16
DOC_MAX = 4096


EPSILON = 1e-05
NEG_FILL = -1e30
SCALING = HEAD ** (-0.5)
SWAP = [(0, 1), (1, 0)]
VMEM_BYTES = 60 * 1024 * 1024


def norm_parts(values, gain, shift):
    row_mean = jnp.mean(values, axis=-1, keepdims=True)
    centered = values - row_mean
    variance = jnp.mean(centered * centered, axis=-1, keepdims=True)
    inverse = lax.rsqrt(variance + EPSILON)
    normed = centered * inverse
    return (normed * gain + shift, normed, inverse)


def norm_back(grad, normed, inverse, gain):
    scaled = grad * gain
    return inverse * (
        scaled
        - jnp.mean(scaled, axis=-1, keepdims=True)
        - normed * jnp.mean(scaled * normed, axis=-1, keepdims=True)
    )


def dot(left, right, lc=1, rc=0):
    return lax.dot_general(
        left, right, (((lc,), (rc,)), ((), ())), preferred_element_type=jnp.float32
    )


DOC_SLOTS = 64


def side_by_side(ref, first, count):
    return jnp.concatenate([ref[first + k, 0:HEAD, :] for k in range(count)], axis=1)


def marked_queries(query_ref, first, count, docs):
    query = side_by_side(query_ref, first, count)
    query = (query.astype(jnp.float32) * SCALING).astype(jnp.bfloat16)
    number = lax.broadcasted_iota(jnp.int32, (DOC_SLOTS, docs.shape[1]), 0)
    marks = jnp.where(number == docs, 0.0, NEG_FILL).astype(jnp.bfloat16)
    return query, jnp.concatenate([query, marks], axis=0)


def marked_keys(pair, bounds_ref, first_pos):
    rows = pair.shape[0]
    place = first_pos + lax.broadcasted_iota(jnp.int32, (rows, DOC_SLOTS), 0)
    marks = (place >= bounds_ref[0:1, :]) & (place < bounds_ref[1:2, :])
    marks = jnp.where(marks, 1.0, 0.0).astype(jnp.bfloat16)
    return jnp.concatenate([pair[:, :HEAD], marks], axis=1)


def causal(scores, first_pos, query_pos):
    row = lax.broadcasted_iota(jnp.int32, scores.shape, 0)
    return jnp.where(row <= query_pos - first_pos, scores, NEG_FILL)


def group_lanes(meta_ref, g, lanes, rows):
    lane = lax.broadcasted_iota(jnp.int32, (1, lanes), 1)
    return meta_ref[g, 2] + lane + jnp.where(lane >= rows, rows, 0)


def span_walk(meta_ref, g, size, two, block, state):
    def spot(t):
        first = pl.multiple_of(t * size, size)
        return pl.ds(first, size), meta_ref[0, 4] + first

    def walk(first, end, alone, state):
        return lax.fori_loop(first, end, lambda t, state: block(*spot(t), False, alone, state), state)

    if two:
        state = walk(meta_ref[g, 0], meta_ref[g, 6], True, state)
    state = walk(meta_ref[g, 6], meta_ref[g, 1], False, state)
    return block(*spot(meta_ref[g, 1]), True, False, state)


def span_copies(remote, places, semaphores, t):
    spot = pl.ds(2 * t, 2)
    return [
        pltpu.make_async_copy(source.at[spot], place.at[spot], semaphores.at[t, i])
        for i, (source, place) in enumerate(zip(remote, places))
    ]


def start_spans(meta_ref, groups, remote, places, semaphores):
    def start(t, carry):
        for copy in span_copies(remote, places, semaphores, t):
            copy.start()
        return carry

    lax.fori_loop(meta_ref[0, 5], meta_ref[groups - 1, 1] + 1, start, 0)


def new_blocks(meta_ref, g, remote, places, semaphores, rows, use):
    core = meta_ref[0, 3]

    def span(t, carry):
        for copy in span_copies(remote, places, semaphores, t):
            copy.wait()
        for k in range(2):
            for place, side in zip(places, (core, 1 - core)):
                use(pl.multiple_of(((2 * t + k) * 2 + side) * rows, rows), place.at[2 * t + k])
        return carry

    lax.fori_loop(meta_ref[g, 5], meta_ref[g, 1] + 1, span, 0)


def forward_kernel(
    pair_at, first_chunk, per_group, meta_ref, docs_ref, bounds_ref, own_ref, other_ref, *refs
):
    apart = len(refs) - 8
    query_ref, (low_ref, mixed_ref, lse_ref, own_place, other_place) = refs[0], refs[apart : apart + 5]
    keys_ref, values_ref, semaphores = refs[apart + 5 :]
    query_ref = query_ref if apart else own_place
    groups, _, lanes = docs_ref.shape
    rows = own_place.shape[2]
    remote, places = (own_ref, other_ref), (own_place, other_place)
    first_key = meta_ref[0, 4]
    start_spans(meta_ref, groups, remote, places, semaphores)

    def spread(first, pair_ref):
        pair = pair_ref[pair_at : pair_at + 2 * HEAD, :]
        keys_ref[pl.ds(first, rows), :] = marked_keys(pair.T, bounds_ref, first_key + first)
        values_ref[:, pl.ds(first, rows)] = pair[HEAD:]

    def group(g, carry):
        new_blocks(meta_ref, g, remote, places, semaphores, rows, spread)
        _, query = marked_queries(query_ref, first_chunk + g * per_group, per_group, docs_ref[g])
        query_pos = group_lanes(meta_ref, g, lanes, rows)

        def block(spot, first_pos, last, alone, state):
            cut = slice(0, rows if alone else lanes)
            row_max, row_sum, total = (part[:, cut] for part in state)
            scores = dot(keys_ref[spot, :], query[:, cut])
            if last:
                scores = causal(scores, first_pos, query_pos)
            new_max = jnp.maximum(row_max, jnp.max(scores, axis=0, keepdims=True))
            probs = jnp.exp(scores - new_max)
            shrink = jnp.exp(row_max - new_max)
            row_sum = row_sum * shrink + jnp.sum(probs, axis=0, keepdims=True)
            total = total * shrink + dot(values_ref[:, spot], probs.astype(jnp.bfloat16))
            new = (new_max, row_sum, total)
            if alone:
                new = tuple(jnp.concatenate([x, y[:, rows:]], axis=1) for x, y in zip(new, state))
            return new

        state = (
            jnp.full((1, lanes), NEG_FILL, jnp.float32),
            jnp.zeros((1, lanes), jnp.float32),
            jnp.zeros((HEAD, lanes), jnp.float32),
        )
        row_max, row_sum, total = span_walk(meta_ref, g, 4 * rows, per_group == 2, block, state)
        mixed = total / row_sum
        mixed_ref[g] = mixed
        for k in range(per_group):
            low_ref[g * per_group + k] = mixed[:, k * rows : (k + 1) * rows].astype(jnp.bfloat16)
        lse_ref[g] = row_max + jnp.log(row_sum)
        return carry

    lax.fori_loop(0, groups, group, 0)


def backward_kernel(
    pair_at, first_chunk, per_group, turned, meta_ref, docs_ref, bounds_ref, own_ref, other_ref, *refs
):
    apart = len(refs) - 16
    grad_ref, mixed_ref, lse_ref = refs[apart : apart + 3]
    dq_ref, kept_ref, sent_ref, own_place, other_place, kept_place, sent_place = refs[apart + 3 : apart + 10]
    keys_ref, rows_ref, keys_t_ref, sum_ref, semaphores, out_semaphores = refs[apart + 10 :]
    query_ref = refs[0] if apart else own_place
    groups, _, lanes = docs_ref.shape
    blocks, _, rows = own_place.shape
    remote, places = (own_ref, other_ref), (own_place, other_place)
    core, first_key = meta_ref[0, 3], meta_ref[0, 4]
    start_spans(meta_ref, groups, remote, places, semaphores)
    if apart:
        sum_ref[...] = jnp.zeros(sum_ref.shape, jnp.float32)

    def spread(first, pair_ref):
        pair = pair_ref[pair_at : pair_at + 2 * HEAD, :]
        turned_pair = pair.T
        rows_ref[pl.ds(first, rows), :] = turned_pair
        keys_ref[pl.ds(first, rows), :] = marked_keys(turned_pair, bounds_ref, first_key + first)
        keys_t_ref[:, pl.ds(first, rows)] = pair[:HEAD]
        if not apart:
            sum_ref[pl.ds(first, rows), :] = jnp.zeros((rows, 2 * HEAD), jnp.float32)

    def group(g, carry):
        new_blocks(meta_ref, g, remote, places, semaphores, rows, spread)
        first = first_chunk + g * per_group
        query, query_marked = marked_queries(query_ref, first, per_group, docs_ref[g])
        grad = side_by_side(grad_ref, g * per_group, per_group)
        nothing = jnp.zeros_like(query)
        query_low = jnp.concatenate([query, nothing], axis=0)
        grad_high = jnp.concatenate([nothing, grad], axis=0)
        both = jnp.concatenate([query_low, grad_high], axis=1).T
        delta = jnp.sum(grad.astype(jnp.float32) * mixed_ref[g], axis=0, keepdims=True)
        lse = lse_ref[g]
        query_pos = group_lanes(meta_ref, g, lanes, rows)

        def block(spot, first_pos, last, alone, total):
            cut = slice(0, rows if alone else lanes)
            scores = dot(keys_ref[spot, :], query_marked[:, cut])
            if last:
                scores = causal(scores, first_pos, query_pos)
            probs = jnp.exp(scores - lse[:, cut])
            prob_grad = dot(rows_ref[spot, :], grad_high[:, cut])
            score_grad = (probs * (prob_grad - delta[:, cut])).astype(jnp.bfloat16)
            turned_back = both
            if alone:
                turned_back = jnp.concatenate([both[:rows], both[lanes : lanes + rows]], axis=0)
            sum_ref[spot, :] += dot(
                jnp.concatenate([score_grad, probs.astype(jnp.bfloat16)], axis=1), turned_back
            )
            new = total[:, cut] + dot(keys_t_ref[:, spot], score_grad)
            return jnp.concatenate([new, total[:, rows:]], axis=1) if alone else new

        total = span_walk(
            meta_ref, g, 4 * rows, per_group == 2, block, jnp.zeros((HEAD, lanes), jnp.float32)
        )
        total = (total * SCALING).astype(jnp.bfloat16)
        for k in range(per_group):
            dq_ref[g * per_group + k, 0:HEAD, :] = total[:, k * rows : (k + 1) * rows]
        return carry

    lax.fori_loop(0, groups, group, 0)

    def out_copies(j):
        return [
            pltpu.make_async_copy(place.at[j], ref.at[j], out_semaphores.at[j, i])
            for i, (place, ref) in enumerate(((kept_place, kept_ref), (sent_place, sent_ref)))
        ]

    def finish(j, carry):
        for ref, side in ((kept_place, core), (sent_place, 1 - core)):
            spot = pl.ds(pl.multiple_of((2 * j + side) * rows, rows), rows)
            total = sum_ref[spot, :]
            ref[j] = (total.T if turned else total).astype(ref.dtype)
        for copy in out_copies(j):
            copy.start()
        return carry

    def finished(j, carry):
        for copy in out_copies(j):
            copy.wait()
        return carry

    lax.fori_loop(0, blocks, finish, 0)
    lax.fori_loop(0, blocks, finished, 0)


def cost(microseconds):
    return pl.CostEstimate(
        flops=microseconds * 1_000_000_000, bytes_accessed=microseconds * 1_000_000, transcendentals=0
    )


SMEM_SPEC = pl.BlockSpec(memory_space=pltpu.SMEM)
VMEM_SPEC = pl.BlockSpec(memory_space=pltpu.VMEM)


ANY_SPEC = pl.BlockSpec(memory_space=pl.ANY)


def attention_forward(plan, own, other, query, name, microseconds):
    meta, docs, bounds, pair_at, first_chunk, per_group = plan
    groups, _, lanes = docs.shape
    blocks, _, rows = own.shape
    keys = blocks * 2 * rows
    return pl.pallas_call(
        functools.partial(forward_kernel, pair_at, first_chunk, per_group),
        out_shape=(
            jax.ShapeDtypeStruct((groups * per_group, HEAD, rows), jnp.bfloat16),
            jax.ShapeDtypeStruct((groups, HEAD, lanes), jnp.float32),
            jax.ShapeDtypeStruct((groups, 1, lanes), jnp.float32),
        ),
        in_specs=[SMEM_SPEC] + [VMEM_SPEC] * 2 + [ANY_SPEC] * 2 + [VMEM_SPEC] * len(query),
        out_specs=(VMEM_SPEC,) * 3,
        scratch_shapes=[
            *[pltpu.VMEM(own.shape, jnp.bfloat16)] * 2,
            pltpu.VMEM((keys, HEAD + DOC_SLOTS), jnp.bfloat16),
            pltpu.VMEM((HEAD, keys), jnp.bfloat16),
            pltpu.SemaphoreType.DMA((blocks // 2, 2)),
        ],
        compiler_params=pltpu.CompilerParams(vmem_limit_bytes=VMEM_BYTES),
        cost_estimate=cost(microseconds),
        name=name,
    )(meta, docs, bounds, own, other, *query)


def attention_backward(plan, own, other, query, grad, mixed, lse, turned, name, microseconds):
    meta, docs, bounds, pair_at, first_chunk, per_group = plan
    groups, _, lanes = docs.shape
    blocks, _, rows = own.shape
    keys = blocks * 2 * rows
    part = (blocks, 2 * HEAD, rows) if turned else (blocks, rows, 2 * HEAD)
    return pl.pallas_call(
        functools.partial(backward_kernel, pair_at, first_chunk, per_group, turned),
        out_shape=(
            jax.ShapeDtypeStruct((groups * per_group, (3 if turned else 1) * HEAD, rows), jnp.bfloat16),
            jax.ShapeDtypeStruct(part, jnp.float32),
            jax.ShapeDtypeStruct(part, jnp.bfloat16),
        ),
        in_specs=[SMEM_SPEC] + [VMEM_SPEC] * 2 + [ANY_SPEC] * 2 + [VMEM_SPEC] * (len(query) + 3),
        out_specs=(VMEM_SPEC, ANY_SPEC, ANY_SPEC),
        scratch_shapes=[
            *[pltpu.VMEM(own.shape, jnp.bfloat16)] * 2,
            pltpu.VMEM(part, jnp.float32),
            pltpu.VMEM(part, jnp.bfloat16),
            pltpu.VMEM((keys, HEAD + DOC_SLOTS), jnp.bfloat16),
            pltpu.VMEM((keys, 2 * HEAD), jnp.bfloat16),
            pltpu.VMEM((HEAD, keys), jnp.bfloat16),
            pltpu.VMEM((keys, 2 * HEAD), jnp.float32),
            pltpu.SemaphoreType.DMA((blocks // 2, 2)),
            pltpu.SemaphoreType.DMA((blocks, 2)),
        ],
        compiler_params=pltpu.CompilerParams(vmem_limit_bytes=VMEM_BYTES),
        cost_estimate=cost(microseconds),
        name=name,
    )(meta, docs, bounds, own, other, *query, grad, mixed, lse)


def gelu_parts(value):
    scale = (2.0 / math.pi) ** 0.5
    square = value * value
    bent = jnp.tanh(scale * value * (1.0 + 0.044715 * square))
    upper = 0.5 * (1.0 + bent)
    slope = 0.5 * value * (1.0 - bent * bent) * scale * (1.0 + 3 * 0.044715 * square)
    return value * upper, upper + slope


def column_norm(values, gain, shift):
    row_mean = jnp.mean(values, axis=0, keepdims=True)
    centered = values - row_mean
    variance = jnp.mean(centered * centered, axis=0, keepdims=True)
    inverse = lax.rsqrt(variance + EPSILON)
    normed = centered * inverse
    return (normed * gain + shift, normed, inverse)


def column_norm_back(grad, normed, inverse, gain):
    scaled = grad * gain
    return inverse * (
        scaled
        - jnp.mean(scaled, axis=0, keepdims=True)
        - normed * jnp.mean(scaled * normed, axis=0, keepdims=True)
    )


def fetched(refs, places, semaphores):
    copies = [
        pltpu.make_async_copy(ref, place, semaphores.at[i])
        for i, (ref, place) in enumerate(zip(refs, places))
    ]
    for copy in copies:
        copy.start()
    return copies


def half_rows(core, half):
    return (
        pl.ds(pl.multiple_of(core * half, 32), half),
        pl.ds(pl.multiple_of((1 - core) * half, 32), half),
    )


def ahead_kernel(
    tile, core_ref, mask_ref, cotangent_ref, b_down_ref, *refs
):
    remote, (active_grad_ref, down_grad_ref), refs = refs[:3], refs[3:5], refs[5:]
    down_w_ref, a_down_ref, place_ref, semaphores, out_semaphores = refs
    half, wide = remote[0].shape
    sides = half_rows(core_ref[0], half)
    spots = [slice(k, min(k + tile, wide)) for k in range(0, wide, tile)]
    copies = []
    for k, spot in enumerate(spots):
        pairs = [(remote[i].at[:, spot], down_w_ref.at[sides[i], spot]) for i in range(2)]
        pairs += [(remote[2].at[spot, :], a_down_ref.at[spot, :])]
        for i, (source, place) in enumerate(pairs):
            copies.append(pltpu.make_async_copy(source, place, semaphores.at[k, i]))
    for copy in copies:
        copy.start()
    rows = cotangent_ref[...].T
    down_grad = dot(rows, b_down_ref[...]).astype(jnp.bfloat16) * mask_ref[...].astype(jnp.bfloat16)
    down_grad_ref[...] = down_grad
    given = []
    for k, spot in enumerate(spots):
        for copy in copies[3 * k : 3 * k + 3]:
            copy.wait()
        grad = dot(rows, down_w_ref[:, spot]) + dot(down_grad, a_down_ref[spot, :].T)
        place_ref[:, spot] = grad
        given.append(
            pltpu.make_async_copy(place_ref.at[:, spot], active_grad_ref.at[:, spot], out_semaphores.at[k])
        )
        given[-1].start()
    for copy in given:
        copy.wait()


def ahead_part(core, mask, cotangent_t, b_down_t, down_pair_t, a_down):
    width, rows = cotangent_t.shape
    wide, inner = a_down.shape
    tile = 1024
    count = -(-wide // tile)
    return pl.pallas_call(
        functools.partial(ahead_kernel, tile),
        out_shape=(
            jax.ShapeDtypeStruct((rows, wide), jnp.float32),
            jax.ShapeDtypeStruct((rows, inner), jnp.bfloat16),
        ),
        in_specs=[SMEM_SPEC] + [VMEM_SPEC] * 3 + [ANY_SPEC] * 3,
        out_specs=(ANY_SPEC, VMEM_SPEC),
        scratch_shapes=[
            pltpu.VMEM((width, wide), jnp.bfloat16),
            pltpu.VMEM((wide, inner), jnp.bfloat16),
            pltpu.VMEM((rows, wide), jnp.float32),
            pltpu.SemaphoreType.DMA((count, 3)),
            pltpu.SemaphoreType.DMA((count,)),
        ],
        compiler_params=pltpu.CompilerParams(vmem_limit_bytes=VMEM_BYTES),
        cost_estimate=cost(1),
        name="ahead_part",
    )(core, mask, cotangent_t, b_down_t, *down_pair_t, a_down)


def middle_kernel(
    tile, core_ref, *refs
):
    sources, remote, results, (kept_ref, sent_ref), places, result_places, refs = (
        refs[:11], refs[11:20], refs[20:24], refs[24:26], refs[26:37], refs[37:41], refs[41:],
    )
    (
        mixed_main_ref, mixed_last_ref, mask_ref, a_out_ref, b_out_ref, stream_ref, gains_ref,
        a_up_ref, down_grad_ref, cotangent_ref, b_down_ref,
    ) = places
    output_ref, middle_grad_ref, main_grad_ref, last_grad_ref = result_places
    (
        out_ref, up_ref, b_up_ref, down_w_ref, a_down_ref, kept_place, sent_place,
        active_grad_ref, mixed_ref, middle_ref, hidden_ref, hidden_rows_ref, inner_out_ref,
        inner_up_ref, inner_down_ref, up_grad_ref, down_ref, back_ref,
        semaphores, out_semaphores, place_semaphores, result_semaphores,
    ) = refs
    core = core_ref[0]
    half, wide = remote[2].shape
    width = 2 * half
    full = wide // tile
    low = jnp.bfloat16
    sides = half_rows(core, half)

    def copies(first, size, number):
        spot = pl.ds(first, size)
        pairs = [(remote[2 + i].at[:, spot], up_ref.at[sides[i], spot]) for i in range(2)]
        pairs += [(remote[5 + i].at[:, spot], down_w_ref.at[sides[i], spot]) for i in range(2)]
        pairs += [(remote[4].at[:, spot], b_up_ref.at[:, spot])]
        pairs += [(remote[7].at[spot, :], a_down_ref.at[spot, :])]
        pairs += [(remote[8].at[:, spot], active_grad_ref.at[:, spot])]
        return [
            pltpu.make_async_copy(source, place, semaphores.at[number, i])
            for i, (source, place) in enumerate(pairs)
        ]

    firsts = [
        pltpu.make_async_copy(remote[i], out_ref.at[sides[i], :], semaphores.at[full + 1, i])
        for i in range(2)
    ]
    given = fetched(sources[:4], places[:4], place_semaphores)
    for copy in firsts:
        copy.start()
    later = [
        pltpu.make_async_copy(sources[i], places[i], place_semaphores.at[i]) for i in range(4, 11)
    ]
    for copy in later:
        copy.start()

    def give(i):
        copy = pltpu.make_async_copy(result_places[i], results[i], result_semaphores.at[i])
        copy.start()
        return copy

    def start_chunk(k):
        @pl.when(k < full)
        def _():
            for copy in copies(pl.multiple_of(k * tile, tile), tile, k):
                copy.start()

        if wide % tile:

            @pl.when(k == full)
            def _():
                for copy in copies(full * tile, wide % tile, full):
                    copy.start()

    def out_copies(first, size, number):
        spot = pl.ds(first, size)
        pairs = ((kept_place, kept_ref), (sent_place, sent_ref))
        return [
            pltpu.make_async_copy(place.at[spot, :], ref.at[spot, :], out_semaphores.at[number, i])
            for i, (place, ref) in enumerate(pairs)
        ]

    def put(first, rows, other):
        spot = pl.ds(first, rows.shape[0])

        @pl.when(core == 0)
        def _():
            kept_place[spot, :] = rows
            sent_place[spot, :] = other

        @pl.when(core == 1)
        def _():
            kept_place[spot, :] = other
            sent_place[spot, :] = rows

    for copy in given[:4]:
        copy.wait()
    mask = mask_ref[...]
    mask_low = mask.astype(low)
    main = mixed_main_ref.shape[0] * HEAD
    mixed_ref[:main, :] = mixed_main_ref[...].reshape(main, mixed_main_ref.shape[2])
    mixed_ref[main:, :] = mixed_last_ref[0]
    mixed_rows = mixed_ref[...].T
    inner_out = (mask * (dot(mixed_rows, a_out_ref[...]))).astype(low)
    inner_out_ref[...] = inner_out
    for copy in (*firsts, *later):
        copy.wait()
    start_chunk(0)
    start_chunk(1)
    branch = dot(mixed_rows, out_ref[...]).T + dot(b_out_ref[...], inner_out.T)
    middle = stream_ref[...].astype(jnp.float32) + branch
    middle_ref[...] = middle
    hidden = column_norm(middle, gains_ref[:, 2:3], gains_ref[:, 3:4])[0].astype(low)
    hidden_ref[...] = hidden
    hidden_rows = hidden.T
    hidden_rows_ref[...] = hidden_rows
    inner_up_ref[...] = (mask * dot(hidden_rows, a_up_ref[...])).astype(low)
    for ref in (inner_down_ref, up_grad_ref, down_ref, back_ref):
        ref[...] = jnp.zeros(ref.shape, ref.dtype)

    def step(k, size):
        first = k * tile if isinstance(k, int) else pl.multiple_of(k * tile, tile)
        for copy in copies(first, size, k):
            copy.wait()
        start_chunk(k + 2)
        spot = pl.ds(first, size)
        up, b_up, down_w, a_down = up_ref[:, spot], b_up_ref[:, spot], down_w_ref[:, spot], a_down_ref[spot, :]
        inner_up, down_grad = inner_up_ref[...], down_grad_ref[...]
        upward = dot(hidden_rows_ref[...], up) + dot(inner_up, b_up)
        active, slope = gelu_parts(upward)
        active = active.astype(low)
        up_grad = (active_grad_ref[:, spot] * slope).astype(low)
        active_t, up_grad_t = active.T, up_grad.T
        down_ref[...] += dot(down_w, active_t)
        back_ref[...] += dot(up, up_grad_t)
        inner_down_ref[...] += dot(active, a_down)
        up_grad_ref[...] += dot(b_up, up_grad_t)
        put(first, dot(up_grad_t, inner_up).astype(low), dot(active_t, down_grad).astype(low))
        for copy in out_copies(first, size, k):
            copy.start()

    def loop(k, carry):
        step(k, tile)
        return carry

    lax.fori_loop(0, full, loop, 0)
    if wide % tile:
        step(full, wide % tile)

    inner_down = (mask * inner_down_ref[...]).astype(low)
    middle = middle_ref[...]
    inner_grad = up_grad_ref[...].astype(low).T * mask_low
    hidden_grad = back_ref[...] + dot(a_up_ref[...], inner_grad.T)
    gain = gains_ref[:, 2:3]
    _, normed, inverse = column_norm(middle, gain, gain)
    middle_grad = cotangent_ref[...].astype(jnp.float32)
    middle_grad = middle_grad + column_norm_back(hidden_grad, normed, inverse, gain)
    middle_grad_ref[...] = middle_grad
    given = [give(1)]
    branch = middle_grad.astype(low)
    out_grad = dot(branch.T, b_out_ref[...]).astype(low) * mask_low
    put(wide, dot(cotangent_ref[...], inner_down).astype(low), dot(mixed_ref[...], out_grad).astype(low))
    put(
        wide + width,
        dot(hidden_ref[...], inner_grad).astype(low),
        dot(branch, inner_out_ref[...]).astype(low),
    )
    narrow = kept_place.shape[0] - wide
    spare = narrow - 2 * width
    if spare:
        nothing = jnp.zeros((spare, kept_place.shape[1]), low)
        put(wide + 2 * width, nothing, nothing)
    for copy in out_copies(wide, narrow, full + 1):
        copy.start()
    back = (dot(out_ref[...], branch) + dot(a_out_ref[...], out_grad.T)).astype(low)
    main_grad_ref[...] = back[:main].reshape(main_grad_ref.shape)
    last_grad_ref[0] = back[main:]
    given += [give(2), give(3)]
    down = down_ref[...] + dot(b_down_ref[...], inner_down.T)
    output_ref[...] = (middle + down).astype(low)
    given += [give(0)]

    def finished(k, carry):
        for copy in out_copies(pl.multiple_of(k * tile, tile), tile, k):
            copy.wait()
        return carry

    lax.fori_loop(0, full, finished, 0)
    if wide % tile:
        for copy in out_copies(full * tile, wide % tile, full):
            copy.wait()
    for copy in (*out_copies(wide, narrow, full + 1), *given):
        copy.wait()


def padded(size, unit):
    return -(-size // unit) * unit


def middle_part(
    core, mixed_main, mixed_last, tokens_t, cotangent_t, mask, gains_t, out_pair, a_out, b_out_t,
    a_up, b_down_t, up_pair, b_up, down_pair_t, a_down, active_grad, down_grad, unit,
):
    width, rows = tokens_t.shape
    half = width // 2
    inner, wide = b_up.shape
    tile = 512
    low = jnp.bfloat16
    operands = (
        mixed_main, mixed_last, mask, a_out, b_out_t, tokens_t, gains_t, a_up, down_grad,
        cotangent_t, b_down_t,
    )
    remote = (*out_pair, *up_pair, b_up, *down_pair_t, a_down, active_grad)
    share = (padded(wide + 2 * width, unit), inner)
    shapes = (
        ((width, rows), low), ((width, rows), jnp.float32), (mixed_main.shape, low),
        (mixed_last.shape, low), (share, low), (share, low),
    )
    return pl.pallas_call(
        functools.partial(middle_kernel, tile),
        out_shape=tuple(jax.ShapeDtypeStruct(*item) for item in shapes),
        in_specs=[SMEM_SPEC] + [ANY_SPEC] * (len(operands) + len(remote)),
        out_specs=(ANY_SPEC,) * 6,
        scratch_shapes=[
            *[pltpu.VMEM(item.shape, item.dtype) for item in operands],
            *[pltpu.VMEM(*item) for item in shapes[:4]],
            pltpu.VMEM((width, width), low),
            pltpu.VMEM((width, wide), low),
            pltpu.VMEM((inner, wide), low),
            pltpu.VMEM((width, wide), low),
            pltpu.VMEM((wide, inner), low),
            *[pltpu.VMEM(share, low)] * 2,
            pltpu.VMEM((rows, wide), jnp.float32),
            pltpu.VMEM((width, rows), low),
            pltpu.VMEM((width, rows), jnp.float32),
            pltpu.VMEM((width, rows), low),
            pltpu.VMEM((rows, width), low),
            *[pltpu.VMEM((rows, inner), low)] * 2,
            pltpu.VMEM((rows, inner), jnp.float32),
            pltpu.VMEM((inner, rows), jnp.float32),
            *[pltpu.VMEM((width, rows), jnp.float32)] * 2,
            pltpu.SemaphoreType.DMA((wide // tile + 2, 7)),
            pltpu.SemaphoreType.DMA((wide // tile + 2, 2)),
            pltpu.SemaphoreType.DMA((len(operands),)),
            pltpu.SemaphoreType.DMA((4,)),
        ],
        compiler_params=pltpu.CompilerParams(vmem_limit_bytes=VMEM_BYTES),
        cost_estimate=cost(20),
        name="middle_part",
    )(core, *operands, *remote)


def whole_call(kernel, shapes, scratch, operands, remote, microseconds, name):
    space = [pltpu.VMEM(item.shape, item.dtype) for item in remote]
    return pl.pallas_call(
        kernel,
        out_shape=tuple(jax.ShapeDtypeStruct(*item) for item in shapes),
        in_specs=[SMEM_SPEC]
        + [VMEM_SPEC] * (len(operands) - 1)
        + [pl.BlockSpec(memory_space=pl.ANY)] * len(remote),
        out_specs=(VMEM_SPEC,) * len(shapes),
        scratch_shapes=[pltpu.VMEM(*item) for item in scratch]
        + space
        + ([pltpu.SemaphoreType.DMA((len(remote),))] if remote else []),
        compiler_params=pltpu.CompilerParams(vmem_limit_bytes=VMEM_BYTES),
        cost_estimate=cost(microseconds),
        name=name,
    )(*operands, *remote)


def entry_kernel(
    place_ref, lengths_ref, adapters_ref, tokens_ref, gains_own_ref, gains_other_ref, *refs
):
    remote, results, refs = refs[:12], refs[12:19], refs[19:]
    places, (weight_ref, up_ref, down_ref, semaphores, result_semaphores) = refs[:7], refs[7:]
    hidden_ref, inner_ref, mask_ref, gains_ref, heads_ref, query_ref, pairs_ref = places
    rows, inner = mask_ref.shape
    half = gains_own_ref.shape[1]
    sides = half_rows(place_ref[0], half)
    copies = []
    for n in range(3):
        down, own, up, other = remote[4 * n : 4 * n + 4]
        pairs = (
            (down, down_ref.at[n]), (up, up_ref.at[n]),
            (own, weight_ref.at[n, sides[0], :]), (other, weight_ref.at[n, sides[1], :]),
        )
        for i, (source, place) in enumerate(pairs):
            copies.append(pltpu.make_async_copy(source, place, semaphores.at[4 * n + i]))
    for copy in copies:
        copy.start()

    def give(i):
        copy = pltpu.make_async_copy(places[i], results[i], result_semaphores.at[i])
        copy.start()
        return copy

    for spot, ref in zip(sides, (gains_own_ref, gains_other_ref)):
        gains_ref[spot, :] = ref[...].astype(jnp.float32).T
    values = tokens_ref[...].astype(jnp.float32)
    hidden = column_norm(values, gains_ref[:, 0:1], gains_ref[:, 1:2])[0].astype(jnp.bfloat16)
    hidden_ref[...] = hidden
    hidden_rows = hidden.T
    place = place_ref[1] + lax.broadcasted_iota(jnp.int32, (rows, inner), 0)
    column = lax.broadcasted_iota(jnp.int32, (rows, inner), 1) // RANK

    def document(d, state):
        start, mask = state
        end = start + lengths_ref[d]
        chosen = (place >= start) & (place < end) & (column == adapters_ref[d])
        return end, jnp.where(chosen, 1.0, mask)

    state = (jnp.int32(0), jnp.zeros((rows, inner), jnp.float32))
    _, mask = lax.fori_loop(0, lengths_ref.shape[0], document, state)
    mask_ref[...] = mask
    given = [give(0), give(2), give(3)]
    count = heads_ref.shape[0]

    def give_part(n):
        spot = pl.ds(n * HEAD, HEAD)
        copy = pltpu.make_async_copy(
            heads_ref.at[:, spot, :], results[4].at[:, spot, :], result_semaphores.at[7 + n]
        )
        copy.start()
        return copy

    for n in range(3):
        for copy in copies[4 * n : 4 * n + 4]:
            copy.wait()
        products = (mask * dot(hidden_rows, down_ref[n])).astype(jnp.bfloat16)
        inner_ref[n] = products
        total = dot(hidden_rows, weight_ref[n]).T + dot(up_ref[n], products.T)
        total = total.astype(jnp.bfloat16)
        for c in range(count):
            heads_ref[c, n * HEAD : (n + 1) * HEAD, :] = total[c * HEAD : (c + 1) * HEAD]
        if n == 0:
            query_ref[0] = total[count * HEAD :]
        else:
            for c in range(count):
                pairs_ref[c, (n - 1) * HEAD : n * HEAD, :] = total[count * HEAD :]
        given.append(give_part(n))
    for copy in (*given, *[give(i) for i in (1, 5, 6)]):
        copy.wait()


def projections(place, lengths, adapters, tokens_t, gains, gains_other, weights, others, downs, ups_t):
    width, rows = tokens_t.shape
    inner = downs[0].shape[1]
    low = jnp.bfloat16
    count = width // HEAD - 1
    remote = [item for group in zip(downs, weights, ups_t, others) for item in group]
    shapes = (
        ((width, rows), low), ((3, rows, inner), low), ((rows, inner), jnp.float32),
        ((width, gains.shape[0]), jnp.float32), ((count, 3 * HEAD, rows), low),
        ((1, HEAD, rows), low), ((count, 2 * HEAD, rows), low),
    )
    return pl.pallas_call(
        entry_kernel,
        out_shape=tuple(jax.ShapeDtypeStruct(*item) for item in shapes),
        in_specs=[SMEM_SPEC] * 3 + [VMEM_SPEC] * 3 + [ANY_SPEC] * len(remote),
        out_specs=(ANY_SPEC,) * len(shapes),
        scratch_shapes=[pltpu.VMEM(*item) for item in shapes]
        + [
            pltpu.VMEM((3, width, width), low),
            pltpu.VMEM((3, width, inner), low),
            pltpu.VMEM((3, width, inner), low),
            pltpu.SemaphoreType.DMA((12,)),
            pltpu.SemaphoreType.DMA((len(shapes) + 3,)),
        ],
        compiler_params=pltpu.CompilerParams(vmem_limit_bytes=VMEM_BYTES),
        cost_estimate=cost(6),
        name="entry",
    )(place, lengths, adapters, tokens_t, gains, gains_other, *remote)


def gathered_grad(n, heads_ref, last_query_ref, last_pair_ref, grad_ref):
    count = heads_ref.shape[0]
    for c in range(count):
        grad_ref[c * HEAD : (c + 1) * HEAD, :] = heads_ref[c, n * HEAD : (n + 1) * HEAD, :]
    if n == 0:
        grad_ref[count * HEAD :, :] = last_query_ref[0]
    else:
        grad_ref[count * HEAD :, :] = last_pair_ref[...].T[(n - 1) * HEAD : n * HEAD]
    return grad_ref[...]


def projections_late_kernel(core_ref, *refs):
    sources, (kept_ref, sent_ref, inner_grad_ref), refs = refs[:9], refs[9:12], refs[12:]
    places, (kept_place, sent_place, grad_ref, semaphores, out_semaphores) = refs[:9], refs[9:]
    heads_ref, last_query_ref, last_pair_ref, mask_ref, hidden_ref, inner_ref, *ups = places
    copies = fetched(sources, places, semaphores)
    core = core_ref[0]
    low = jnp.bfloat16
    width, share = hidden_ref.shape[0], kept_place.shape[0]

    def store(side, spot, rows):
        @pl.when(core == side)
        def _():
            kept_place[spot, :] = rows

        @pl.when(core != side)
        def _():
            sent_place[spot, :] = rows

    def keep(first, rows):
        done = 0
        while done < rows.shape[0]:
            side, spot = divmod(first + done, share)
            size = min(rows.shape[0] - done, share - spot)
            store(side, slice(spot, spot + size), rows[done : done + size])
            done += size

    keep(6 * width, jnp.zeros((2 * share - 6 * width, kept_place.shape[1]), low))
    for copy in copies[:6]:
        copy.wait()
    mask_low = mask_ref[...].astype(low)
    hidden = hidden_ref[...]
    for n in range(3):
        grad = gathered_grad(n, heads_ref, last_query_ref, last_pair_ref, grad_ref)
        copies[6 + n].wait()
        inner_grad = dot(grad.T, ups[n][...]).astype(low) * mask_low
        inner_grad_ref[n] = inner_grad
        keep(2 * n * width, dot(hidden, inner_grad).astype(low))
        keep((2 * n + 1) * width, dot(grad, inner_ref[n]).astype(low))
    given = fetched((kept_place, sent_place), (kept_ref, sent_ref), out_semaphores)
    for copy in given:
        copy.wait()


def projections_late(core, heads, last_query, last_pair, hidden_t, inners, mask, ups_t, unit):
    width, rows = hidden_t.shape
    low = jnp.bfloat16
    share = (padded(6 * width, 2 * unit) // 2, mask.shape[1])
    operands = (heads, last_query, last_pair, mask, hidden_t, inners, *ups_t)
    return pl.pallas_call(
        projections_late_kernel,
        out_shape=(
            jax.ShapeDtypeStruct(share, low),
            jax.ShapeDtypeStruct(share, low),
            jax.ShapeDtypeStruct(inners.shape, low),
        ),
        in_specs=[SMEM_SPEC] + [ANY_SPEC] * len(operands),
        out_specs=(ANY_SPEC, ANY_SPEC, VMEM_SPEC),
        scratch_shapes=[pltpu.VMEM(item.shape, item.dtype) for item in operands]
        + [
            pltpu.VMEM(share, low),
            pltpu.VMEM(share, low),
            pltpu.VMEM((width, rows), low),
            pltpu.SemaphoreType.DMA((len(operands),)),
            pltpu.SemaphoreType.DMA((2,)),
        ],
        compiler_params=pltpu.CompilerParams(vmem_limit_bytes=VMEM_BYTES),
        cost_estimate=cost(5),
        name="projections_late",
    )(core, *operands)


def projections_back_kernel(
    core_ref, heads_ref, last_query_ref, last_pair_ref, inner_grad_ref, gains_ref, tokens_ref, *refs
):
    remote, (grad_in_ref, grad_ref, sum_ref), local_refs, semaphores = (
        refs[:10], refs[10:13], refs[13:23], refs[23],
    )
    copies = fetched(remote, local_refs, semaphores)
    downs, weights, others, middle_grad_ref = (
        local_refs[:3], local_refs[3:6], local_refs[6:9], local_refs[9],
    )
    own_rows, other_rows = half_rows(core_ref[0], weights[0].shape[0])
    for n in range(3):
        grad = gathered_grad(n, heads_ref, last_query_ref, last_pair_ref, grad_ref)
        turned = inner_grad_ref[n].T
        copies[n].wait()
        for rows, weight, copy in (
            (own_rows, weights[n], copies[3 + n]), (other_rows, others[n], copies[6 + n])
        ):
            copy.wait()
            part = dot(weight[...], grad) + dot(downs[n][rows, :], turned)
            sum_ref[rows, :] = part if n == 0 else sum_ref[rows, :] + part
    gain = gains_ref[:, 0:1]
    _, normed, inverse = column_norm(tokens_ref[...].astype(jnp.float32), gain, gain)
    back = column_norm_back(sum_ref[...], normed, inverse, gain)
    copies[9].wait()
    grad_in_ref[...] = (middle_grad_ref[...] + back).astype(jnp.bfloat16)


def projections_back(
    core, heads, last_query, last_pair, inner_grads, gains_t, tokens_t, middle_grad_t,
    weights, others, downs,
):
    width, rows = tokens_t.shape
    low = jnp.bfloat16
    return whole_call(
        projections_back_kernel,
        (((width, rows), low),),
        (((width, rows), low), ((width, rows), jnp.float32)),
        (core, heads, last_query, last_pair, inner_grads, gains_t, tokens_t),
        (*downs, *weights, *others, middle_grad_t),
        8, "projections_back",
    )[0]


def steps_of(cycle_size):
    bits = cycle_size.bit_length() - 1
    return [(bit, min(2, bits - bit)) for bit in range(0, bits, 2)]


def partners(cycle_size, step, k):
    return [(i, i ^ (k << step[0])) for i in range(cycle_size)]


def scattered(array, step, cycle_size):
    count = 1 << step[1]
    mine = (lax.axis_index("ctx") >> step[0]) & (count - 1)
    blocks = array.reshape(count, array.shape[0] // count, array.shape[1])

    def block(number):
        return lax.dynamic_index_in_dim(blocks, number, 0, keepdims=False)

    total = block(mine).astype(jnp.float32)
    for k in range(1, count):
        got = lax.ppermute(block(mine ^ k), "ctx", partners(cycle_size, step, k))
        total = total + got.astype(jnp.float32)
    return total.astype(array.dtype)


def collected(share, step, cycle_size):
    count = 1 << step[1]
    mine = (lax.axis_index("ctx") >> step[0]) & (count - 1)
    blocks = [share]
    for k in range(1, count):
        blocks.append(lax.ppermute(share, "ctx", partners(cycle_size, step, k)))
    for bit in range(step[1]):
        turned = ((mine >> bit) & 1) == 1
        blocks = [jnp.where(turned, blocks[k ^ (1 << bit)], blocks[k]) for k in range(count)]
    return jnp.concatenate(blocks, axis=0)


def pair_sum(kept, sent):
    return kept + lax.ppermute(sent, "wsh", SWAP)


def early_finish_kernel(
    factor, core_ref, own_source, other_source,
    b_up_ref, a_down_ref, b_down_ref, a_up_ref, a_out_ref, b_out_ref, own_ref, other_ref, semaphores,
):
    for copy in fetched((own_source, other_source), (own_ref, other_ref), semaphores):
        copy.wait()
    wide, width = a_down_ref.shape[0], a_up_ref.shape[0]

    def finish(first_ref, second_ref):
        def part(ref, first, count):
            return ref[first : first + count, :].astype(jnp.float32) * factor

        for k in range(wide // 256):
            b_up_ref[:, k * 256 : (k + 1) * 256] = part(first_ref, k * 256, 256).T
        a_down_ref[...] = part(second_ref, 0, wide)
        b_down_ref[...] = part(first_ref, wide, width)
        a_up_ref[...] = part(first_ref, wide + width, width)
        a_out_ref[...] = part(second_ref, wide, width)
        b_out_ref[...] = part(second_ref, wide + width, width)

    @pl.when(core_ref[0] == 0)
    def _():
        finish(own_ref, other_ref)

    @pl.when(core_ref[0] == 1)
    def _():
        finish(other_ref, own_ref)


def late_finish_kernel(factor, core_ref, own_ref, other_ref, *refs):
    core = core_ref[0]
    targets, late_ref, own_place, other_place, semaphores = refs[:6], *refs[6:]
    places = (own_place, other_place)
    copies = fetched((own_ref, other_ref), places, semaphores)
    for side, ref, copy in zip((core, 1 - core), places, copies):
        copy.wait()
        late_ref[side] = ref[...].astype(jnp.float32) * factor
    width, share = targets[0].shape[0], late_ref.shape[1]
    for n, ref in enumerate(targets):
        done = 0
        while done < width:
            side, spot = divmod(n * width + done, share)
            rows = min(width - done, share - spot)
            ref[done : done + rows, :] = late_ref[side, spot : spot + rows, :]
            done += rows


def finished(kernel, factor, core, own, other, shapes, scratch, name):
    return whole_call(
        functools.partial(kernel, factor), [(shape, jnp.float32) for shape in shapes], scratch,
        (core,), (own, other), 1, name,
    )


def local(
    tokens_in,
    doc_lengths,
    doc_adapter,
    norm1_gain,
    norm1_bias,
    norm2_gain,
    norm2_bias,
    w_query,
    w_key,
    w_value,
    w_out,
    w_up,
    w_down,
    a_query,
    b_query,
    a_key,
    b_key,
    a_value,
    b_value,
    a_out,
    b_out,
    a_up,
    b_up,
    a_down,
    b_down,
    cotangent,
):
    group_size = lax.axis_size("wsh")
    cycle_size = lax.axis_size("ctx")
    tok_dev, width_all = tokens_in.shape
    head_count = width_all // HEAD
    block_len = tok_dev * group_size
    hop_count = (DOC_MAX + block_len - 2) // block_len
    span = head_count - 1
    cycle_pos = lax.axis_index("ctx")
    core = lax.axis_index("wsh")
    half = width_all // group_size

    first_row = cycle_pos * block_len + core * tok_dev
    doc_ends = jnp.cumsum(doc_lengths)
    doc_starts = doc_ends - doc_lengths

    team = cycle_pos // span
    past = hop_count if cycle_size > span else 0
    first_key = (team * span - past) * block_len
    key_blocks = past + span

    slots = DOC_SLOTS - doc_lengths.shape[0]
    bounds = jnp.stack([jnp.pad(doc_starts, (0, slots)), jnp.pad(doc_ends, (0, slots))])

    def plan(chunk_pos, pair_at, first_chunk, per_group):
        groups = chunk_pos.shape[0] // per_group
        row_pos = chunk_pos[:, None] + jnp.arange(tok_dev, dtype=jnp.int32)[None, :]
        row_docs = jnp.sum((doc_ends[None, None, :] <= row_pos[:, :, None]).astype(jnp.int32), axis=2)
        row_docs = row_docs.reshape(groups, 1, per_group * tok_dev)
        chunk_pos = chunk_pos.reshape(groups, per_group)
        began = jnp.where(doc_starts[None, None, :] <= chunk_pos[:, :, None], doc_starts[None, None, :], 0)
        began = (jnp.max(began, axis=2) - first_key) // (2 * block_len)
        first = began[:, 0]
        last = (chunk_pos[:, -1] - first_key) // (2 * block_len)
        same = jnp.ones((groups,), jnp.int32)
        whole = per_group > 1
        meta = [
            first,
            last,
            chunk_pos[:, 0],
            same * core,
            same * first_key,
            jnp.concatenate([first[:1] * 0, last[:-1] + 1]) if whole else first,
            began[:, -1],
        ]
        meta = jnp.stack(meta, axis=1).astype(jnp.int32)
        docs = row_docs.astype(jnp.int32)
        return meta, docs, bounds.astype(jnp.int32), pair_at, first_chunk, per_group

    team_pos = (team * span + jnp.arange(span, dtype=jnp.int32)) * block_len + core * tok_dev
    main_plan = plan(team_pos.astype(jnp.int32), HEAD, past, 2)
    last_plan = plan(first_row[None].astype(jnp.int32), 0, 0, 1)

    def swap(array):
        return lax.ppermute(array, "wsh", SWAP)

    if cycle_size > span:
        teams = [[t * span + i for i in range(span)] for t in range(cycle_size // span)]
    else:
        teams = None

    def exchange(blocks):
        return lax.all_to_all(blocks, "ctx", 0, 0, tiled=True, axis_index_groups=teams)

    gains = jnp.stack([norm1_gain, norm1_bias, norm2_gain, norm2_bias])
    weights = [w_query, w_key, w_value, w_out, w_up, w_down.T]
    others = [swap(item) for item in weights[:3]]
    gains_other = swap(gains)
    *others, gains_other, w_late = lax.optimization_barrier((*others, gains_other, tuple(weights[3:])))
    others = others + [swap(item) for item in w_late]

    downs = (a_query, a_key, a_value)
    ups_t = (b_query.T, b_key.T, b_value.T)
    tokens_t = tokens_in.T
    core_1 = jnp.stack([core, first_row]).astype(jnp.int32)
    hidden_t, inners, adapter_mask, gains_t, heads, last_query, last_pairs = projections(
        core_1, doc_lengths, doc_adapter, tokens_t, gains, gains_other, weights[:3], others[:3],
        downs, ups_t,
    )

    ahead = [(i, i + span) for i in range(cycle_size - span)]
    back = [(i + span, i) for i in range(cycle_size - span)]

    def with_past(blocks):
        if not past:
            return blocks
        return jnp.concatenate([lax.ppermute(blocks[span - past :], "ctx", ahead), blocks], axis=0)

    steps = steps_of(cycle_size)
    unit = 16 * cycle_size
    incoming = exchange(heads)
    active_grad, down_grad = ahead_part(
        core_1, adapter_mask, cotangent.T, b_down.T, (w_down.T, others[5]), a_down
    )
    incoming, last_pairs, active_grad = lax.optimization_barrier((incoming, last_pairs, active_grad))
    own = with_past(incoming)
    other = swap(own)
    last_own = exchange(last_pairs)
    low_main, total_main, lse_main = attention_forward(
        main_plan, own, other, (), "attention_forward", 30
    )
    low_main, last_own = lax.optimization_barrier((low_main, last_own))
    last_own = with_past(last_own)
    last_other = swap(last_own)
    low_last, mixed_last, lse_last = attention_forward(
        last_plan, last_own, last_other, (last_query,), "last_forward", 0
    )
    mixed_main = exchange(low_main)

    output_t, middle_grad_t, main_grad, last_out_grad, early_kept, early_sent = middle_part(
        core_1, mixed_main, low_last, tokens_t, cotangent.T, adapter_mask, gains_t,
        (w_out, others[3]), a_out, b_out.T, a_up, b_down.T, (w_up, others[4]), b_up,
        (w_down.T, others[5]), a_down, active_grad, down_grad, unit,
    )

    def pair_total(kept, sent):
        total = kept + swap(sent).astype(jnp.float32)
        if past:
            returned = lax.ppermute(total[:past].astype(jnp.bfloat16), "ctx", back)
            total = total[past:].at[span - past :].add(returned.astype(jnp.float32))
        return total

    def pair_back(dq, kept, sent):
        total = pair_total(kept, sent).astype(jnp.bfloat16)
        return lax.dynamic_update_slice(dq, total, (0, HEAD, 0))

    dq_last, kept_last, sent_last = attention_backward(
        last_plan, last_own, last_other, (last_query,),
        last_out_grad, mixed_last, lse_last, False, "last_backward", 0,
    )
    grad_main = exchange(main_grad)
    grad_main, dq_last, kept_last, sent_last = lax.optimization_barrier(
        (grad_main, dq_last, kept_last, sent_last)
    )
    dpair_last = pair_total(kept_last, sent_last).astype(jnp.bfloat16)
    plane = 1 << steps[0][1]
    lines = cycle_size // plane
    digits = (2,) * (cycle_size.bit_length() - 3) + (plane,)
    if cycle_size > span:
        zero = jnp.zeros((cycle_size // span, *dpair_last.shape), dpair_last.dtype)
        dpair_last = lax.dynamic_update_index_in_dim(zero, dpair_last, team, 0)
    order = tuple(reversed(range(len(digits)))) + (len(digits), len(digits) + 1)
    dpair_last = jnp.transpose(dpair_last.reshape(digits + dpair_last.shape[-2:]), order)
    early = pair_sum(early_kept, early_sent)
    lanes = early.shape[1]
    early_rows, last_rows = early.shape[0] // cycle_size, tok_dev
    early = early.reshape(plane, lines, early_rows, lanes)
    dpair_last = dpair_last.reshape(plane, lines, last_rows, lanes)

    def meant_for(k):
        parts = [lax.dynamic_index_in_dim(x, (cycle_pos % plane) ^ k, 0, False) for x in (early, dpair_last)]
        return jnp.concatenate(parts, axis=1)

    meant = [meant_for(k) for k in range(plane)]
    grad_main, *meant = lax.optimization_barrier((grad_main, *meant))
    shared = [meant[0]] + [
        lax.ppermute(meant[k], "ctx", partners(cycle_size, steps[0], k)) for k in range(1, plane)
    ]
    dq_main, kept_main, sent_main = attention_backward(
        main_plan, own, other, (), grad_main, total_main, lse_main,
        True, "attention_backward", 40
    )
    dq_main, kept_main, sent_main, *shared = lax.optimization_barrier(
        (dq_main, kept_main, sent_main, *shared)
    )
    shared = sum(part.astype(jnp.float32) for part in shared).astype(jnp.bfloat16)
    shared = shared.reshape(lines * (early_rows + last_rows), lanes)
    incoming_back = exchange(pair_back(dq_main, kept_main, sent_main))
    singles = [(bit, 1) for bit in range(2, cycle_size.bit_length() - 1)]
    for step in singles:
        shared = scattered(shared, step, cycle_size)
    early, last_sum = shared[:early_rows], shared[early_rows:]

    late_kept, late_sent, inner_grads = projections_late(
        core_1, incoming_back, dq_last, last_sum, hidden_t, inners, adapter_mask, ups_t, unit
    )
    singles = singles[::-1]
    late, early, inner_grads = lax.optimization_barrier(
        (pair_sum(late_kept, late_sent), early, inner_grads)
    )
    grad_in_t = projections_back(
        core_1, incoming_back, dq_last, last_sum, inner_grads, gains_t, tokens_t, middle_grad_t,
        weights[:3], others[:3], downs,
    )

    norm_factor = (tok_dev * group_size * cycle_size) ** (-0.5)
    late = scattered(late, steps[0], cycle_size)
    for step in singles:
        early = collected(early, step, cycle_size)
    late, early = lax.optimization_barrier((late, early))
    for step in steps[1:]:
        late = scattered(late, step, cycle_size)
    early = collected(early, steps[0], cycle_size)
    late, early, grad_in_t = lax.optimization_barrier((late, early, grad_in_t))
    early_other = swap(early)
    for step in reversed(steps[1:]):
        late = collected(late, step, cycle_size)
    late, early_other = lax.optimization_barrier((late, early_other))
    late = collected(late, steps[0], cycle_size)
    wide = b_up.shape[1]
    early = finished(
        early_finish_kernel, norm_factor, core_1, early, early_other,
        [(lanes, wide), (wide, lanes)] + [(width_all, lanes)] * 4, (), "early_finish",
    )
    late, early = lax.optimization_barrier((late, early))
    g_b_up, g_a_down, g_b_down, g_a_up, g_a_out, g_b_out = early
    late = finished(
        late_finish_kernel, norm_factor, core_1, late, swap(late), [(width_all, lanes)] * 6,
        (((2, *late.shape), jnp.float32),), "late_finish",
    )
    return (
        output_t.T,
        grad_in_t.T,
        late[0],
        late[1].T,
        late[2],
        late[3].T,
        late[4],
        late[5].T,
        g_a_out,
        g_b_out.T,
        g_a_up,
        g_b_up,
        g_a_down,
        g_b_down.T,
    )


def solution(mesh):
    return jax.shard_map(
        local,
        mesh=mesh,
        in_specs=(
            P(("ctx", "wsh"), None),
            P(),
            P(),
            P("wsh"),
            P("wsh"),
            P("wsh"),
            P("wsh"),
            P("wsh", None),
            P("wsh", None),
            P("wsh", None),
            P("wsh", None),
            P("wsh", None),
            P(None, "wsh"),
            P(),
            P(),
            P(),
            P(),
            P(),
            P(),
            P(),
            P(),
            P(),
            P(),
            P(),
            P(),
            P(("ctx", "wsh"), None),
        ),
        out_specs=(
            P(("ctx", "wsh"), None),
            P(("ctx", "wsh"), None),
            P(),
            P(),
            P(),
            P(),
            P(),
            P(),
            P(),
            P(),
            P(),
            P(),
            P(),
            P(),
        ),
        check_vma=False,
    )
```

```python
import functools
import math

import jax
import jax.numpy as jnp
from jax import lax
from jax.experimental import pallas as pl
from jax.experimental.pallas import tpu as pltpu
from jax.sharding import PartitionSpec as P

HEAD = 64
RANK = 16
DOC_MAX = 4096


EPSILON = 1e-05
NEG_FILL = -1e30
SCALING = HEAD ** (-0.5)
SWAP = [(0, 1), (1, 0)]
VMEM_BYTES = 60 * 1024 * 1024
SMALL_BYTES = 24 * 1024 * 1024


def norm_parts(values, gain, shift):
    row_mean = jnp.mean(values, axis=-1, keepdims=True)
    centered = values - row_mean
    variance = jnp.mean(centered * centered, axis=-1, keepdims=True)
    inverse = lax.rsqrt(variance + EPSILON)
    normed = centered * inverse
    return (normed * gain + shift, normed, inverse)


def norm_back(grad, normed, inverse, gain):
    scaled = grad * gain
    return inverse * (
        scaled
        - jnp.mean(scaled, axis=-1, keepdims=True)
        - normed * jnp.mean(scaled * normed, axis=-1, keepdims=True)
    )


def dot(left, right, lc=1, rc=0):
    return lax.dot_general(
        left, right, (((lc,), (rc,)), ((), ())), preferred_element_type=jnp.float32
    )


DOC_SLOTS = 64


def side_by_side(ref, first, count):
    return jnp.concatenate([ref[first + k, 0:HEAD, :] for k in range(count)], axis=1)


def marked_queries(query_ref, first, count, docs):
    query = side_by_side(query_ref, first, count)
    query = (query.astype(jnp.float32) * SCALING).astype(jnp.bfloat16)
    number = lax.broadcasted_iota(jnp.int32, (DOC_SLOTS, docs.shape[1]), 0)
    marks = jnp.where(number == docs, 0.0, NEG_FILL).astype(jnp.bfloat16)
    return query, jnp.concatenate([query, marks], axis=0)


def marked_keys(pair, bounds_ref, first_pos):
    rows = pair.shape[0]
    place = first_pos + lax.broadcasted_iota(jnp.int32, (rows, DOC_SLOTS), 0)
    marks = (place >= bounds_ref[0:1, :]) & (place < bounds_ref[1:2, :])
    marks = jnp.where(marks, 1.0, 0.0).astype(jnp.bfloat16)
    return jnp.concatenate([pair[:, :HEAD], marks], axis=1)


def causal(scores, first_pos, query_pos):
    row = lax.broadcasted_iota(jnp.int32, scores.shape, 0)
    return jnp.where(row <= query_pos - first_pos, scores, NEG_FILL)


def group_lanes(meta_ref, g, lanes, rows):
    lane = lax.broadcasted_iota(jnp.int32, (1, lanes), 1)
    return meta_ref[g, 2] + lane + jnp.where(lane >= rows, rows, 0)


def span_walk(meta_ref, g, size, two, block, state):
    def spot(t):
        first = pl.multiple_of(t * size, size)
        return pl.ds(first, size), meta_ref[0, 4] + first

    def walk(first, end, alone, state):
        return lax.fori_loop(first, end, lambda t, state: block(*spot(t), False, alone, state), state)

    if two:
        state = walk(meta_ref[g, 0], meta_ref[g, 6], True, state)
    state = walk(meta_ref[g, 6], meta_ref[g, 1], False, state)
    return block(*spot(meta_ref[g, 1]), True, False, state)


def span_copies(remote, places, semaphores, t):
    spot = pl.ds(2 * t, 2)
    return [
        pltpu.make_async_copy(source.at[spot], place.at[spot], semaphores.at[t, i])
        for i, (source, place) in enumerate(zip(remote, places))
    ]


def start_spans(meta_ref, groups, remote, places, semaphores):
    def start(t, carry):
        for copy in span_copies(remote, places, semaphores, t):
            copy.start()
        return carry

    lax.fori_loop(meta_ref[0, 5], meta_ref[groups - 1, 1] + 1, start, 0)


def new_blocks(meta_ref, g, remote, places, semaphores, rows, use):
    core = meta_ref[0, 3]

    def span(t, carry):
        for copy in span_copies(remote, places, semaphores, t):
            copy.wait()
        for k in range(2):
            for place, side in zip(places, (core, 1 - core)):
                use(pl.multiple_of(((2 * t + k) * 2 + side) * rows, rows), place.at[2 * t + k])
        return carry

    lax.fori_loop(meta_ref[g, 5], meta_ref[g, 1] + 1, span, 0)


def forward_kernel(
    pair_at, first_chunk, per_group, meta_ref, docs_ref, bounds_ref, own_ref, other_ref, *refs
):
    apart = len(refs) - 8
    query_ref, (low_ref, mixed_ref, lse_ref, own_place, other_place) = refs[0], refs[apart : apart + 5]
    keys_ref, values_ref, semaphores = refs[apart + 5 :]
    query_ref = query_ref if apart else own_place
    groups, _, lanes = docs_ref.shape
    rows = own_place.shape[2]
    remote, places = (own_ref, other_ref), (own_place, other_place)
    first_key = meta_ref[0, 4]
    start_spans(meta_ref, groups, remote, places, semaphores)

    def spread(first, pair_ref):
        pair = pair_ref[pair_at : pair_at + 2 * HEAD, :]
        keys_ref[pl.ds(first, rows), :] = marked_keys(pair.T, bounds_ref, first_key + first)
        values_ref[:, pl.ds(first, rows)] = pair[HEAD:]

    def group(g, carry):
        new_blocks(meta_ref, g, remote, places, semaphores, rows, spread)
        _, query = marked_queries(query_ref, first_chunk + g * per_group, per_group, docs_ref[g])
        query_pos = group_lanes(meta_ref, g, lanes, rows)

        def block(spot, first_pos, last, alone, state):
            cut = slice(0, rows if alone else lanes)
            row_max, row_sum, total = (part[:, cut] for part in state)
            scores = dot(keys_ref[spot, :], query[:, cut])
            if last:
                scores = causal(scores, first_pos, query_pos)
            new_max = jnp.maximum(row_max, jnp.max(scores, axis=0, keepdims=True))
            probs = jnp.exp(scores - new_max)
            shrink = jnp.exp(row_max - new_max)
            row_sum = row_sum * shrink + jnp.sum(probs, axis=0, keepdims=True)
            total = total * shrink + dot(values_ref[:, spot], probs.astype(jnp.bfloat16))
            new = (new_max, row_sum, total)
            if alone:
                new = tuple(jnp.concatenate([x, y[:, rows:]], axis=1) for x, y in zip(new, state))
            return new

        state = (
            jnp.full((1, lanes), NEG_FILL, jnp.float32),
            jnp.zeros((1, lanes), jnp.float32),
            jnp.zeros((HEAD, lanes), jnp.float32),
        )
        row_max, row_sum, total = span_walk(meta_ref, g, 4 * rows, per_group == 2, block, state)
        mixed = total / row_sum
        mixed_ref[g] = mixed
        for k in range(per_group):
            low_ref[g * per_group + k] = mixed[:, k * rows : (k + 1) * rows].astype(jnp.bfloat16)
        lse_ref[g] = row_max + jnp.log(row_sum)
        return carry

    lax.fori_loop(0, groups, group, 0)


def backward_kernel(
    pair_at, first_chunk, per_group, turned, meta_ref, docs_ref, bounds_ref, own_ref, other_ref, *refs
):
    apart = len(refs) - 16
    grad_ref, mixed_ref, lse_ref = refs[apart : apart + 3]
    dq_ref, kept_ref, sent_ref, own_place, other_place, kept_place, sent_place = refs[apart + 3 : apart + 10]
    keys_ref, rows_ref, keys_t_ref, sum_ref, semaphores, out_semaphores = refs[apart + 10 :]
    query_ref = refs[0] if apart else own_place
    groups, _, lanes = docs_ref.shape
    blocks, _, rows = own_place.shape
    remote, places = (own_ref, other_ref), (own_place, other_place)
    core, first_key = meta_ref[0, 3], meta_ref[0, 4]
    start_spans(meta_ref, groups, remote, places, semaphores)
    if apart:
        sum_ref[...] = jnp.zeros(sum_ref.shape, jnp.float32)

    def spread(first, pair_ref):
        pair = pair_ref[pair_at : pair_at + 2 * HEAD, :]
        turned_pair = pair.T
        rows_ref[pl.ds(first, rows), :] = turned_pair
        keys_ref[pl.ds(first, rows), :] = marked_keys(turned_pair, bounds_ref, first_key + first)
        keys_t_ref[:, pl.ds(first, rows)] = pair[:HEAD]
        if not apart:
            sum_ref[pl.ds(first, rows), :] = jnp.zeros((rows, 2 * HEAD), jnp.float32)

    def group(g, carry):
        new_blocks(meta_ref, g, remote, places, semaphores, rows, spread)
        first = first_chunk + g * per_group
        query, query_marked = marked_queries(query_ref, first, per_group, docs_ref[g])
        grad = side_by_side(grad_ref, g * per_group, per_group)
        nothing = jnp.zeros_like(query)
        query_low = jnp.concatenate([query, nothing], axis=0)
        grad_high = jnp.concatenate([nothing, grad], axis=0)
        both = jnp.concatenate([query_low, grad_high], axis=1).T
        delta = jnp.sum(grad.astype(jnp.float32) * mixed_ref[g], axis=0, keepdims=True)
        lse = lse_ref[g]
        query_pos = group_lanes(meta_ref, g, lanes, rows)

        def block(spot, first_pos, last, alone, total):
            cut = slice(0, rows if alone else lanes)
            scores = dot(keys_ref[spot, :], query_marked[:, cut])
            if last:
                scores = causal(scores, first_pos, query_pos)
            probs = jnp.exp(scores - lse[:, cut])
            prob_grad = dot(rows_ref[spot, :], grad_high[:, cut])
            score_grad = (probs * (prob_grad - delta[:, cut])).astype(jnp.bfloat16)
            turned_back = both
            if alone:
                turned_back = jnp.concatenate([both[:rows], both[lanes : lanes + rows]], axis=0)
            sum_ref[spot, :] += dot(
                jnp.concatenate([score_grad, probs.astype(jnp.bfloat16)], axis=1), turned_back
            )
            new = total[:, cut] + dot(keys_t_ref[:, spot], score_grad)
            return jnp.concatenate([new, total[:, rows:]], axis=1) if alone else new

        total = span_walk(
            meta_ref, g, 4 * rows, per_group == 2, block, jnp.zeros((HEAD, lanes), jnp.float32)
        )
        total = (total * SCALING).astype(jnp.bfloat16)
        for k in range(per_group):
            dq_ref[g * per_group + k, 0:HEAD, :] = total[:, k * rows : (k + 1) * rows]
        return carry

    lax.fori_loop(0, groups, group, 0)

    def out_copies(j):
        return [
            pltpu.make_async_copy(place.at[j], ref.at[j], out_semaphores.at[j, i])
            for i, (place, ref) in enumerate(((kept_place, kept_ref), (sent_place, sent_ref)))
        ]

    def finish(j, carry):
        for ref, side in ((kept_place, core), (sent_place, 1 - core)):
            spot = pl.ds(pl.multiple_of((2 * j + side) * rows, rows), rows)
            total = sum_ref[spot, :].astype(ref.dtype)
            ref[j] = total.T if turned else total
        for copy in out_copies(j):
            copy.start()
        return carry

    def finished(j, carry):
        for copy in out_copies(j):
            copy.wait()
        return carry

    lax.fori_loop(0, blocks, finish, 0)
    lax.fori_loop(0, blocks, finished, 0)


def cost(microseconds):
    return pl.CostEstimate(
        flops=microseconds * 1_000_000_000, bytes_accessed=microseconds * 1_000_000, transcendentals=0
    )


SMEM_SPEC = pl.BlockSpec(memory_space=pltpu.SMEM)
VMEM_SPEC = pl.BlockSpec(memory_space=pltpu.VMEM)


ANY_SPEC = pl.BlockSpec(memory_space=pl.ANY)


def attention_forward(plan, own, other, query, name, microseconds):
    meta, docs, bounds, pair_at, first_chunk, per_group = plan
    groups, _, lanes = docs.shape
    blocks, _, rows = own.shape
    keys = blocks * 2 * rows
    return pl.pallas_call(
        functools.partial(forward_kernel, pair_at, first_chunk, per_group),
        out_shape=(
            jax.ShapeDtypeStruct((groups * per_group, HEAD, rows), jnp.bfloat16),
            jax.ShapeDtypeStruct((groups, HEAD, lanes), jnp.float32),
            jax.ShapeDtypeStruct((groups, 1, lanes), jnp.float32),
        ),
        in_specs=[SMEM_SPEC] + [VMEM_SPEC] * 2 + [ANY_SPEC] * 2 + [VMEM_SPEC] * len(query),
        out_specs=(VMEM_SPEC,) * 3,
        scratch_shapes=[
            *[pltpu.VMEM(own.shape, jnp.bfloat16)] * 2,
            pltpu.VMEM((keys, HEAD + DOC_SLOTS), jnp.bfloat16),
            pltpu.VMEM((HEAD, keys), jnp.bfloat16),
            pltpu.SemaphoreType.DMA((blocks // 2, 2)),
        ],
        compiler_params=pltpu.CompilerParams(vmem_limit_bytes=VMEM_BYTES),
        cost_estimate=cost(microseconds),
        name=name,
    )(meta, docs, bounds, own, other, *query)


def attention_backward(plan, own, other, query, grad, mixed, lse, turned, name, microseconds):
    meta, docs, bounds, pair_at, first_chunk, per_group = plan
    groups, _, lanes = docs.shape
    blocks, _, rows = own.shape
    keys = blocks * 2 * rows
    part = (blocks, 2 * HEAD, rows) if turned else (blocks, rows, 2 * HEAD)
    return pl.pallas_call(
        functools.partial(backward_kernel, pair_at, first_chunk, per_group, turned),
        out_shape=(
            jax.ShapeDtypeStruct((groups * per_group, (3 if turned else 1) * HEAD, rows), jnp.bfloat16),
            jax.ShapeDtypeStruct(part, jnp.bfloat16),
            jax.ShapeDtypeStruct(part, jnp.bfloat16),
        ),
        in_specs=[SMEM_SPEC] + [VMEM_SPEC] * 2 + [ANY_SPEC] * 2 + [VMEM_SPEC] * (len(query) + 3),
        out_specs=(VMEM_SPEC, ANY_SPEC, ANY_SPEC),
        scratch_shapes=[
            *[pltpu.VMEM(own.shape, jnp.bfloat16)] * 2,
            pltpu.VMEM(part, jnp.bfloat16),
            pltpu.VMEM(part, jnp.bfloat16),
            pltpu.VMEM((keys, HEAD + DOC_SLOTS), jnp.bfloat16),
            pltpu.VMEM((keys, 2 * HEAD), jnp.bfloat16),
            pltpu.VMEM((HEAD, keys), jnp.bfloat16),
            pltpu.VMEM((keys, 2 * HEAD), jnp.float32),
            pltpu.SemaphoreType.DMA((blocks // 2, 2)),
            pltpu.SemaphoreType.DMA((blocks, 2)),
        ],
        compiler_params=pltpu.CompilerParams(vmem_limit_bytes=VMEM_BYTES),
        cost_estimate=cost(microseconds),
        name=name,
    )(meta, docs, bounds, own, other, *query, grad, mixed, lse)


def gelu_parts(value):
    scale = (2.0 / math.pi) ** 0.5
    square = value * value
    bent = jnp.tanh(scale * value * (1.0 + 0.044715 * square))
    upper = 0.5 * (1.0 + bent)
    slope = 0.5 * value * (1.0 - bent * bent) * scale * (1.0 + 3 * 0.044715 * square)
    return value * upper, upper + slope


def column_norm(values, gain, shift):
    row_mean = jnp.mean(values, axis=0, keepdims=True)
    centered = values - row_mean
    variance = jnp.mean(centered * centered, axis=0, keepdims=True)
    inverse = lax.rsqrt(variance + EPSILON)
    normed = centered * inverse
    return (normed * gain + shift, normed, inverse)


def column_norm_back(grad, normed, inverse, gain):
    scaled = grad * gain
    return inverse * (
        scaled
        - jnp.mean(scaled, axis=0, keepdims=True)
        - normed * jnp.mean(scaled * normed, axis=0, keepdims=True)
    )


def fetched(refs, places, semaphores):
    copies = [
        pltpu.make_async_copy(ref, place, semaphores.at[i])
        for i, (ref, place) in enumerate(zip(refs, places))
    ]
    for copy in copies:
        copy.start()
    return copies


def half_rows(core, half):
    return (
        pl.ds(pl.multiple_of(core * half, 32), half),
        pl.ds(pl.multiple_of((1 - core) * half, 32), half),
    )


def ahead_kernel(
    tile, core_ref, mask_ref, cotangent_ref, b_down_ref, *refs
):
    remote, (active_grad_ref, down_grad_ref), refs = refs[:3], refs[3:5], refs[5:]
    down_w_ref, a_down_ref, place_ref, semaphores, out_semaphores = refs
    half, wide = remote[0].shape
    sides = half_rows(core_ref[0], half)
    spots = [slice(k, min(k + tile, wide)) for k in range(0, wide, tile)]
    copies = []
    for k, spot in enumerate(spots):
        pairs = [(remote[i].at[:, spot], down_w_ref.at[sides[i], spot]) for i in range(2)]
        pairs += [(remote[2].at[spot, :], a_down_ref.at[spot, :])]
        for i, (source, place) in enumerate(pairs):
            copies.append(pltpu.make_async_copy(source, place, semaphores.at[k, i]))
    for copy in copies:
        copy.start()
    rows = cotangent_ref[...].T
    down_grad = dot(rows, b_down_ref[...]).astype(jnp.bfloat16) * mask_ref[...].astype(jnp.bfloat16)
    down_grad_ref[...] = down_grad
    given = []
    for k, spot in enumerate(spots):
        for copy in copies[3 * k : 3 * k + 3]:
            copy.wait()
        grad = dot(rows, down_w_ref[:, spot]) + dot(down_grad, a_down_ref[spot, :].T)
        place_ref[:, spot] = grad
        given.append(
            pltpu.make_async_copy(place_ref.at[:, spot], active_grad_ref.at[:, spot], out_semaphores.at[k])
        )
        given[-1].start()
    for copy in given:
        copy.wait()


def ahead_part(core, mask, cotangent_t, b_down_t, down_pair_t, a_down):
    width, rows = cotangent_t.shape
    wide, inner = a_down.shape
    tile = 1024
    count = -(-wide // tile)
    return pl.pallas_call(
        functools.partial(ahead_kernel, tile),
        out_shape=(
            jax.ShapeDtypeStruct((rows, wide), jnp.float32),
            jax.ShapeDtypeStruct((rows, inner), jnp.bfloat16),
        ),
        in_specs=[SMEM_SPEC] + [VMEM_SPEC] * 3 + [ANY_SPEC] * 3,
        out_specs=(ANY_SPEC, VMEM_SPEC),
        scratch_shapes=[
            pltpu.VMEM((width, wide), jnp.bfloat16),
            pltpu.VMEM((wide, inner), jnp.bfloat16),
            pltpu.VMEM((rows, wide), jnp.float32),
            pltpu.SemaphoreType.DMA((count, 3)),
            pltpu.SemaphoreType.DMA((count,)),
        ],
        compiler_params=pltpu.CompilerParams(vmem_limit_bytes=VMEM_BYTES),
        cost_estimate=cost(1),
        name="ahead_part",
    )(core, mask, cotangent_t, b_down_t, *down_pair_t, a_down)


def middle_kernel(
    tile, core_ref, *refs
):
    sources, remote, results, (kept_ref, sent_ref), places, result_places, refs = (
        refs[:11], refs[11:20], refs[20:24], refs[24:26], refs[26:37], refs[37:41], refs[41:],
    )
    (
        mixed_main_ref, mixed_last_ref, mask_ref, a_out_ref, b_out_ref, stream_ref, gains_ref,
        a_up_ref, down_grad_ref, cotangent_ref, b_down_ref,
    ) = places
    output_ref, middle_grad_ref, main_grad_ref, last_grad_ref = result_places
    (
        out_ref, up_ref, b_up_ref, down_w_ref, a_down_ref, kept_place, sent_place,
        active_grad_ref, mixed_ref, middle_ref, hidden_ref, hidden_rows_ref, inner_out_ref,
        inner_up_ref, inner_down_ref, up_grad_ref, down_ref, back_ref,
        semaphores, out_semaphores, place_semaphores, result_semaphores,
    ) = refs
    core = core_ref[0]
    half, wide = remote[2].shape
    width = 2 * half
    full = wide // tile
    low = jnp.bfloat16
    sides = half_rows(core, half)

    def copies(first, size, number):
        spot = pl.ds(first, size)
        pairs = [(remote[2 + i].at[:, spot], up_ref.at[sides[i], spot]) for i in range(2)]
        pairs += [(remote[5 + i].at[:, spot], down_w_ref.at[sides[i], spot]) for i in range(2)]
        pairs += [(remote[4].at[:, spot], b_up_ref.at[:, spot])]
        pairs += [(remote[7].at[spot, :], a_down_ref.at[spot, :])]
        pairs += [(remote[8].at[:, spot], active_grad_ref.at[:, spot])]
        return [
            pltpu.make_async_copy(source, place, semaphores.at[number, i])
            for i, (source, place) in enumerate(pairs)
        ]

    firsts = [
        pltpu.make_async_copy(remote[i], out_ref.at[sides[i], :], semaphores.at[full + 1, i])
        for i in range(2)
    ]
    given = fetched(sources[:4], places[:4], place_semaphores)
    for copy in firsts:
        copy.start()
    later = [
        pltpu.make_async_copy(sources[i], places[i], place_semaphores.at[i]) for i in range(4, 11)
    ]
    for copy in later:
        copy.start()

    def give(i):
        copy = pltpu.make_async_copy(result_places[i], results[i], result_semaphores.at[i])
        copy.start()
        return copy

    def start_chunk(k):
        @pl.when(k < full)
        def _():
            for copy in copies(pl.multiple_of(k * tile, tile), tile, k):
                copy.start()

        if wide % tile:

            @pl.when(k == full)
            def _():
                for copy in copies(full * tile, wide % tile, full):
                    copy.start()

    def out_copies(first, size, number):
        spot = pl.ds(first, size)
        pairs = ((kept_place, kept_ref), (sent_place, sent_ref))
        return [
            pltpu.make_async_copy(place.at[spot, :], ref.at[spot, :], out_semaphores.at[number, i])
            for i, (place, ref) in enumerate(pairs)
        ]

    def put(first, rows, other):
        spot = pl.ds(first, rows.shape[0])

        @pl.when(core == 0)
        def _():
            kept_place[spot, :] = rows
            sent_place[spot, :] = other

        @pl.when(core == 1)
        def _():
            kept_place[spot, :] = other
            sent_place[spot, :] = rows

    for copy in given[:4]:
        copy.wait()
    mask = mask_ref[...]
    mask_low = mask.astype(low)
    main = mixed_main_ref.shape[0] * HEAD
    mixed_ref[:main, :] = mixed_main_ref[...].reshape(main, mixed_main_ref.shape[2])
    mixed_ref[main:, :] = mixed_last_ref[0]
    mixed_rows = mixed_ref[...].T
    inner_out = (mask * (dot(mixed_rows, a_out_ref[...]))).astype(low)
    inner_out_ref[...] = inner_out
    for copy in (*firsts, *later):
        copy.wait()
    start_chunk(0)
    start_chunk(1)
    branch = dot(mixed_rows, out_ref[...]).T + dot(b_out_ref[...], inner_out.T)
    middle = stream_ref[...].astype(jnp.float32) + branch
    middle_ref[...] = middle
    hidden = column_norm(middle, gains_ref[:, 2:3], gains_ref[:, 3:4])[0].astype(low)
    hidden_ref[...] = hidden
    hidden_rows = hidden.T
    hidden_rows_ref[...] = hidden_rows
    inner_up_ref[...] = (mask * dot(hidden_rows, a_up_ref[...])).astype(low)
    for ref in (inner_down_ref, up_grad_ref, down_ref, back_ref):
        ref[...] = jnp.zeros(ref.shape, ref.dtype)

    def step(k, size):
        first = k * tile if isinstance(k, int) else pl.multiple_of(k * tile, tile)
        for copy in copies(first, size, k):
            copy.wait()
        start_chunk(k + 2)
        spot = pl.ds(first, size)
        up, b_up, down_w, a_down = up_ref[:, spot], b_up_ref[:, spot], down_w_ref[:, spot], a_down_ref[spot, :]
        inner_up, down_grad = inner_up_ref[...], down_grad_ref[...]
        upward = dot(hidden_rows_ref[...], up) + dot(inner_up, b_up)
        active, slope = gelu_parts(upward)
        active = active.astype(low)
        up_grad = (active_grad_ref[:, spot] * slope).astype(low)
        active_t, up_grad_t = active.T, up_grad.T
        down_ref[...] += dot(down_w, active_t)
        back_ref[...] += dot(up, up_grad_t)
        inner_down_ref[...] += dot(active, a_down)
        up_grad_ref[...] += dot(b_up, up_grad_t)
        put(first, dot(up_grad_t, inner_up).astype(low), dot(active_t, down_grad).astype(low))
        for copy in out_copies(first, size, k):
            copy.start()

    def loop(k, carry):
        step(k, tile)
        return carry

    lax.fori_loop(0, full, loop, 0)
    if wide % tile:
        step(full, wide % tile)

    inner_down = (mask * inner_down_ref[...]).astype(low)
    middle = middle_ref[...]
    inner_grad = up_grad_ref[...].astype(low).T * mask_low
    hidden_grad = back_ref[...] + dot(a_up_ref[...], inner_grad.T)
    gain = gains_ref[:, 2:3]
    _, normed, inverse = column_norm(middle, gain, gain)
    middle_grad = cotangent_ref[...].astype(jnp.float32)
    middle_grad = middle_grad + column_norm_back(hidden_grad, normed, inverse, gain)
    middle_grad_ref[...] = middle_grad
    given = [give(1)]
    branch = middle_grad.astype(low)
    out_grad = dot(branch.T, b_out_ref[...]).astype(low) * mask_low
    put(wide, dot(cotangent_ref[...], inner_down).astype(low), dot(mixed_ref[...], out_grad).astype(low))
    put(
        wide + width,
        dot(hidden_ref[...], inner_grad).astype(low),
        dot(branch, inner_out_ref[...]).astype(low),
    )
    narrow = kept_place.shape[0] - wide
    spare = narrow - 2 * width
    if spare:
        nothing = jnp.zeros((spare, kept_place.shape[1]), low)
        put(wide + 2 * width, nothing, nothing)
    for copy in out_copies(wide, narrow, full + 1):
        copy.start()
    back = (dot(out_ref[...], branch) + dot(a_out_ref[...], out_grad.T)).astype(low)
    main_grad_ref[...] = back[:main].reshape(main_grad_ref.shape)
    last_grad_ref[0] = back[main:]
    given += [give(2), give(3)]
    down = down_ref[...] + dot(b_down_ref[...], inner_down.T)
    output_ref[...] = (middle + down).astype(low)
    given += [give(0)]

    def finished(k, carry):
        for copy in out_copies(pl.multiple_of(k * tile, tile), tile, k):
            copy.wait()
        return carry

    lax.fori_loop(0, full, finished, 0)
    if wide % tile:
        for copy in out_copies(full * tile, wide % tile, full):
            copy.wait()
    for copy in (*out_copies(wide, narrow, full + 1), *given):
        copy.wait()


def padded(size, unit):
    return -(-size // unit) * unit


def middle_part(
    core, mixed_main, mixed_last, tokens_t, cotangent_t, mask, gains_t, out_pair, a_out, b_out_t,
    a_up, b_down_t, up_pair, b_up, down_pair_t, a_down, active_grad, down_grad, unit,
):
    width, rows = tokens_t.shape
    half = width // 2
    inner, wide = b_up.shape
    tile = 512
    low = jnp.bfloat16
    operands = (
        mixed_main, mixed_last, mask, a_out, b_out_t, tokens_t, gains_t, a_up, down_grad,
        cotangent_t, b_down_t,
    )
    remote = (*out_pair, *up_pair, b_up, *down_pair_t, a_down, active_grad)
    share = (padded(wide + 2 * width, unit), inner)
    shapes = (
        ((width, rows), low), ((width, rows), jnp.float32), (mixed_main.shape, low),
        (mixed_last.shape, low), (share, low), (share, low),
    )
    return pl.pallas_call(
        functools.partial(middle_kernel, tile),
        out_shape=tuple(jax.ShapeDtypeStruct(*item) for item in shapes),
        in_specs=[SMEM_SPEC] + [ANY_SPEC] * (len(operands) + len(remote)),
        out_specs=(ANY_SPEC,) * 6,
        scratch_shapes=[
            *[pltpu.VMEM(item.shape, item.dtype) for item in operands],
            *[pltpu.VMEM(*item) for item in shapes[:4]],
            pltpu.VMEM((width, width), low),
            pltpu.VMEM((width, wide), low),
            pltpu.VMEM((inner, wide), low),
            pltpu.VMEM((width, wide), low),
            pltpu.VMEM((wide, inner), low),
            *[pltpu.VMEM(share, low)] * 2,
            pltpu.VMEM((rows, wide), jnp.float32),
            pltpu.VMEM((width, rows), low),
            pltpu.VMEM((width, rows), jnp.float32),
            pltpu.VMEM((width, rows), low),
            pltpu.VMEM((rows, width), low),
            *[pltpu.VMEM((rows, inner), low)] * 2,
            pltpu.VMEM((rows, inner), jnp.float32),
            pltpu.VMEM((inner, rows), jnp.float32),
            *[pltpu.VMEM((width, rows), jnp.float32)] * 2,
            pltpu.SemaphoreType.DMA((wide // tile + 2, 7)),
            pltpu.SemaphoreType.DMA((wide // tile + 2, 2)),
            pltpu.SemaphoreType.DMA((len(operands),)),
            pltpu.SemaphoreType.DMA((4,)),
        ],
        compiler_params=pltpu.CompilerParams(vmem_limit_bytes=VMEM_BYTES),
        cost_estimate=cost(20),
        name="middle_part",
    )(core, *operands, *remote)


def whole_call(kernel, shapes, scratch, operands, remote, microseconds, name):
    space = [pltpu.VMEM(item.shape, item.dtype) for item in remote]
    return pl.pallas_call(
        kernel,
        out_shape=tuple(jax.ShapeDtypeStruct(*item) for item in shapes),
        in_specs=[SMEM_SPEC]
        + [VMEM_SPEC] * (len(operands) - 1)
        + [pl.BlockSpec(memory_space=pl.ANY)] * len(remote),
        out_specs=(VMEM_SPEC,) * len(shapes),
        scratch_shapes=[pltpu.VMEM(*item) for item in scratch]
        + space
        + ([pltpu.SemaphoreType.DMA((len(remote),))] if remote else []),
        compiler_params=pltpu.CompilerParams(vmem_limit_bytes=VMEM_BYTES if len(remote) > 2 else SMALL_BYTES),
        cost_estimate=cost(microseconds),
        name=name,
    )(*operands, *remote)


def entry_kernel(
    place_ref, lengths_ref, adapters_ref, tokens_ref, gains_own_ref, gains_other_ref, *refs
):
    remote, results, refs = refs[:12], refs[12:19], refs[19:]
    places, (weight_ref, up_ref, down_ref, semaphores, result_semaphores) = refs[:7], refs[7:]
    hidden_ref, inner_ref, mask_ref, gains_ref, heads_ref, query_ref, pairs_ref = places
    rows, inner = mask_ref.shape
    half = gains_own_ref.shape[1]
    sides = half_rows(place_ref[0], half)
    copies = []
    for n in range(3):
        down, own, up, other = remote[4 * n : 4 * n + 4]
        pairs = (
            (down, down_ref.at[n]), (up, up_ref.at[n]),
            (own, weight_ref.at[n, sides[0], :]), (other, weight_ref.at[n, sides[1], :]),
        )
        for i, (source, place) in enumerate(pairs):
            copies.append(pltpu.make_async_copy(source, place, semaphores.at[4 * n + i]))
    for copy in copies:
        copy.start()

    def give(i):
        copy = pltpu.make_async_copy(places[i], results[i], result_semaphores.at[i])
        copy.start()
        return copy

    for spot, ref in zip(sides, (gains_own_ref, gains_other_ref)):
        gains_ref[spot, :] = ref[...].astype(jnp.float32).T
    values = tokens_ref[...].astype(jnp.float32)
    hidden = column_norm(values, gains_ref[:, 0:1], gains_ref[:, 1:2])[0].astype(jnp.bfloat16)
    hidden_ref[...] = hidden
    hidden_rows = hidden.T
    place = place_ref[1] + lax.broadcasted_iota(jnp.int32, (rows, inner), 0)
    column = lax.broadcasted_iota(jnp.int32, (rows, inner), 1) // RANK

    def document(d, state):
        start, mask = state
        end = start + lengths_ref[d]
        chosen = (place >= start) & (place < end) & (column == adapters_ref[d])
        return end, jnp.where(chosen, 1.0, mask)

    state = (jnp.int32(0), jnp.zeros((rows, inner), jnp.float32))
    _, mask = lax.fori_loop(0, lengths_ref.shape[0], document, state)
    mask_ref[...] = mask
    given = [give(0), give(2), give(3)]
    count = heads_ref.shape[0]

    def give_part(n):
        spot = pl.ds(n * HEAD, HEAD)
        copy = pltpu.make_async_copy(
            heads_ref.at[:, spot, :], results[4].at[:, spot, :], result_semaphores.at[7 + n]
        )
        copy.start()
        return copy

    for n in range(3):
        for copy in copies[4 * n : 4 * n + 4]:
            copy.wait()
        products = (mask * dot(hidden_rows, down_ref[n])).astype(jnp.bfloat16)
        inner_ref[n] = products
        total = dot(hidden_rows, weight_ref[n]).T + dot(up_ref[n], products.T)
        total = total.astype(jnp.bfloat16)
        for c in range(count):
            heads_ref[c, n * HEAD : (n + 1) * HEAD, :] = total[c * HEAD : (c + 1) * HEAD]
        if n == 0:
            query_ref[0] = total[count * HEAD :]
        else:
            for c in range(count):
                pairs_ref[c, (n - 1) * HEAD : n * HEAD, :] = total[count * HEAD :]
        given.append(give_part(n))
    for copy in (*given, *[give(i) for i in (1, 5, 6)]):
        copy.wait()


def projections(place, lengths, adapters, tokens_t, gains, gains_other, weights, others, downs, ups_t):
    width, rows = tokens_t.shape
    inner = downs[0].shape[1]
    low = jnp.bfloat16
    count = width // HEAD - 1
    remote = [item for group in zip(downs, weights, ups_t, others) for item in group]
    shapes = (
        ((width, rows), low), ((3, rows, inner), low), ((rows, inner), jnp.float32),
        ((width, gains.shape[0]), jnp.float32), ((count, 3 * HEAD, rows), low),
        ((1, HEAD, rows), low), ((count, 2 * HEAD, rows), low),
    )
    return pl.pallas_call(
        entry_kernel,
        out_shape=tuple(jax.ShapeDtypeStruct(*item) for item in shapes),
        in_specs=[SMEM_SPEC] * 3 + [VMEM_SPEC] * 3 + [ANY_SPEC] * len(remote),
        out_specs=(ANY_SPEC,) * len(shapes),
        scratch_shapes=[pltpu.VMEM(*item) for item in shapes]
        + [
            pltpu.VMEM((3, width, width), low),
            pltpu.VMEM((3, width, inner), low),
            pltpu.VMEM((3, width, inner), low),
            pltpu.SemaphoreType.DMA((12,)),
            pltpu.SemaphoreType.DMA((len(shapes) + 3,)),
        ],
        compiler_params=pltpu.CompilerParams(vmem_limit_bytes=VMEM_BYTES),
        cost_estimate=cost(6),
        name="entry",
    )(place, lengths, adapters, tokens_t, gains, gains_other, *remote)


def gathered_grad(n, heads_ref, last_query_ref, last_pair_ref, grad_ref):
    count = heads_ref.shape[0]
    for c in range(count):
        grad_ref[c * HEAD : (c + 1) * HEAD, :] = heads_ref[c, n * HEAD : (n + 1) * HEAD, :]
    if n == 0:
        grad_ref[count * HEAD :, :] = last_query_ref[0]
    else:
        grad_ref[count * HEAD :, :] = last_pair_ref[...].T[(n - 1) * HEAD : n * HEAD]
    return grad_ref[...]


def projections_late_kernel(core_ref, *refs):
    sources, (kept_ref, sent_ref, inner_grad_ref), refs = refs[:9], refs[9:12], refs[12:]
    places, (kept_place, sent_place, grad_ref, semaphores, out_semaphores) = refs[:9], refs[9:]
    heads_ref, last_query_ref, last_pair_ref, mask_ref, hidden_ref, inner_ref, *ups = places
    copies = fetched(sources, places, semaphores)
    core = core_ref[0]
    low = jnp.bfloat16
    width, share = hidden_ref.shape[0], kept_place.shape[0]

    def store(side, spot, rows):
        @pl.when(core == side)
        def _():
            kept_place[spot, :] = rows

        @pl.when(core != side)
        def _():
            sent_place[spot, :] = rows

    def keep(first, rows):
        done = 0
        while done < rows.shape[0]:
            side, spot = divmod(first + done, share)
            size = min(rows.shape[0] - done, share - spot)
            store(side, slice(spot, spot + size), rows[done : done + size])
            done += size

    keep(6 * width, jnp.zeros((2 * share - 6 * width, kept_place.shape[1]), low))
    for copy in copies[:6]:
        copy.wait()
    mask_low = mask_ref[...].astype(low)
    hidden = hidden_ref[...]
    for n in range(3):
        grad = gathered_grad(n, heads_ref, last_query_ref, last_pair_ref, grad_ref)
        copies[6 + n].wait()
        inner_grad = dot(grad.T, ups[n][...]).astype(low) * mask_low
        inner_grad_ref[n] = inner_grad
        keep(2 * n * width, dot(hidden, inner_grad).astype(low))
        keep((2 * n + 1) * width, dot(grad, inner_ref[n]).astype(low))
    given = fetched((kept_place, sent_place), (kept_ref, sent_ref), out_semaphores)
    for copy in given:
        copy.wait()


def projections_late(core, heads, last_query, last_pair, hidden_t, inners, mask, ups_t, unit):
    width, rows = hidden_t.shape
    low = jnp.bfloat16
    share = (padded(6 * width, 2 * unit) // 2, mask.shape[1])
    operands = (heads, last_query, last_pair, mask, hidden_t, inners, *ups_t)
    return pl.pallas_call(
        projections_late_kernel,
        out_shape=(
            jax.ShapeDtypeStruct(share, low),
            jax.ShapeDtypeStruct(share, low),
            jax.ShapeDtypeStruct(inners.shape, low),
        ),
        in_specs=[SMEM_SPEC] + [ANY_SPEC] * len(operands),
        out_specs=(ANY_SPEC, ANY_SPEC, VMEM_SPEC),
        scratch_shapes=[pltpu.VMEM(item.shape, item.dtype) for item in operands]
        + [
            pltpu.VMEM(share, low),
            pltpu.VMEM(share, low),
            pltpu.VMEM((width, rows), low),
            pltpu.SemaphoreType.DMA((len(operands),)),
            pltpu.SemaphoreType.DMA((2,)),
        ],
        compiler_params=pltpu.CompilerParams(vmem_limit_bytes=VMEM_BYTES),
        cost_estimate=cost(5),
        name="projections_late",
    )(core, *operands)


def projections_back_kernel(
    core_ref, heads_ref, last_query_ref, last_pair_ref, inner_grad_ref, gains_ref, tokens_ref, *refs
):
    remote, (grad_in_ref, grad_ref, sum_ref), local_refs, semaphores = (
        refs[:10], refs[10:13], refs[13:23], refs[23],
    )
    copies = fetched(remote, local_refs, semaphores)
    downs, weights, others, middle_grad_ref = (
        local_refs[:3], local_refs[3:6], local_refs[6:9], local_refs[9],
    )
    own_rows, other_rows = half_rows(core_ref[0], weights[0].shape[0])
    for n in range(3):
        grad = gathered_grad(n, heads_ref, last_query_ref, last_pair_ref, grad_ref)
        turned = inner_grad_ref[n].T
        copies[n].wait()
        for rows, weight, copy in (
            (own_rows, weights[n], copies[3 + n]), (other_rows, others[n], copies[6 + n])
        ):
            copy.wait()
            part = dot(weight[...], grad) + dot(downs[n][rows, :], turned)
            sum_ref[rows, :] = part if n == 0 else sum_ref[rows, :] + part
    gain = gains_ref[:, 0:1]
    _, normed, inverse = column_norm(tokens_ref[...].astype(jnp.float32), gain, gain)
    back = column_norm_back(sum_ref[...], normed, inverse, gain)
    copies[9].wait()
    grad_in_ref[...] = (middle_grad_ref[...] + back).astype(jnp.bfloat16)


def projections_back(
    core, heads, last_query, last_pair, inner_grads, gains_t, tokens_t, middle_grad_t,
    weights, others, downs,
):
    width, rows = tokens_t.shape
    low = jnp.bfloat16
    return whole_call(
        projections_back_kernel,
        (((width, rows), low),),
        (((width, rows), low), ((width, rows), jnp.float32)),
        (core, heads, last_query, last_pair, inner_grads, gains_t, tokens_t),
        (*downs, *weights, *others, middle_grad_t),
        8, "projections_back",
    )[0]


def steps_of(cycle_size):
    bits = cycle_size.bit_length() - 1
    return [(bit, min(2, bits - bit)) for bit in range(0, bits, 2)]


def partners(cycle_size, step, k):
    return [(i, i ^ (k << step[0])) for i in range(cycle_size)]


def scattered(array, step, cycle_size):
    count = 1 << step[1]
    mine = (lax.axis_index("ctx") >> step[0]) & (count - 1)
    blocks = array.reshape(count, array.shape[0] // count, array.shape[1])

    def block(number):
        return lax.dynamic_index_in_dim(blocks, number, 0, keepdims=False)

    total = block(mine).astype(jnp.float32)
    for k in range(1, count):
        got = lax.ppermute(block(mine ^ k), "ctx", partners(cycle_size, step, k))
        total = total + got.astype(jnp.float32)
    return total.astype(array.dtype)


def collected(share, step, cycle_size):
    count = 1 << step[1]
    mine = (lax.axis_index("ctx") >> step[0]) & (count - 1)
    blocks = [share]
    for k in range(1, count):
        blocks.append(lax.ppermute(share, "ctx", partners(cycle_size, step, k)))
    for bit in range(step[1]):
        turned = ((mine >> bit) & 1) == 1
        blocks = [jnp.where(turned, blocks[k ^ (1 << bit)], blocks[k]) for k in range(count)]
    return jnp.concatenate(blocks, axis=0)


def pair_sum(kept, sent):
    return kept + lax.ppermute(sent, "wsh", SWAP)


def early_finish_kernel(
    factor, core_ref, own_source, other_source,
    b_up_ref, a_down_ref, b_down_ref, a_up_ref, a_out_ref, b_out_ref, own_ref, other_ref, semaphores,
):
    for copy in fetched((own_source, other_source), (own_ref, other_ref), semaphores):
        copy.wait()
    wide, width = a_down_ref.shape[0], a_up_ref.shape[0]

    def finish(first_ref, second_ref):
        def part(ref, first, count):
            return ref[first : first + count, :].astype(jnp.float32) * factor

        for k in range(wide // 256):
            b_up_ref[:, k * 256 : (k + 1) * 256] = part(first_ref, k * 256, 256).T
        a_down_ref[...] = part(second_ref, 0, wide)
        b_down_ref[...] = part(first_ref, wide, width)
        a_up_ref[...] = part(first_ref, wide + width, width)
        a_out_ref[...] = part(second_ref, wide, width)
        b_out_ref[...] = part(second_ref, wide + width, width)

    @pl.when(core_ref[0] == 0)
    def _():
        finish(own_ref, other_ref)

    @pl.when(core_ref[0] == 1)
    def _():
        finish(other_ref, own_ref)


def late_finish_kernel(factor, core_ref, own_ref, other_ref, *refs):
    core = core_ref[0]
    targets, late_ref, own_place, other_place, semaphores = refs[:6], *refs[6:]
    places = (own_place, other_place)
    copies = fetched((own_ref, other_ref), places, semaphores)
    for side, ref, copy in zip((core, 1 - core), places, copies):
        copy.wait()
        late_ref[side] = ref[...].astype(jnp.float32) * factor
    width, share = targets[0].shape[0], late_ref.shape[1]
    for n, ref in enumerate(targets):
        done = 0
        while done < width:
            side, spot = divmod(n * width + done, share)
            rows = min(width - done, share - spot)
            ref[done : done + rows, :] = late_ref[side, spot : spot + rows, :]
            done += rows


def finished(kernel, factor, core, own, other, shapes, scratch, name):
    return whole_call(
        functools.partial(kernel, factor), [(shape, jnp.float32) for shape in shapes], scratch,
        (core,), (own, other), 1, name,
    )


def local(
    tokens_in,
    doc_lengths,
    doc_adapter,
    norm1_gain,
    norm1_bias,
    norm2_gain,
    norm2_bias,
    w_query,
    w_key,
    w_value,
    w_out,
    w_up,
    w_down,
    a_query,
    b_query,
    a_key,
    b_key,
    a_value,
    b_value,
    a_out,
    b_out,
    a_up,
    b_up,
    a_down,
    b_down,
    cotangent,
):
    group_size = lax.axis_size("wsh")
    cycle_size = lax.axis_size("ctx")
    tok_dev, width_all = tokens_in.shape
    head_count = width_all // HEAD
    block_len = tok_dev * group_size
    hop_count = (DOC_MAX + block_len - 2) // block_len
    span = head_count - 1
    cycle_pos = lax.axis_index("ctx")
    core = lax.axis_index("wsh")
    half = width_all // group_size

    first_row = cycle_pos * block_len + core * tok_dev
    doc_ends = jnp.cumsum(doc_lengths)
    doc_starts = doc_ends - doc_lengths

    team = cycle_pos // span
    past = hop_count if cycle_size > span else 0
    first_key = (team * span - past) * block_len
    key_blocks = past + span

    slots = DOC_SLOTS - doc_lengths.shape[0]
    bounds = jnp.stack([jnp.pad(doc_starts, (0, slots)), jnp.pad(doc_ends, (0, slots))])

    def plan(chunk_pos, pair_at, first_chunk, per_group):
        groups = chunk_pos.shape[0] // per_group
        row_pos = chunk_pos[:, None] + jnp.arange(tok_dev, dtype=jnp.int32)[None, :]
        row_docs = jnp.sum((doc_ends[None, None, :] <= row_pos[:, :, None]).astype(jnp.int32), axis=2)
        row_docs = row_docs.reshape(groups, 1, per_group * tok_dev)
        chunk_pos = chunk_pos.reshape(groups, per_group)
        began = jnp.where(doc_starts[None, None, :] <= chunk_pos[:, :, None], doc_starts[None, None, :], 0)
        began = (jnp.max(began, axis=2) - first_key) // (2 * block_len)
        first = began[:, 0]
        last = (chunk_pos[:, -1] - first_key) // (2 * block_len)
        same = jnp.ones((groups,), jnp.int32)
        whole = per_group > 1
        meta = [
            first,
            last,
            chunk_pos[:, 0],
            same * core,
            same * first_key,
            jnp.concatenate([first[:1] * 0, last[:-1] + 1]) if whole else first,
            began[:, -1],
        ]
        meta = jnp.stack(meta, axis=1).astype(jnp.int32)
        docs = row_docs.astype(jnp.int32)
        return meta, docs, bounds.astype(jnp.int32), pair_at, first_chunk, per_group

    team_pos = (team * span + jnp.arange(span, dtype=jnp.int32)) * block_len + core * tok_dev
    main_plan = plan(team_pos.astype(jnp.int32), HEAD, past, 2)
    last_plan = plan(first_row[None].astype(jnp.int32), 0, 0, 1)

    def swap(array):
        return lax.ppermute(array, "wsh", SWAP)

    if cycle_size > span:
        teams = [[t * span + i for i in range(span)] for t in range(cycle_size // span)]
    else:
        teams = None

    def exchange(blocks):
        return lax.all_to_all(blocks, "ctx", 0, 0, tiled=True, axis_index_groups=teams)

    gains = jnp.stack([norm1_gain, norm1_bias, norm2_gain, norm2_bias])
    weights = [w_query, w_key, w_value, w_out, w_up, w_down.T]
    others = [swap(item) for item in weights[:3]]
    gains_other = swap(gains)
    *others, gains_other, w_late = lax.optimization_barrier((*others, gains_other, tuple(weights[3:])))
    others = others + [swap(item) for item in w_late]

    downs = (a_query, a_key, a_value)
    ups_t = (b_query.T, b_key.T, b_value.T)
    tokens_t = tokens_in.T
    core_1 = jnp.stack([core, first_row]).astype(jnp.int32)
    hidden_t, inners, adapter_mask, gains_t, heads, last_query, last_pairs = projections(
        core_1, doc_lengths, doc_adapter, tokens_t, gains, gains_other, weights[:3], others[:3],
        downs, ups_t,
    )

    ahead = [(i, i + span) for i in range(cycle_size - span)]
    back = [(i + span, i) for i in range(cycle_size - span)]

    def with_past(blocks):
        if not past:
            return blocks
        return jnp.concatenate([lax.ppermute(blocks[span - past :], "ctx", ahead), blocks], axis=0)

    steps = steps_of(cycle_size)
    unit = 16 * cycle_size
    incoming = exchange(heads)
    active_grad, down_grad = ahead_part(
        core_1, adapter_mask, cotangent.T, b_down.T, (w_down.T, others[5]), a_down
    )
    incoming, last_pairs, active_grad = lax.optimization_barrier((incoming, last_pairs, active_grad))
    own = with_past(incoming)
    other = swap(own)
    last_own = exchange(last_pairs)
    low_main, total_main, lse_main = attention_forward(
        main_plan, own, other, (), "attention_forward", 30
    )
    low_main, last_own = lax.optimization_barrier((low_main, last_own))
    last_own = with_past(last_own)
    last_other = swap(last_own)
    low_last, mixed_last, lse_last = attention_forward(
        last_plan, last_own, last_other, (last_query,), "last_forward", 0
    )
    mixed_main = exchange(low_main)

    output_t, middle_grad_t, main_grad, last_out_grad, early_kept, early_sent = middle_part(
        core_1, mixed_main, low_last, tokens_t, cotangent.T, adapter_mask, gains_t,
        (w_out, others[3]), a_out, b_out.T, a_up, b_down.T, (w_up, others[4]), b_up,
        (w_down.T, others[5]), a_down, active_grad, down_grad, unit,
    )

    def pair_total(kept, sent):
        total = kept.astype(jnp.float32) + swap(sent).astype(jnp.float32)
        if past:
            returned = lax.ppermute(total[:past].astype(jnp.bfloat16), "ctx", back)
            total = total[past:].at[span - past :].add(returned.astype(jnp.float32))
        return total

    def pair_back(dq, kept, sent):
        total = pair_total(kept, sent).astype(jnp.bfloat16)
        return lax.dynamic_update_slice(dq, total, (0, HEAD, 0))

    dq_last, kept_last, sent_last = attention_backward(
        last_plan, last_own, last_other, (last_query,),
        last_out_grad, mixed_last, lse_last, False, "last_backward", 0,
    )
    grad_main = exchange(main_grad)
    grad_main, dq_last, kept_last, sent_last = lax.optimization_barrier(
        (grad_main, dq_last, kept_last, sent_last)
    )
    dpair_last = pair_total(kept_last, sent_last).astype(jnp.bfloat16)
    plane = 1 << steps[0][1]
    lines = cycle_size // plane
    digits = (2,) * (cycle_size.bit_length() - 3) + (plane,)
    if cycle_size > span:
        zero = jnp.zeros((cycle_size // span, *dpair_last.shape), dpair_last.dtype)
        dpair_last = lax.dynamic_update_index_in_dim(zero, dpair_last, team, 0)
    order = tuple(reversed(range(len(digits)))) + (len(digits), len(digits) + 1)
    dpair_last = jnp.transpose(dpair_last.reshape(digits + dpair_last.shape[-2:]), order)
    early = pair_sum(early_kept, early_sent)
    lanes = early.shape[1]
    early_rows, last_rows = early.shape[0] // cycle_size, tok_dev
    early = early.reshape(plane, lines, early_rows, lanes)
    dpair_last = dpair_last.reshape(plane, lines, last_rows, lanes)

    def meant_for(k):
        parts = [lax.dynamic_index_in_dim(x, (cycle_pos % plane) ^ k, 0, False) for x in (early, dpair_last)]
        return jnp.concatenate(parts, axis=1)

    meant = [meant_for(k) for k in range(plane)]
    grad_main, *meant = lax.optimization_barrier((grad_main, *meant))
    shared = [meant[0]] + [
        lax.ppermute(meant[k], "ctx", partners(cycle_size, steps[0], k)) for k in range(1, plane)
    ]
    dq_main, kept_main, sent_main = attention_backward(
        main_plan, own, other, (), grad_main, total_main, lse_main,
        True, "attention_backward", 40
    )
    dq_main, kept_main, sent_main, *shared = lax.optimization_barrier(
        (dq_main, kept_main, sent_main, *shared)
    )
    shared = sum(part.astype(jnp.float32) for part in shared).astype(jnp.bfloat16)
    shared = shared.reshape(lines * (early_rows + last_rows), lanes)
    outgoing_back = pair_back(dq_main, kept_main, sent_main)
    outgoing_back, shared = lax.optimization_barrier((outgoing_back, shared))
    singles = [(bit, 1) for bit in range(2, cycle_size.bit_length() - 1)]
    shared = shared.reshape(lines, early_rows + last_rows, lanes)
    early = shared[:, :early_rows].reshape(lines * early_rows, lanes)
    last_sum = shared[:, early_rows:].reshape(lines * last_rows, lanes)
    incoming_back = exchange(outgoing_back)
    for step in singles:
        last_sum = scattered(last_sum, step, cycle_size)
    for step in singles:
        early = scattered(early, step, cycle_size)

    late_kept, late_sent, inner_grads = projections_late(
        core_1, incoming_back, dq_last, last_sum, hidden_t, inners, adapter_mask, ups_t, unit
    )
    singles = singles[::-1]
    late, early, inner_grads = lax.optimization_barrier(
        (pair_sum(late_kept, late_sent), early, inner_grads)
    )
    grad_in_t = projections_back(
        core_1, incoming_back, dq_last, last_sum, inner_grads, gains_t, tokens_t, middle_grad_t,
        weights[:3], others[:3], downs,
    )

    norm_factor = (tok_dev * group_size * cycle_size) ** (-0.5)
    late = scattered(late, steps[0], cycle_size)
    for step in singles:
        early = collected(early, step, cycle_size)
    late, early = lax.optimization_barrier((late, early))
    for step in steps[1:]:
        late = scattered(late, step, cycle_size)
    early = collected(early, steps[0], cycle_size)
    late, early, grad_in_t = lax.optimization_barrier((late, early, grad_in_t))
    early_other = swap(early)
    for step in reversed(steps[1:]):
        late = collected(late, step, cycle_size)
    late, early_other = lax.optimization_barrier((late, early_other))
    late = collected(late, steps[0], cycle_size)
    wide = b_up.shape[1]
    early = finished(
        early_finish_kernel, norm_factor, core_1, early, early_other,
        [(lanes, wide), (wide, lanes)] + [(width_all, lanes)] * 4, (), "early_finish",
    )
    late, early = lax.optimization_barrier((late, early))
    g_b_up, g_a_down, g_b_down, g_a_up, g_a_out, g_b_out = early
    late = finished(
        late_finish_kernel, norm_factor, core_1, late, swap(late), [(width_all, lanes)] * 6,
        (((2, *late.shape), jnp.float32),), "late_finish",
    )
    return (
        output_t.T,
        grad_in_t.T,
        late[0],
        late[1].T,
        late[2],
        late[3].T,
        late[4],
        late[5].T,
        g_a_out,
        g_b_out.T,
        g_a_up,
        g_b_up,
        g_a_down,
        g_b_down.T,
    )


def solution(mesh):
    return jax.shard_map(
        local,
        mesh=mesh,
        in_specs=(
            P(("ctx", "wsh"), None),
            P(),
            P(),
            P("wsh"),
            P("wsh"),
            P("wsh"),
            P("wsh"),
            P("wsh", None),
            P("wsh", None),
            P("wsh", None),
            P("wsh", None),
            P("wsh", None),
            P(None, "wsh"),
            P(),
            P(),
            P(),
            P(),
            P(),
            P(),
            P(),
            P(),
            P(),
            P(),
            P(),
            P(),
            P(("ctx", "wsh"), None),
        ),
        out_specs=(
            P(("ctx", "wsh"), None),
            P(("ctx", "wsh"), None),
            P(),
            P(),
            P(),
            P(),
            P(),
            P(),
            P(),
            P(),
            P(),
            P(),
            P(),
            P(),
        ),
        check_vma=False,
    )
```

```python
import functools
import math

import jax
import jax.numpy as jnp
from jax import lax
from jax.experimental import pallas as pl
from jax.experimental.pallas import tpu as pltpu
from jax.sharding import PartitionSpec as P

HEAD = 64
RANK = 16
DOC_MAX = 4096


EPSILON = 1e-05
NEG_FILL = -1e30
SCALING = HEAD ** (-0.5)
SWAP = [(0, 1), (1, 0)]
VMEM_BYTES = 60 * 1024 * 1024
SMALL_BYTES = 24 * 1024 * 1024


def norm_parts(values, gain, shift):
    row_mean = jnp.mean(values, axis=-1, keepdims=True)
    centered = values - row_mean
    variance = jnp.mean(centered * centered, axis=-1, keepdims=True)
    inverse = lax.rsqrt(variance + EPSILON)
    normed = centered * inverse
    return (normed * gain + shift, normed, inverse)


def norm_back(grad, normed, inverse, gain):
    scaled = grad * gain
    return inverse * (
        scaled
        - jnp.mean(scaled, axis=-1, keepdims=True)
        - normed * jnp.mean(scaled * normed, axis=-1, keepdims=True)
    )


def dot(left, right, lc=1, rc=0):
    return lax.dot_general(
        left, right, (((lc,), (rc,)), ((), ())), preferred_element_type=jnp.float32
    )


DOC_SLOTS = 64


def side_by_side(ref, first, count):
    return jnp.concatenate([ref[first + k, 0:HEAD, :] for k in range(count)], axis=1)


def marked_queries(query_ref, first, count, docs):
    query = side_by_side(query_ref, first, count)
    query = (query.astype(jnp.float32) * SCALING).astype(jnp.bfloat16)
    number = lax.broadcasted_iota(jnp.int32, (DOC_SLOTS, docs.shape[1]), 0)
    marks = jnp.where(number == docs, 0.0, NEG_FILL).astype(jnp.bfloat16)
    return query, jnp.concatenate([query, marks], axis=0)


def marked_keys(pair, bounds_ref, first_pos):
    rows = pair.shape[0]
    place = first_pos + lax.broadcasted_iota(jnp.int32, (rows, DOC_SLOTS), 0)
    marks = (place >= bounds_ref[0:1, :]) & (place < bounds_ref[1:2, :])
    marks = jnp.where(marks, 1.0, 0.0).astype(jnp.bfloat16)
    return jnp.concatenate([pair[:, :HEAD], marks], axis=1)


def causal(scores, first_pos, query_pos):
    row = lax.broadcasted_iota(jnp.int32, scores.shape, 0)
    return jnp.where(row <= query_pos - first_pos, scores, NEG_FILL)


def group_lanes(meta_ref, g, lanes, rows):
    lane = lax.broadcasted_iota(jnp.int32, (1, lanes), 1)
    return meta_ref[g, 2] + lane + jnp.where(lane >= rows, rows, 0)


def span_walk(meta_ref, g, size, two, block, state):
    def spot(t):
        first = pl.multiple_of(t * size, size)
        return pl.ds(first, size), meta_ref[0, 4] + first

    def walk(first, end, alone, state):
        return lax.fori_loop(first, end, lambda t, state: block(*spot(t), False, alone, state), state)

    if two:
        state = walk(meta_ref[g, 0], meta_ref[g, 6], True, state)
    state = walk(meta_ref[g, 6], meta_ref[g, 1], False, state)
    return block(*spot(meta_ref[g, 1]), True, False, state)


def span_copies(remote, places, semaphores, t):
    spot = pl.ds(2 * t, 2)
    return [
        pltpu.make_async_copy(source.at[spot], place.at[spot], semaphores.at[t, i])
        for i, (source, place) in enumerate(zip(remote, places))
    ]


def start_spans(meta_ref, groups, remote, places, semaphores):
    def start(t, carry):
        for copy in span_copies(remote, places, semaphores, t):
            copy.start()
        return carry

    lax.fori_loop(meta_ref[0, 5], meta_ref[groups - 1, 1] + 1, start, 0)


def new_blocks(meta_ref, g, remote, places, semaphores, rows, use):
    core = meta_ref[0, 3]

    def span(t, carry):
        for copy in span_copies(remote, places, semaphores, t):
            copy.wait()
        for k in range(2):
            for place, side in zip(places, (core, 1 - core)):
                use(pl.multiple_of(((2 * t + k) * 2 + side) * rows, rows), place.at[2 * t + k])
        return carry

    lax.fori_loop(meta_ref[g, 5], meta_ref[g, 1] + 1, span, 0)


def forward_kernel(
    pair_at, first_chunk, per_group, meta_ref, docs_ref, bounds_ref, own_ref, other_ref, *refs
):
    apart = len(refs) - 11
    query_ref, (low_ref, mixed_ref, lse_ref, own_place, other_place) = refs[0], refs[apart : apart + 5]
    low_place, mixed_place, keys_ref, values_ref, semaphores, out_semaphores = refs[apart + 5 :]
    query_ref = query_ref if apart else own_place
    groups, _, lanes = docs_ref.shape
    rows = own_place.shape[2]
    remote, places = (own_ref, other_ref), (own_place, other_place)
    first_key = meta_ref[0, 4]
    start_spans(meta_ref, groups, remote, places, semaphores)

    def spread(first, pair_ref):
        pair = pair_ref[pair_at : pair_at + 2 * HEAD, :]
        keys_ref[pl.ds(first, rows), :] = marked_keys(pair.T, bounds_ref, first_key + first)
        values_ref[:, pl.ds(first, rows)] = pair[HEAD:]

    def group(g, carry):
        new_blocks(meta_ref, g, remote, places, semaphores, rows, spread)
        _, query = marked_queries(query_ref, first_chunk + g * per_group, per_group, docs_ref[g])
        query_pos = group_lanes(meta_ref, g, lanes, rows)

        def block(spot, first_pos, last, alone, state):
            cut = slice(0, rows if alone else lanes)
            row_max, row_sum, total = (part[:, cut] for part in state)
            scores = dot(keys_ref[spot, :], query[:, cut])
            if last:
                scores = causal(scores, first_pos, query_pos)
            new_max = jnp.maximum(row_max, jnp.max(scores, axis=0, keepdims=True))
            probs = jnp.exp(scores - new_max)
            shrink = jnp.exp(row_max - new_max)
            row_sum = row_sum * shrink + jnp.sum(probs, axis=0, keepdims=True)
            total = total * shrink + dot(values_ref[:, spot], probs.astype(jnp.bfloat16))
            new = (new_max, row_sum, total)
            if alone:
                new = tuple(jnp.concatenate([x, y[:, rows:]], axis=1) for x, y in zip(new, state))
            return new

        state = (
            jnp.full((1, lanes), NEG_FILL, jnp.float32),
            jnp.zeros((1, lanes), jnp.float32),
            jnp.zeros((HEAD, lanes), jnp.float32),
        )
        row_max, row_sum, total = span_walk(meta_ref, g, 4 * rows, per_group == 2, block, state)
        mixed = total / row_sum
        mixed_place[g] = mixed
        for k in range(per_group):
            low_place[g * per_group + k] = mixed[:, k * rows : (k + 1) * rows].astype(jnp.bfloat16)
        lse_ref[g] = row_max + jnp.log(row_sum)
        for copy in out_copies(g):
            copy.start()
        return carry

    def out_copies(g):
        spot = pl.ds(g * per_group, per_group)
        return (
            pltpu.make_async_copy(mixed_place.at[g], mixed_ref.at[g], out_semaphores.at[g, 0]),
            pltpu.make_async_copy(low_place.at[spot], low_ref.at[spot], out_semaphores.at[g, 1]),
        )

    def finished(g, carry):
        for copy in out_copies(g):
            copy.wait()
        return carry

    lax.fori_loop(0, groups, group, 0)
    lax.fori_loop(0, groups, finished, 0)


def backward_kernel(
    pair_at, first_chunk, per_group, turned, meta_ref, docs_ref, bounds_ref, own_ref, other_ref, *refs
):
    apart = len(refs) - 18
    grad_ref, mixed_ref, lse_ref = refs[apart : apart + 3]
    dq_ref, kept_ref, sent_ref, own_place, other_place, kept_place, sent_place = refs[apart + 3 : apart + 10]
    dq_place, keys_ref, rows_ref, keys_t_ref, sum_ref = refs[apart + 10 : apart + 15]
    semaphores, out_semaphores, dq_semaphores = refs[apart + 15 :]
    query_ref = refs[0] if apart else own_place
    groups, _, lanes = docs_ref.shape
    blocks, _, rows = own_place.shape
    remote, places = (own_ref, other_ref), (own_place, other_place)
    core, first_key = meta_ref[0, 3], meta_ref[0, 4]
    start_spans(meta_ref, groups, remote, places, semaphores)
    if apart:
        sum_ref[...] = jnp.zeros(sum_ref.shape, jnp.float32)

    def spread(first, pair_ref):
        pair = pair_ref[pair_at : pair_at + 2 * HEAD, :]
        turned_pair = pair.T
        rows_ref[pl.ds(first, rows), :] = turned_pair
        keys_ref[pl.ds(first, rows), :] = marked_keys(turned_pair, bounds_ref, first_key + first)
        keys_t_ref[:, pl.ds(first, rows)] = pair[:HEAD]
        if not apart:
            sum_ref[pl.ds(first, rows), :] = jnp.zeros((rows, 2 * HEAD), jnp.float32)

    def group(g, carry):
        new_blocks(meta_ref, g, remote, places, semaphores, rows, spread)
        first = first_chunk + g * per_group
        query, query_marked = marked_queries(query_ref, first, per_group, docs_ref[g])
        grad = side_by_side(grad_ref, g * per_group, per_group)
        nothing = jnp.zeros_like(query)
        query_low = jnp.concatenate([query, nothing], axis=0)
        grad_high = jnp.concatenate([nothing, grad], axis=0)
        both = jnp.concatenate([query_low, grad_high], axis=1).T
        delta = jnp.sum(grad.astype(jnp.float32) * mixed_ref[g], axis=0, keepdims=True)
        lse = lse_ref[g]
        query_pos = group_lanes(meta_ref, g, lanes, rows)

        def block(spot, first_pos, last, alone, total):
            cut = slice(0, rows if alone else lanes)
            scores = dot(keys_ref[spot, :], query_marked[:, cut])
            if last:
                scores = causal(scores, first_pos, query_pos)
            probs = jnp.exp(scores - lse[:, cut])
            prob_grad = dot(rows_ref[spot, :], grad_high[:, cut])
            score_grad = (probs * (prob_grad - delta[:, cut])).astype(jnp.bfloat16)
            turned_back = both
            if alone:
                turned_back = jnp.concatenate([both[:rows], both[lanes : lanes + rows]], axis=0)
            sum_ref[spot, :] += dot(
                jnp.concatenate([score_grad, probs.astype(jnp.bfloat16)], axis=1), turned_back
            )
            new = total[:, cut] + dot(keys_t_ref[:, spot], score_grad)
            return jnp.concatenate([new, total[:, rows:]], axis=1) if alone else new

        total = span_walk(
            meta_ref, g, 4 * rows, per_group == 2, block, jnp.zeros((HEAD, lanes), jnp.float32)
        )
        total = (total * SCALING).astype(jnp.bfloat16)
        for k in range(per_group):
            dq_place[g * per_group + k] = total[:, k * rows : (k + 1) * rows]
        dq_copy(g).start()
        return carry

    def dq_copy(g):
        spot = pl.ds(g * per_group, per_group)
        return pltpu.make_async_copy(
            dq_place.at[spot], dq_ref.at[spot, 0:HEAD, :], dq_semaphores.at[g]
        )

    lax.fori_loop(0, groups, group, 0)

    def out_copies(j):
        return [
            pltpu.make_async_copy(place.at[j], ref.at[j], out_semaphores.at[j, i])
            for i, (place, ref) in enumerate(((kept_place, kept_ref), (sent_place, sent_ref)))
        ]

    def finish(j, carry):
        for ref, side in ((kept_place, core), (sent_place, 1 - core)):
            spot = pl.ds(pl.multiple_of((2 * j + side) * rows, rows), rows)
            total = sum_ref[spot, :].astype(ref.dtype)
            ref[j] = total.T if turned else total
        for copy in out_copies(j):
            copy.start()
        return carry

    def finished(j, carry):
        for copy in out_copies(j):
            copy.wait()
        return carry

    def dq_finished(g, carry):
        dq_copy(g).wait()
        return carry

    lax.fori_loop(0, blocks, finish, 0)
    lax.fori_loop(0, groups, dq_finished, 0)
    lax.fori_loop(0, blocks, finished, 0)


def cost(microseconds):
    return pl.CostEstimate(
        flops=microseconds * 1_000_000_000, bytes_accessed=microseconds * 1_000_000, transcendentals=0
    )


SMEM_SPEC = pl.BlockSpec(memory_space=pltpu.SMEM)
VMEM_SPEC = pl.BlockSpec(memory_space=pltpu.VMEM)


ANY_SPEC = pl.BlockSpec(memory_space=pl.ANY)


def attention_forward(plan, own, other, query, name, microseconds):
    meta, docs, bounds, pair_at, first_chunk, per_group = plan
    groups, _, lanes = docs.shape
    blocks, _, rows = own.shape
    keys = blocks * 2 * rows
    return pl.pallas_call(
        functools.partial(forward_kernel, pair_at, first_chunk, per_group),
        out_shape=(
            jax.ShapeDtypeStruct((groups * per_group, HEAD, rows), jnp.bfloat16),
            jax.ShapeDtypeStruct((groups, HEAD, lanes), jnp.float32),
            jax.ShapeDtypeStruct((groups, 1, lanes), jnp.float32),
        ),
        in_specs=[SMEM_SPEC] + [VMEM_SPEC] * 2 + [ANY_SPEC] * 2 + [VMEM_SPEC] * len(query),
        out_specs=(ANY_SPEC, ANY_SPEC, VMEM_SPEC),
        scratch_shapes=[
            *[pltpu.VMEM(own.shape, jnp.bfloat16)] * 2,
            pltpu.VMEM((groups * per_group, HEAD, rows), jnp.bfloat16),
            pltpu.VMEM((groups, HEAD, lanes), jnp.float32),
            pltpu.VMEM((keys, HEAD + DOC_SLOTS), jnp.bfloat16),
            pltpu.VMEM((HEAD, keys), jnp.bfloat16),
            pltpu.SemaphoreType.DMA((blocks // 2, 2)),
            pltpu.SemaphoreType.DMA((groups, 2)),
        ],
        compiler_params=pltpu.CompilerParams(vmem_limit_bytes=VMEM_BYTES),
        cost_estimate=cost(microseconds),
        name=name,
    )(meta, docs, bounds, own, other, *query)


def attention_backward(plan, own, other, query, grad, mixed, lse, turned, name, microseconds):
    meta, docs, bounds, pair_at, first_chunk, per_group = plan
    groups, _, lanes = docs.shape
    blocks, _, rows = own.shape
    keys = blocks * 2 * rows
    part = (blocks, 2 * HEAD, rows) if turned else (blocks, rows, 2 * HEAD)
    return pl.pallas_call(
        functools.partial(backward_kernel, pair_at, first_chunk, per_group, turned),
        out_shape=(
            jax.ShapeDtypeStruct((groups * per_group, (3 if turned else 1) * HEAD, rows), jnp.bfloat16),
            jax.ShapeDtypeStruct(part, jnp.bfloat16),
            jax.ShapeDtypeStruct(part, jnp.bfloat16),
        ),
        in_specs=[SMEM_SPEC] + [VMEM_SPEC] * 2 + [ANY_SPEC] * 2 + [VMEM_SPEC] * (len(query) + 3),
        out_specs=(ANY_SPEC, ANY_SPEC, ANY_SPEC),
        scratch_shapes=[
            *[pltpu.VMEM(own.shape, jnp.bfloat16)] * 2,
            pltpu.VMEM(part, jnp.bfloat16),
            pltpu.VMEM(part, jnp.bfloat16),
            pltpu.VMEM((groups * per_group, HEAD, rows), jnp.bfloat16),
            pltpu.VMEM((keys, HEAD + DOC_SLOTS), jnp.bfloat16),
            pltpu.VMEM((keys, 2 * HEAD), jnp.bfloat16),
            pltpu.VMEM((HEAD, keys), jnp.bfloat16),
            pltpu.VMEM((keys, 2 * HEAD), jnp.float32),
            pltpu.SemaphoreType.DMA((blocks // 2, 2)),
            pltpu.SemaphoreType.DMA((blocks, 2)),
            pltpu.SemaphoreType.DMA((groups,)),
        ],
        compiler_params=pltpu.CompilerParams(vmem_limit_bytes=VMEM_BYTES),
        cost_estimate=cost(microseconds),
        name=name,
    )(meta, docs, bounds, own, other, *query, grad, mixed, lse)


def gelu_parts(value):
    scale = (2.0 / math.pi) ** 0.5
    square = value * value
    bent = jnp.tanh(scale * value * (1.0 + 0.044715 * square))
    upper = 0.5 * (1.0 + bent)
    slope = 0.5 * value * (1.0 - bent * bent) * scale * (1.0 + 3 * 0.044715 * square)
    return value * upper, upper + slope


def column_norm(values, gain, shift):
    row_mean = jnp.mean(values, axis=0, keepdims=True)
    centered = values - row_mean
    variance = jnp.mean(centered * centered, axis=0, keepdims=True)
    inverse = lax.rsqrt(variance + EPSILON)
    normed = centered * inverse
    return (normed * gain + shift, normed, inverse)


def column_norm_back(grad, normed, inverse, gain):
    scaled = grad * gain
    return inverse * (
        scaled
        - jnp.mean(scaled, axis=0, keepdims=True)
        - normed * jnp.mean(scaled * normed, axis=0, keepdims=True)
    )


def fetched(refs, places, semaphores):
    copies = [
        pltpu.make_async_copy(ref, place, semaphores.at[i])
        for i, (ref, place) in enumerate(zip(refs, places))
    ]
    for copy in copies:
        copy.start()
    return copies


def half_rows(core, half):
    return (
        pl.ds(pl.multiple_of(core * half, 32), half),
        pl.ds(pl.multiple_of((1 - core) * half, 32), half),
    )


def ahead_kernel(
    tile, core_ref, mask_ref, cotangent_ref, b_down_ref, *refs
):
    remote, (active_grad_ref, down_grad_ref), refs = refs[:3], refs[3:5], refs[5:]
    down_w_ref, a_down_ref, place_ref, semaphores, out_semaphores = refs
    half, wide = remote[0].shape
    sides = half_rows(core_ref[0], half)
    spots = [slice(k, min(k + tile, wide)) for k in range(0, wide, tile)]
    copies = []
    for k, spot in enumerate(spots):
        pairs = [(remote[i].at[:, spot], down_w_ref.at[sides[i], spot]) for i in range(2)]
        pairs += [(remote[2].at[spot, :], a_down_ref.at[spot, :])]
        for i, (source, place) in enumerate(pairs):
            copies.append(pltpu.make_async_copy(source, place, semaphores.at[k, i]))
    for copy in copies:
        copy.start()
    rows = cotangent_ref[...].T
    down_grad = dot(rows, b_down_ref[...]).astype(jnp.bfloat16) * mask_ref[...].astype(jnp.bfloat16)
    down_grad_ref[...] = down_grad
    given = []
    for k, spot in enumerate(spots):
        for copy in copies[3 * k : 3 * k + 3]:
            copy.wait()
        grad = dot(rows, down_w_ref[:, spot]) + dot(down_grad, a_down_ref[spot, :].T)
        place_ref[:, spot] = grad
        given.append(
            pltpu.make_async_copy(place_ref.at[:, spot], active_grad_ref.at[:, spot], out_semaphores.at[k])
        )
        given[-1].start()
    for copy in given:
        copy.wait()


def ahead_part(core, mask, cotangent_t, b_down_t, down_pair_t, a_down):
    width, rows = cotangent_t.shape
    wide, inner = a_down.shape
    tile = 1024
    count = -(-wide // tile)
    return pl.pallas_call(
        functools.partial(ahead_kernel, tile),
        out_shape=(
            jax.ShapeDtypeStruct((rows, wide), jnp.float32),
            jax.ShapeDtypeStruct((rows, inner), jnp.bfloat16),
        ),
        in_specs=[SMEM_SPEC] + [VMEM_SPEC] * 3 + [ANY_SPEC] * 3,
        out_specs=(ANY_SPEC, VMEM_SPEC),
        scratch_shapes=[
            pltpu.VMEM((width, wide), jnp.bfloat16),
            pltpu.VMEM((wide, inner), jnp.bfloat16),
            pltpu.VMEM((rows, wide), jnp.float32),
            pltpu.SemaphoreType.DMA((count, 3)),
            pltpu.SemaphoreType.DMA((count,)),
        ],
        compiler_params=pltpu.CompilerParams(vmem_limit_bytes=VMEM_BYTES),
        cost_estimate=cost(1),
        name="ahead_part",
    )(core, mask, cotangent_t, b_down_t, *down_pair_t, a_down)


def middle_kernel(
    tile, core_ref, *refs
):
    sources, remote, results, (kept_ref, sent_ref), places, result_places, refs = (
        refs[:11], refs[11:20], refs[20:24], refs[24:26], refs[26:37], refs[37:41], refs[41:],
    )
    (
        mixed_main_ref, mixed_last_ref, mask_ref, a_out_ref, b_out_ref, stream_ref, gains_ref,
        a_up_ref, down_grad_ref, cotangent_ref, b_down_ref,
    ) = places
    output_ref, middle_grad_ref, main_grad_ref, last_grad_ref = result_places
    (
        out_ref, up_ref, b_up_ref, down_w_ref, a_down_ref, kept_place, sent_place,
        active_grad_ref, mixed_ref, middle_ref, hidden_ref, hidden_rows_ref, inner_out_ref,
        inner_up_ref, inner_down_ref, up_grad_ref, down_ref, back_ref,
        semaphores, out_semaphores, place_semaphores, result_semaphores,
    ) = refs
    core = core_ref[0]
    half, wide = remote[2].shape
    width = 2 * half
    full = wide // tile
    low = jnp.bfloat16
    sides = half_rows(core, half)

    def copies(first, size, number):
        spot = pl.ds(first, size)
        pairs = [(remote[2 + i].at[:, spot], up_ref.at[sides[i], spot]) for i in range(2)]
        pairs += [(remote[5 + i].at[:, spot], down_w_ref.at[sides[i], spot]) for i in range(2)]
        pairs += [(remote[4].at[:, spot], b_up_ref.at[:, spot])]
        pairs += [(remote[7].at[spot, :], a_down_ref.at[spot, :])]
        pairs += [(remote[8].at[:, spot], active_grad_ref.at[:, spot])]
        return [
            pltpu.make_async_copy(source, place, semaphores.at[number, i])
            for i, (source, place) in enumerate(pairs)
        ]

    firsts = [
        pltpu.make_async_copy(remote[i], out_ref.at[sides[i], :], semaphores.at[full + 1, i])
        for i in range(2)
    ]
    given = fetched(sources[:4], places[:4], place_semaphores)
    for copy in firsts:
        copy.start()
    later = [
        pltpu.make_async_copy(sources[i], places[i], place_semaphores.at[i]) for i in range(4, 11)
    ]
    for copy in later:
        copy.start()

    def give(i):
        copy = pltpu.make_async_copy(result_places[i], results[i], result_semaphores.at[i])
        copy.start()
        return copy

    def start_chunk(k):
        @pl.when(k < full)
        def _():
            for copy in copies(pl.multiple_of(k * tile, tile), tile, k):
                copy.start()

        if wide % tile:

            @pl.when(k == full)
            def _():
                for copy in copies(full * tile, wide % tile, full):
                    copy.start()

    def out_copies(first, size, number):
        spot = pl.ds(first, size)
        pairs = ((kept_place, kept_ref), (sent_place, sent_ref))
        return [
            pltpu.make_async_copy(place.at[spot, :], ref.at[spot, :], out_semaphores.at[number, i])
            for i, (place, ref) in enumerate(pairs)
        ]

    def put(first, rows, other):
        spot = pl.ds(first, rows.shape[0])

        @pl.when(core == 0)
        def _():
            kept_place[spot, :] = rows
            sent_place[spot, :] = other

        @pl.when(core == 1)
        def _():
            kept_place[spot, :] = other
            sent_place[spot, :] = rows

    for copy in given[:4]:
        copy.wait()
    mask = mask_ref[...]
    mask_low = mask.astype(low)
    main = mixed_main_ref.shape[0] * HEAD
    mixed_ref[:main, :] = mixed_main_ref[...].reshape(main, mixed_main_ref.shape[2])
    mixed_ref[main:, :] = mixed_last_ref[0]
    mixed_rows = mixed_ref[...].T
    inner_out = (mask * (dot(mixed_rows, a_out_ref[...]))).astype(low)
    inner_out_ref[...] = inner_out
    for copy in (*firsts, *later):
        copy.wait()
    start_chunk(0)
    start_chunk(1)
    branch = dot(mixed_rows, out_ref[...]).T + dot(b_out_ref[...], inner_out.T)
    middle = stream_ref[...].astype(jnp.float32) + branch
    middle_ref[...] = middle
    hidden = column_norm(middle, gains_ref[:, 2:3], gains_ref[:, 3:4])[0].astype(low)
    hidden_ref[...] = hidden
    hidden_rows = hidden.T
    hidden_rows_ref[...] = hidden_rows
    inner_up_ref[...] = (mask * dot(hidden_rows, a_up_ref[...])).astype(low)
    for ref in (inner_down_ref, up_grad_ref, down_ref, back_ref):
        ref[...] = jnp.zeros(ref.shape, ref.dtype)

    def step(k, size):
        first = k * tile if isinstance(k, int) else pl.multiple_of(k * tile, tile)
        for copy in copies(first, size, k):
            copy.wait()
        start_chunk(k + 2)
        spot = pl.ds(first, size)
        up, b_up, down_w, a_down = up_ref[:, spot], b_up_ref[:, spot], down_w_ref[:, spot], a_down_ref[spot, :]
        inner_up, down_grad = inner_up_ref[...], down_grad_ref[...]
        upward = dot(hidden_rows_ref[...], up) + dot(inner_up, b_up)
        active, slope = gelu_parts(upward)
        active = active.astype(low)
        up_grad = (active_grad_ref[:, spot] * slope).astype(low)
        active_t, up_grad_t = active.T, up_grad.T
        down_ref[...] += dot(down_w, active_t)
        back_ref[...] += dot(up, up_grad_t)
        inner_down_ref[...] += dot(active, a_down)
        up_grad_ref[...] += dot(b_up, up_grad_t)
        put(first, dot(up_grad_t, inner_up).astype(low), dot(active_t, down_grad).astype(low))
        for copy in out_copies(first, size, k):
            copy.start()

    def loop(k, carry):
        step(k, tile)
        return carry

    lax.fori_loop(0, full, loop, 0)
    if wide % tile:
        step(full, wide % tile)

    inner_down = (mask * inner_down_ref[...]).astype(low)
    middle = middle_ref[...]
    inner_grad = up_grad_ref[...].astype(low).T * mask_low
    hidden_grad = back_ref[...] + dot(a_up_ref[...], inner_grad.T)
    gain = gains_ref[:, 2:3]
    _, normed, inverse = column_norm(middle, gain, gain)
    middle_grad = cotangent_ref[...].astype(jnp.float32)
    middle_grad = middle_grad + column_norm_back(hidden_grad, normed, inverse, gain)
    middle_grad_ref[...] = middle_grad
    given = [give(1)]
    branch = middle_grad.astype(low)
    out_grad = dot(branch.T, b_out_ref[...]).astype(low) * mask_low
    put(wide, dot(cotangent_ref[...], inner_down).astype(low), dot(mixed_ref[...], out_grad).astype(low))
    put(
        wide + width,
        dot(hidden_ref[...], inner_grad).astype(low),
        dot(branch, inner_out_ref[...]).astype(low),
    )
    narrow = kept_place.shape[0] - wide
    spare = narrow - 2 * width
    if spare:
        nothing = jnp.zeros((spare, kept_place.shape[1]), low)
        put(wide + 2 * width, nothing, nothing)
    for copy in out_copies(wide, narrow, full + 1):
        copy.start()
    back = (dot(out_ref[...], branch) + dot(a_out_ref[...], out_grad.T)).astype(low)
    main_grad_ref[...] = back[:main].reshape(main_grad_ref.shape)
    last_grad_ref[0] = back[main:]
    given += [give(2), give(3)]
    down = down_ref[...] + dot(b_down_ref[...], inner_down.T)
    output_ref[...] = (middle + down).astype(low)
    given += [give(0)]

    def finished(k, carry):
        for copy in out_copies(pl.multiple_of(k * tile, tile), tile, k):
            copy.wait()
        return carry

    lax.fori_loop(0, full, finished, 0)
    if wide % tile:
        for copy in out_copies(full * tile, wide % tile, full):
            copy.wait()
    for copy in (*out_copies(wide, narrow, full + 1), *given):
        copy.wait()


def padded(size, unit):
    return -(-size // unit) * unit


def middle_part(
    core, mixed_main, mixed_last, tokens_t, cotangent_t, mask, gains_t, out_pair, a_out, b_out_t,
    a_up, b_down_t, up_pair, b_up, down_pair_t, a_down, active_grad, down_grad, unit,
):
    width, rows = tokens_t.shape
    half = width // 2
    inner, wide = b_up.shape
    tile = 512
    low = jnp.bfloat16
    operands = (
        mixed_main, mixed_last, mask, a_out, b_out_t, tokens_t, gains_t, a_up, down_grad,
        cotangent_t, b_down_t,
    )
    remote = (*out_pair, *up_pair, b_up, *down_pair_t, a_down, active_grad)
    share = (padded(wide + 2 * width, unit), inner)
    shapes = (
        ((width, rows), low), ((width, rows), jnp.float32), (mixed_main.shape, low),
        (mixed_last.shape, low), (share, low), (share, low),
    )
    return pl.pallas_call(
        functools.partial(middle_kernel, tile),
        out_shape=tuple(jax.ShapeDtypeStruct(*item) for item in shapes),
        in_specs=[SMEM_SPEC] + [ANY_SPEC] * (len(operands) + len(remote)),
        out_specs=(ANY_SPEC,) * 6,
        scratch_shapes=[
            *[pltpu.VMEM(item.shape, item.dtype) for item in operands],
            *[pltpu.VMEM(*item) for item in shapes[:4]],
            pltpu.VMEM((width, width), low),
            pltpu.VMEM((width, wide), low),
            pltpu.VMEM((inner, wide), low),
            pltpu.VMEM((width, wide), low),
            pltpu.VMEM((wide, inner), low),
            *[pltpu.VMEM(share, low)] * 2,
            pltpu.VMEM((rows, wide), jnp.float32),
            pltpu.VMEM((width, rows), low),
            pltpu.VMEM((width, rows), jnp.float32),
            pltpu.VMEM((width, rows), low),
            pltpu.VMEM((rows, width), low),
            *[pltpu.VMEM((rows, inner), low)] * 2,
            pltpu.VMEM((rows, inner), jnp.float32),
            pltpu.VMEM((inner, rows), jnp.float32),
            *[pltpu.VMEM((width, rows), jnp.float32)] * 2,
            pltpu.SemaphoreType.DMA((wide // tile + 2, 7)),
            pltpu.SemaphoreType.DMA((wide // tile + 2, 2)),
            pltpu.SemaphoreType.DMA((len(operands),)),
            pltpu.SemaphoreType.DMA((4,)),
        ],
        compiler_params=pltpu.CompilerParams(vmem_limit_bytes=VMEM_BYTES),
        cost_estimate=cost(20),
        name="middle_part",
    )(core, *operands, *remote)


def whole_call(kernel, shapes, scratch, operands, remote, microseconds, name):
    space = [pltpu.VMEM(item.shape, item.dtype) for item in remote]
    return pl.pallas_call(
        kernel,
        out_shape=tuple(jax.ShapeDtypeStruct(*item) for item in shapes),
        in_specs=[SMEM_SPEC]
        + [VMEM_SPEC] * (len(operands) - 1)
        + [pl.BlockSpec(memory_space=pl.ANY)] * len(remote),
        out_specs=(VMEM_SPEC,) * len(shapes),
        scratch_shapes=[pltpu.VMEM(*item) for item in scratch]
        + space
        + ([pltpu.SemaphoreType.DMA((len(remote),))] if remote else []),
        compiler_params=pltpu.CompilerParams(vmem_limit_bytes=VMEM_BYTES if len(remote) > 2 else SMALL_BYTES),
        cost_estimate=cost(microseconds),
        name=name,
    )(*operands, *remote)


def entry_kernel(
    place_ref, lengths_ref, adapters_ref, tokens_ref, gains_own_ref, gains_other_ref, *refs
):
    remote, results, refs = refs[:12], refs[12:19], refs[19:]
    places, (weight_ref, up_ref, down_ref, semaphores, result_semaphores) = refs[:7], refs[7:]
    hidden_ref, inner_ref, mask_ref, gains_ref, heads_ref, query_ref, pairs_ref = places
    rows, inner = mask_ref.shape
    half = gains_own_ref.shape[1]
    sides = half_rows(place_ref[0], half)
    copies = []
    for n in range(3):
        down, own, up, other = remote[4 * n : 4 * n + 4]
        pairs = (
            (down, down_ref.at[n]), (up, up_ref.at[n]),
            (own, weight_ref.at[n, sides[0], :]), (other, weight_ref.at[n, sides[1], :]),
        )
        for i, (source, place) in enumerate(pairs):
            copies.append(pltpu.make_async_copy(source, place, semaphores.at[4 * n + i]))
    for copy in copies:
        copy.start()

    def give(i):
        copy = pltpu.make_async_copy(places[i], results[i], result_semaphores.at[i])
        copy.start()
        return copy

    for spot, ref in zip(sides, (gains_own_ref, gains_other_ref)):
        gains_ref[spot, :] = ref[...].astype(jnp.float32).T
    values = tokens_ref[...].astype(jnp.float32)
    hidden = column_norm(values, gains_ref[:, 0:1], gains_ref[:, 1:2])[0].astype(jnp.bfloat16)
    hidden_ref[...] = hidden
    hidden_rows = hidden.T
    place = place_ref[1] + lax.broadcasted_iota(jnp.int32, (rows, inner), 0)
    column = lax.broadcasted_iota(jnp.int32, (rows, inner), 1) // RANK

    def document(d, state):
        start, mask = state
        end = start + lengths_ref[d]
        chosen = (place >= start) & (place < end) & (column == adapters_ref[d])
        return end, jnp.where(chosen, 1.0, mask)

    state = (jnp.int32(0), jnp.zeros((rows, inner), jnp.float32))
    _, mask = lax.fori_loop(0, lengths_ref.shape[0], document, state)
    mask_ref[...] = mask
    given = [give(0), give(2), give(3)]
    count = heads_ref.shape[0]

    def give_part(n):
        spot = pl.ds(n * HEAD, HEAD)
        copy = pltpu.make_async_copy(
            heads_ref.at[:, spot, :], results[4].at[:, spot, :], result_semaphores.at[7 + n]
        )
        copy.start()
        return copy

    for n in range(3):
        for copy in copies[4 * n : 4 * n + 4]:
            copy.wait()
        products = (mask * dot(hidden_rows, down_ref[n])).astype(jnp.bfloat16)
        inner_ref[n] = products
        total = dot(hidden_rows, weight_ref[n]).T + dot(up_ref[n], products.T)
        total = total.astype(jnp.bfloat16)
        for c in range(count):
            heads_ref[c, n * HEAD : (n + 1) * HEAD, :] = total[c * HEAD : (c + 1) * HEAD]
        if n == 0:
            query_ref[0] = total[count * HEAD :]
        else:
            for c in range(count):
                pairs_ref[c, (n - 1) * HEAD : n * HEAD, :] = total[count * HEAD :]
        given.append(give_part(n))
    for copy in (*given, *[give(i) for i in (1, 5, 6)]):
        copy.wait()


def projections(place, lengths, adapters, tokens_t, gains, gains_other, weights, others, downs, ups_t):
    width, rows = tokens_t.shape
    inner = downs[0].shape[1]
    low = jnp.bfloat16
    count = width // HEAD - 1
    remote = [item for group in zip(downs, weights, ups_t, others) for item in group]
    shapes = (
        ((width, rows), low), ((3, rows, inner), low), ((rows, inner), jnp.float32),
        ((width, gains.shape[0]), jnp.float32), ((count, 3 * HEAD, rows), low),
        ((1, HEAD, rows), low), ((count, 2 * HEAD, rows), low),
    )
    return pl.pallas_call(
        entry_kernel,
        out_shape=tuple(jax.ShapeDtypeStruct(*item) for item in shapes),
        in_specs=[SMEM_SPEC] * 3 + [VMEM_SPEC] * 3 + [ANY_SPEC] * len(remote),
        out_specs=(ANY_SPEC,) * len(shapes),
        scratch_shapes=[pltpu.VMEM(*item) for item in shapes]
        + [
            pltpu.VMEM((3, width, width), low),
            pltpu.VMEM((3, width, inner), low),
            pltpu.VMEM((3, width, inner), low),
            pltpu.SemaphoreType.DMA((12,)),
            pltpu.SemaphoreType.DMA((len(shapes) + 3,)),
        ],
        compiler_params=pltpu.CompilerParams(vmem_limit_bytes=VMEM_BYTES),
        cost_estimate=cost(6),
        name="entry",
    )(place, lengths, adapters, tokens_t, gains, gains_other, *remote)


def gathered_grad(n, heads_ref, last_query_ref, last_pair_ref, grad_ref):
    count = heads_ref.shape[0]
    for c in range(count):
        grad_ref[c * HEAD : (c + 1) * HEAD, :] = heads_ref[c, n * HEAD : (n + 1) * HEAD, :]
    if n == 0:
        grad_ref[count * HEAD :, :] = last_query_ref[0]
    else:
        grad_ref[count * HEAD :, :] = last_pair_ref[...].T[(n - 1) * HEAD : n * HEAD]
    return grad_ref[...]


def projections_late_kernel(core_ref, *refs):
    sources, (kept_ref, sent_ref, inner_grad_ref), refs = refs[:9], refs[9:12], refs[12:]
    places, (kept_place, sent_place, grad_ref, semaphores, out_semaphores) = refs[:9], refs[9:]
    heads_ref, last_query_ref, last_pair_ref, mask_ref, hidden_ref, inner_ref, *ups = places
    copies = fetched(sources, places, semaphores)
    core = core_ref[0]
    low = jnp.bfloat16
    width, share = hidden_ref.shape[0], kept_place.shape[0]

    def store(side, spot, rows):
        @pl.when(core == side)
        def _():
            kept_place[spot, :] = rows

        @pl.when(core != side)
        def _():
            sent_place[spot, :] = rows

    def keep(first, rows):
        done = 0
        while done < rows.shape[0]:
            side, spot = divmod(first + done, share)
            size = min(rows.shape[0] - done, share - spot)
            store(side, slice(spot, spot + size), rows[done : done + size])
            done += size

    keep(6 * width, jnp.zeros((2 * share - 6 * width, kept_place.shape[1]), low))
    turned = []
    for copy, up in zip(copies[6:], ups):
        copy.wait()
        turned.append(up[...].T)
    for copy in copies[:6]:
        copy.wait()
    mask_low = mask_ref[...].astype(low)
    hidden = hidden_ref[...]
    for n in range(3):
        grad = gathered_grad(n, heads_ref, last_query_ref, last_pair_ref, grad_ref)
        inner_grad = dot(turned[n], grad).astype(low).T * mask_low
        inner_grad_ref[n] = inner_grad
        keep(2 * n * width, dot(hidden, inner_grad).astype(low))
        keep((2 * n + 1) * width, dot(grad, inner_ref[n]).astype(low))
    given = fetched((kept_place, sent_place), (kept_ref, sent_ref), out_semaphores)
    for copy in given:
        copy.wait()


def projections_late(core, heads, last_query, last_pair, hidden_t, inners, mask, ups_t, unit):
    width, rows = hidden_t.shape
    low = jnp.bfloat16
    share = (padded(6 * width, 2 * unit) // 2, mask.shape[1])
    operands = (heads, last_query, last_pair, mask, hidden_t, inners, *ups_t)
    return pl.pallas_call(
        projections_late_kernel,
        out_shape=(
            jax.ShapeDtypeStruct(share, low),
            jax.ShapeDtypeStruct(share, low),
            jax.ShapeDtypeStruct(inners.shape, low),
        ),
        in_specs=[SMEM_SPEC] + [ANY_SPEC] * len(operands),
        out_specs=(ANY_SPEC, ANY_SPEC, VMEM_SPEC),
        scratch_shapes=[pltpu.VMEM(item.shape, item.dtype) for item in operands]
        + [
            pltpu.VMEM(share, low),
            pltpu.VMEM(share, low),
            pltpu.VMEM((width, rows), low),
            pltpu.SemaphoreType.DMA((len(operands),)),
            pltpu.SemaphoreType.DMA((2,)),
        ],
        compiler_params=pltpu.CompilerParams(vmem_limit_bytes=VMEM_BYTES),
        cost_estimate=cost(5),
        name="projections_late",
    )(core, *operands)


def projections_back_kernel(
    core_ref, heads_ref, last_query_ref, last_pair_ref, inner_grad_ref, gains_ref, tokens_ref, *refs
):
    remote, (grad_in_ref, grad_ref, sum_ref), local_refs, semaphores = (
        refs[:10], refs[10:13], refs[13:23], refs[23],
    )
    copies = fetched(remote, local_refs, semaphores)
    downs, weights, others, middle_grad_ref = (
        local_refs[:3], local_refs[3:6], local_refs[6:9], local_refs[9],
    )
    own_rows, other_rows = half_rows(core_ref[0], weights[0].shape[0])
    for n in range(3):
        grad = gathered_grad(n, heads_ref, last_query_ref, last_pair_ref, grad_ref)
        turned = inner_grad_ref[n].T
        copies[n].wait()
        for rows, weight, copy in (
            (own_rows, weights[n], copies[3 + n]), (other_rows, others[n], copies[6 + n])
        ):
            copy.wait()
            part = dot(weight[...], grad) + dot(downs[n][rows, :], turned)
            sum_ref[rows, :] = part if n == 0 else sum_ref[rows, :] + part
    gain = gains_ref[:, 0:1]
    _, normed, inverse = column_norm(tokens_ref[...].astype(jnp.float32), gain, gain)
    back = column_norm_back(sum_ref[...], normed, inverse, gain)
    copies[9].wait()
    grad_in_ref[...] = (middle_grad_ref[...] + back).astype(jnp.bfloat16)


def projections_back(
    core, heads, last_query, last_pair, inner_grads, gains_t, tokens_t, middle_grad_t,
    weights, others, downs,
):
    width, rows = tokens_t.shape
    low = jnp.bfloat16
    return whole_call(
        projections_back_kernel,
        (((width, rows), low),),
        (((width, rows), low), ((width, rows), jnp.float32)),
        (core, heads, last_query, last_pair, inner_grads, gains_t, tokens_t),
        (*downs, *weights, *others, middle_grad_t),
        8, "projections_back",
    )[0]


def steps_of(cycle_size):
    bits = cycle_size.bit_length() - 1
    return [(bit, min(2, bits - bit)) for bit in range(0, bits, 2)]


def partners(cycle_size, step, k):
    return [(i, i ^ (k << step[0])) for i in range(cycle_size)]


def scattered(array, step, cycle_size):
    count = 1 << step[1]
    mine = (lax.axis_index("ctx") >> step[0]) & (count - 1)
    blocks = array.reshape(count, array.shape[0] // count, array.shape[1])

    def block(number):
        return lax.dynamic_index_in_dim(blocks, number, 0, keepdims=False)

    total = block(mine).astype(jnp.float32)
    for k in range(1, count):
        got = lax.ppermute(block(mine ^ k), "ctx", partners(cycle_size, step, k))
        total = total + got.astype(jnp.float32)
    return total.astype(array.dtype)


def collected(share, step, cycle_size):
    count = 1 << step[1]
    mine = (lax.axis_index("ctx") >> step[0]) & (count - 1)
    blocks = [share]
    for k in range(1, count):
        blocks.append(lax.ppermute(share, "ctx", partners(cycle_size, step, k)))
    for bit in range(step[1]):
        turned = ((mine >> bit) & 1) == 1
        blocks = [jnp.where(turned, blocks[k ^ (1 << bit)], blocks[k]) for k in range(count)]
    return jnp.concatenate(blocks, axis=0)


def pair_sum(kept, sent):
    return kept + lax.ppermute(sent, "wsh", SWAP)


def early_finish_kernel(
    factor, core_ref, own_source, other_source,
    b_up_ref, a_down_ref, b_down_ref, a_up_ref, a_out_ref, b_out_ref, own_ref, other_ref, semaphores,
):
    for copy in fetched((own_source, other_source), (own_ref, other_ref), semaphores):
        copy.wait()
    wide, width = a_down_ref.shape[0], a_up_ref.shape[0]

    def finish(first_ref, second_ref):
        def part(ref, first, count):
            return ref[first : first + count, :].astype(jnp.float32) * factor

        for k in range(wide // 256):
            b_up_ref[:, k * 256 : (k + 1) * 256] = part(first_ref, k * 256, 256).T
        a_down_ref[...] = part(second_ref, 0, wide)
        b_down_ref[...] = part(first_ref, wide, width)
        a_up_ref[...] = part(first_ref, wide + width, width)
        a_out_ref[...] = part(second_ref, wide, width)
        b_out_ref[...] = part(second_ref, wide + width, width)

    @pl.when(core_ref[0] == 0)
    def _():
        finish(own_ref, other_ref)

    @pl.when(core_ref[0] == 1)
    def _():
        finish(other_ref, own_ref)


def late_finish_kernel(factor, core_ref, own_ref, other_ref, *refs):
    core = core_ref[0]
    targets, late_ref, own_place, other_place, semaphores = refs[:6], *refs[6:]
    places = (own_place, other_place)
    copies = fetched((own_ref, other_ref), places, semaphores)
    for side, ref, copy in zip((core, 1 - core), places, copies):
        copy.wait()
        late_ref[side] = ref[...].astype(jnp.float32) * factor
    width, share = targets[0].shape[0], late_ref.shape[1]
    for n, ref in enumerate(targets):
        done = 0
        while done < width:
            side, spot = divmod(n * width + done, share)
            rows = min(width - done, share - spot)
            ref[done : done + rows, :] = late_ref[side, spot : spot + rows, :]
            done += rows


def finished(kernel, factor, core, own, other, shapes, scratch, name):
    return whole_call(
        functools.partial(kernel, factor), [(shape, jnp.float32) for shape in shapes], scratch,
        (core,), (own, other), 1, name,
    )


def local(
    tokens_in,
    doc_lengths,
    doc_adapter,
    norm1_gain,
    norm1_bias,
    norm2_gain,
    norm2_bias,
    w_query,
    w_key,
    w_value,
    w_out,
    w_up,
    w_down,
    a_query,
    b_query,
    a_key,
    b_key,
    a_value,
    b_value,
    a_out,
    b_out,
    a_up,
    b_up,
    a_down,
    b_down,
    cotangent,
):
    group_size = lax.axis_size("wsh")
    cycle_size = lax.axis_size("ctx")
    tok_dev, width_all = tokens_in.shape
    head_count = width_all // HEAD
    block_len = tok_dev * group_size
    hop_count = (DOC_MAX + block_len - 2) // block_len
    span = head_count - 1
    cycle_pos = lax.axis_index("ctx")
    core = lax.axis_index("wsh")
    half = width_all // group_size

    first_row = cycle_pos * block_len + core * tok_dev
    doc_ends = jnp.cumsum(doc_lengths)
    doc_starts = doc_ends - doc_lengths

    team = cycle_pos // span
    past = hop_count if cycle_size > span else 0
    first_key = (team * span - past) * block_len
    key_blocks = past + span

    slots = DOC_SLOTS - doc_lengths.shape[0]
    bounds = jnp.stack([jnp.pad(doc_starts, (0, slots)), jnp.pad(doc_ends, (0, slots))])

    def plan(chunk_pos, pair_at, first_chunk, per_group):
        groups = chunk_pos.shape[0] // per_group
        row_pos = chunk_pos[:, None] + jnp.arange(tok_dev, dtype=jnp.int32)[None, :]
        row_docs = jnp.sum((doc_ends[None, None, :] <= row_pos[:, :, None]).astype(jnp.int32), axis=2)
        row_docs = row_docs.reshape(groups, 1, per_group * tok_dev)
        chunk_pos = chunk_pos.reshape(groups, per_group)
        began = jnp.where(doc_starts[None, None, :] <= chunk_pos[:, :, None], doc_starts[None, None, :], 0)
        began = (jnp.max(began, axis=2) - first_key) // (2 * block_len)
        first = began[:, 0]
        last = (chunk_pos[:, -1] - first_key) // (2 * block_len)
        same = jnp.ones((groups,), jnp.int32)
        whole = per_group > 1
        meta = [
            first,
            last,
            chunk_pos[:, 0],
            same * core,
            same * first_key,
            jnp.concatenate([first[:1] * 0, last[:-1] + 1]) if whole else first,
            began[:, -1],
        ]
        meta = jnp.stack(meta, axis=1).astype(jnp.int32)
        docs = row_docs.astype(jnp.int32)
        return meta, docs, bounds.astype(jnp.int32), pair_at, first_chunk, per_group

    team_pos = (team * span + jnp.arange(span, dtype=jnp.int32)) * block_len + core * tok_dev
    main_plan = plan(team_pos.astype(jnp.int32), HEAD, past, 2)
    last_plan = plan(first_row[None].astype(jnp.int32), 0, 0, 1)

    def swap(array):
        return lax.ppermute(array, "wsh", SWAP)

    if cycle_size > span:
        teams = [[t * span + i for i in range(span)] for t in range(cycle_size // span)]
    else:
        teams = None

    def exchange(blocks):
        return lax.all_to_all(blocks, "ctx", 0, 0, tiled=True, axis_index_groups=teams)

    gains = jnp.stack([norm1_gain, norm1_bias, norm2_gain, norm2_bias])
    weights = [w_query, w_key, w_value, w_out, w_up, w_down.T]
    others = [swap(item) for item in weights[:3]]
    gains_other = swap(gains)
    *others, gains_other, w_late = lax.optimization_barrier((*others, gains_other, tuple(weights[3:])))
    others = others + [swap(item) for item in w_late]

    downs = (a_query, a_key, a_value)
    ups_t = (b_query.T, b_key.T, b_value.T)
    tokens_t = tokens_in.T
    core_1 = jnp.stack([core, first_row]).astype(jnp.int32)
    hidden_t, inners, adapter_mask, gains_t, heads, last_query, last_pairs = projections(
        core_1, doc_lengths, doc_adapter, tokens_t, gains, gains_other, weights[:3], others[:3],
        downs, ups_t,
    )

    ahead = [(i, i + span) for i in range(cycle_size - span)]
    back = [(i + span, i) for i in range(cycle_size - span)]

    def with_past(blocks):
        if not past:
            return blocks
        return jnp.concatenate([lax.ppermute(blocks[span - past :], "ctx", ahead), blocks], axis=0)

    steps = steps_of(cycle_size)
    unit = 16 * cycle_size
    incoming = exchange(heads)
    active_grad, down_grad = ahead_part(
        core_1, adapter_mask, cotangent.T, b_down.T, (w_down.T, others[5]), a_down
    )
    incoming, last_pairs, active_grad, ready = lax.optimization_barrier(
        (incoming, last_pairs, active_grad, main_plan[:3])
    )
    main_plan = (*ready, *main_plan[3:])
    own = with_past(incoming)
    other = swap(own)
    last_own = exchange(last_pairs)
    low_main, total_main, lse_main = attention_forward(
        main_plan, own, other, (), "attention_forward", 30
    )
    low_main, last_own = lax.optimization_barrier((low_main, last_own))
    last_own = with_past(last_own)
    last_other = swap(last_own)
    low_last, mixed_last, lse_last = attention_forward(
        last_plan, last_own, last_other, (last_query,), "last_forward", 0
    )
    mixed_main = exchange(low_main)

    output_t, middle_grad_t, main_grad, last_out_grad, early_kept, early_sent = middle_part(
        core_1, mixed_main, low_last, tokens_t, cotangent.T, adapter_mask, gains_t,
        (w_out, others[3]), a_out, b_out.T, a_up, b_down.T, (w_up, others[4]), b_up,
        (w_down.T, others[5]), a_down, active_grad, down_grad, unit,
    )

    def pair_total(kept, sent):
        total = kept.astype(jnp.float32) + swap(sent).astype(jnp.float32)
        if past:
            returned = lax.ppermute(total[:past].astype(jnp.bfloat16), "ctx", back)
            total = total[past:].at[span - past :].add(returned.astype(jnp.float32))
        return total

    def pair_back(dq, kept, sent):
        total = pair_total(kept, sent).astype(jnp.bfloat16)
        return lax.dynamic_update_slice(dq, total, (0, HEAD, 0))

    dq_last, kept_last, sent_last = attention_backward(
        last_plan, last_own, last_other, (last_query,),
        last_out_grad, mixed_last, lse_last, False, "last_backward", 0,
    )
    grad_main = exchange(main_grad)
    grad_main, dq_last, kept_last, sent_last = lax.optimization_barrier(
        (grad_main, dq_last, kept_last, sent_last)
    )
    dpair_last = pair_total(kept_last, sent_last).astype(jnp.bfloat16)
    plane = 1 << steps[0][1]
    lines = cycle_size // plane
    digits = (2,) * (cycle_size.bit_length() - 3) + (plane,)
    if cycle_size > span:
        zero = jnp.zeros((cycle_size // span, *dpair_last.shape), dpair_last.dtype)
        dpair_last = lax.dynamic_update_index_in_dim(zero, dpair_last, team, 0)
    order = tuple(reversed(range(len(digits)))) + (len(digits), len(digits) + 1)
    dpair_last = jnp.transpose(dpair_last.reshape(digits + dpair_last.shape[-2:]), order)
    early = pair_sum(early_kept, early_sent)
    lanes = early.shape[1]
    early_rows, last_rows = early.shape[0] // cycle_size, tok_dev
    early = early.reshape(plane, lines, early_rows, lanes)
    dpair_last = dpair_last.reshape(plane, lines, last_rows, lanes)

    def meant_for(k):
        parts = [lax.dynamic_index_in_dim(x, (cycle_pos % plane) ^ k, 0, False) for x in (early, dpair_last)]
        return jnp.concatenate(parts, axis=1)

    meant = [meant_for(k) for k in range(plane)]
    grad_main, *meant = lax.optimization_barrier((grad_main, *meant))
    shared = [meant[0]] + [
        lax.ppermute(meant[k], "ctx", partners(cycle_size, steps[0], k)) for k in range(1, plane)
    ]
    dq_main, kept_main, sent_main = attention_backward(
        main_plan, own, other, (), grad_main, total_main, lse_main,
        True, "attention_backward", 40
    )
    dq_main, kept_main, sent_main, *shared = lax.optimization_barrier(
        (dq_main, kept_main, sent_main, *shared)
    )
    shared = sum(part.astype(jnp.float32) for part in shared).astype(jnp.bfloat16)
    shared = shared.reshape(lines * (early_rows + last_rows), lanes)
    outgoing_back = pair_back(dq_main, kept_main, sent_main)
    outgoing_back, shared = lax.optimization_barrier((outgoing_back, shared))
    singles = [(bit, 1) for bit in range(2, cycle_size.bit_length() - 1)]
    shared = shared.reshape(lines, early_rows + last_rows, lanes)
    early = shared[:, :early_rows].reshape(lines * early_rows, lanes)
    last_sum = shared[:, early_rows:].reshape(lines * last_rows, lanes)
    incoming_back = exchange(outgoing_back)
    for step in singles:
        last_sum = scattered(last_sum, step, cycle_size)
    for step in singles:
        early = scattered(early, step, cycle_size)

    late_kept, late_sent, inner_grads = projections_late(
        core_1, incoming_back, dq_last, last_sum, hidden_t, inners, adapter_mask, ups_t, unit
    )
    singles = singles[::-1]
    late, early, inner_grads = lax.optimization_barrier(
        (pair_sum(late_kept, late_sent), early, inner_grads)
    )
    grad_in_t = projections_back(
        core_1, incoming_back, dq_last, last_sum, inner_grads, gains_t, tokens_t, middle_grad_t,
        weights[:3], others[:3], downs,
    )

    norm_factor = (tok_dev * group_size * cycle_size) ** (-0.5)
    late = scattered(late, steps[0], cycle_size)
    for step in singles:
        early = collected(early, step, cycle_size)
    late, early = lax.optimization_barrier((late, early))
    for step in steps[1:]:
        late = scattered(late, step, cycle_size)
    early = collected(early, steps[0], cycle_size)
    late, early, grad_in_t = lax.optimization_barrier((late, early, grad_in_t))
    early_other = swap(early)
    for step in reversed(steps[1:]):
        late = collected(late, step, cycle_size)
    late, early_other = lax.optimization_barrier((late, early_other))
    late = collected(late, steps[0], cycle_size)
    wide = b_up.shape[1]
    early = finished(
        early_finish_kernel, norm_factor, core_1, early, early_other,
        [(lanes, wide), (wide, lanes)] + [(width_all, lanes)] * 4, (), "early_finish",
    )
    late, early = lax.optimization_barrier((late, early))
    g_b_up, g_a_down, g_b_down, g_a_up, g_a_out, g_b_out = early
    late = finished(
        late_finish_kernel, norm_factor, core_1, late, swap(late), [(width_all, lanes)] * 6,
        (((2, *late.shape), jnp.float32),), "late_finish",
    )
    return (
        output_t.T,
        grad_in_t.T,
        late[0],
        late[1].T,
        late[2],
        late[3].T,
        late[4],
        late[5].T,
        g_a_out,
        g_b_out.T,
        g_a_up,
        g_b_up,
        g_a_down,
        g_b_down.T,
    )


def solution(mesh):
    return jax.shard_map(
        local,
        mesh=mesh,
        in_specs=(
            P(("ctx", "wsh"), None),
            P(),
            P(),
            P("wsh"),
            P("wsh"),
            P("wsh"),
            P("wsh"),
            P("wsh", None),
            P("wsh", None),
            P("wsh", None),
            P("wsh", None),
            P("wsh", None),
            P(None, "wsh"),
            P(),
            P(),
            P(),
            P(),
            P(),
            P(),
            P(),
            P(),
            P(),
            P(),
            P(),
            P(),
            P(("ctx", "wsh"), None),
        ),
        out_specs=(
            P(("ctx", "wsh"), None),
            P(("ctx", "wsh"), None),
            P(),
            P(),
            P(),
            P(),
            P(),
            P(),
            P(),
            P(),
            P(),
            P(),
            P(),
            P(),
        ),
        check_vma=False,
    )
```

```python
import functools
import math

import jax
import jax.numpy as jnp
from jax import lax
from jax.experimental import pallas as pl
from jax.experimental.pallas import tpu as pltpu
from jax.sharding import PartitionSpec as P

HEAD = 64
RANK = 16
DOC_MAX = 4096


EPSILON = 1e-05
NEG_FILL = -1e30
SCALING = HEAD ** (-0.5)
SWAP = [(0, 1), (1, 0)]
VMEM_BYTES = 60 * 1024 * 1024
SMALL_BYTES = 24 * 1024 * 1024


def norm_parts(values, gain, shift):
    row_mean = jnp.mean(values, axis=-1, keepdims=True)
    centered = values - row_mean
    variance = jnp.mean(centered * centered, axis=-1, keepdims=True)
    inverse = lax.rsqrt(variance + EPSILON)
    normed = centered * inverse
    return (normed * gain + shift, normed, inverse)


def norm_back(grad, normed, inverse, gain):
    scaled = grad * gain
    return inverse * (
        scaled
        - jnp.mean(scaled, axis=-1, keepdims=True)
        - normed * jnp.mean(scaled * normed, axis=-1, keepdims=True)
    )


def dot(left, right, lc=1, rc=0):
    return lax.dot_general(
        left, right, (((lc,), (rc,)), ((), ())), preferred_element_type=jnp.float32
    )


DOC_SLOTS = 64


def side_by_side(ref, first, count):
    return jnp.concatenate([ref[first + k, 0:HEAD, :] for k in range(count)], axis=1)


def marked_queries(query_ref, first, count, docs):
    query = side_by_side(query_ref, first, count)
    query = (query.astype(jnp.float32) * SCALING).astype(jnp.bfloat16)
    number = lax.broadcasted_iota(jnp.int32, (DOC_SLOTS, docs.shape[1]), 0)
    marks = jnp.where(number == docs, 0.0, NEG_FILL).astype(jnp.bfloat16)
    return query, jnp.concatenate([query, marks], axis=0)


def marked_keys(pair, bounds_ref, first_pos):
    rows = pair.shape[0]
    place = first_pos + lax.broadcasted_iota(jnp.int32, (rows, DOC_SLOTS), 0)
    marks = (place >= bounds_ref[0:1, :]) & (place < bounds_ref[1:2, :])
    marks = jnp.where(marks, 1.0, 0.0).astype(jnp.bfloat16)
    return jnp.concatenate([pair[:, :HEAD], marks], axis=1)


def causal(scores, first_pos, query_pos):
    row = lax.broadcasted_iota(jnp.int32, scores.shape, 0)
    return jnp.where(row <= query_pos - first_pos, scores, NEG_FILL)


def group_lanes(meta_ref, g, lanes, rows):
    lane = lax.broadcasted_iota(jnp.int32, (1, lanes), 1)
    return meta_ref[g, 2] + lane + jnp.where(lane >= rows, rows, 0)


def span_walk(meta_ref, g, size, two, block, state):
    def spot(t):
        first = pl.multiple_of(t * size, size)
        return pl.ds(first, size), meta_ref[0, 4] + first

    def walk(first, end, alone, state):
        return lax.fori_loop(first, end, lambda t, state: block(*spot(t), False, alone, state), state)

    if two:
        state = walk(meta_ref[g, 0], meta_ref[g, 6], True, state)
    state = walk(meta_ref[g, 6], meta_ref[g, 1], False, state)
    return block(*spot(meta_ref[g, 1]), True, False, state)


def span_copies(remote, places, semaphores, t):
    spot = pl.ds(2 * t, 2)
    return [
        pltpu.make_async_copy(source.at[spot], place.at[spot], semaphores.at[t, i])
        for i, (source, place) in enumerate(zip(remote, places))
    ]


def start_spans(meta_ref, groups, remote, places, semaphores):
    def start(t, carry):
        for copy in span_copies(remote, places, semaphores, t):
            copy.start()
        return carry

    lax.fori_loop(meta_ref[0, 5], meta_ref[groups - 1, 1] + 1, start, 0)


def new_blocks(meta_ref, g, remote, places, semaphores, rows, use):
    core = meta_ref[0, 3]

    def span(t, carry):
        for copy in span_copies(remote, places, semaphores, t):
            copy.wait()
        for k in range(2):
            for place, side in zip(places, (core, 1 - core)):
                use(pl.multiple_of(((2 * t + k) * 2 + side) * rows, rows), place.at[2 * t + k])
        return carry

    lax.fori_loop(meta_ref[g, 5], meta_ref[g, 1] + 1, span, 0)


def forward_kernel(
    pair_at, first_chunk, per_group, meta_ref, docs_ref, bounds_ref, own_ref, other_ref, *refs
):
    apart = len(refs) - 11
    query_ref, (low_ref, mixed_ref, lse_ref, own_place, other_place) = refs[0], refs[apart : apart + 5]
    low_place, mixed_place, keys_ref, values_ref, semaphores, out_semaphores = refs[apart + 5 :]
    query_ref = query_ref if apart else own_place
    groups, _, lanes = docs_ref.shape
    rows = own_place.shape[2]
    remote, places = (own_ref, other_ref), (own_place, other_place)
    first_key = meta_ref[0, 4]
    start_spans(meta_ref, groups, remote, places, semaphores)

    def spread(first, pair_ref):
        pair = pair_ref[pair_at : pair_at + 2 * HEAD, :]
        keys_ref[pl.ds(first, rows), :] = marked_keys(pair.T, bounds_ref, first_key + first)
        values_ref[:, pl.ds(first, rows)] = pair[HEAD:]

    def group(g, carry):
        new_blocks(meta_ref, g, remote, places, semaphores, rows, spread)
        _, query = marked_queries(query_ref, first_chunk + g * per_group, per_group, docs_ref[g])
        query_pos = group_lanes(meta_ref, g, lanes, rows)

        def block(spot, first_pos, last, alone, state):
            cut = slice(0, rows if alone else lanes)
            row_max, row_sum, total = (part[:, cut] for part in state)
            scores = dot(keys_ref[spot, :], query[:, cut])
            if last:
                scores = causal(scores, first_pos, query_pos)
            new_max = jnp.maximum(row_max, jnp.max(scores, axis=0, keepdims=True))
            probs = jnp.exp(scores - new_max)
            shrink = jnp.exp(row_max - new_max)
            row_sum = row_sum * shrink + jnp.sum(probs, axis=0, keepdims=True)
            total = total * shrink + dot(values_ref[:, spot], probs.astype(jnp.bfloat16))
            new = (new_max, row_sum, total)
            if alone:
                new = tuple(jnp.concatenate([x, y[:, rows:]], axis=1) for x, y in zip(new, state))
            return new

        state = (
            jnp.full((1, lanes), NEG_FILL, jnp.float32),
            jnp.zeros((1, lanes), jnp.float32),
            jnp.zeros((HEAD, lanes), jnp.float32),
        )
        row_max, row_sum, total = span_walk(meta_ref, g, 4 * rows, per_group == 2, block, state)
        mixed = total / row_sum
        mixed_place[g] = mixed
        for k in range(per_group):
            low_place[g * per_group + k] = mixed[:, k * rows : (k + 1) * rows].astype(jnp.bfloat16)
        lse_ref[g] = row_max + jnp.log(row_sum)
        for copy in out_copies(g):
            copy.start()
        return carry

    def out_copies(g):
        spot = pl.ds(g * per_group, per_group)
        return (
            pltpu.make_async_copy(mixed_place.at[g], mixed_ref.at[g], out_semaphores.at[g, 0]),
            pltpu.make_async_copy(low_place.at[spot], low_ref.at[spot], out_semaphores.at[g, 1]),
        )

    def finished(g, carry):
        for copy in out_copies(g):
            copy.wait()
        return carry

    lax.fori_loop(0, groups, group, 0)
    lax.fori_loop(0, groups, finished, 0)


def backward_kernel(
    pair_at, first_chunk, per_group, turned, meta_ref, docs_ref, bounds_ref, own_ref, other_ref, *refs
):
    apart = len(refs) - 18
    grad_ref, mixed_ref, lse_ref = refs[apart : apart + 3]
    dq_ref, kept_ref, sent_ref, own_place, other_place, kept_place, sent_place = refs[apart + 3 : apart + 10]
    dq_place, keys_ref, rows_ref, keys_t_ref, sum_ref = refs[apart + 10 : apart + 15]
    semaphores, out_semaphores, dq_semaphores = refs[apart + 15 :]
    query_ref = refs[0] if apart else own_place
    groups, _, lanes = docs_ref.shape
    blocks, _, rows = own_place.shape
    remote, places = (own_ref, other_ref), (own_place, other_place)
    core, first_key = meta_ref[0, 3], meta_ref[0, 4]
    start_spans(meta_ref, groups, remote, places, semaphores)
    if apart:
        sum_ref[...] = jnp.zeros(sum_ref.shape, jnp.float32)

    def spread(first, pair_ref):
        pair = pair_ref[pair_at : pair_at + 2 * HEAD, :]
        turned_pair = pair.T
        rows_ref[pl.ds(first, rows), :] = turned_pair
        keys_ref[pl.ds(first, rows), :] = marked_keys(turned_pair, bounds_ref, first_key + first)
        keys_t_ref[:, pl.ds(first, rows)] = pair[:HEAD]
        if not apart:
            sum_ref[pl.ds(first, rows), :] = jnp.zeros((rows, 2 * HEAD), jnp.float32)

    def group(g, carry):
        new_blocks(meta_ref, g, remote, places, semaphores, rows, spread)
        first = first_chunk + g * per_group
        query, query_marked = marked_queries(query_ref, first, per_group, docs_ref[g])
        grad = side_by_side(grad_ref, g * per_group, per_group)
        nothing = jnp.zeros_like(query)
        query_low = jnp.concatenate([query, nothing], axis=0)
        grad_high = jnp.concatenate([nothing, grad], axis=0)
        both = jnp.concatenate([query_low, grad_high], axis=1).T
        delta = jnp.sum(grad.astype(jnp.float32) * mixed_ref[g], axis=0, keepdims=True)
        lse = lse_ref[g]
        query_pos = group_lanes(meta_ref, g, lanes, rows)

        def block(spot, first_pos, last, alone, total):
            cut = slice(0, rows if alone else lanes)
            scores = dot(keys_ref[spot, :], query_marked[:, cut])
            if last:
                scores = causal(scores, first_pos, query_pos)
            probs = jnp.exp(scores - lse[:, cut])
            prob_grad = dot(rows_ref[spot, :], grad_high[:, cut])
            score_grad = (probs * (prob_grad - delta[:, cut])).astype(jnp.bfloat16)
            turned_back = both
            if alone:
                turned_back = jnp.concatenate([both[:rows], both[lanes : lanes + rows]], axis=0)
            sum_ref[spot, :] += dot(
                jnp.concatenate([score_grad, probs.astype(jnp.bfloat16)], axis=1), turned_back
            )
            new = total[:, cut] + dot(keys_t_ref[:, spot], score_grad)
            return jnp.concatenate([new, total[:, rows:]], axis=1) if alone else new

        total = span_walk(
            meta_ref, g, 4 * rows, per_group == 2, block, jnp.zeros((HEAD, lanes), jnp.float32)
        )
        total = (total * SCALING).astype(jnp.bfloat16)
        for k in range(per_group):
            dq_place[g * per_group + k] = total[:, k * rows : (k + 1) * rows]
        dq_copy(g).start()
        return carry

    def dq_copy(g):
        spot = pl.ds(g * per_group, per_group)
        return pltpu.make_async_copy(
            dq_place.at[spot], dq_ref.at[spot, 0:HEAD, :], dq_semaphores.at[g]
        )

    lax.fori_loop(0, groups, group, 0)

    def out_copies(j):
        return [
            pltpu.make_async_copy(place.at[j], ref.at[j], out_semaphores.at[j, i])
            for i, (place, ref) in enumerate(((kept_place, kept_ref), (sent_place, sent_ref)))
        ]

    def finish(j, carry):
        for ref, side in ((kept_place, core), (sent_place, 1 - core)):
            spot = pl.ds(pl.multiple_of((2 * j + side) * rows, rows), rows)
            total = sum_ref[spot, :].astype(ref.dtype)
            ref[j] = total.T if turned else total
        for copy in out_copies(j):
            copy.start()
        return carry

    def finished(j, carry):
        for copy in out_copies(j):
            copy.wait()
        return carry

    def dq_finished(g, carry):
        dq_copy(g).wait()
        return carry

    lax.fori_loop(0, blocks, finish, 0)
    lax.fori_loop(0, groups, dq_finished, 0)
    lax.fori_loop(0, blocks, finished, 0)


def cost(microseconds):
    return pl.CostEstimate(
        flops=microseconds * 1_000_000_000, bytes_accessed=microseconds * 1_000_000, transcendentals=0
    )


SMEM_SPEC = pl.BlockSpec(memory_space=pltpu.SMEM)
VMEM_SPEC = pl.BlockSpec(memory_space=pltpu.VMEM)


ANY_SPEC = pl.BlockSpec(memory_space=pl.ANY)


def attention_forward(plan, own, other, query, name, microseconds):
    meta, docs, bounds, pair_at, first_chunk, per_group = plan
    groups, _, lanes = docs.shape
    blocks, _, rows = own.shape
    keys = blocks * 2 * rows
    return pl.pallas_call(
        functools.partial(forward_kernel, pair_at, first_chunk, per_group),
        out_shape=(
            jax.ShapeDtypeStruct((groups * per_group, HEAD, rows), jnp.bfloat16),
            jax.ShapeDtypeStruct((groups, HEAD, lanes), jnp.float32),
            jax.ShapeDtypeStruct((groups, 1, lanes), jnp.float32),
        ),
        in_specs=[SMEM_SPEC] + [VMEM_SPEC] * 2 + [ANY_SPEC] * 2 + [VMEM_SPEC] * len(query),
        out_specs=(ANY_SPEC, ANY_SPEC, VMEM_SPEC),
        scratch_shapes=[
            *[pltpu.VMEM(own.shape, jnp.bfloat16)] * 2,
            pltpu.VMEM((groups * per_group, HEAD, rows), jnp.bfloat16),
            pltpu.VMEM((groups, HEAD, lanes), jnp.float32),
            pltpu.VMEM((keys, HEAD + DOC_SLOTS), jnp.bfloat16),
            pltpu.VMEM((HEAD, keys), jnp.bfloat16),
            pltpu.SemaphoreType.DMA((blocks // 2, 2)),
            pltpu.SemaphoreType.DMA((groups, 2)),
        ],
        compiler_params=pltpu.CompilerParams(vmem_limit_bytes=VMEM_BYTES),
        cost_estimate=cost(microseconds),
        name=name,
    )(meta, docs, bounds, own, other, *query)


def attention_backward(plan, own, other, query, grad, mixed, lse, turned, name, microseconds):
    meta, docs, bounds, pair_at, first_chunk, per_group = plan
    groups, _, lanes = docs.shape
    blocks, _, rows = own.shape
    keys = blocks * 2 * rows
    part = (blocks, 2 * HEAD, rows) if turned else (blocks, rows, 2 * HEAD)
    return pl.pallas_call(
        functools.partial(backward_kernel, pair_at, first_chunk, per_group, turned),
        out_shape=(
            jax.ShapeDtypeStruct((groups * per_group, (3 if turned else 1) * HEAD, rows), jnp.bfloat16),
            jax.ShapeDtypeStruct(part, jnp.bfloat16),
            jax.ShapeDtypeStruct(part, jnp.bfloat16),
        ),
        in_specs=[SMEM_SPEC] + [VMEM_SPEC] * 2 + [ANY_SPEC] * 2 + [VMEM_SPEC] * (len(query) + 3),
        out_specs=(ANY_SPEC, ANY_SPEC, ANY_SPEC),
        scratch_shapes=[
            *[pltpu.VMEM(own.shape, jnp.bfloat16)] * 2,
            pltpu.VMEM(part, jnp.bfloat16),
            pltpu.VMEM(part, jnp.bfloat16),
            pltpu.VMEM((groups * per_group, HEAD, rows), jnp.bfloat16),
            pltpu.VMEM((keys, HEAD + DOC_SLOTS), jnp.bfloat16),
            pltpu.VMEM((keys, 2 * HEAD), jnp.bfloat16),
            pltpu.VMEM((HEAD, keys), jnp.bfloat16),
            pltpu.VMEM((keys, 2 * HEAD), jnp.float32),
            pltpu.SemaphoreType.DMA((blocks // 2, 2)),
            pltpu.SemaphoreType.DMA((blocks, 2)),
            pltpu.SemaphoreType.DMA((groups,)),
        ],
        compiler_params=pltpu.CompilerParams(vmem_limit_bytes=VMEM_BYTES),
        cost_estimate=cost(microseconds),
        name=name,
    )(meta, docs, bounds, own, other, *query, grad, mixed, lse)


def gelu_parts(value):
    scale = (2.0 / math.pi) ** 0.5
    square = value * value
    bent = jnp.tanh(scale * value * (1.0 + 0.044715 * square))
    upper = 0.5 * (1.0 + bent)
    slope = 0.5 * value * (1.0 - bent * bent) * scale * (1.0 + 3 * 0.044715 * square)
    return value * upper, upper + slope


def column_norm(values, gain, shift):
    row_mean = jnp.mean(values, axis=0, keepdims=True)
    centered = values - row_mean
    variance = jnp.mean(centered * centered, axis=0, keepdims=True)
    inverse = lax.rsqrt(variance + EPSILON)
    normed = centered * inverse
    return (normed * gain + shift, normed, inverse)


def column_norm_back(grad, normed, inverse, gain):
    scaled = grad * gain
    return inverse * (
        scaled
        - jnp.mean(scaled, axis=0, keepdims=True)
        - normed * jnp.mean(scaled * normed, axis=0, keepdims=True)
    )


def fetched(refs, places, semaphores):
    copies = [
        pltpu.make_async_copy(ref, place, semaphores.at[i])
        for i, (ref, place) in enumerate(zip(refs, places))
    ]
    for copy in copies:
        copy.start()
    return copies


def half_rows(core, half):
    return (
        pl.ds(pl.multiple_of(core * half, 32), half),
        pl.ds(pl.multiple_of((1 - core) * half, 32), half),
    )


def ahead_kernel(
    tile, core_ref, mask_ref, cotangent_ref, b_down_ref, *refs
):
    remote, (active_grad_ref, down_grad_ref), refs = refs[:3], refs[3:5], refs[5:]
    down_w_ref, a_down_ref, place_ref, semaphores, out_semaphores = refs
    half, wide = remote[0].shape
    sides = half_rows(core_ref[0], half)
    spots = [slice(k, min(k + tile, wide)) for k in range(0, wide, tile)]
    copies = []
    for k, spot in enumerate(spots):
        pairs = [(remote[i].at[:, spot], down_w_ref.at[sides[i], spot]) for i in range(2)]
        pairs += [(remote[2].at[spot, :], a_down_ref.at[spot, :])]
        for i, (source, place) in enumerate(pairs):
            copies.append(pltpu.make_async_copy(source, place, semaphores.at[k, i]))
    for copy in copies:
        copy.start()
    rows = cotangent_ref[...].T
    down_grad = dot(rows, b_down_ref[...]).astype(jnp.bfloat16) * mask_ref[...].astype(jnp.bfloat16)
    down_grad_ref[...] = down_grad
    given = []
    for k, spot in enumerate(spots):
        for copy in copies[3 * k : 3 * k + 3]:
            copy.wait()
        grad = dot(rows, down_w_ref[:, spot]) + dot(down_grad, a_down_ref[spot, :].T)
        place_ref[:, spot] = grad
        given.append(
            pltpu.make_async_copy(place_ref.at[:, spot], active_grad_ref.at[:, spot], out_semaphores.at[k])
        )
        given[-1].start()
    for copy in given:
        copy.wait()


def ahead_part(core, mask, cotangent_t, b_down_t, down_pair_t, a_down):
    width, rows = cotangent_t.shape
    wide, inner = a_down.shape
    tile = 1024
    count = -(-wide // tile)
    return pl.pallas_call(
        functools.partial(ahead_kernel, tile),
        out_shape=(
            jax.ShapeDtypeStruct((rows, wide), jnp.float32),
            jax.ShapeDtypeStruct((rows, inner), jnp.bfloat16),
        ),
        in_specs=[SMEM_SPEC] + [VMEM_SPEC] * 3 + [ANY_SPEC] * 3,
        out_specs=(ANY_SPEC, VMEM_SPEC),
        scratch_shapes=[
            pltpu.VMEM((width, wide), jnp.bfloat16),
            pltpu.VMEM((wide, inner), jnp.bfloat16),
            pltpu.VMEM((rows, wide), jnp.float32),
            pltpu.SemaphoreType.DMA((count, 3)),
            pltpu.SemaphoreType.DMA((count,)),
        ],
        compiler_params=pltpu.CompilerParams(vmem_limit_bytes=VMEM_BYTES),
        cost_estimate=cost(1),
        name="ahead_part",
    )(core, mask, cotangent_t, b_down_t, *down_pair_t, a_down)


def middle_kernel(
    tile, core_ref, *refs
):
    sources, remote, results, (kept_ref, sent_ref), places, result_places, refs = (
        refs[:11], refs[11:20], refs[20:24], refs[24:26], refs[26:37], refs[37:41], refs[41:],
    )
    (
        mixed_main_ref, mixed_last_ref, mask_ref, a_out_ref, b_out_ref, stream_ref, gains_ref,
        a_up_ref, down_grad_ref, cotangent_ref, b_down_ref,
    ) = places
    output_ref, middle_grad_ref, main_grad_ref, last_grad_ref = result_places
    (
        out_ref, up_ref, b_up_ref, down_w_ref, a_down_ref, kept_place, sent_place,
        active_grad_ref, mixed_ref, middle_ref, hidden_ref, hidden_rows_ref, inner_out_ref,
        inner_up_ref, inner_down_ref, up_grad_ref, down_ref, back_ref,
        semaphores, out_semaphores, place_semaphores, result_semaphores,
    ) = refs
    core = core_ref[0]
    half, wide = remote[2].shape
    width = 2 * half
    full = wide // tile
    low = jnp.bfloat16
    sides = half_rows(core, half)

    def copies(first, size, number):
        spot = pl.ds(first, size)
        pairs = [(remote[2 + i].at[:, spot], up_ref.at[sides[i], spot]) for i in range(2)]
        pairs += [(remote[5 + i].at[:, spot], down_w_ref.at[sides[i], spot]) for i in range(2)]
        pairs += [(remote[4].at[:, spot], b_up_ref.at[:, spot])]
        pairs += [(remote[7].at[spot, :], a_down_ref.at[spot, :])]
        pairs += [(remote[8].at[:, spot], active_grad_ref.at[:, spot])]
        return [
            pltpu.make_async_copy(source, place, semaphores.at[number, i])
            for i, (source, place) in enumerate(pairs)
        ]

    firsts = [
        pltpu.make_async_copy(remote[i], out_ref.at[sides[i], :], semaphores.at[full + 1, i])
        for i in range(2)
    ]
    given = fetched(sources[:4], places[:4], place_semaphores)
    for copy in firsts:
        copy.start()
    later = [
        pltpu.make_async_copy(sources[i], places[i], place_semaphores.at[i]) for i in range(4, 11)
    ]
    for copy in later:
        copy.start()

    def give(i):
        copy = pltpu.make_async_copy(result_places[i], results[i], result_semaphores.at[i])
        copy.start()
        return copy

    def start_chunk(k):
        @pl.when(k < full)
        def _():
            for copy in copies(pl.multiple_of(k * tile, tile), tile, k):
                copy.start()

        if wide % tile:

            @pl.when(k == full)
            def _():
                for copy in copies(full * tile, wide % tile, full):
                    copy.start()

    def out_copies(first, size, number):
        spot = pl.ds(first, size)
        pairs = ((kept_place, kept_ref), (sent_place, sent_ref))
        return [
            pltpu.make_async_copy(place.at[spot, :], ref.at[spot, :], out_semaphores.at[number, i])
            for i, (place, ref) in enumerate(pairs)
        ]

    def put(first, rows, other):
        spot = pl.ds(first, rows.shape[0])

        @pl.when(core == 0)
        def _():
            kept_place[spot, :] = rows
            sent_place[spot, :] = other

        @pl.when(core == 1)
        def _():
            kept_place[spot, :] = other
            sent_place[spot, :] = rows

    for copy in given[:4]:
        copy.wait()
    mask = mask_ref[...]
    mask_low = mask.astype(low)
    main = mixed_main_ref.shape[0] * HEAD
    mixed_ref[:main, :] = mixed_main_ref[...].reshape(main, mixed_main_ref.shape[2])
    mixed_ref[main:, :] = mixed_last_ref[0]
    mixed_rows = mixed_ref[...].T
    inner_out = (mask * (dot(mixed_rows, a_out_ref[...]))).astype(low)
    inner_out_ref[...] = inner_out
    for copy in (*firsts, *later):
        copy.wait()
    start_chunk(0)
    start_chunk(1)
    branch = dot(mixed_rows, out_ref[...]).T + dot(b_out_ref[...], inner_out.T)
    middle = stream_ref[...].astype(jnp.float32) + branch
    middle_ref[...] = middle
    hidden = column_norm(middle, gains_ref[:, 2:3], gains_ref[:, 3:4])[0].astype(low)
    hidden_ref[...] = hidden
    hidden_rows = hidden.T
    hidden_rows_ref[...] = hidden_rows
    inner_up_ref[...] = (mask * dot(hidden_rows, a_up_ref[...])).astype(low)
    for ref in (inner_down_ref, up_grad_ref, down_ref, back_ref):
        ref[...] = jnp.zeros(ref.shape, ref.dtype)

    def step(k, size):
        first = k * tile if isinstance(k, int) else pl.multiple_of(k * tile, tile)
        for copy in copies(first, size, k):
            copy.wait()
        start_chunk(k + 2)
        spot = pl.ds(first, size)
        up, b_up, down_w, a_down = up_ref[:, spot], b_up_ref[:, spot], down_w_ref[:, spot], a_down_ref[spot, :]
        inner_up, down_grad = inner_up_ref[...], down_grad_ref[...]
        upward = dot(hidden_rows_ref[...], up) + dot(inner_up, b_up)
        active, slope = gelu_parts(upward)
        active = active.astype(low)
        up_grad = (active_grad_ref[:, spot] * slope).astype(low)
        active_t, up_grad_t = active.T, up_grad.T
        down_ref[...] += dot(down_w, active_t)
        back_ref[...] += dot(up, up_grad_t)
        inner_down_ref[...] += dot(active, a_down)
        up_grad_ref[...] += dot(b_up, up_grad_t)
        put(first, dot(up_grad_t, inner_up).astype(low), dot(active_t, down_grad).astype(low))
        for copy in out_copies(first, size, k):
            copy.start()

    def loop(k, carry):
        step(k, tile)
        return carry

    lax.fori_loop(0, full, loop, 0)
    if wide % tile:
        step(full, wide % tile)

    inner_down = (mask * inner_down_ref[...]).astype(low)
    middle = middle_ref[...]
    inner_grad = up_grad_ref[...].astype(low).T * mask_low
    hidden_grad = back_ref[...] + dot(a_up_ref[...], inner_grad.T)
    gain = gains_ref[:, 2:3]
    _, normed, inverse = column_norm(middle, gain, gain)
    middle_grad = cotangent_ref[...].astype(jnp.float32)
    middle_grad = middle_grad + column_norm_back(hidden_grad, normed, inverse, gain)
    middle_grad_ref[...] = middle_grad
    given = [give(1)]
    branch = middle_grad.astype(low)
    out_grad = dot(branch.T, b_out_ref[...]).astype(low) * mask_low
    put(wide, dot(cotangent_ref[...], inner_down).astype(low), dot(mixed_ref[...], out_grad).astype(low))
    put(
        wide + width,
        dot(hidden_ref[...], inner_grad).astype(low),
        dot(branch, inner_out_ref[...]).astype(low),
    )
    narrow = kept_place.shape[0] - wide
    spare = narrow - 2 * width
    if spare:
        nothing = jnp.zeros((spare, kept_place.shape[1]), low)
        put(wide + 2 * width, nothing, nothing)
    for copy in out_copies(wide, narrow, full + 1):
        copy.start()
    back = (dot(out_ref[...], branch) + dot(a_out_ref[...], out_grad.T)).astype(low)
    main_grad_ref[...] = back[:main].reshape(main_grad_ref.shape)
    last_grad_ref[0] = back[main:]
    given += [give(2), give(3)]
    down = down_ref[...] + dot(b_down_ref[...], inner_down.T)
    output_ref[...] = (middle + down).astype(low)
    given += [give(0)]

    def finished(k, carry):
        for copy in out_copies(pl.multiple_of(k * tile, tile), tile, k):
            copy.wait()
        return carry

    lax.fori_loop(0, full, finished, 0)
    if wide % tile:
        for copy in out_copies(full * tile, wide % tile, full):
            copy.wait()
    for copy in (*out_copies(wide, narrow, full + 1), *given):
        copy.wait()


def padded(size, unit):
    return -(-size // unit) * unit


def middle_part(
    core, mixed_main, mixed_last, tokens_t, cotangent_t, mask, gains_t, out_pair, a_out, b_out_t,
    a_up, b_down_t, up_pair, b_up, down_pair_t, a_down, active_grad, down_grad, unit,
):
    width, rows = tokens_t.shape
    half = width // 2
    inner, wide = b_up.shape
    tile = 1024
    low = jnp.bfloat16
    operands = (
        mixed_main, mixed_last, mask, a_out, b_out_t, tokens_t, gains_t, a_up, down_grad,
        cotangent_t, b_down_t,
    )
    remote = (*out_pair, *up_pair, b_up, *down_pair_t, a_down, active_grad)
    share = (padded(wide + 2 * width, unit), inner)
    shapes = (
        ((width, rows), low), ((width, rows), jnp.float32), (mixed_main.shape, low),
        (mixed_last.shape, low), (share, low), (share, low),
    )
    return pl.pallas_call(
        functools.partial(middle_kernel, tile),
        out_shape=tuple(jax.ShapeDtypeStruct(*item) for item in shapes),
        in_specs=[SMEM_SPEC] + [ANY_SPEC] * (len(operands) + len(remote)),
        out_specs=(ANY_SPEC,) * 6,
        scratch_shapes=[
            *[pltpu.VMEM(item.shape, item.dtype) for item in operands],
            *[pltpu.VMEM(*item) for item in shapes[:4]],
            pltpu.VMEM((width, width), low),
            pltpu.VMEM((width, wide), low),
            pltpu.VMEM((inner, wide), low),
            pltpu.VMEM((width, wide), low),
            pltpu.VMEM((wide, inner), low),
            *[pltpu.VMEM(share, low)] * 2,
            pltpu.VMEM((rows, wide), jnp.float32),
            pltpu.VMEM((width, rows), low),
            pltpu.VMEM((width, rows), jnp.float32),
            pltpu.VMEM((width, rows), low),
            pltpu.VMEM((rows, width), low),
            *[pltpu.VMEM((rows, inner), low)] * 2,
            pltpu.VMEM((rows, inner), jnp.float32),
            pltpu.VMEM((inner, rows), jnp.float32),
            *[pltpu.VMEM((width, rows), jnp.float32)] * 2,
            pltpu.SemaphoreType.DMA((wide // tile + 2, 7)),
            pltpu.SemaphoreType.DMA((wide // tile + 2, 2)),
            pltpu.SemaphoreType.DMA((len(operands),)),
            pltpu.SemaphoreType.DMA((4,)),
        ],
        compiler_params=pltpu.CompilerParams(vmem_limit_bytes=VMEM_BYTES),
        cost_estimate=cost(20),
        name="middle_part",
    )(core, *operands, *remote)


def whole_call(kernel, shapes, scratch, operands, remote, microseconds, name):
    space = [pltpu.VMEM(item.shape, item.dtype) for item in remote]
    return pl.pallas_call(
        kernel,
        out_shape=tuple(jax.ShapeDtypeStruct(*item) for item in shapes),
        in_specs=[SMEM_SPEC]
        + [VMEM_SPEC] * (len(operands) - 1)
        + [pl.BlockSpec(memory_space=pl.ANY)] * len(remote),
        out_specs=(VMEM_SPEC,) * len(shapes),
        scratch_shapes=[pltpu.VMEM(*item) for item in scratch]
        + space
        + ([pltpu.SemaphoreType.DMA((len(remote),))] if remote else []),
        compiler_params=pltpu.CompilerParams(vmem_limit_bytes=VMEM_BYTES if len(remote) > 2 else SMALL_BYTES),
        cost_estimate=cost(microseconds),
        name=name,
    )(*operands, *remote)


def entry_kernel(
    place_ref, lengths_ref, adapters_ref, tokens_ref, gains_own_ref, gains_other_ref, *refs
):
    remote, results, refs = refs[:12], refs[12:19], refs[19:]
    places, (weight_ref, up_ref, down_ref, semaphores, result_semaphores) = refs[:7], refs[7:]
    hidden_ref, inner_ref, mask_ref, gains_ref, heads_ref, query_ref, pairs_ref = places
    rows, inner = mask_ref.shape
    half = gains_own_ref.shape[1]
    sides = half_rows(place_ref[0], half)
    copies = []
    for n in range(3):
        down, own, up, other = remote[4 * n : 4 * n + 4]
        pairs = (
            (down, down_ref.at[n]), (up, up_ref.at[n]),
            (own, weight_ref.at[n, sides[0], :]), (other, weight_ref.at[n, sides[1], :]),
        )
        for i, (source, place) in enumerate(pairs):
            copies.append(pltpu.make_async_copy(source, place, semaphores.at[4 * n + i]))
    for copy in copies:
        copy.start()

    def give(i):
        copy = pltpu.make_async_copy(places[i], results[i], result_semaphores.at[i])
        copy.start()
        return copy

    for spot, ref in zip(sides, (gains_own_ref, gains_other_ref)):
        gains_ref[spot, :] = ref[...].astype(jnp.float32).T
    values = tokens_ref[...].astype(jnp.float32)
    hidden = column_norm(values, gains_ref[:, 0:1], gains_ref[:, 1:2])[0].astype(jnp.bfloat16)
    hidden_ref[...] = hidden
    hidden_rows = hidden.T
    place = place_ref[1] + lax.broadcasted_iota(jnp.int32, (rows, inner), 0)
    column = lax.broadcasted_iota(jnp.int32, (rows, inner), 1) // RANK

    def document(d, state):
        start, mask = state
        end = start + lengths_ref[d]
        chosen = (place >= start) & (place < end) & (column == adapters_ref[d])
        return end, jnp.where(chosen, 1.0, mask)

    state = (jnp.int32(0), jnp.zeros((rows, inner), jnp.float32))
    _, mask = lax.fori_loop(0, lengths_ref.shape[0], document, state)
    mask_ref[...] = mask
    given = [give(0), give(2), give(3)]
    count = heads_ref.shape[0]

    def give_part(n):
        spot = pl.ds(n * HEAD, HEAD)
        copy = pltpu.make_async_copy(
            heads_ref.at[:, spot, :], results[4].at[:, spot, :], result_semaphores.at[7 + n]
        )
        copy.start()
        return copy

    for n in range(3):
        for copy in copies[4 * n : 4 * n + 4]:
            copy.wait()
        products = (mask * dot(hidden_rows, down_ref[n])).astype(jnp.bfloat16)
        inner_ref[n] = products
        total = dot(hidden_rows, weight_ref[n]).T + dot(up_ref[n], products.T)
        total = total.astype(jnp.bfloat16)
        for c in range(count):
            heads_ref[c, n * HEAD : (n + 1) * HEAD, :] = total[c * HEAD : (c + 1) * HEAD]
        if n == 0:
            query_ref[0] = total[count * HEAD :]
        else:
            for c in range(count):
                pairs_ref[c, (n - 1) * HEAD : n * HEAD, :] = total[count * HEAD :]
        given.append(give_part(n))
    for copy in (*given, *[give(i) for i in (1, 5, 6)]):
        copy.wait()


def projections(place, lengths, adapters, tokens_t, gains, gains_other, weights, others, downs, ups_t):
    width, rows = tokens_t.shape
    inner = downs[0].shape[1]
    low = jnp.bfloat16
    count = width // HEAD - 1
    remote = [item for group in zip(downs, weights, ups_t, others) for item in group]
    shapes = (
        ((width, rows), low), ((3, rows, inner), low), ((rows, inner), jnp.float32),
        ((width, gains.shape[0]), jnp.float32), ((count, 3 * HEAD, rows), low),
        ((1, HEAD, rows), low), ((count, 2 * HEAD, rows), low),
    )
    return pl.pallas_call(
        entry_kernel,
        out_shape=tuple(jax.ShapeDtypeStruct(*item) for item in shapes),
        in_specs=[SMEM_SPEC] * 3 + [VMEM_SPEC] * 3 + [ANY_SPEC] * len(remote),
        out_specs=(ANY_SPEC,) * len(shapes),
        scratch_shapes=[pltpu.VMEM(*item) for item in shapes]
        + [
            pltpu.VMEM((3, width, width), low),
            pltpu.VMEM((3, width, inner), low),
            pltpu.VMEM((3, width, inner), low),
            pltpu.SemaphoreType.DMA((12,)),
            pltpu.SemaphoreType.DMA((len(shapes) + 3,)),
        ],
        compiler_params=pltpu.CompilerParams(vmem_limit_bytes=VMEM_BYTES),
        cost_estimate=cost(6),
        name="entry",
    )(place, lengths, adapters, tokens_t, gains, gains_other, *remote)


def gathered_grad(n, heads_ref, last_query_ref, last_pair_ref, grad_ref):
    count = heads_ref.shape[0]
    for c in range(count):
        grad_ref[c * HEAD : (c + 1) * HEAD, :] = heads_ref[c, n * HEAD : (n + 1) * HEAD, :]
    if n == 0:
        grad_ref[count * HEAD :, :] = last_query_ref[0]
    else:
        grad_ref[count * HEAD :, :] = last_pair_ref[...].T[(n - 1) * HEAD : n * HEAD]
    return grad_ref[...]


def projections_late_kernel(core_ref, *refs):
    sources, (kept_ref, sent_ref, inner_grad_ref), refs = refs[:9], refs[9:12], refs[12:]
    places, (kept_place, sent_place, grad_ref, semaphores, out_semaphores) = refs[:9], refs[9:]
    heads_ref, last_query_ref, last_pair_ref, mask_ref, hidden_ref, inner_ref, *ups = places
    copies = fetched(sources, places, semaphores)
    core = core_ref[0]
    low = jnp.bfloat16
    width, share = hidden_ref.shape[0], kept_place.shape[0]

    def store(side, spot, rows):
        @pl.when(core == side)
        def _():
            kept_place[spot, :] = rows

        @pl.when(core != side)
        def _():
            sent_place[spot, :] = rows

    def keep(first, rows):
        done = 0
        while done < rows.shape[0]:
            side, spot = divmod(first + done, share)
            size = min(rows.shape[0] - done, share - spot)
            store(side, slice(spot, spot + size), rows[done : done + size])
            done += size

    keep(6 * width, jnp.zeros((2 * share - 6 * width, kept_place.shape[1]), low))
    turned = []
    for copy, up in zip(copies[6:], ups):
        copy.wait()
        turned.append(up[...].T)
    for copy in copies[:6]:
        copy.wait()
    mask_low = mask_ref[...].astype(low)
    hidden = hidden_ref[...]
    for n in range(3):
        grad = gathered_grad(n, heads_ref, last_query_ref, last_pair_ref, grad_ref)
        inner_grad = dot(turned[n], grad).astype(low).T * mask_low
        inner_grad_ref[n] = inner_grad
        keep(2 * n * width, dot(hidden, inner_grad).astype(low))
        keep((2 * n + 1) * width, dot(grad, inner_ref[n]).astype(low))
    given = fetched((kept_place, sent_place), (kept_ref, sent_ref), out_semaphores)
    for copy in given:
        copy.wait()


def projections_late(core, heads, last_query, last_pair, hidden_t, inners, mask, ups_t, unit):
    width, rows = hidden_t.shape
    low = jnp.bfloat16
    share = (padded(6 * width, 2 * unit) // 2, mask.shape[1])
    operands = (heads, last_query, last_pair, mask, hidden_t, inners, *ups_t)
    return pl.pallas_call(
        projections_late_kernel,
        out_shape=(
            jax.ShapeDtypeStruct(share, low),
            jax.ShapeDtypeStruct(share, low),
            jax.ShapeDtypeStruct(inners.shape, low),
        ),
        in_specs=[SMEM_SPEC] + [ANY_SPEC] * len(operands),
        out_specs=(ANY_SPEC, ANY_SPEC, VMEM_SPEC),
        scratch_shapes=[pltpu.VMEM(item.shape, item.dtype) for item in operands]
        + [
            pltpu.VMEM(share, low),
            pltpu.VMEM(share, low),
            pltpu.VMEM((width, rows), low),
            pltpu.SemaphoreType.DMA((len(operands),)),
            pltpu.SemaphoreType.DMA((2,)),
        ],
        compiler_params=pltpu.CompilerParams(vmem_limit_bytes=VMEM_BYTES),
        cost_estimate=cost(5),
        name="projections_late",
    )(core, *operands)


def projections_back_kernel(
    core_ref, heads_ref, last_query_ref, last_pair_ref, inner_grad_ref, gains_ref, tokens_ref, *refs
):
    remote, (grad_in_ref, grad_ref, sum_ref), local_refs, semaphores = (
        refs[:10], refs[10:13], refs[13:23], refs[23],
    )
    copies = fetched(remote, local_refs, semaphores)
    downs, weights, others, middle_grad_ref = (
        local_refs[:3], local_refs[3:6], local_refs[6:9], local_refs[9],
    )
    own_rows, other_rows = half_rows(core_ref[0], weights[0].shape[0])
    for n in range(3):
        grad = gathered_grad(n, heads_ref, last_query_ref, last_pair_ref, grad_ref)
        turned = inner_grad_ref[n].T
        copies[n].wait()
        for rows, weight, copy in (
            (own_rows, weights[n], copies[3 + n]), (other_rows, others[n], copies[6 + n])
        ):
            copy.wait()
            part = dot(weight[...], grad) + dot(downs[n][rows, :], turned)
            sum_ref[rows, :] = part if n == 0 else sum_ref[rows, :] + part
    gain = gains_ref[:, 0:1]
    _, normed, inverse = column_norm(tokens_ref[...].astype(jnp.float32), gain, gain)
    back = column_norm_back(sum_ref[...], normed, inverse, gain)
    copies[9].wait()
    grad_in_ref[...] = (middle_grad_ref[...] + back).astype(jnp.bfloat16)


def projections_back(
    core, heads, last_query, last_pair, inner_grads, gains_t, tokens_t, middle_grad_t,
    weights, others, downs,
):
    width, rows = tokens_t.shape
    low = jnp.bfloat16
    return whole_call(
        projections_back_kernel,
        (((width, rows), low),),
        (((width, rows), low), ((width, rows), jnp.float32)),
        (core, heads, last_query, last_pair, inner_grads, gains_t, tokens_t),
        (*downs, *weights, *others, middle_grad_t),
        8, "projections_back",
    )[0]


def steps_of(cycle_size):
    bits = cycle_size.bit_length() - 1
    return [(bit, min(2, bits - bit)) for bit in range(0, bits, 2)]


def partners(cycle_size, step, k):
    return [(i, i ^ (k << step[0])) for i in range(cycle_size)]


def scattered(array, step, cycle_size):
    count = 1 << step[1]
    mine = (lax.axis_index("ctx") >> step[0]) & (count - 1)
    blocks = array.reshape(count, array.shape[0] // count, array.shape[1])

    def block(number):
        return lax.dynamic_index_in_dim(blocks, number, 0, keepdims=False)

    total = block(mine).astype(jnp.float32)
    for k in range(1, count):
        got = lax.ppermute(block(mine ^ k), "ctx", partners(cycle_size, step, k))
        total = total + got.astype(jnp.float32)
    return total.astype(array.dtype)


def collected(share, step, cycle_size):
    count = 1 << step[1]
    mine = (lax.axis_index("ctx") >> step[0]) & (count - 1)
    blocks = [share]
    for k in range(1, count):
        blocks.append(lax.ppermute(share, "ctx", partners(cycle_size, step, k)))
    for bit in range(step[1]):
        turned = ((mine >> bit) & 1) == 1
        blocks = [jnp.where(turned, blocks[k ^ (1 << bit)], blocks[k]) for k in range(count)]
    return jnp.concatenate(blocks, axis=0)


def pair_sum(kept, sent):
    return kept + lax.ppermute(sent, "wsh", SWAP)


def early_finish_kernel(
    factor, core_ref, own_source, other_source,
    b_up_ref, a_down_ref, b_down_ref, a_up_ref, a_out_ref, b_out_ref, own_ref, other_ref, semaphores,
):
    for copy in fetched((own_source, other_source), (own_ref, other_ref), semaphores):
        copy.wait()
    wide, width = a_down_ref.shape[0], a_up_ref.shape[0]

    def finish(first_ref, second_ref):
        def part(ref, first, count):
            return ref[first : first + count, :].astype(jnp.float32) * factor

        for k in range(wide // 256):
            b_up_ref[:, k * 256 : (k + 1) * 256] = part(first_ref, k * 256, 256).T
        a_down_ref[...] = part(second_ref, 0, wide)
        b_down_ref[...] = part(first_ref, wide, width)
        a_up_ref[...] = part(first_ref, wide + width, width)
        a_out_ref[...] = part(second_ref, wide, width)
        b_out_ref[...] = part(second_ref, wide + width, width)

    @pl.when(core_ref[0] == 0)
    def _():
        finish(own_ref, other_ref)

    @pl.when(core_ref[0] == 1)
    def _():
        finish(other_ref, own_ref)


def late_finish_kernel(factor, core_ref, own_ref, other_ref, *refs):
    core = core_ref[0]
    targets, late_ref, own_place, other_place, semaphores = refs[:6], *refs[6:]
    places = (own_place, other_place)
    copies = fetched((own_ref, other_ref), places, semaphores)
    for side, ref, copy in zip((core, 1 - core), places, copies):
        copy.wait()
        late_ref[side] = ref[...].astype(jnp.float32) * factor
    width, share = targets[0].shape[0], late_ref.shape[1]
    for n, ref in enumerate(targets):
        done = 0
        while done < width:
            side, spot = divmod(n * width + done, share)
            rows = min(width - done, share - spot)
            ref[done : done + rows, :] = late_ref[side, spot : spot + rows, :]
            done += rows


def finished(kernel, factor, core, own, other, shapes, scratch, name):
    return whole_call(
        functools.partial(kernel, factor), [(shape, jnp.float32) for shape in shapes], scratch,
        (core,), (own, other), 1, name,
    )


def local(
    tokens_in,
    doc_lengths,
    doc_adapter,
    norm1_gain,
    norm1_bias,
    norm2_gain,
    norm2_bias,
    w_query,
    w_key,
    w_value,
    w_out,
    w_up,
    w_down,
    a_query,
    b_query,
    a_key,
    b_key,
    a_value,
    b_value,
    a_out,
    b_out,
    a_up,
    b_up,
    a_down,
    b_down,
    cotangent,
):
    group_size = lax.axis_size("wsh")
    cycle_size = lax.axis_size("ctx")
    tok_dev, width_all = tokens_in.shape
    head_count = width_all // HEAD
    block_len = tok_dev * group_size
    hop_count = (DOC_MAX + block_len - 2) // block_len
    span = head_count - 1
    cycle_pos = lax.axis_index("ctx")
    core = lax.axis_index("wsh")
    half = width_all // group_size

    first_row = cycle_pos * block_len + core * tok_dev
    doc_ends = jnp.cumsum(doc_lengths)
    doc_starts = doc_ends - doc_lengths

    team = cycle_pos // span
    past = hop_count if cycle_size > span else 0
    first_key = (team * span - past) * block_len
    key_blocks = past + span

    slots = DOC_SLOTS - doc_lengths.shape[0]
    bounds = jnp.stack([jnp.pad(doc_starts, (0, slots)), jnp.pad(doc_ends, (0, slots))])

    def plan(chunk_pos, pair_at, first_chunk, per_group):
        groups = chunk_pos.shape[0] // per_group
        row_pos = chunk_pos[:, None] + jnp.arange(tok_dev, dtype=jnp.int32)[None, :]
        row_docs = jnp.sum((doc_ends[None, None, :] <= row_pos[:, :, None]).astype(jnp.int32), axis=2)
        row_docs = row_docs.reshape(groups, 1, per_group * tok_dev)
        chunk_pos = chunk_pos.reshape(groups, per_group)
        began = jnp.where(doc_starts[None, None, :] <= chunk_pos[:, :, None], doc_starts[None, None, :], 0)
        began = (jnp.max(began, axis=2) - first_key) // (2 * block_len)
        first = began[:, 0]
        last = (chunk_pos[:, -1] - first_key) // (2 * block_len)
        same = jnp.ones((groups,), jnp.int32)
        whole = per_group > 1
        meta = [
            first,
            last,
            chunk_pos[:, 0],
            same * core,
            same * first_key,
            jnp.concatenate([first[:1] * 0, last[:-1] + 1]) if whole else first,
            began[:, -1],
        ]
        meta = jnp.stack(meta, axis=1).astype(jnp.int32)
        docs = row_docs.astype(jnp.int32)
        return meta, docs, bounds.astype(jnp.int32), pair_at, first_chunk, per_group

    team_pos = (team * span + jnp.arange(span, dtype=jnp.int32)) * block_len + core * tok_dev
    main_plan = plan(team_pos.astype(jnp.int32), HEAD, past, 2)
    last_plan = plan(first_row[None].astype(jnp.int32), 0, 0, 1)

    def swap(array):
        return lax.ppermute(array, "wsh", SWAP)

    if cycle_size > span:
        teams = [[t * span + i for i in range(span)] for t in range(cycle_size // span)]
    else:
        teams = None

    def exchange(blocks):
        return lax.all_to_all(blocks, "ctx", 0, 0, tiled=True, axis_index_groups=teams)

    gains = jnp.stack([norm1_gain, norm1_bias, norm2_gain, norm2_bias])
    weights = [w_query, w_key, w_value, w_out, w_up, w_down.T]
    others = [swap(item) for item in weights[:3]]
    gains_other = swap(gains)
    *others, gains_other, w_late = lax.optimization_barrier((*others, gains_other, tuple(weights[3:])))
    others = others + [swap(item) for item in w_late]

    downs = (a_query, a_key, a_value)
    ups_t = (b_query.T, b_key.T, b_value.T)
    tokens_t = tokens_in.T
    core_1 = jnp.stack([core, first_row]).astype(jnp.int32)
    hidden_t, inners, adapter_mask, gains_t, heads, last_query, last_pairs = projections(
        core_1, doc_lengths, doc_adapter, tokens_t, gains, gains_other, weights[:3], others[:3],
        downs, ups_t,
    )

    ahead = [(i, i + span) for i in range(cycle_size - span)]
    back = [(i + span, i) for i in range(cycle_size - span)]

    def with_past(blocks):
        if not past:
            return blocks
        return jnp.concatenate([lax.ppermute(blocks[span - past :], "ctx", ahead), blocks], axis=0)

    steps = steps_of(cycle_size)
    unit = 16 * cycle_size
    incoming = exchange(heads)
    active_grad, down_grad = ahead_part(
        core_1, adapter_mask, cotangent.T, b_down.T, (w_down.T, others[5]), a_down
    )
    incoming, last_pairs, active_grad, ready = lax.optimization_barrier(
        (incoming, last_pairs, active_grad, main_plan[:3])
    )
    main_plan = (*ready, *main_plan[3:])
    own = with_past(incoming)
    other = swap(own)
    last_own = exchange(last_pairs)
    low_main, total_main, lse_main = attention_forward(
        main_plan, own, other, (), "attention_forward", 30
    )
    low_main, last_own = lax.optimization_barrier((low_main, last_own))
    last_own = with_past(last_own)
    last_other = swap(last_own)
    low_last, mixed_last, lse_last = attention_forward(
        last_plan, last_own, last_other, (last_query,), "last_forward", 0
    )
    mixed_main = exchange(low_main)

    output_t, middle_grad_t, main_grad, last_out_grad, early_kept, early_sent = middle_part(
        core_1, mixed_main, low_last, tokens_t, cotangent.T, adapter_mask, gains_t,
        (w_out, others[3]), a_out, b_out.T, a_up, b_down.T, (w_up, others[4]), b_up,
        (w_down.T, others[5]), a_down, active_grad, down_grad, unit,
    )

    def pair_total(kept, sent):
        total = kept.astype(jnp.float32) + swap(sent).astype(jnp.float32)
        if past:
            returned = lax.ppermute(total[:past].astype(jnp.bfloat16), "ctx", back)
            total = total[past:].at[span - past :].add(returned.astype(jnp.float32))
        return total

    def pair_back(dq, kept, sent):
        total = pair_total(kept, sent).astype(jnp.bfloat16)
        return lax.dynamic_update_slice(dq, total, (0, HEAD, 0))

    dq_last, kept_last, sent_last = attention_backward(
        last_plan, last_own, last_other, (last_query,),
        last_out_grad, mixed_last, lse_last, False, "last_backward", 0,
    )
    grad_main = exchange(main_grad)
    grad_main, dq_last, kept_last, sent_last = lax.optimization_barrier(
        (grad_main, dq_last, kept_last, sent_last)
    )
    dpair_last = pair_total(kept_last, sent_last).astype(jnp.bfloat16)
    plane = 1 << steps[0][1]
    lines = cycle_size // plane
    digits = (2,) * (cycle_size.bit_length() - 3) + (plane,)
    if cycle_size > span:
        zero = jnp.zeros((cycle_size // span, *dpair_last.shape), dpair_last.dtype)
        dpair_last = lax.dynamic_update_index_in_dim(zero, dpair_last, team, 0)
    order = tuple(reversed(range(len(digits)))) + (len(digits), len(digits) + 1)
    dpair_last = jnp.transpose(dpair_last.reshape(digits + dpair_last.shape[-2:]), order)
    early = pair_sum(early_kept, early_sent)
    lanes = early.shape[1]
    early_rows, last_rows = early.shape[0] // cycle_size, tok_dev
    early = early.reshape(plane, lines, early_rows, lanes)
    dpair_last = dpair_last.reshape(plane, lines, last_rows, lanes)

    def meant_for(k):
        parts = [lax.dynamic_index_in_dim(x, (cycle_pos % plane) ^ k, 0, False) for x in (early, dpair_last)]
        return jnp.concatenate(parts, axis=1)

    meant = [meant_for(k) for k in range(plane)]
    grad_main, *meant = lax.optimization_barrier((grad_main, *meant))
    shared = [meant[0]] + [
        lax.ppermute(meant[k], "ctx", partners(cycle_size, steps[0], k)) for k in range(1, plane)
    ]
    dq_main, kept_main, sent_main = attention_backward(
        main_plan, own, other, (), grad_main, total_main, lse_main,
        True, "attention_backward", 40
    )
    dq_main, kept_main, sent_main, *shared = lax.optimization_barrier(
        (dq_main, kept_main, sent_main, *shared)
    )
    shared = sum(part.astype(jnp.float32) for part in shared).astype(jnp.bfloat16)
    shared = shared.reshape(lines * (early_rows + last_rows), lanes)
    outgoing_back = pair_back(dq_main, kept_main, sent_main)
    outgoing_back, shared = lax.optimization_barrier((outgoing_back, shared))
    singles = [(bit, 1) for bit in range(2, cycle_size.bit_length() - 1)]
    shared = shared.reshape(lines, early_rows + last_rows, lanes)
    early = shared[:, :early_rows].reshape(lines * early_rows, lanes)
    last_sum = shared[:, early_rows:].reshape(lines * last_rows, lanes)
    incoming_back = exchange(outgoing_back)
    for step in singles:
        last_sum = scattered(last_sum, step, cycle_size)
    for step in singles:
        early = scattered(early, step, cycle_size)

    late_kept, late_sent, inner_grads = projections_late(
        core_1, incoming_back, dq_last, last_sum, hidden_t, inners, adapter_mask, ups_t, unit
    )
    singles = singles[::-1]
    late, early, inner_grads = lax.optimization_barrier(
        (pair_sum(late_kept, late_sent), early, inner_grads)
    )
    grad_in_t = projections_back(
        core_1, incoming_back, dq_last, last_sum, inner_grads, gains_t, tokens_t, middle_grad_t,
        weights[:3], others[:3], downs,
    )

    norm_factor = (tok_dev * group_size * cycle_size) ** (-0.5)
    late = scattered(late, steps[0], cycle_size)
    for step in singles:
        early = collected(early, step, cycle_size)
    late, early = lax.optimization_barrier((late, early))
    for step in steps[1:]:
        late = scattered(late, step, cycle_size)
    early = collected(early, steps[0], cycle_size)
    late, early, grad_in_t = lax.optimization_barrier((late, early, grad_in_t))
    early_other = swap(early)
    for step in reversed(steps[1:]):
        late = collected(late, step, cycle_size)
    late, early_other = lax.optimization_barrier((late, early_other))
    late = collected(late, steps[0], cycle_size)
    wide = b_up.shape[1]
    early = finished(
        early_finish_kernel, norm_factor, core_1, early, early_other,
        [(lanes, wide), (wide, lanes)] + [(width_all, lanes)] * 4, (), "early_finish",
    )
    late, early = lax.optimization_barrier((late, early))
    g_b_up, g_a_down, g_b_down, g_a_up, g_a_out, g_b_out = early
    late = finished(
        late_finish_kernel, norm_factor, core_1, late, swap(late), [(width_all, lanes)] * 6,
        (((2, *late.shape), jnp.float32),), "late_finish",
    )
    return (
        output_t.T,
        grad_in_t.T,
        late[0],
        late[1].T,
        late[2],
        late[3].T,
        late[4],
        late[5].T,
        g_a_out,
        g_b_out.T,
        g_a_up,
        g_b_up,
        g_a_down,
        g_b_down.T,
    )


def solution(mesh):
    return jax.shard_map(
        local,
        mesh=mesh,
        in_specs=(
            P(("ctx", "wsh"), None),
            P(),
            P(),
            P("wsh"),
            P("wsh"),
            P("wsh"),
            P("wsh"),
            P("wsh", None),
            P("wsh", None),
            P("wsh", None),
            P("wsh", None),
            P("wsh", None),
            P(None, "wsh"),
            P(),
            P(),
            P(),
            P(),
            P(),
            P(),
            P(),
            P(),
            P(),
            P(),
            P(),
            P(),
            P(("ctx", "wsh"), None),
        ),
        out_specs=(
            P(("ctx", "wsh"), None),
            P(("ctx", "wsh"), None),
            P(),
            P(),
            P(),
            P(),
            P(),
            P(),
            P(),
            P(),
            P(),
            P(),
            P(),
            P(),
        ),
        check_vma=False,
    )
```

```python
import functools
import math

import jax
import jax.numpy as jnp
from jax import lax
from jax.experimental import pallas as pl
from jax.experimental.pallas import tpu as pltpu
from jax.sharding import PartitionSpec as P

HEAD = 64
RANK = 16
DOC_MAX = 4096


EPSILON = 1e-05
NEG_FILL = -1e30
SCALING = HEAD ** (-0.5)
SWAP = [(0, 1), (1, 0)]
VMEM_BYTES = 60 * 1024 * 1024
SMALL_BYTES = 24 * 1024 * 1024


def norm_parts(values, gain, shift):
    row_mean = jnp.mean(values, axis=-1, keepdims=True)
    centered = values - row_mean
    variance = jnp.mean(centered * centered, axis=-1, keepdims=True)
    inverse = lax.rsqrt(variance + EPSILON)
    normed = centered * inverse
    return (normed * gain + shift, normed, inverse)


def norm_back(grad, normed, inverse, gain):
    scaled = grad * gain
    return inverse * (
        scaled
        - jnp.mean(scaled, axis=-1, keepdims=True)
        - normed * jnp.mean(scaled * normed, axis=-1, keepdims=True)
    )


def dot(left, right, lc=1, rc=0):
    return lax.dot_general(
        left, right, (((lc,), (rc,)), ((), ())), preferred_element_type=jnp.float32
    )


DOC_SLOTS = 64


def side_by_side(ref, first, count):
    return jnp.concatenate([ref[first + k, 0:HEAD, :] for k in range(count)], axis=1)


def marked_queries(query_ref, first, count, docs):
    query = side_by_side(query_ref, first, count)
    query = (query.astype(jnp.float32) * SCALING).astype(jnp.bfloat16)
    number = lax.broadcasted_iota(jnp.int32, (DOC_SLOTS, docs.shape[1]), 0)
    marks = jnp.where(number == docs, 0.0, NEG_FILL).astype(jnp.bfloat16)
    return query, jnp.concatenate([query, marks], axis=0)


def marked_keys(pair, bounds_ref, first_pos):
    rows = pair.shape[0]
    place = first_pos + lax.broadcasted_iota(jnp.int32, (rows, DOC_SLOTS), 0)
    marks = (place >= bounds_ref[0:1, :]) & (place < bounds_ref[1:2, :])
    marks = jnp.where(marks, 1.0, 0.0).astype(jnp.bfloat16)
    return jnp.concatenate([pair[:, :HEAD], marks], axis=1)


def causal(scores, first_pos, query_pos):
    row = lax.broadcasted_iota(jnp.int32, scores.shape, 0)
    return jnp.where(row <= query_pos - first_pos, scores, NEG_FILL)


def group_lanes(meta_ref, g, lanes, rows):
    lane = lax.broadcasted_iota(jnp.int32, (1, lanes), 1)
    return meta_ref[g, 2] + lane + jnp.where(lane >= rows, rows, 0)


def span_walk(meta_ref, g, size, two, block, state):
    def spot(t):
        first = pl.multiple_of(t * size, size)
        return pl.ds(first, size), meta_ref[0, 4] + first

    def walk(first, end, alone, state):
        return lax.fori_loop(first, end, lambda t, state: block(*spot(t), False, alone, state), state)

    if two:
        state = walk(meta_ref[g, 0], meta_ref[g, 6], True, state)
    state = walk(meta_ref[g, 6], meta_ref[g, 1], False, state)
    return block(*spot(meta_ref[g, 1]), True, False, state)


def span_copies(remote, places, semaphores, t):
    spot = pl.ds(2 * t, 2)
    return [
        pltpu.make_async_copy(source.at[spot], place.at[spot], semaphores.at[t, i])
        for i, (source, place) in enumerate(zip(remote, places))
    ]


def start_spans(meta_ref, groups, remote, places, semaphores):
    def start(t, carry):
        for copy in span_copies(remote, places, semaphores, t):
            copy.start()
        return carry

    lax.fori_loop(meta_ref[0, 5], meta_ref[groups - 1, 1] + 1, start, 0)


def new_blocks(meta_ref, g, remote, places, semaphores, rows, use):
    core = meta_ref[0, 3]

    def span(t, carry):
        for copy in span_copies(remote, places, semaphores, t):
            copy.wait()
        for k in range(2):
            for place, side in zip(places, (core, 1 - core)):
                use(pl.multiple_of(((2 * t + k) * 2 + side) * rows, rows), place.at[2 * t + k])
        return carry

    lax.fori_loop(meta_ref[g, 5], meta_ref[g, 1] + 1, span, 0)


def forward_kernel(
    pair_at, first_chunk, per_group, meta_ref, docs_ref, bounds_ref, own_ref, other_ref, *refs
):
    apart = len(refs) - 11
    query_ref, (low_ref, mixed_ref, lse_ref, own_place, other_place) = refs[0], refs[apart : apart + 5]
    low_place, mixed_place, keys_ref, values_ref, semaphores, out_semaphores = refs[apart + 5 :]
    query_ref = query_ref if apart else own_place
    groups, _, lanes = docs_ref.shape
    rows = own_place.shape[2]
    remote, places = (own_ref, other_ref), (own_place, other_place)
    first_key = meta_ref[0, 4]
    start_spans(meta_ref, groups, remote, places, semaphores)

    def spread(first, pair_ref):
        pair = pair_ref[pair_at : pair_at + 2 * HEAD, :]
        keys_ref[pl.ds(first, rows), :] = marked_keys(pair.T, bounds_ref, first_key + first)
        values_ref[:, pl.ds(first, rows)] = pair[HEAD:]

    def group(g, carry):
        new_blocks(meta_ref, g, remote, places, semaphores, rows, spread)
        _, query = marked_queries(query_ref, first_chunk + g * per_group, per_group, docs_ref[g])
        query_pos = group_lanes(meta_ref, g, lanes, rows)

        def block(spot, first_pos, last, alone, state):
            cut = slice(0, rows if alone else lanes)
            row_max, row_sum, total = (part[:, cut] for part in state)
            scores = dot(keys_ref[spot, :], query[:, cut])
            if last:
                scores = causal(scores, first_pos, query_pos)
            new_max = jnp.maximum(row_max, jnp.max(scores, axis=0, keepdims=True))
            probs = jnp.exp(scores - new_max)
            shrink = jnp.exp(row_max - new_max)
            row_sum = row_sum * shrink + jnp.sum(probs, axis=0, keepdims=True)
            total = total * shrink + dot(values_ref[:, spot], probs.astype(jnp.bfloat16))
            new = (new_max, row_sum, total)
            if alone:
                new = tuple(jnp.concatenate([x, y[:, rows:]], axis=1) for x, y in zip(new, state))
            return new

        state = (
            jnp.full((1, lanes), NEG_FILL, jnp.float32),
            jnp.zeros((1, lanes), jnp.float32),
            jnp.zeros((HEAD, lanes), jnp.float32),
        )
        row_max, row_sum, total = span_walk(meta_ref, g, 4 * rows, per_group == 2, block, state)
        mixed = total / row_sum
        mixed_place[g] = mixed
        for k in range(per_group):
            low_place[g * per_group + k] = mixed[:, k * rows : (k + 1) * rows].astype(jnp.bfloat16)
        lse_ref[g] = row_max + jnp.log(row_sum)
        for copy in out_copies(g):
            copy.start()
        return carry

    def out_copies(g):
        spot = pl.ds(g * per_group, per_group)
        return (
            pltpu.make_async_copy(mixed_place.at[g], mixed_ref.at[g], out_semaphores.at[g, 0]),
            pltpu.make_async_copy(low_place.at[spot], low_ref.at[spot], out_semaphores.at[g, 1]),
        )

    def finished(g, carry):
        for copy in out_copies(g):
            copy.wait()
        return carry

    lax.fori_loop(0, groups, group, 0)
    lax.fori_loop(0, groups, finished, 0)


def backward_kernel(
    pair_at, first_chunk, per_group, turned, meta_ref, docs_ref, bounds_ref, own_ref, other_ref, *refs
):
    apart = len(refs) - 18
    grad_ref, mixed_ref, lse_ref = refs[apart : apart + 3]
    dq_ref, kept_ref, sent_ref, own_place, other_place, kept_place, sent_place = refs[apart + 3 : apart + 10]
    dq_place, keys_ref, rows_ref, keys_t_ref, sum_ref = refs[apart + 10 : apart + 15]
    semaphores, out_semaphores, dq_semaphores = refs[apart + 15 :]
    query_ref = refs[0] if apart else own_place
    groups, _, lanes = docs_ref.shape
    blocks, _, rows = own_place.shape
    remote, places = (own_ref, other_ref), (own_place, other_place)
    core, first_key = meta_ref[0, 3], meta_ref[0, 4]
    start_spans(meta_ref, groups, remote, places, semaphores)
    if apart:
        sum_ref[...] = jnp.zeros(sum_ref.shape, jnp.float32)

    def spread(first, pair_ref):
        pair = pair_ref[pair_at : pair_at + 2 * HEAD, :]
        turned_pair = pair.T
        rows_ref[pl.ds(first, rows), :] = turned_pair
        keys_ref[pl.ds(first, rows), :] = marked_keys(turned_pair, bounds_ref, first_key + first)
        keys_t_ref[:, pl.ds(first, rows)] = pair[:HEAD]
        if not apart:
            sum_ref[pl.ds(first, rows), :] = jnp.zeros((rows, 2 * HEAD), jnp.float32)

    def group(g, carry):
        new_blocks(meta_ref, g, remote, places, semaphores, rows, spread)
        first = first_chunk + g * per_group
        query, query_marked = marked_queries(query_ref, first, per_group, docs_ref[g])
        grad = side_by_side(grad_ref, g * per_group, per_group)
        nothing = jnp.zeros_like(query)
        query_low = jnp.concatenate([query, nothing], axis=0)
        grad_high = jnp.concatenate([nothing, grad], axis=0)
        both = jnp.concatenate([query_low, grad_high], axis=1).T
        delta = jnp.sum(grad.astype(jnp.float32) * mixed_ref[g], axis=0, keepdims=True)
        lse = lse_ref[g]
        query_pos = group_lanes(meta_ref, g, lanes, rows)

        def block(spot, first_pos, last, alone, total):
            cut = slice(0, rows if alone else lanes)
            scores = dot(keys_ref[spot, :], query_marked[:, cut])
            if last:
                scores = causal(scores, first_pos, query_pos)
            probs = jnp.exp(scores - lse[:, cut])
            prob_grad = dot(rows_ref[spot, :], grad_high[:, cut])
            score_grad = (probs * (prob_grad - delta[:, cut])).astype(jnp.bfloat16)
            turned_back = both
            if alone:
                turned_back = jnp.concatenate([both[:rows], both[lanes : lanes + rows]], axis=0)
            sum_ref[spot, :] += dot(
                jnp.concatenate([score_grad, probs.astype(jnp.bfloat16)], axis=1), turned_back
            )
            new = total[:, cut] + dot(keys_t_ref[:, spot], score_grad)
            return jnp.concatenate([new, total[:, rows:]], axis=1) if alone else new

        total = span_walk(
            meta_ref, g, 4 * rows, per_group == 2, block, jnp.zeros((HEAD, lanes), jnp.float32)
        )
        total = (total * SCALING).astype(jnp.bfloat16)
        for k in range(per_group):
            dq_place[g * per_group + k] = total[:, k * rows : (k + 1) * rows]
        dq_copy(g).start()
        return carry

    def dq_copy(g):
        spot = pl.ds(g * per_group, per_group)
        return pltpu.make_async_copy(
            dq_place.at[spot], dq_ref.at[spot, 0:HEAD, :], dq_semaphores.at[g]
        )

    lax.fori_loop(0, groups, group, 0)

    def out_copies(j):
        return [
            pltpu.make_async_copy(place.at[j], ref.at[j], out_semaphores.at[j, i])
            for i, (place, ref) in enumerate(((kept_place, kept_ref), (sent_place, sent_ref)))
        ]

    def finish(j, carry):
        for ref, side in ((kept_place, core), (sent_place, 1 - core)):
            spot = pl.ds(pl.multiple_of((2 * j + side) * rows, rows), rows)
            total = sum_ref[spot, :].astype(ref.dtype)
            ref[j] = total.T if turned else total
        for copy in out_copies(j):
            copy.start()
        return carry

    def finished(j, carry):
        for copy in out_copies(j):
            copy.wait()
        return carry

    def dq_finished(g, carry):
        dq_copy(g).wait()
        return carry

    lax.fori_loop(0, blocks, finish, 0)
    lax.fori_loop(0, groups, dq_finished, 0)
    lax.fori_loop(0, blocks, finished, 0)


def cost(microseconds):
    return pl.CostEstimate(
        flops=microseconds * 1_000_000_000, bytes_accessed=microseconds * 1_000_000, transcendentals=0
    )


SMEM_SPEC = pl.BlockSpec(memory_space=pltpu.SMEM)
VMEM_SPEC = pl.BlockSpec(memory_space=pltpu.VMEM)


ANY_SPEC = pl.BlockSpec(memory_space=pl.ANY)


def attention_forward(plan, own, other, query, name, microseconds):
    meta, docs, bounds, pair_at, first_chunk, per_group = plan
    groups, _, lanes = docs.shape
    blocks, _, rows = own.shape
    keys = blocks * 2 * rows
    return pl.pallas_call(
        functools.partial(forward_kernel, pair_at, first_chunk, per_group),
        out_shape=(
            jax.ShapeDtypeStruct((groups * per_group, HEAD, rows), jnp.bfloat16),
            jax.ShapeDtypeStruct((groups, HEAD, lanes), jnp.float32),
            jax.ShapeDtypeStruct((groups, 1, lanes), jnp.float32),
        ),
        in_specs=[SMEM_SPEC] + [VMEM_SPEC] * 2 + [ANY_SPEC] * 2 + [VMEM_SPEC] * len(query),
        out_specs=(ANY_SPEC, ANY_SPEC, VMEM_SPEC),
        scratch_shapes=[
            *[pltpu.VMEM(own.shape, jnp.bfloat16)] * 2,
            pltpu.VMEM((groups * per_group, HEAD, rows), jnp.bfloat16),
            pltpu.VMEM((groups, HEAD, lanes), jnp.float32),
            pltpu.VMEM((keys, HEAD + DOC_SLOTS), jnp.bfloat16),
            pltpu.VMEM((HEAD, keys), jnp.bfloat16),
            pltpu.SemaphoreType.DMA((blocks // 2, 2)),
            pltpu.SemaphoreType.DMA((groups, 2)),
        ],
        compiler_params=pltpu.CompilerParams(vmem_limit_bytes=VMEM_BYTES),
        cost_estimate=cost(microseconds),
        name=name,
    )(meta, docs, bounds, own, other, *query)


def attention_backward(plan, own, other, query, grad, mixed, lse, turned, name, microseconds):
    meta, docs, bounds, pair_at, first_chunk, per_group = plan
    groups, _, lanes = docs.shape
    blocks, _, rows = own.shape
    keys = blocks * 2 * rows
    part = (blocks, 2 * HEAD, rows) if turned else (blocks, rows, 2 * HEAD)
    return pl.pallas_call(
        functools.partial(backward_kernel, pair_at, first_chunk, per_group, turned),
        out_shape=(
            jax.ShapeDtypeStruct((groups * per_group, (3 if turned else 1) * HEAD, rows), jnp.bfloat16),
            jax.ShapeDtypeStruct(part, jnp.bfloat16),
            jax.ShapeDtypeStruct(part, jnp.bfloat16),
        ),
        in_specs=[SMEM_SPEC] + [VMEM_SPEC] * 2 + [ANY_SPEC] * 2 + [VMEM_SPEC] * (len(query) + 3),
        out_specs=(ANY_SPEC, ANY_SPEC, ANY_SPEC),
        scratch_shapes=[
            *[pltpu.VMEM(own.shape, jnp.bfloat16)] * 2,
            pltpu.VMEM(part, jnp.bfloat16),
            pltpu.VMEM(part, jnp.bfloat16),
            pltpu.VMEM((groups * per_group, HEAD, rows), jnp.bfloat16),
            pltpu.VMEM((keys, HEAD + DOC_SLOTS), jnp.bfloat16),
            pltpu.VMEM((keys, 2 * HEAD), jnp.bfloat16),
            pltpu.VMEM((HEAD, keys), jnp.bfloat16),
            pltpu.VMEM((keys, 2 * HEAD), jnp.float32),
            pltpu.SemaphoreType.DMA((blocks // 2, 2)),
            pltpu.SemaphoreType.DMA((blocks, 2)),
            pltpu.SemaphoreType.DMA((groups,)),
        ],
        compiler_params=pltpu.CompilerParams(vmem_limit_bytes=VMEM_BYTES),
        cost_estimate=cost(microseconds),
        name=name,
    )(meta, docs, bounds, own, other, *query, grad, mixed, lse)


def gelu_parts(value):
    scale = (2.0 / math.pi) ** 0.5
    square = value * value
    bent = jnp.tanh(scale * value * (1.0 + 0.044715 * square))
    upper = 0.5 * (1.0 + bent)
    slope = 0.5 * value * (1.0 - bent * bent) * scale * (1.0 + 3 * 0.044715 * square)
    return value * upper, upper + slope


def column_norm(values, gain, shift):
    row_mean = jnp.mean(values, axis=0, keepdims=True)
    centered = values - row_mean
    variance = jnp.mean(centered * centered, axis=0, keepdims=True)
    inverse = lax.rsqrt(variance + EPSILON)
    normed = centered * inverse
    return (normed * gain + shift, normed, inverse)


def column_norm_back(grad, normed, inverse, gain):
    scaled = grad * gain
    return inverse * (
        scaled
        - jnp.mean(scaled, axis=0, keepdims=True)
        - normed * jnp.mean(scaled * normed, axis=0, keepdims=True)
    )


def fetched(refs, places, semaphores):
    copies = [
        pltpu.make_async_copy(ref, place, semaphores.at[i])
        for i, (ref, place) in enumerate(zip(refs, places))
    ]
    for copy in copies:
        copy.start()
    return copies


def half_rows(core, half):
    return (
        pl.ds(pl.multiple_of(core * half, 32), half),
        pl.ds(pl.multiple_of((1 - core) * half, 32), half),
    )


def ahead_kernel(
    tile, core_ref, mask_ref, cotangent_ref, b_down_ref, *refs
):
    remote, (active_grad_ref, down_grad_ref), refs = refs[:3], refs[3:5], refs[5:]
    down_w_ref, a_down_ref, place_ref, semaphores, out_semaphores = refs
    half, wide = remote[0].shape
    sides = half_rows(core_ref[0], half)
    spots = [slice(k, min(k + tile, wide)) for k in range(0, wide, tile)]
    copies = []
    for k, spot in enumerate(spots):
        pairs = [(remote[i].at[:, spot], down_w_ref.at[sides[i], spot]) for i in range(2)]
        pairs += [(remote[2].at[spot, :], a_down_ref.at[spot, :])]
        for i, (source, place) in enumerate(pairs):
            copies.append(pltpu.make_async_copy(source, place, semaphores.at[k, i]))
    for copy in copies:
        copy.start()
    rows = cotangent_ref[...].T
    down_grad = dot(rows, b_down_ref[...]).astype(jnp.bfloat16) * mask_ref[...].astype(jnp.bfloat16)
    down_grad_ref[...] = down_grad
    given = []
    for k, spot in enumerate(spots):
        for copy in copies[3 * k : 3 * k + 3]:
            copy.wait()
        grad = dot(rows, down_w_ref[:, spot]) + dot(down_grad, a_down_ref[spot, :].T)
        place_ref[:, spot] = grad
        given.append(
            pltpu.make_async_copy(place_ref.at[:, spot], active_grad_ref.at[:, spot], out_semaphores.at[k])
        )
        given[-1].start()
    for copy in given:
        copy.wait()


def ahead_part(core, mask, cotangent_t, b_down_t, down_pair_t, a_down):
    width, rows = cotangent_t.shape
    wide, inner = a_down.shape
    tile = 1024
    count = -(-wide // tile)
    return pl.pallas_call(
        functools.partial(ahead_kernel, tile),
        out_shape=(
            jax.ShapeDtypeStruct((rows, wide), jnp.float32),
            jax.ShapeDtypeStruct((rows, inner), jnp.bfloat16),
        ),
        in_specs=[SMEM_SPEC] + [VMEM_SPEC] * 3 + [ANY_SPEC] * 3,
        out_specs=(ANY_SPEC, VMEM_SPEC),
        scratch_shapes=[
            pltpu.VMEM((width, wide), jnp.bfloat16),
            pltpu.VMEM((wide, inner), jnp.bfloat16),
            pltpu.VMEM((rows, wide), jnp.float32),
            pltpu.SemaphoreType.DMA((count, 3)),
            pltpu.SemaphoreType.DMA((count,)),
        ],
        compiler_params=pltpu.CompilerParams(vmem_limit_bytes=VMEM_BYTES),
        cost_estimate=cost(1),
        name="ahead_part",
    )(core, mask, cotangent_t, b_down_t, *down_pair_t, a_down)


def middle_kernel(
    tile, core_ref, *refs
):
    sources, remote, results, (kept_ref, sent_ref), places, result_places, refs = (
        refs[:11], refs[11:20], refs[20:24], refs[24:26], refs[26:37], refs[37:41], refs[41:],
    )
    (
        mixed_main_ref, mixed_last_ref, mask_ref, a_out_ref, b_out_ref, stream_ref, gains_ref,
        a_up_ref, down_grad_ref, cotangent_ref, b_down_ref,
    ) = places
    output_ref, middle_grad_ref, main_grad_ref, last_grad_ref = result_places
    (
        out_ref, up_ref, b_up_ref, down_w_ref, a_down_ref, kept_place, sent_place,
        active_grad_ref, mixed_ref, middle_ref, hidden_ref, hidden_rows_ref, inner_out_ref,
        inner_up_ref, inner_down_ref, up_grad_ref, down_ref, back_ref,
        semaphores, out_semaphores, place_semaphores, result_semaphores,
    ) = refs
    core = core_ref[0]
    half, wide = remote[2].shape
    width = 2 * half
    full = wide // tile
    low = jnp.bfloat16
    sides = half_rows(core, half)

    def copies(first, size, number):
        spot = pl.ds(first, size)
        pairs = [(remote[2 + i].at[:, spot], up_ref.at[sides[i], spot]) for i in range(2)]
        pairs += [(remote[5 + i].at[:, spot], down_w_ref.at[sides[i], spot]) for i in range(2)]
        pairs += [(remote[4].at[:, spot], b_up_ref.at[:, spot])]
        pairs += [(remote[7].at[spot, :], a_down_ref.at[spot, :])]
        pairs += [(remote[8].at[:, spot], active_grad_ref.at[:, spot])]
        return [
            pltpu.make_async_copy(source, place, semaphores.at[number, i])
            for i, (source, place) in enumerate(pairs)
        ]

    firsts = [
        pltpu.make_async_copy(remote[i], out_ref.at[sides[i], :], semaphores.at[full + 1, i])
        for i in range(2)
    ]
    given = fetched(sources[:4], places[:4], place_semaphores)
    for copy in firsts:
        copy.start()
    later = [
        pltpu.make_async_copy(sources[i], places[i], place_semaphores.at[i]) for i in range(4, 11)
    ]
    for copy in later:
        copy.start()

    def give(i):
        copy = pltpu.make_async_copy(result_places[i], results[i], result_semaphores.at[i])
        copy.start()
        return copy

    def start_chunk(k):
        @pl.when(k < full)
        def _():
            for copy in copies(pl.multiple_of(k * tile, tile), tile, k):
                copy.start()

        if wide % tile:

            @pl.when(k == full)
            def _():
                for copy in copies(full * tile, wide % tile, full):
                    copy.start()

    def out_copies(first, size, number):
        spot = pl.ds(first, size)
        pairs = ((kept_place, kept_ref), (sent_place, sent_ref))
        return [
            pltpu.make_async_copy(place.at[spot, :], ref.at[spot, :], out_semaphores.at[number, i])
            for i, (place, ref) in enumerate(pairs)
        ]

    def put(first, rows, other):
        spot = pl.ds(first, rows.shape[0])

        @pl.when(core == 0)
        def _():
            kept_place[spot, :] = rows
            sent_place[spot, :] = other

        @pl.when(core == 1)
        def _():
            kept_place[spot, :] = other
            sent_place[spot, :] = rows

    for copy in given[:4]:
        copy.wait()
    mask = mask_ref[...]
    mask_low = mask.astype(low)
    main = mixed_main_ref.shape[0] * HEAD
    mixed_ref[:main, :] = mixed_main_ref[...].reshape(main, mixed_main_ref.shape[2])
    mixed_ref[main:, :] = mixed_last_ref[0]
    mixed_rows = mixed_ref[...].T
    inner_out = (mask * (dot(mixed_rows, a_out_ref[...]))).astype(low)
    inner_out_ref[...] = inner_out
    for copy in (*firsts, *later):
        copy.wait()
    start_chunk(0)
    start_chunk(1)
    branch = dot(mixed_rows, out_ref[...]).T + dot(b_out_ref[...], inner_out.T)
    middle = stream_ref[...].astype(jnp.float32) + branch
    middle_ref[...] = middle
    hidden = column_norm(middle, gains_ref[:, 2:3], gains_ref[:, 3:4])[0].astype(low)
    hidden_ref[...] = hidden
    hidden_rows = hidden.T
    hidden_rows_ref[...] = hidden_rows
    inner_up_ref[...] = (mask * dot(hidden_rows, a_up_ref[...])).astype(low)
    for ref in (inner_down_ref, up_grad_ref, down_ref, back_ref):
        ref[...] = jnp.zeros(ref.shape, ref.dtype)

    def step(k, size):
        first = k * tile if isinstance(k, int) else pl.multiple_of(k * tile, tile)
        for copy in copies(first, size, k):
            copy.wait()
        start_chunk(k + 2)
        spot = pl.ds(first, size)
        up, b_up, down_w, a_down = up_ref[:, spot], b_up_ref[:, spot], down_w_ref[:, spot], a_down_ref[spot, :]
        inner_up, down_grad = inner_up_ref[...], down_grad_ref[...]
        upward = dot(hidden_rows_ref[...], up) + dot(inner_up, b_up)
        active, slope = gelu_parts(upward)
        active = active.astype(low)
        up_grad = (active_grad_ref[:, spot] * slope).astype(low)
        active_t, up_grad_t = active.T, up_grad.T
        down_ref[...] += dot(down_w, active_t)
        back_ref[...] += dot(up, up_grad_t)
        inner_down_ref[...] += dot(active, a_down)
        up_grad_ref[...] += dot(b_up, up_grad_t)
        put(first, dot(up_grad_t, inner_up).astype(low), dot(active_t, down_grad).astype(low))
        for copy in out_copies(first, size, k):
            copy.start()

    def loop(k, carry):
        step(k, tile)
        return carry

    lax.fori_loop(0, full, loop, 0)
    if wide % tile:
        step(full, wide % tile)

    inner_down = (mask * inner_down_ref[...]).astype(low)
    middle = middle_ref[...]
    inner_grad = up_grad_ref[...].astype(low).T * mask_low
    hidden_grad = back_ref[...] + dot(a_up_ref[...], inner_grad.T)
    gain = gains_ref[:, 2:3]
    _, normed, inverse = column_norm(middle, gain, gain)
    middle_grad = cotangent_ref[...].astype(jnp.float32)
    middle_grad = middle_grad + column_norm_back(hidden_grad, normed, inverse, gain)
    middle_grad_ref[...] = middle_grad
    given = [give(1)]
    branch = middle_grad.astype(low)
    out_grad = dot(branch.T, b_out_ref[...]).astype(low) * mask_low
    put(wide, dot(cotangent_ref[...], inner_down).astype(low), dot(mixed_ref[...], out_grad).astype(low))
    put(
        wide + width,
        dot(hidden_ref[...], inner_grad).astype(low),
        dot(branch, inner_out_ref[...]).astype(low),
    )
    narrow = kept_place.shape[0] - wide
    spare = narrow - 2 * width
    if spare:
        nothing = jnp.zeros((spare, kept_place.shape[1]), low)
        put(wide + 2 * width, nothing, nothing)
    for copy in out_copies(wide, narrow, full + 1):
        copy.start()
    back = (dot(out_ref[...], branch) + dot(a_out_ref[...], out_grad.T)).astype(low)
    main_grad_ref[...] = back[:main].reshape(main_grad_ref.shape)
    last_grad_ref[0] = back[main:]
    given += [give(2), give(3)]
    down = down_ref[...] + dot(b_down_ref[...], inner_down.T)
    output_ref[...] = (middle + down).astype(low)
    given += [give(0)]

    def finished(k, carry):
        for copy in out_copies(pl.multiple_of(k * tile, tile), tile, k):
            copy.wait()
        return carry

    lax.fori_loop(0, full, finished, 0)
    if wide % tile:
        for copy in out_copies(full * tile, wide % tile, full):
            copy.wait()
    for copy in (*out_copies(wide, narrow, full + 1), *given):
        copy.wait()


def padded(size, unit):
    return -(-size // unit) * unit


def middle_part(
    core, mixed_main, mixed_last, tokens_t, cotangent_t, mask, gains_t, out_pair, a_out, b_out_t,
    a_up, b_down_t, up_pair, b_up, down_pair_t, a_down, active_grad, down_grad, unit,
):
    width, rows = tokens_t.shape
    half = width // 2
    inner, wide = b_up.shape
    tile = 1024
    low = jnp.bfloat16
    operands = (
        mixed_main, mixed_last, mask, a_out, b_out_t, tokens_t, gains_t, a_up, down_grad,
        cotangent_t, b_down_t,
    )
    remote = (*out_pair, *up_pair, b_up, *down_pair_t, a_down, active_grad)
    share = (padded(wide + 2 * width, unit), inner)
    shapes = (
        ((width, rows), low), ((width, rows), jnp.float32), (mixed_main.shape, low),
        (mixed_last.shape, low), (share, low), (share, low),
    )
    return pl.pallas_call(
        functools.partial(middle_kernel, tile),
        out_shape=tuple(jax.ShapeDtypeStruct(*item) for item in shapes),
        in_specs=[SMEM_SPEC] + [ANY_SPEC] * (len(operands) + len(remote)),
        out_specs=(ANY_SPEC,) * 6,
        scratch_shapes=[
            *[pltpu.VMEM(item.shape, item.dtype) for item in operands],
            *[pltpu.VMEM(*item) for item in shapes[:4]],
            pltpu.VMEM((width, width), low),
            pltpu.VMEM((width, wide), low),
            pltpu.VMEM((inner, wide), low),
            pltpu.VMEM((width, wide), low),
            pltpu.VMEM((wide, inner), low),
            *[pltpu.VMEM(share, low)] * 2,
            pltpu.VMEM((rows, wide), jnp.float32),
            pltpu.VMEM((width, rows), low),
            pltpu.VMEM((width, rows), jnp.float32),
            pltpu.VMEM((width, rows), low),
            pltpu.VMEM((rows, width), low),
            *[pltpu.VMEM((rows, inner), low)] * 2,
            pltpu.VMEM((rows, inner), jnp.float32),
            pltpu.VMEM((inner, rows), jnp.float32),
            *[pltpu.VMEM((width, rows), jnp.float32)] * 2,
            pltpu.SemaphoreType.DMA((wide // tile + 2, 7)),
            pltpu.SemaphoreType.DMA((wide // tile + 2, 2)),
            pltpu.SemaphoreType.DMA((len(operands),)),
            pltpu.SemaphoreType.DMA((4,)),
        ],
        compiler_params=pltpu.CompilerParams(vmem_limit_bytes=VMEM_BYTES),
        cost_estimate=cost(20),
        name="middle_part",
    )(core, *operands, *remote)


def whole_call(kernel, shapes, scratch, operands, remote, microseconds, name):
    space = [pltpu.VMEM(item.shape, item.dtype) for item in remote]
    return pl.pallas_call(
        kernel,
        out_shape=tuple(jax.ShapeDtypeStruct(*item) for item in shapes),
        in_specs=[SMEM_SPEC]
        + [VMEM_SPEC] * (len(operands) - 1)
        + [pl.BlockSpec(memory_space=pl.ANY)] * len(remote),
        out_specs=(VMEM_SPEC,) * len(shapes),
        scratch_shapes=[pltpu.VMEM(*item) for item in scratch]
        + space
        + ([pltpu.SemaphoreType.DMA((len(remote),))] if remote else []),
        compiler_params=pltpu.CompilerParams(vmem_limit_bytes=VMEM_BYTES if len(remote) > 2 else SMALL_BYTES),
        cost_estimate=cost(microseconds),
        name=name,
    )(*operands, *remote)


def entry_kernel(
    place_ref, lengths_ref, adapters_ref, tokens_ref, gains_own_ref, gains_other_ref, *refs
):
    remote, results, refs = refs[:12], refs[12:19], refs[19:]
    places, (weight_ref, up_ref, down_ref, semaphores, result_semaphores) = refs[:7], refs[7:]
    hidden_ref, inner_ref, mask_ref, gains_ref, heads_ref, query_ref, pairs_ref = places
    rows, inner = mask_ref.shape
    half = gains_own_ref.shape[1]
    sides = half_rows(place_ref[0], half)
    copies = []
    for n in range(3):
        down, own, up, other = remote[4 * n : 4 * n + 4]
        pairs = (
            (down, down_ref.at[n]), (up, up_ref.at[n]),
            (own, weight_ref.at[n, sides[0], :]), (other, weight_ref.at[n, sides[1], :]),
        )
        for i, (source, place) in enumerate(pairs):
            copies.append(pltpu.make_async_copy(source, place, semaphores.at[4 * n + i]))
    for copy in copies:
        copy.start()

    def give(i):
        copy = pltpu.make_async_copy(places[i], results[i], result_semaphores.at[i])
        copy.start()
        return copy

    for spot, ref in zip(sides, (gains_own_ref, gains_other_ref)):
        gains_ref[spot, :] = ref[...].astype(jnp.float32).T
    values = tokens_ref[...].astype(jnp.float32)
    hidden = column_norm(values, gains_ref[:, 0:1], gains_ref[:, 1:2])[0].astype(jnp.bfloat16)
    hidden_ref[...] = hidden
    hidden_rows = hidden.T
    place = place_ref[1] + lax.broadcasted_iota(jnp.int32, (rows, inner), 0)
    column = lax.broadcasted_iota(jnp.int32, (rows, inner), 1) // RANK

    def document(d, state):
        start, mask = state
        end = start + lengths_ref[d]
        chosen = (place >= start) & (place < end) & (column == adapters_ref[d])
        return end, jnp.where(chosen, 1.0, mask)

    state = (jnp.int32(0), jnp.zeros((rows, inner), jnp.float32))
    _, mask = lax.fori_loop(0, lengths_ref.shape[0], document, state)
    mask_ref[...] = mask
    given = [give(0), give(2), give(3)]
    count = heads_ref.shape[0]

    def give_part(n):
        spot = pl.ds(n * HEAD, HEAD)
        copy = pltpu.make_async_copy(
            heads_ref.at[:, spot, :], results[4].at[:, spot, :], result_semaphores.at[7 + n]
        )
        copy.start()
        return copy

    for n in range(3):
        for copy in copies[4 * n : 4 * n + 4]:
            copy.wait()
        products = (mask * dot(hidden_rows, down_ref[n])).astype(jnp.bfloat16)
        inner_ref[n] = products
        total = dot(hidden_rows, weight_ref[n]).T + dot(up_ref[n], products.T)
        total = total.astype(jnp.bfloat16)
        for c in range(count):
            heads_ref[c, n * HEAD : (n + 1) * HEAD, :] = total[c * HEAD : (c + 1) * HEAD]
        if n == 0:
            query_ref[0] = total[count * HEAD :]
        else:
            for c in range(count):
                pairs_ref[c, (n - 1) * HEAD : n * HEAD, :] = total[count * HEAD :]
        given.append(give_part(n))
    for copy in (*given, *[give(i) for i in (1, 5, 6)]):
        copy.wait()


def projections(place, lengths, adapters, tokens_t, gains, gains_other, weights, others, downs, ups_t):
    width, rows = tokens_t.shape
    inner = downs[0].shape[1]
    low = jnp.bfloat16
    count = width // HEAD - 1
    remote = [item for group in zip(downs, weights, ups_t, others) for item in group]
    shapes = (
        ((width, rows), low), ((3, rows, inner), low), ((rows, inner), jnp.float32),
        ((width, gains.shape[0]), jnp.float32), ((count, 3 * HEAD, rows), low),
        ((1, HEAD, rows), low), ((count, 2 * HEAD, rows), low),
    )
    return pl.pallas_call(
        entry_kernel,
        out_shape=tuple(jax.ShapeDtypeStruct(*item) for item in shapes),
        in_specs=[SMEM_SPEC] * 3 + [VMEM_SPEC] * 3 + [ANY_SPEC] * len(remote),
        out_specs=(ANY_SPEC,) * len(shapes),
        scratch_shapes=[pltpu.VMEM(*item) for item in shapes]
        + [
            pltpu.VMEM((3, width, width), low),
            pltpu.VMEM((3, width, inner), low),
            pltpu.VMEM((3, width, inner), low),
            pltpu.SemaphoreType.DMA((12,)),
            pltpu.SemaphoreType.DMA((len(shapes) + 3,)),
        ],
        compiler_params=pltpu.CompilerParams(vmem_limit_bytes=VMEM_BYTES),
        cost_estimate=cost(6),
        name="entry",
    )(place, lengths, adapters, tokens_t, gains, gains_other, *remote)


def gathered_grad(n, heads_ref, last_query_ref, last_pair_ref, grad_ref):
    count = heads_ref.shape[0]
    for c in range(count):
        grad_ref[c * HEAD : (c + 1) * HEAD, :] = heads_ref[c, n * HEAD : (n + 1) * HEAD, :]
    if n == 0:
        grad_ref[count * HEAD :, :] = last_query_ref[0]
    else:
        grad_ref[count * HEAD :, :] = last_pair_ref[...].T[(n - 1) * HEAD : n * HEAD]
    return grad_ref[...]


def projections_late_kernel(core_ref, *refs):
    sources, (kept_ref, sent_ref, inner_grad_ref), refs = refs[:9], refs[9:12], refs[12:]
    places, (kept_place, sent_place, grad_ref, semaphores, out_semaphores) = refs[:9], refs[9:]
    heads_ref, last_query_ref, last_pair_ref, mask_ref, hidden_ref, inner_ref, *ups = places
    copies = fetched(sources, places, semaphores)
    core = core_ref[0]
    low = jnp.bfloat16
    width, share = hidden_ref.shape[0], kept_place.shape[0]

    def store(side, spot, rows):
        @pl.when(core == side)
        def _():
            kept_place[spot, :] = rows

        @pl.when(core != side)
        def _():
            sent_place[spot, :] = rows

    def keep(first, rows):
        done = 0
        while done < rows.shape[0]:
            side, spot = divmod(first + done, share)
            size = min(rows.shape[0] - done, share - spot)
            store(side, slice(spot, spot + size), rows[done : done + size])
            done += size

    keep(6 * width, jnp.zeros((2 * share - 6 * width, kept_place.shape[1]), low))
    given = [
        pltpu.make_async_copy(place, ref, out_semaphores.at[i])
        for i, (place, ref) in enumerate(((kept_place, kept_ref), (sent_place, sent_ref)))
    ]
    turned = []
    for copy, up in zip(copies[6:], ups):
        copy.wait()
        turned.append(up[...].T)
    for copy in copies[:6]:
        copy.wait()
    mask_low = mask_ref[...].astype(low)
    hidden = hidden_ref[...]
    for n in range(3):
        grad = gathered_grad(n, heads_ref, last_query_ref, last_pair_ref, grad_ref)
        inner_grad = dot(turned[n], grad).astype(low).T * mask_low
        inner_grad_ref[n] = inner_grad
        keep(2 * n * width, dot(hidden, inner_grad).astype(low))
        keep((2 * n + 1) * width, dot(grad, inner_ref[n]).astype(low))
        if n == 1:
            for side in range(2):
                pl.when(core == side)(given[side].start)
    for side in range(2):
        pl.when(core != side)(given[side].start)
    for copy in given:
        copy.wait()


def projections_late(core, heads, last_query, last_pair, hidden_t, inners, mask, ups_t, unit):
    width, rows = hidden_t.shape
    low = jnp.bfloat16
    share = (padded(6 * width, 2 * unit) // 2, mask.shape[1])
    operands = (heads, last_query, last_pair, mask, hidden_t, inners, *ups_t)
    return pl.pallas_call(
        projections_late_kernel,
        out_shape=(
            jax.ShapeDtypeStruct(share, low),
            jax.ShapeDtypeStruct(share, low),
            jax.ShapeDtypeStruct(inners.shape, low),
        ),
        in_specs=[SMEM_SPEC] + [ANY_SPEC] * len(operands),
        out_specs=(ANY_SPEC, ANY_SPEC, VMEM_SPEC),
        scratch_shapes=[pltpu.VMEM(item.shape, item.dtype) for item in operands]
        + [
            pltpu.VMEM(share, low),
            pltpu.VMEM(share, low),
            pltpu.VMEM((width, rows), low),
            pltpu.SemaphoreType.DMA((len(operands),)),
            pltpu.SemaphoreType.DMA((2,)),
        ],
        compiler_params=pltpu.CompilerParams(vmem_limit_bytes=VMEM_BYTES),
        cost_estimate=cost(5),
        name="projections_late",
    )(core, *operands)


def projections_back_kernel(
    core_ref, heads_ref, last_query_ref, last_pair_ref, inner_grad_ref, gains_ref, tokens_ref, *refs
):
    remote, (grad_in_ref, grad_ref, sum_ref), local_refs, semaphores = (
        refs[:10], refs[10:13], refs[13:23], refs[23],
    )
    copies = fetched(remote, local_refs, semaphores)
    downs, weights, others, middle_grad_ref = (
        local_refs[:3], local_refs[3:6], local_refs[6:9], local_refs[9],
    )
    own_rows, other_rows = half_rows(core_ref[0], weights[0].shape[0])
    for n in range(3):
        grad = gathered_grad(n, heads_ref, last_query_ref, last_pair_ref, grad_ref)
        turned = inner_grad_ref[n].T
        copies[n].wait()
        for rows, weight, copy in (
            (own_rows, weights[n], copies[3 + n]), (other_rows, others[n], copies[6 + n])
        ):
            copy.wait()
            part = dot(weight[...], grad) + dot(downs[n][rows, :], turned)
            sum_ref[rows, :] = part if n == 0 else sum_ref[rows, :] + part
    gain = gains_ref[:, 0:1]
    _, normed, inverse = column_norm(tokens_ref[...].astype(jnp.float32), gain, gain)
    back = column_norm_back(sum_ref[...], normed, inverse, gain)
    copies[9].wait()
    grad_in_ref[...] = (middle_grad_ref[...] + back).astype(jnp.bfloat16)


def projections_back(
    core, heads, last_query, last_pair, inner_grads, gains_t, tokens_t, middle_grad_t,
    weights, others, downs,
):
    width, rows = tokens_t.shape
    low = jnp.bfloat16
    return whole_call(
        projections_back_kernel,
        (((width, rows), low),),
        (((width, rows), low), ((width, rows), jnp.float32)),
        (core, heads, last_query, last_pair, inner_grads, gains_t, tokens_t),
        (*downs, *weights, *others, middle_grad_t),
        8, "projections_back",
    )[0]


def steps_of(cycle_size):
    bits = cycle_size.bit_length() - 1
    return [(bit, min(2, bits - bit)) for bit in range(0, bits, 2)]


def partners(cycle_size, step, k):
    return [(i, i ^ (k << step[0])) for i in range(cycle_size)]


def scattered(array, step, cycle_size):
    count = 1 << step[1]
    mine = (lax.axis_index("ctx") >> step[0]) & (count - 1)
    blocks = array.reshape(count, array.shape[0] // count, array.shape[1])

    def block(number):
        return lax.dynamic_index_in_dim(blocks, number, 0, keepdims=False)

    total = block(mine).astype(jnp.float32)
    for k in range(1, count):
        got = lax.ppermute(block(mine ^ k), "ctx", partners(cycle_size, step, k))
        total = total + got.astype(jnp.float32)
    return total.astype(array.dtype)


def collected(share, step, cycle_size):
    count = 1 << step[1]
    mine = (lax.axis_index("ctx") >> step[0]) & (count - 1)
    blocks = [share]
    for k in range(1, count):
        blocks.append(lax.ppermute(share, "ctx", partners(cycle_size, step, k)))
    for bit in range(step[1]):
        turned = ((mine >> bit) & 1) == 1
        blocks = [jnp.where(turned, blocks[k ^ (1 << bit)], blocks[k]) for k in range(count)]
    return jnp.concatenate(blocks, axis=0)


def pair_sum(kept, sent):
    return kept + lax.ppermute(sent, "wsh", SWAP)


def early_finish_kernel(
    factor, core_ref, own_source, other_source,
    b_up_ref, a_down_ref, b_down_ref, a_up_ref, a_out_ref, b_out_ref, own_ref, other_ref, semaphores,
):
    for copy in fetched((own_source, other_source), (own_ref, other_ref), semaphores):
        copy.wait()
    wide, width = a_down_ref.shape[0], a_up_ref.shape[0]

    def finish(first_ref, second_ref):
        def part(ref, first, count):
            return ref[first : first + count, :].astype(jnp.float32) * factor

        for k in range(wide // 256):
            b_up_ref[:, k * 256 : (k + 1) * 256] = part(first_ref, k * 256, 256).T
        a_down_ref[...] = part(second_ref, 0, wide)
        b_down_ref[...] = part(first_ref, wide, width)
        a_up_ref[...] = part(first_ref, wide + width, width)
        a_out_ref[...] = part(second_ref, wide, width)
        b_out_ref[...] = part(second_ref, wide + width, width)

    @pl.when(core_ref[0] == 0)
    def _():
        finish(own_ref, other_ref)

    @pl.when(core_ref[0] == 1)
    def _():
        finish(other_ref, own_ref)


def late_finish_kernel(factor, core_ref, own_ref, other_ref, *refs):
    core = core_ref[0]
    targets, late_ref, own_place, other_place, semaphores = refs[:6], *refs[6:]
    places = (own_place, other_place)
    copies = fetched((own_ref, other_ref), places, semaphores)
    for side, ref, copy in zip((core, 1 - core), places, copies):
        copy.wait()
        late_ref[side] = ref[...].astype(jnp.float32) * factor
    width, share = targets[0].shape[0], late_ref.shape[1]
    for n, ref in enumerate(targets):
        done = 0
        while done < width:
            side, spot = divmod(n * width + done, share)
            rows = min(width - done, share - spot)
            ref[done : done + rows, :] = late_ref[side, spot : spot + rows, :]
            done += rows


def finished(kernel, factor, core, own, other, shapes, scratch, name):
    return whole_call(
        functools.partial(kernel, factor), [(shape, jnp.float32) for shape in shapes], scratch,
        (core,), (own, other), 1, name,
    )


def local(
    tokens_in,
    doc_lengths,
    doc_adapter,
    norm1_gain,
    norm1_bias,
    norm2_gain,
    norm2_bias,
    w_query,
    w_key,
    w_value,
    w_out,
    w_up,
    w_down,
    a_query,
    b_query,
    a_key,
    b_key,
    a_value,
    b_value,
    a_out,
    b_out,
    a_up,
    b_up,
    a_down,
    b_down,
    cotangent,
):
    group_size = lax.axis_size("wsh")
    cycle_size = lax.axis_size("ctx")
    tok_dev, width_all = tokens_in.shape
    head_count = width_all // HEAD
    block_len = tok_dev * group_size
    hop_count = (DOC_MAX + block_len - 2) // block_len
    span = head_count - 1
    cycle_pos = lax.axis_index("ctx")
    core = lax.axis_index("wsh")
    half = width_all // group_size

    first_row = cycle_pos * block_len + core * tok_dev
    doc_ends = jnp.cumsum(doc_lengths)
    doc_starts = doc_ends - doc_lengths

    team = cycle_pos // span
    past = hop_count if cycle_size > span else 0
    first_key = (team * span - past) * block_len
    key_blocks = past + span

    slots = DOC_SLOTS - doc_lengths.shape[0]
    bounds = jnp.stack([jnp.pad(doc_starts, (0, slots)), jnp.pad(doc_ends, (0, slots))])

    def plan(chunk_pos, pair_at, first_chunk, per_group):
        groups = chunk_pos.shape[0] // per_group
        row_pos = chunk_pos[:, None] + jnp.arange(tok_dev, dtype=jnp.int32)[None, :]
        row_docs = jnp.sum((doc_ends[None, None, :] <= row_pos[:, :, None]).astype(jnp.int32), axis=2)
        row_docs = row_docs.reshape(groups, 1, per_group * tok_dev)
        chunk_pos = chunk_pos.reshape(groups, per_group)
        began = jnp.where(doc_starts[None, None, :] <= chunk_pos[:, :, None], doc_starts[None, None, :], 0)
        began = (jnp.max(began, axis=2) - first_key) // (2 * block_len)
        first = began[:, 0]
        last = (chunk_pos[:, -1] - first_key) // (2 * block_len)
        same = jnp.ones((groups,), jnp.int32)
        whole = per_group > 1
        meta = [
            first,
            last,
            chunk_pos[:, 0],
            same * core,
            same * first_key,
            jnp.concatenate([first[:1] * 0, last[:-1] + 1]) if whole else first,
            began[:, -1],
        ]
        meta = jnp.stack(meta, axis=1).astype(jnp.int32)
        docs = row_docs.astype(jnp.int32)
        return meta, docs, bounds.astype(jnp.int32), pair_at, first_chunk, per_group

    team_pos = (team * span + jnp.arange(span, dtype=jnp.int32)) * block_len + core * tok_dev
    main_plan = plan(team_pos.astype(jnp.int32), HEAD, past, 2)
    last_plan = plan(first_row[None].astype(jnp.int32), 0, 0, 1)

    def swap(array):
        return lax.ppermute(array, "wsh", SWAP)

    if cycle_size > span:
        teams = [[t * span + i for i in range(span)] for t in range(cycle_size // span)]
    else:
        teams = None

    def exchange(blocks):
        return lax.all_to_all(blocks, "ctx", 0, 0, tiled=True, axis_index_groups=teams)

    gains = jnp.stack([norm1_gain, norm1_bias, norm2_gain, norm2_bias])
    weights = [w_query, w_key, w_value, w_out, w_up, w_down.T]
    others = [swap(item) for item in weights[:3]]
    gains_other = swap(gains)
    core_1 = jnp.stack([core, first_row]).astype(jnp.int32)
    *others, gains_other, w_late, core_1 = lax.optimization_barrier(
        (*others, gains_other, tuple(weights[3:]), core_1)
    )
    others = others + [swap(item) for item in w_late]

    downs = (a_query, a_key, a_value)
    ups_t = (b_query.T, b_key.T, b_value.T)
    tokens_t = tokens_in.T
    hidden_t, inners, adapter_mask, gains_t, heads, last_query, last_pairs = projections(
        core_1, doc_lengths, doc_adapter, tokens_t, gains, gains_other, weights[:3], others[:3],
        downs, ups_t,
    )

    ahead = [(i, i + span) for i in range(cycle_size - span)]
    back = [(i + span, i) for i in range(cycle_size - span)]

    def with_past(blocks):
        if not past:
            return blocks
        return jnp.concatenate([lax.ppermute(blocks[span - past :], "ctx", ahead), blocks], axis=0)

    steps = steps_of(cycle_size)
    unit = 16 * cycle_size
    incoming = exchange(heads)
    active_grad, down_grad = ahead_part(
        core_1, adapter_mask, cotangent.T, b_down.T, (w_down.T, others[5]), a_down
    )
    incoming, last_pairs, active_grad, ready = lax.optimization_barrier(
        (incoming, last_pairs, active_grad, main_plan[:3])
    )
    main_plan = (*ready, *main_plan[3:])
    own = with_past(incoming)
    other = swap(own)
    last_own = exchange(last_pairs)
    low_main, total_main, lse_main = attention_forward(
        main_plan, own, other, (), "attention_forward", 30
    )
    low_main, last_own = lax.optimization_barrier((low_main, last_own))
    last_own = with_past(last_own)
    last_other = swap(last_own)
    low_last, mixed_last, lse_last = attention_forward(
        last_plan, last_own, last_other, (last_query,), "last_forward", 0
    )
    mixed_main = exchange(low_main)

    output_t, middle_grad_t, main_grad, last_out_grad, early_kept, early_sent = middle_part(
        core_1, mixed_main, low_last, tokens_t, cotangent.T, adapter_mask, gains_t,
        (w_out, others[3]), a_out, b_out.T, a_up, b_down.T, (w_up, others[4]), b_up,
        (w_down.T, others[5]), a_down, active_grad, down_grad, unit,
    )

    def pair_total(kept, sent):
        total = kept.astype(jnp.float32) + swap(sent).astype(jnp.float32)
        if past:
            returned = lax.ppermute(total[:past].astype(jnp.bfloat16), "ctx", back)
            total = total[past:].at[span - past :].add(returned.astype(jnp.float32))
        return total

    def pair_back(dq, kept, sent):
        total = pair_total(kept, sent).astype(jnp.bfloat16)
        return lax.dynamic_update_slice(dq, total, (0, HEAD, 0))

    dq_last, kept_last, sent_last = attention_backward(
        last_plan, last_own, last_other, (last_query,),
        last_out_grad, mixed_last, lse_last, False, "last_backward", 0,
    )
    grad_main = exchange(main_grad)
    grad_main, dq_last, kept_last, sent_last = lax.optimization_barrier(
        (grad_main, dq_last, kept_last, sent_last)
    )
    dpair_last = pair_total(kept_last, sent_last).astype(jnp.bfloat16)
    plane = 1 << steps[0][1]
    lines = cycle_size // plane
    digits = (2,) * (cycle_size.bit_length() - 3) + (plane,)
    if cycle_size > span:
        zero = jnp.zeros((cycle_size // span, *dpair_last.shape), dpair_last.dtype)
        dpair_last = lax.dynamic_update_index_in_dim(zero, dpair_last, team, 0)
    order = tuple(reversed(range(len(digits)))) + (len(digits), len(digits) + 1)
    dpair_last = jnp.transpose(dpair_last.reshape(digits + dpair_last.shape[-2:]), order)
    early = pair_sum(early_kept, early_sent)
    lanes = early.shape[1]
    early_rows, last_rows = early.shape[0] // cycle_size, tok_dev
    early = early.reshape(plane, lines, early_rows, lanes)
    dpair_last = dpair_last.reshape(plane, lines, last_rows, lanes)

    def meant_for(k):
        parts = [lax.dynamic_index_in_dim(x, (cycle_pos % plane) ^ k, 0, False) for x in (early, dpair_last)]
        return jnp.concatenate(parts, axis=1)

    meant = [meant_for(k) for k in range(plane)]
    grad_main, *meant = lax.optimization_barrier((grad_main, *meant))
    shared = [meant[0]] + [
        lax.ppermute(meant[k], "ctx", partners(cycle_size, steps[0], k)) for k in range(1, plane)
    ]
    dq_main, kept_main, sent_main = attention_backward(
        main_plan, own, other, (), grad_main, total_main, lse_main,
        True, "attention_backward", 40
    )
    dq_main, kept_main, sent_main, *shared = lax.optimization_barrier(
        (dq_main, kept_main, sent_main, *shared)
    )
    shared = sum(part.astype(jnp.float32) for part in shared).astype(jnp.bfloat16)
    shared = shared.reshape(lines * (early_rows + last_rows), lanes)
    outgoing_back = pair_back(dq_main, kept_main, sent_main)
    outgoing_back, shared = lax.optimization_barrier((outgoing_back, shared))
    singles = [(bit, 1) for bit in range(2, cycle_size.bit_length() - 1)]
    shared = shared.reshape(lines, early_rows + last_rows, lanes)
    early = shared[:, :early_rows].reshape(lines * early_rows, lanes)
    last_sum = shared[:, early_rows:].reshape(lines * last_rows, lanes)
    incoming_back = exchange(outgoing_back)
    for step in singles:
        last_sum = scattered(last_sum, step, cycle_size)
    for step in singles:
        early = scattered(early, step, cycle_size)

    late_kept, late_sent, inner_grads = projections_late(
        core_1, incoming_back, dq_last, last_sum, hidden_t, inners, adapter_mask, ups_t, unit
    )
    singles = singles[::-1]
    late, early, inner_grads = lax.optimization_barrier(
        (pair_sum(late_kept, late_sent), early, inner_grads)
    )
    grad_in_t = projections_back(
        core_1, incoming_back, dq_last, last_sum, inner_grads, gains_t, tokens_t, middle_grad_t,
        weights[:3], others[:3], downs,
    )

    norm_factor = (tok_dev * group_size * cycle_size) ** (-0.5)
    late = scattered(late, steps[0], cycle_size)
    for step in singles:
        early = collected(early, step, cycle_size)
    late, early = lax.optimization_barrier((late, early))
    for step in steps[1:]:
        late = scattered(late, step, cycle_size)
    early = collected(early, steps[0], cycle_size)
    late, early, grad_in_t = lax.optimization_barrier((late, early, grad_in_t))
    early_other = swap(early)
    for step in reversed(steps[1:]):
        late = collected(late, step, cycle_size)
    late, early_other = lax.optimization_barrier((late, early_other))
    late = collected(late, steps[0], cycle_size)
    wide = b_up.shape[1]
    early = finished(
        early_finish_kernel, norm_factor, core_1, early, early_other,
        [(lanes, wide), (wide, lanes)] + [(width_all, lanes)] * 4, (), "early_finish",
    )
    late, early = lax.optimization_barrier((late, early))
    g_b_up, g_a_down, g_b_down, g_a_up, g_a_out, g_b_out = early
    late = finished(
        late_finish_kernel, norm_factor, core_1, late, swap(late), [(width_all, lanes)] * 6,
        (((2, *late.shape), jnp.float32),), "late_finish",
    )
    return (
        output_t.T,
        grad_in_t.T,
        late[0],
        late[1].T,
        late[2],
        late[3].T,
        late[4],
        late[5].T,
        g_a_out,
        g_b_out.T,
        g_a_up,
        g_b_up,
        g_a_down,
        g_b_down.T,
    )


def solution(mesh):
    return jax.shard_map(
        local,
        mesh=mesh,
        in_specs=(
            P(("ctx", "wsh"), None),
            P(),
            P(),
            P("wsh"),
            P("wsh"),
            P("wsh"),
            P("wsh"),
            P("wsh", None),
            P("wsh", None),
            P("wsh", None),
            P("wsh", None),
            P("wsh", None),
            P(None, "wsh"),
            P(),
            P(),
            P(),
            P(),
            P(),
            P(),
            P(),
            P(),
            P(),
            P(),
            P(),
            P(),
            P(("ctx", "wsh"), None),
        ),
        out_specs=(
            P(("ctx", "wsh"), None),
            P(("ctx", "wsh"), None),
            P(),
            P(),
            P(),
            P(),
            P(),
            P(),
            P(),
            P(),
            P(),
            P(),
            P(),
            P(),
        ),
        check_vma=False,
    )
```
